32 devices in a mesh: rows: 16 (over z, y, x), cols: 2 (over core).
Axes of the slice: x: 2, y: 2, z: 4, core: 2. Of those that a mesh axis runs over, the one named last changes fastest.
Arguments:
- node_features: bfloat16 [16384, 512], P('rows', 'cols'), may hold values from -6 to 6
- weight: bfloat16 [512, 512], replicated, may hold values from -0.25 to 0.25
- tile_values: bfloat16 [1024, 128, 128], P('rows'), may hold values from -0.1875 to 0.1875
- tile_row: int32 [1024], P('rows'), may hold values from 0 to 7
- source_owner: int32 [1024, 1], P('rows'), may hold values from 0 to 15; in each aligned block of 64 rows (0 to 63, 64 to 127, ...) at most 8 rows name the same one
- source_block: int32 [1024], P('rows'), may hold values from 0 to 7
- labels: int32 [16384], P('rows'), may hold values from 0 to 511
Outputs:
- activations: bfloat16 [16384, 512], P('rows', 'cols')
- weight_grad: float32 [512, 512], P(None, 'cols')
- feature_grad: bfloat16 [16384, 512], P('rows', 'cols')
The draws below stay inside these ranges and needn't reach their ends.
Inputs may be any that keep to these rules, and one draw needn't show every extreme that they name: `source_owner`: of the 64 tiles of one index of rows, at most 8 name the same owner.
All inputs are finite; a program needn't handle non-finite values.
Results may differ from the reference program's by a relative error of at most 0.0095.
Values may be sent and summed in bfloat16 or wider, within the bound.
No kernel may reach another device: no remote copies, remote signals or barrier semaphores. Data moves between devices by JAX's collectives and lax.ppermute only.
A program may use at most 128 MiB of HBM per device.

```python
import math
import jax
import jax.numpy as jnp
import numpy as np
from jax import lax

F = 512
BLK = 128
NB_DEV = 8
TILES_DEV = 64
CAP = 8
TILES = 1024
NBLK = 128
NODES = 16384
N_ROWS = 16


def touch_ends(entries, key, least, top_value):
    spot = [jax.random.randint(jax.random.fold_in(key, axis), (), 0, length) for axis, length in enumerate(entries.shape)]
    longest = entries.shape.index(max(entries.shape))
    neighbour = spot[:longest] + [(spot[longest] + 1) % entries.shape[longest]] + spot[longest + 1:]
    return entries.at[tuple(spot)].set(least).at[tuple(neighbour)].set(top_value)


def shard_levels(rng, shape, shards, low, largest):
    loudness, own = 1.0, jax.random.fold_in(rng, 6)
    for axis_at, blocks in shards:
        steps = jnp.exp(jax.random.uniform(jax.random.fold_in(own, axis_at), (blocks,), jnp.float32, low / len(shards), largest / len(shards)))
        loudness = loudness * jnp.repeat(steps, shape[axis_at] // blocks).reshape([-1 if axis == axis_at else 1 for axis in range(len(shape))])
    return loudness


def shared_out(own_key, own, number, rows, number_of, top, limit, lean):
    order = jax.random.permutation(own_key, number_of)
    crowded, usual = portions_of(number_of, rows * top, limit, lean, True), portions_of(number_of, rows * top, limit, lean, False)
    places = jnp.arange(number_of)

    def named(lengths, offset_by):
        used = int((lengths > 0).sum())
        fixed = max(1, used // 4)
        shifted = fixed + (places - fixed + offset_by * (used - fixed)) % max(1, number_of - fixed)
        return jnp.zeros((number_of,), jnp.int32).at[order[jnp.where(places < fixed, places, shifted)]].set(jnp.asarray(lengths, jnp.int32))

    lengths = jnp.where(number % 4 == 0, named(crowded, number // 4), named(usual, number - number // 4 - 1))
    mixed = jax.random.permutation(jax.random.fold_in(own, 3), number_of)
    donor, sink = mixed[0:number_of // 2 * 2:2], mixed[1:number_of // 2 * 2:2]
    slack = jnp.minimum(lengths[donor] - 1, limit - lengths[sink]) // 2
    slack = jnp.where((donor == order[0]) | (sink == order[0]) | (lengths[sink] == 0), 0, jnp.maximum(slack, 0))
    shifted = jax.random.randint(jax.random.fold_in(own, 4), (number_of // 2,), 0, 1 << 20) % (slack + 1)
    lengths = lengths.at[donor].add(-shifted).at[sink].add(shifted)
    members = jnp.searchsorted(jnp.cumsum(lengths), jnp.arange(rows * top), side="right").astype(jnp.int32)
    table = members.reshape(top, rows).T
    table = table[jax.random.permutation(jax.random.fold_in(own, 1), rows)]
    offset_by = jax.random.randint(jax.random.fold_in(own, 2), (rows, 1), 0, top)
    return jnp.take_along_axis(table, (jnp.arange(top)[None, :] + offset_by) % top, axis=1)


def portions_of(count, total, most, skew, full):
    portions = [(1 << 20) // math.isqrt(standing ** skew) + 1 for standing in range(1, count + 1)]
    largest = most if full else min(most, max(-(-total // count), total * portions[0] // sum(portions)))
    least = 1 if total - largest >= count - 1 else 0
    given, surplus = [largest] + [least] * (count - 1), total - largest - least * (count - 1)
    while surplus > 0:
        free = [i for i in range(1, count) if given[i] < largest] or [i for i in range(1, count) if given[i] < most]
        pool, left = sum([portions[i] for i in free]), surplus
        for i in free:
            addition = min(most - given[i], max(1, left * portions[i] // pool), surplus)
            given[i] = given[i] + addition
            surplus = surplus - addition
    return np.array(given)


def gaussian(own_key, extent, width, most, pieces=(), kind=jnp.bfloat16):
    values = width * jax.random.normal(own_key, extent, jnp.float32)
    if pieces:
        values = values * shard_levels(own_key, extent, pieces, -0.22, 0.18)
    return jnp.clip(values, -most, most).astype(kind)


def setup_inputs(seed: int = 0) -> dict:
    seeds = jax.random.split(jax.random.key(seed), 8)
    node_features = gaussian(seeds[0], (NODES, F), 1.0, 6.0, ((0, 16), (1, 2)))
    weight = gaussian(seeds[1], (F, F), F ** -0.5, 0.25)
    tile_values = gaussian(seeds[2], (TILES, BLK, BLK), (BLK * TILES_DEV // NB_DEV) ** -0.5, 0.1875, ((0, 16),))
    tile_row = touch_ends(jax.random.randint(seeds[3], (TILES,), 0, NB_DEV), jax.random.fold_in(seeds[3], 1), 0, NB_DEV - 1).astype(jnp.int32)
    source_owner_keys = jax.random.split(jax.random.fold_in(seeds[4], 1), TILES // TILES_DEV)
    source_owner_turns = jax.random.permutation(jax.random.fold_in(seeds[4], 3), TILES // TILES_DEV)
    source_owner = jax.vmap(lambda own, number: shared_out(jax.random.fold_in(seeds[4], 2), own, number, TILES_DEV, N_ROWS, 1, CAP, 2))(source_owner_keys, source_owner_turns).reshape((TILES, 1))
    source_block = touch_ends(jax.random.randint(seeds[5], (TILES,), 0, NB_DEV), jax.random.fold_in(seeds[5], 1), 0, NB_DEV - 1).astype(jnp.int32)
    labels = touch_ends(jax.random.randint(seeds[6], (NODES,), 0, F), jax.random.fold_in(seeds[6], 1), 0, F - 1).astype(jnp.int32)
    return {"node_features": node_features, "weight": weight, "tile_values": tile_values, "tile_row": tile_row, "source_owner": source_owner, "source_block": source_block, "labels": labels}


def reference(node_features, weight, tile_values, tile_row, source_owner, source_block, labels):
    feature_blocks = node_features.reshape(NBLK, BLK, F)
    device_ids = jnp.arange(N_ROWS, dtype=jnp.int32)
    block_ids = jnp.arange(NB_DEV, dtype=jnp.int32)
    tiles_grouped = tile_values.reshape(N_ROWS, TILES_DEV, BLK, BLK)
    rows_grouped = tile_row.astype(jnp.int32).reshape(N_ROWS, TILES_DEV)
    cols_grouped = (source_owner[:, 0] * NB_DEV + source_block).astype(jnp.int32).reshape(N_ROWS, TILES_DEV)

    def aggregate(group_data):
        tile_block, rows_here, cols_here = group_data
        gathered = feature_blocks[cols_here].astype(jnp.float32)
        products = jnp.einsum('tij,tjf->tif', tile_block.astype(jnp.float32), gathered, precision=lax.Precision.HIGHEST)
        onehot = (rows_here[:, None] == block_ids[None, :]).astype(jnp.float32)
        return jnp.einsum('tb,tif->bif', onehot, products, precision=lax.Precision.HIGHEST)
    summed = lax.map(aggregate, (tiles_grouped, rows_grouped, cols_grouped))
    aggregated = summed.reshape(NODES, F).astype(jnp.bfloat16)
    hidden = jnp.dot(aggregated, weight, preferred_element_type=jnp.float32)
    sigmoid = jax.nn.sigmoid(hidden)
    activated = hidden * sigmoid
    slopes = sigmoid * (1.0 + hidden * (1.0 - sigmoid))
    target = (labels[:, None] == jnp.arange(F, dtype=jnp.int32)[None, :]).astype(jnp.float32)
    out_grad = ((activated - target) * slopes).astype(jnp.bfloat16)
    weight_grad = jnp.dot(aggregated.T, out_grad, preferred_element_type=jnp.float32) / math.sqrt(NODES)
    agg_grad = jnp.dot(out_grad, weight.T, preferred_element_type=jnp.float32).astype(jnp.bfloat16)
    grad_blocks = agg_grad.reshape(NBLK, BLK, F)

    def spread(running, group_data):
        tile_block, rows_here, cols_here, device = group_data
        sources = grad_blocks[device * NB_DEV + rows_here].astype(jnp.float32)
        tile_terms = jnp.einsum('tji,tjf->tif', tile_block.astype(jnp.float32), sources, precision=lax.Precision.HIGHEST)
        return (running.at[cols_here].add(tile_terms), None)
    grad_total, unused = lax.scan(spread, jnp.zeros((NBLK, BLK, F), jnp.float32), (tiles_grouped, rows_grouped, cols_grouped, device_ids))
    feature_grad = grad_total.reshape(NODES, F).astype(jnp.bfloat16)
    return (activated.astype(jnp.bfloat16), weight_grad, feature_grad)
```

```python
import functools
import math

import jax
import jax.numpy as jnp
from jax import lax
from jax.experimental import pallas as pl
from jax.experimental.pallas import tpu as pltpu
from jax.sharding import PartitionSpec as P

VMEM = pl.BlockSpec(memory_space=pltpu.VMEM)
SMEM = pl.BlockSpec(memory_space=pltpu.SMEM)
VMEM_BYTES = 56 * 1024 * 1024


def forward_kernel(row_ref, col_ref, tiles_ref, blocks_ref, out_ref, acc_ref):
    acc_ref[...] = jnp.zeros_like(acc_ref)

    def step(t, carry):
        acc_ref[row_ref[t]] += jnp.dot(
            tiles_ref[t], blocks_ref[col_ref[t]], preferred_element_type=jnp.float32
        )
        return carry

    lax.fori_loop(0, tiles_ref.shape[0], step, 0, unroll=4)
    out_ref[...] = acc_ref[...].astype(out_ref.dtype)


def aggregate_tiles(tile_row, column_block, tile_values, blocks, local_blocks):
    block_size, width = blocks.shape[1:]
    shape = (local_blocks, block_size, width)
    return pl.pallas_call(
        forward_kernel,
        out_shape=jax.ShapeDtypeStruct(shape, jnp.bfloat16),
        in_specs=[SMEM, SMEM, VMEM, VMEM],
        out_specs=VMEM,
        scratch_shapes=[pltpu.VMEM(shape, jnp.float32)],
        compiler_params=pltpu.CompilerParams(vmem_limit_bytes=VMEM_BYTES),
        name="forward_tiles",
    )(tile_row, column_block, tile_values, blocks)


def dense_kernel(scale, chunk, row_ref, col_ref, tiles_ref, labels_ref, weight_ref, *refs):
    parts, (act_ref, wgrad_ref, terms_ref, grad_ref) = refs[:-4], refs[-4:]
    rows, width = parts[0].shape
    features = weight_ref.shape[0]
    block_size = tiles_ref.shape[1]
    wgrad_ref[...] = jnp.zeros_like(wgrad_ref)

    def rows_step(i, carry):
        here = pl.ds(pl.multiple_of(i * chunk, chunk), chunk)
        hidden = jnp.zeros((chunk, features), jnp.float32)
        for k, part in enumerate(parts):
            hidden += jnp.dot(
                part[here, :],
                weight_ref[k * width : (k + 1) * width, :],
                preferred_element_type=jnp.float32,
            )
        sigmoid = jax.nn.sigmoid(hidden)
        activated = hidden * sigmoid
        act_ref[here, :] = activated[:, :width].astype(act_ref.dtype)
        slopes = sigmoid * (1.0 + hidden * (1.0 - sigmoid))
        ids = lax.broadcasted_iota(jnp.int32, (chunk, features), 1)
        target = (labels_ref[here, :] == ids).astype(jnp.float32)
        out_grad = ((activated - target) * slopes).astype(jnp.bfloat16)
        for k, part in enumerate(parts):
            wgrad_ref[k * width : (k + 1) * width, :] += lax.dot_general(
                part[here, :],
                out_grad[:, :width],
                (((0,), (0,)), ((), ())),
                preferred_element_type=jnp.float32,
            )
        agg_grad = lax.dot_general(
            out_grad,
            weight_ref[:width, :],
            (((1,), (1,)), ((), ())),
            preferred_element_type=jnp.float32,
        ).astype(jnp.bfloat16)
        for b in range(chunk // block_size):
            grad_ref[i * (chunk // block_size) + b] = agg_grad[b * block_size : (b + 1) * block_size]
        return carry

    lax.fori_loop(0, rows // chunk, rows_step, 0)
    wgrad_ref[...] = wgrad_ref[...] * scale
    terms_ref[...] = jnp.zeros_like(terms_ref)

    def step(t, carry):
        product = lax.dot_general(
            tiles_ref[t],
            grad_ref[row_ref[t]],
            (((0,), (0,)), ((), ())),
            preferred_element_type=jnp.float32,
        )
        at = col_ref[t]
        terms_ref[at] = (terms_ref[at].astype(jnp.float32) + product).astype(jnp.bfloat16)
        return carry

    lax.fori_loop(0, tiles_ref.shape[0], step, 0, unroll=4)


def dense_and_spread(
    tile_row, column_block, tile_values, labels, weight, parts, all_blocks, node_total
):
    rows, width = parts[0].shape
    block_size = tile_values.shape[1]
    return pl.pallas_call(
        functools.partial(dense_kernel, 1.0 / math.sqrt(node_total), 2 * block_size),
        out_shape=(
            jax.ShapeDtypeStruct((rows, width), jnp.bfloat16),
            jax.ShapeDtypeStruct((weight.shape[0], width), jnp.float32),
            jax.ShapeDtypeStruct((all_blocks, block_size, width), jnp.bfloat16),
        ),
        in_specs=[SMEM, SMEM] + [VMEM] * (3 + len(parts)),
        out_specs=(VMEM, VMEM, VMEM),
        scratch_shapes=[pltpu.VMEM((rows // block_size, block_size, width), jnp.bfloat16)],
        compiler_params=pltpu.CompilerParams(vmem_limit_bytes=VMEM_BYTES),
        name="dense_spread",
    )(tile_row, column_block, tile_values, labels, weight, *parts)


def per_device(node_features, weight, tile_values, tile_row, source_owner, source_block, labels):
    local_rows, width = node_features.shape
    block_size = tile_values.shape[1]
    local_blocks = local_rows // block_size
    row_devices = lax.axis_size("rows")
    col_devices = lax.axis_size("cols")
    all_blocks = row_devices * local_blocks
    features = weight.shape[0]
    column_block = source_owner[:, 0] * local_blocks + source_block

    gathered = lax.all_gather(node_features, "rows", axis=0, tiled=True)
    first = lax.axis_index("cols") * width
    own_first = jnp.roll(weight, (-first, -first), (0, 1))
    own_labels = ((labels - first) % features)[:, None]
    aggregated = aggregate_tiles(
        tile_row,
        column_block,
        tile_values,
        gathered.reshape(all_blocks, block_size, width),
        local_blocks,
    ).reshape(local_rows, width)
    parts = [aggregated] + [
        lax.ppermute(
            aggregated, "cols", [((c + k) % col_devices, c) for c in range(col_devices)]
        )
        for k in range(1, col_devices)
    ]
    activations, weight_terms, terms = dense_and_spread(
        tile_row,
        column_block,
        tile_values,
        own_labels,
        own_first,
        parts,
        all_blocks,
        local_rows * row_devices,
    )
    weight_grad = jnp.roll(lax.psum(weight_terms, "rows"), first, 0)
    feature_grad = lax.psum_scatter(
        terms.reshape(all_blocks * block_size, width), "rows", scatter_dimension=0, tiled=True
    )
    return activations, weight_grad, feature_grad


def solution(mesh):
    return jax.shard_map(
        per_device,
        mesh=mesh,
        in_specs=(
            P("rows", "cols"),
            P(),
            P("rows", None, None),
            P("rows"),
            P("rows", None),
            P("rows"),
            P("rows"),
        ),
        out_specs=(P("rows", "cols"), P(None, "cols"), P("rows", "cols")),
        check_vma=False,
    )
```

```python
import functools
import math

import jax
import jax.numpy as jnp
from jax import lax
from jax.experimental import pallas as pl
from jax.experimental.pallas import tpu as pltpu
from jax.sharding import PartitionSpec as P

VMEM = pl.BlockSpec(memory_space=pltpu.VMEM)
SMEM = pl.BlockSpec(memory_space=pltpu.SMEM)
ANY = pl.BlockSpec(memory_space=pl.ANY)
VMEM_BYTES = 56 * 1024 * 1024
UNROLL = 4
LARGEST_PLANE = 4


def params():
    return pltpu.CompilerParams(vmem_limit_bytes=VMEM_BYTES)


def shuffle(x, pairs):
    return lax.ppermute(x, "rows", pairs)


def across_plane(x, k, line, plane):
    return shuffle(x, [(r, r ^ k) for r in range(line * plane)])


def pack_kernel(plane, cols, me_ref, owner_ref, tiles_ref, *out_refs):
    place, col = me_ref[1], me_ref[2]

    def step(t, counts):
        distance = lax.rem(owner_ref[t], plane) ^ place
        after = []
        for k, out_ref in enumerate(out_refs, 1):
            slot = counts[k - 1]
            mine = distance == k

            @pl.when(mine & (lax.rem(slot, cols) == col))
            def _():
                out_ref[lax.div(slot, cols)] = tiles_ref[t]

            after.append(slot + mine.astype(jnp.int32))
        return tuple(after)

    lax.fori_loop(0, tiles_ref.shape[0], step, (jnp.int32(0),) * len(out_refs))


def pack_tiles(me, owners, tile_values, plane, cols, slots):
    shape = jax.ShapeDtypeStruct((slots,) + tile_values.shape[1:], tile_values.dtype)
    return pl.pallas_call(
        functools.partial(pack_kernel, plane, cols),
        out_shape=(shape,) * (plane - 1),
        in_specs=[SMEM, SMEM, VMEM],
        out_specs=(VMEM,) * (plane - 1),
        compiler_params=params(),
        name="pack_tiles",
    )(me, owners, tile_values)


def plan_kernel(plane, cols, slots, blocks, me_ref, *refs):
    code_refs, (pos_ref, src_ref, dst_ref, count_ref) = refs[:plane], refs[plane:]
    place, col = me_ref[1], me_ref[2]
    tiles = code_refs[0].shape[0]
    found = jnp.int32(0)
    for k, code_ref in enumerate(code_refs):

        def step(t, carry, k=k, code_ref=code_ref):
            at, slot = carry
            code = code_ref[t]
            block = lax.div(code, blocks)
            owner = lax.div(block, blocks)
            if k == 0:
                position = t
            else:
                column = lax.rem(lax.rem(slot, cols) - col + cols, cols)
                position = tiles + ((k - 1) * cols + column) * slots + lax.div(slot, cols)
            pos_ref[at] = position
            src_ref[at] = lax.div(owner, plane) * blocks + lax.rem(block, blocks)
            dst_ref[at] = k * blocks + lax.rem(code, blocks)
            one = (lax.rem(owner, plane) == place).astype(jnp.int32)
            return at + one, slot + one

        found, _ = lax.fori_loop(0, tiles, step, (found, jnp.int32(0)), unroll=4)
    for i in range(UNROLL):
        pos_ref[found + i] = tiles + (plane - 1) * cols * slots
        src_ref[found + i] = 0
        dst_ref[found + i] = 0
    count_ref[0] = lax.div(found + UNROLL - 1, UNROLL)


def plan_tiles(me, codes, plane, cols, slots, blocks):
    entries = codes[0].shape[0] * plane + UNROLL
    shape = jax.ShapeDtypeStruct((entries,), jnp.int32)
    return pl.pallas_call(
        functools.partial(plan_kernel, plane, cols, slots, blocks),
        out_shape=(shape, shape, shape, jax.ShapeDtypeStruct((1,), jnp.int32)),
        in_specs=[SMEM] * (1 + plane),
        out_specs=(SMEM,) * 4,
        compiler_params=params(),
        name="plan_tiles",
    )(me, *codes)


def load_tiles(tile_refs, tiles_ref, sems):
    copies, first = [], 0
    for i, ref in enumerate(tile_refs):
        copy = pltpu.make_async_copy(ref, tiles_ref.at[pl.ds(first, ref.shape[0])], sems.at[i])
        copy.start()
        copies.append(copy)
        first += ref.shape[0]
    tiles_ref[first] = jnp.zeros_like(tiles_ref[first])
    return copies


def block_rows(index, size):
    return pl.ds(pl.multiple_of(index * size, size), size)


def forward_kernel(line, n_tiles, me_ref, pos_ref, src_ref, dst_ref, count_ref, *refs):
    tile_refs, refs = refs[:n_tiles], refs[n_tiles:]
    part_refs, refs = refs[: 2 * line - 1], refs[2 * line - 1 :]
    out_refs, (tiles_ref, nodes_ref, acc_ref, tile_sems, part_sems) = refs[:-5], refs[-5:]
    rows = part_refs[0].shape[0]
    size = tiles_ref.shape[1]
    mine = me_ref[0]

    def each_part(act):
        for i, ref in enumerate(part_refs):
            source = mine + i - (line - 1)

            @pl.when((source >= 0) & (source < line))
            def _():
                act(
                    pltpu.make_async_copy(
                        ref, nodes_ref.at[block_rows(source, rows)], part_sems.at[i]
                    )
                )

    copies = load_tiles(tile_refs, tiles_ref, tile_sems)
    each_part(lambda copy: copy.start())
    acc_ref[...] = jnp.zeros_like(acc_ref)
    for copy in copies:
        copy.wait()
    each_part(lambda copy: copy.wait())

    def step(i, carry):
        for j in range(UNROLL):
            t = i * UNROLL + j
            acc_ref[block_rows(dst_ref[t], size)] += jnp.dot(
                tiles_ref[pos_ref[t]],
                nodes_ref[block_rows(src_ref[t], size)],
                preferred_element_type=jnp.float32,
            )
        return carry

    lax.fori_loop(0, count_ref[0], step, 0)
    for k, ref in enumerate(out_refs):
        ref[...] = acc_ref[k * rows : (k + 1) * rows].astype(ref.dtype)


def forward_tiles(me, plan, tile_parts, node_parts, plane):
    line = (len(node_parts) + 1) // 2
    rows, width = node_parts[0].shape
    n_tiles = sum(part.shape[0] for part in tile_parts) + 1
    block = tile_parts[0].shape[1:]
    kinds = [jnp.float32] + [jnp.bfloat16] * (plane - 1)
    return pl.pallas_call(
        functools.partial(forward_kernel, line, len(tile_parts)),
        out_shape=tuple(jax.ShapeDtypeStruct((rows, width), kind) for kind in kinds),
        in_specs=[SMEM] * 5 + [ANY] * (len(tile_parts) + len(node_parts)),
        out_specs=(VMEM,) * plane,
        scratch_shapes=[
            pltpu.VMEM((n_tiles,) + block, jnp.bfloat16),
            pltpu.VMEM((line * rows, width), jnp.bfloat16),
            pltpu.VMEM((plane * rows, width), jnp.float32),
            pltpu.SemaphoreType.DMA((len(tile_parts),)),
            pltpu.SemaphoreType.DMA((len(node_parts),)),
        ],
        compiler_params=params(),
        name="forward_tiles",
    )(me, *plan, *tile_parts, *node_parts)


def dense_kernel(scale, chunk, halves, labels_ref, weight_ref, *refs):
    parts, outs = refs[: -2 - halves], refs[-2 - halves :]
    act_ref, wgrad_ref, grad_refs = outs[0], outs[1], outs[2:]
    rows, part_width = parts[0].shape
    width = part_width * halves
    features = weight_ref.shape[0]
    wgrad_ref[...] = jnp.zeros_like(wgrad_ref)

    def rows_step(i, carry):
        here = block_rows(i, chunk)
        agg = jnp.concatenate([part[here, :] for part in parts], axis=1)
        hidden = jnp.dot(agg, weight_ref[...], preferred_element_type=jnp.float32)
        sigmoid = jax.nn.sigmoid(hidden)
        activated = hidden * sigmoid
        act_ref[here, :] = activated[:, :width].astype(act_ref.dtype)
        slopes = sigmoid * (1.0 + hidden * (1.0 - sigmoid))
        ids = lax.broadcasted_iota(jnp.int32, (chunk, features), 1)
        target = (labels_ref[here, :] == ids).astype(jnp.float32)
        out_grad = ((activated - target) * slopes).astype(jnp.bfloat16)
        agg_grad = lax.dot_general(
            out_grad,
            weight_ref[:width, :],
            (((1,), (1,)), ((), ())),
            preferred_element_type=jnp.float32,
        ).astype(jnp.bfloat16)
        for h, ref in enumerate(grad_refs):
            ref[here, :] = agg_grad[:, h * part_width : (h + 1) * part_width]
        wgrad_ref[...] += lax.dot_general(
            agg,
            out_grad[:, :width],
            (((0,), (0,)), ((), ())),
            preferred_element_type=jnp.float32,
        )
        return carry

    lax.fori_loop(0, rows // chunk, rows_step, 0)
    wgrad_ref[...] = wgrad_ref[...] * scale


def dense(labels, weight, parts, halves, node_total):
    rows, part_width = parts[0].shape
    width = part_width * halves
    chunk = math.gcd(rows, 256)
    return pl.pallas_call(
        functools.partial(dense_kernel, 1.0 / math.sqrt(node_total), chunk, halves),
        out_shape=(
            jax.ShapeDtypeStruct((rows, width), jnp.bfloat16),
            jax.ShapeDtypeStruct((weight.shape[0], width), jnp.float32),
        )
        + (jax.ShapeDtypeStruct((rows, part_width), jnp.bfloat16),) * halves,
        in_specs=[VMEM] * (2 + len(parts)),
        out_specs=(VMEM,) * (2 + halves),
        compiler_params=params(),
        name="dense",
    )(labels, weight, *parts)


def spread_kernel(line, n_tiles, plane, me_ref, pos_ref, src_ref, dst_ref, count_ref, *refs):
    tile_refs, refs = refs[:n_tiles], refs[n_tiles:]
    grad_refs, refs = refs[:plane], refs[plane:]
    out_refs, (tiles_ref, grads_ref, acc_ref, tile_sems, grad_sems) = refs[:-5], refs[-5:]
    rows = grad_refs[0].shape[0]
    size = tiles_ref.shape[1]
    mine = me_ref[0]
    copies = load_tiles(tile_refs, tiles_ref, tile_sems)
    for k, ref in enumerate(grad_refs):
        copy = pltpu.make_async_copy(
            ref, grads_ref.at[pl.ds(k * rows, rows)], grad_sems.at[k]
        )
        copy.start()
        copies.append(copy)
    acc_ref[...] = jnp.zeros_like(acc_ref)
    for copy in copies:
        copy.wait()

    def step(i, carry):
        for j in range(UNROLL):
            t = i * UNROLL + j
            acc_ref[block_rows(src_ref[t], size)] += lax.dot_general(
                tiles_ref[pos_ref[t]],
                grads_ref[block_rows(dst_ref[t], size)],
                (((0,), (0,)), ((), ())),
                preferred_element_type=jnp.float32,
            )
        return carry

    lax.fori_loop(0, count_ref[0], step, 0)
    for i, ref in enumerate(out_refs):
        target = mine + i - (line - 1)

        @pl.when((target >= 0) & (target < line))
        def _():
            ref[...] = acc_ref[block_rows(target, rows)].astype(ref.dtype)


def spread_tiles(me, plan, tile_parts, grads, line):
    plane = len(grads)
    rows, width = grads[0].shape
    n_tiles = sum(part.shape[0] for part in tile_parts) + 1
    block = tile_parts[0].shape[1:]
    kinds = [jnp.float32 if i == line - 1 else jnp.bfloat16 for i in range(2 * line - 1)]
    return pl.pallas_call(
        functools.partial(spread_kernel, line, len(tile_parts), plane),
        out_shape=tuple(jax.ShapeDtypeStruct((rows, width), kind) for kind in kinds),
        in_specs=[SMEM] * 5 + [ANY] * (len(tile_parts) + plane),
        out_specs=(VMEM,) * (2 * line - 1),
        scratch_shapes=[
            pltpu.VMEM((n_tiles,) + block, jnp.bfloat16),
            pltpu.VMEM((plane * rows, width), jnp.bfloat16),
            pltpu.VMEM((line * rows, width), jnp.float32),
            pltpu.SemaphoreType.DMA((len(tile_parts),)),
            pltpu.SemaphoreType.DMA((plane,)),
        ],
        compiler_params=params(),
        name="spread_tiles",
    )(me, *plan, *tile_parts, *grads)


def line_steps(line, plane, step, reach):
    return [
        (z * plane + q, (z + step) * plane + q)
        for z in range(line)
        if 0 <= z + step < line and 0 <= z + reach < line
        for q in range(plane)
    ]


def line_gather(x, line, plane):
    down, up = [x], [x]
    for k in range(1, line):
        up.append(shuffle(up[-1], line_steps(line, plane, 1, 1 - k)))
        down.append(shuffle(down[-1], line_steps(line, plane, -1, k - 1)))
    return up[:0:-1] + down


def line_sum(terms, line, plane):
    total = terms[line - 1]
    for step in (1, -1):
        moved = None
        for k in range(line - 1, 0, -1):
            term = terms[line - 1 + step * k]
            if moved is not None:
                term = (term.astype(jnp.float32) + moved.astype(jnp.float32)).astype(term.dtype)
            moved = shuffle(term, line_steps(line, plane, step, step * k))
        if moved is not None:
            total = total + moved.astype(jnp.float32)
    return total.astype(jnp.bfloat16)


def sum_everywhere(terms, z, q, line, plane):
    quarters = terms.reshape((plane, terms.shape[0] // plane) + terms.shape[1:])
    pick = lambda i: lax.dynamic_index_in_dim(quarters, i, 0, keepdims=False)
    total = pick(q)
    for k in range(1, plane):
        sent = across_plane(pick(q ^ k).astype(jnp.bfloat16), k, line, plane)
        total = total + sent.astype(jnp.float32)
    mine = total.astype(jnp.bfloat16)
    around = [
        mine if k == 0 else shuffle(mine, line_steps(line, plane, -k, 0))
        for k in range(1 - line, line)
    ]
    ordered = lax.dynamic_slice_in_dim(jnp.stack(around), line - 1 - z, line, 0)
    total = jnp.sum(ordered.astype(jnp.float32), axis=0)
    parts = [total] + [across_plane(total, k, line, plane) for k in range(1, plane)]
    return jnp.stack(parts)[jnp.arange(plane) ^ q].reshape(terms.shape)


def per_device(node_features, weight, tile_values, tile_row, source_owner, source_block, labels):
    local_rows, width = node_features.shape
    n_tiles, block_size = tile_values.shape[:2]
    blocks = local_rows // block_size
    rows, cols = lax.axis_size("rows"), lax.axis_size("cols")
    plane = math.gcd(rows, LARGEST_PLANE)
    line = rows // plane
    halves = 2 if width % 256 == 0 else 1
    part_width = width // halves
    slots = -(-min(n_tiles, line * (2 * n_tiles // rows)) // cols)
    features = weight.shape[0]
    owners = source_owner[:, 0]

    index = lax.axis_index("rows")
    col = lax.axis_index("cols")
    z, q = index // plane, index % plane
    me = jnp.stack([z, q, col]).astype(jnp.int32)

    def other_cols(x):
        return [
            lax.ppermute(x, "cols", [((c + k) % cols, c) for c in range(cols)])
            for k in range(1, cols)
        ]

    node_parts = [
        line_gather(node_features[:, h * part_width : (h + 1) * part_width], line, plane)
        for h in range(halves)
    ]
    code = (owners * blocks + source_block) * blocks + tile_row
    packed = pack_tiles(me, owners, tile_values, plane, cols, slots)
    codes = [code] + [across_plane(code, k, line, plane) for k in range(1, plane)]
    plan = plan_tiles(me, codes, plane, cols, slots, blocks)
    tile_parts = [tile_values]
    for k in range(1, plane):
        arrived = across_plane(packed[k - 1], k, line, plane)
        tile_parts += [arrived] + other_cols(arrived)

    first = col * width
    own_first = jnp.roll(weight, (-first, -first), (0, 1))
    own_labels = ((labels - first) % features)[:, None]

    aggregated = []
    for h in range(halves):
        sums = forward_tiles(me, plan, tile_parts, node_parts[h], plane)
        total = sums[0]
        for k in range(1, plane):
            total = total + across_plane(sums[k], k, line, plane).astype(jnp.float32)
        mine = total.astype(jnp.bfloat16)
        aggregated.append([mine] + other_cols(mine))
    parts = [aggregated[h][c] for c in range(cols) for h in range(halves)]

    outs = dense(own_labels, own_first, parts, halves, local_rows * rows)
    activations, weight_terms, own_grads = outs[0], outs[1], outs[2:]

    feature_grads = []
    for h in range(halves):
        grads = [own_grads[h]] + [
            across_plane(own_grads[h], k, line, plane) for k in range(1, plane)
        ]
        terms = spread_tiles(me, plan, tile_parts, grads, line)
        feature_grads.append(line_sum(terms, line, plane))
    weight_grad = jnp.roll(sum_everywhere(weight_terms, z, q, line, plane), first, 0)
    return activations, weight_grad, jnp.concatenate(feature_grads, axis=1)


def solution(mesh):
    return jax.shard_map(
        per_device,
        mesh=mesh,
        in_specs=(
            P("rows", "cols"),
            P(),
            P("rows", None, None),
            P("rows"),
            P("rows", None),
            P("rows"),
            P("rows"),
        ),
        out_specs=(P("rows", "cols"), P(None, "cols"), P("rows", "cols")),
        check_vma=False,
    )
```

```python
import functools
import math

import jax
import jax.numpy as jnp
from jax import lax
from jax.experimental import pallas as pl
from jax.experimental.pallas import tpu as pltpu
from jax.sharding import PartitionSpec as P

VMEM = pl.BlockSpec(memory_space=pltpu.VMEM)
SMEM = pl.BlockSpec(memory_space=pltpu.SMEM)
ANY = pl.BlockSpec(memory_space=pl.ANY)
SPARE_BYTES = 6 * 1024 * 1024
UNROLL = 8
LARGEST_PLANE = 4


def params(*shapes):
    room = SPARE_BYTES
    for shape in shapes:
        *lead, high, wide = shape.shape
        room += math.prod(lead) * high * (-(-wide // 128) * 128) * jnp.dtype(shape.dtype).itemsize
    return pltpu.CompilerParams(vmem_limit_bytes=room)


def shuffle(x, pairs):
    return lax.ppermute(x, "rows", pairs)


def across_plane(x, k, line, plane):
    return shuffle(x, [(r, r ^ k) for r in range(line * plane)])


def pack_kernel(plane, cols, me_ref, owner_ref, tiles_ref, *refs):
    out_refs, (list_ref, slot_ref) = refs[:-2], refs[-2:]
    place, col = me_ref[1], me_ref[2]
    slots = out_refs[0].shape[0]
    spare = len(out_refs) * slots
    for k in range(plane):
        slot_ref[k] = 0
    for i in range(spare):
        list_ref[i] = 0

    def step(t, carry):
        k = lax.rem(owner_ref[t], plane) ^ place
        slot = slot_ref[k]
        slot_ref[k] = slot + 1
        sent = (k > 0) & (lax.rem(slot, cols) == col)
        list_ref[jnp.where(sent, (k - 1) * slots + lax.div(slot, cols), spare)] = t
        return carry

    lax.fori_loop(0, tiles_ref.shape[0], step, 0, unroll=4)
    for k, out_ref in enumerate(out_refs):
        for slot in range(slots):
            out_ref[slot] = tiles_ref[list_ref[k * slots + slot]]


def pack_tiles(me, owners, tile_values, plane, cols, slots):
    shape = jax.ShapeDtypeStruct((slots,) + tile_values.shape[1:], tile_values.dtype)
    return pl.pallas_call(
        functools.partial(pack_kernel, plane, cols),
        out_shape=(shape,) * (plane - 1),
        in_specs=[SMEM, SMEM, VMEM],
        out_specs=(VMEM,) * (plane - 1),
        scratch_shapes=[
            pltpu.SMEM(((plane - 1) * slots + 1,), jnp.int32),
            pltpu.SMEM((plane,), jnp.int32),
        ],
        compiler_params=params(tile_values, *(shape,) * (plane - 1)),
        name="pack_tiles",
    )(me, owners, tile_values)


DST_BIT, SRC_BIT = 10, 18


def plan_kernel(plane, cols, slots, blocks, tiles, me_ref, codes_ref, plan_ref, count_ref):
    line, place, col = me_ref[0], me_ref[1], me_ref[2]
    found = jnp.int32(0)
    for k in range(plane):
        device = line * plane + (place ^ k)

        def step(t, carry, k=k, device=device):
            at, slot = carry
            code = codes_ref[device, t]
            if k == 0:
                position = t
            else:
                column = lax.rem(slot + (cols - col), cols)
                position = tiles + ((k - 1) * cols + column) * slots + lax.div(slot, cols)
            plan_ref[at] = (code & (-1 << DST_BIT)) + (position + (k * blocks << DST_BIT))
            one = ((code & ((1 << DST_BIT) - 1)) == place).astype(jnp.int32)
            return at + one, slot + one

        found, _ = lax.fori_loop(0, tiles, step, (found, jnp.int32(0)), unroll=8)
    for i in range(UNROLL):
        plan_ref[found + i] = tiles + (plane - 1) * cols * slots
    count_ref[0] = lax.div(found + UNROLL - 1, UNROLL)


def plan_tiles(me, codes, plane, cols, slots, blocks, tiles):
    entries = tiles * plane + UNROLL
    return pl.pallas_call(
        functools.partial(plan_kernel, plane, cols, slots, blocks, tiles),
        out_shape=(
            jax.ShapeDtypeStruct((entries,), jnp.int32),
            jax.ShapeDtypeStruct((1,), jnp.int32),
        ),
        in_specs=[SMEM, SMEM],
        out_specs=(SMEM, SMEM),
        compiler_params=params(),
        name="plan_tiles",
    )(me, codes)


def planned(plan_ref, t):
    entry = plan_ref[t]
    position = entry & ((1 << DST_BIT) - 1)
    dst = (entry >> DST_BIT) & ((1 << (SRC_BIT - DST_BIT)) - 1)
    return position, dst, entry >> SRC_BIT


def load_tiles(tile_refs, tiles_ref, sems):
    copies, first = [], 0
    for i, ref in enumerate(tile_refs):
        copy = pltpu.make_async_copy(ref, tiles_ref.at[pl.ds(first, ref.shape[0])], sems.at[i])
        copy.start()
        copies.append(copy)
        first += ref.shape[0]
    tiles_ref[first] = jnp.zeros_like(tiles_ref[first])
    return copies


def block_rows(index, size):
    return pl.ds(pl.multiple_of(index * size, size), size)


def forward_kernel(line, n_tiles, lanes, me_ref, plan_ref, count_ref, *refs):
    tile_refs, refs = refs[:n_tiles], refs[n_tiles:]
    part_refs, refs = refs[: 2 * line - 1], refs[2 * line - 1 :]
    out_refs, (tiles_ref, nodes_ref, acc_ref, tile_sems, part_sems) = refs[:-5], refs[-5:]
    rows, width = part_refs[0].shape[0], nodes_ref.shape[1]
    size = tiles_ref.shape[1]
    mine = me_ref[0]

    def each_part(act):
        for i, ref in enumerate(part_refs):
            source = mine + i - (line - 1)

            @pl.when((source >= 0) & (source < line))
            def _():
                here = ref.at[:, lanes] if ref.shape != (rows, width) else ref
                act(
                    pltpu.make_async_copy(
                        here, nodes_ref.at[block_rows(source, rows)], part_sems.at[i]
                    )
                )

    copies = load_tiles(tile_refs, tiles_ref, tile_sems)
    each_part(lambda copy: copy.start())
    acc_ref[...] = jnp.zeros_like(acc_ref)
    for copy in copies:
        copy.wait()
    each_part(lambda copy: copy.wait())

    def step(i, carry):
        for j in range(UNROLL):
            position, dst, src = planned(plan_ref, i * UNROLL + j)
            acc_ref[block_rows(dst, size)] += jnp.dot(
                tiles_ref[position],
                nodes_ref[block_rows(src, size)],
                preferred_element_type=jnp.float32,
            )
        return carry

    lax.fori_loop(0, count_ref[0], step, 0)
    for k, ref in enumerate(out_refs):
        ref[...] = acc_ref[k * rows : (k + 1) * rows].astype(ref.dtype)


def forward_tiles(me, plan, tile_parts, node_parts, plane, lanes):
    line = (len(node_parts) + 1) // 2
    rows, width = node_parts[0].shape[0], lanes.size
    n_tiles = sum(part.shape[0] for part in tile_parts) + 1
    block = tile_parts[0].shape[1:]
    kinds = [jnp.float32] + [jnp.bfloat16] * (plane - 1)
    outs = tuple(jax.ShapeDtypeStruct((rows, width), kind) for kind in kinds)
    scratch = [
        pltpu.VMEM((n_tiles,) + block, jnp.bfloat16),
        pltpu.VMEM((line * rows, width), jnp.bfloat16),
        pltpu.VMEM((plane * rows, width), jnp.float32),
    ]
    return pl.pallas_call(
        functools.partial(forward_kernel, line, len(tile_parts), lanes),
        out_shape=outs,
        in_specs=[SMEM] * 3 + [ANY] * (len(tile_parts) + len(node_parts)),
        out_specs=(VMEM,) * plane,
        scratch_shapes=scratch
        + [
            pltpu.SemaphoreType.DMA((len(tile_parts),)),
            pltpu.SemaphoreType.DMA((len(node_parts),)),
        ],
        compiler_params=params(*outs, *scratch),
        name="forward_tiles",
    )(me, *plan, *tile_parts, *node_parts)


def dense_kernel(scale, chunk, halves, plane, me_ref, labels_ref, weight_ref, *refs):
    parts, outs = refs[: -1 - halves - plane - 1], refs[-1 - halves - plane - 1 :]
    act_ref, grad_refs, rest = outs[0], outs[1 : 1 + halves], outs[1 + halves :]
    quarter_ref, ride_refs, wgrad_ref = rest[0], rest[1:-1], rest[-1]
    rows, part_width = parts[0].shape
    width = part_width * halves
    features = weight_ref.shape[0]
    quarter = features // plane
    wgrad_ref[...] = jnp.zeros_like(wgrad_ref)

    def rows_step(i, carry):
        here = block_rows(i, chunk)
        agg = jnp.concatenate([part[here, :] for part in parts], axis=1)
        hidden = jnp.dot(agg, weight_ref[...], preferred_element_type=jnp.float32)
        sigmoid = jax.nn.sigmoid(hidden)
        activated = hidden * sigmoid
        act_ref[here, :] = activated[:, :width].astype(act_ref.dtype)
        slopes = sigmoid * (1.0 + hidden * (1.0 - sigmoid))
        ids = lax.broadcasted_iota(jnp.int32, (chunk, features), 1)
        target = (labels_ref[here, :] == ids).astype(jnp.float32)
        out_grad = ((activated - target) * slopes).astype(jnp.bfloat16)
        agg_grad = lax.dot_general(
            out_grad,
            weight_ref[:width, :],
            (((1,), (1,)), ((), ())),
            preferred_element_type=jnp.float32,
        ).astype(jnp.bfloat16)
        for h, ref in enumerate(grad_refs):
            ref[here, :] = agg_grad[:, h * part_width : (h + 1) * part_width]
        for ref in ride_refs:
            ref[here, :] = agg_grad[:, width - part_width :]
        wgrad_ref[...] += lax.dot_general(
            agg,
            out_grad[:, :width],
            (((0,), (0,)), ((), ())),
            preferred_element_type=jnp.float32,
        )
        return carry

    lax.fori_loop(0, rows // chunk, rows_step, 0)
    place = me_ref[1]
    quarter_ref[...] = wgrad_ref[block_rows(place, quarter)] * scale
    for k, ref in enumerate(ride_refs, 1):
        sent = (wgrad_ref[block_rows(place ^ k, quarter)] * scale).astype(ref.dtype)
        for h in range(halves):
            first = rows + h * quarter
            ref[first : first + quarter] = sent[:, h * part_width : (h + 1) * part_width]


def dense(me, labels, weight, parts, halves, plane, node_total):
    rows, part_width = parts[0].shape
    width = part_width * halves
    chunk = math.gcd(rows, 256)
    features = weight.shape[0]
    quarter = features // plane
    outs = (
        (jax.ShapeDtypeStruct((rows, width), jnp.bfloat16),)
        + (jax.ShapeDtypeStruct((rows, part_width), jnp.bfloat16),) * halves
        + (jax.ShapeDtypeStruct((quarter, width), jnp.float32),)
        + (jax.ShapeDtypeStruct((rows + halves * quarter, part_width), jnp.bfloat16),)
        * (plane - 1)
    )
    terms = pltpu.VMEM((features, width), jnp.float32)
    return pl.pallas_call(
        functools.partial(dense_kernel, 1.0 / math.sqrt(node_total), chunk, halves, plane),
        out_shape=outs,
        in_specs=[SMEM] + [VMEM] * (2 + len(parts)),
        out_specs=(VMEM,) * (1 + halves + plane),
        scratch_shapes=[terms],
        compiler_params=params(labels, weight, *parts, *outs, terms),
        name="dense",
    )(me, labels, weight, *parts)


def spread_kernel(line, n_tiles, plane, me_ref, plan_ref, count_ref, *refs):
    tile_refs, refs = refs[:n_tiles], refs[n_tiles:]
    grad_refs, refs = refs[:plane], refs[plane:]
    out_refs, (tiles_ref, grads_ref, acc_ref, tile_sems, grad_sems) = refs[:-5], refs[-5:]
    rows = grad_refs[0].shape[0]
    size = tiles_ref.shape[1]
    mine = me_ref[0]
    copies = load_tiles(tile_refs, tiles_ref, tile_sems)
    for k, ref in enumerate(grad_refs):
        copy = pltpu.make_async_copy(
            ref.at[pl.ds(0, rows)], grads_ref.at[pl.ds(k * rows, rows)], grad_sems.at[k]
        )
        copy.start()
        copies.append(copy)
    acc_ref[...] = jnp.zeros_like(acc_ref)
    for copy in copies:
        copy.wait()

    def step(i, carry):
        for j in range(UNROLL):
            position, dst, src = planned(plan_ref, i * UNROLL + j)
            acc_ref[block_rows(src, size)] += lax.dot_general(
                tiles_ref[position],
                grads_ref[block_rows(dst, size)],
                (((0,), (0,)), ((), ())),
                preferred_element_type=jnp.float32,
            )
        return carry

    lax.fori_loop(0, count_ref[0], step, 0)
    for i, ref in enumerate(out_refs):
        target = mine + i - (line - 1)

        @pl.when((target >= 0) & (target < line))
        def _():
            ref[...] = acc_ref[block_rows(target, rows)].astype(ref.dtype)


def spread_tiles(me, plan, tile_parts, grads, line):
    plane = len(grads)
    rows, width = grads[0].shape
    n_tiles = sum(part.shape[0] for part in tile_parts) + 1
    block = tile_parts[0].shape[1:]
    kinds = [jnp.float32 if i == line - 1 else jnp.bfloat16 for i in range(2 * line - 1)]
    outs = tuple(jax.ShapeDtypeStruct((rows, width), kind) for kind in kinds)
    scratch = [
        pltpu.VMEM((n_tiles,) + block, jnp.bfloat16),
        pltpu.VMEM((plane * rows, width), jnp.bfloat16),
        pltpu.VMEM((line * rows, width), jnp.float32),
    ]
    return pl.pallas_call(
        functools.partial(spread_kernel, line, len(tile_parts), plane),
        out_shape=outs,
        in_specs=[SMEM] * 3 + [ANY] * (len(tile_parts) + plane),
        out_specs=(VMEM,) * (2 * line - 1),
        scratch_shapes=scratch
        + [
            pltpu.SemaphoreType.DMA((len(tile_parts),)),
            pltpu.SemaphoreType.DMA((plane,)),
        ],
        compiler_params=params(*outs, *scratch),
        name="spread_tiles",
    )(me, *plan, *tile_parts, *grads)


def line_steps(line, plane, step, reach):
    return [
        (z * plane + q, (z + step) * plane + q)
        for z in range(line)
        if 0 <= z + step < line and 0 <= z + reach < line
        for q in range(plane)
    ]


def line_gather(x, line, plane, lanes):
    down, up = [x], [x]
    for k in range(1, line - 1):
        up.append(shuffle(up[-1], line_steps(line, plane, 1, 1 - k)))
        down.append(shuffle(down[-1], line_steps(line, plane, -1, k - 1)))
    parts = []
    for part in lanes:
        first = shuffle(up[-1][:, part], line_steps(line, plane, 1, 2 - line))
        last = shuffle(down[-1][:, part], line_steps(line, plane, -1, line - 2))
        parts.append([first] + up[:0:-1] + down + [last])
    return parts


def line_sum(terms, line, plane):
    total = terms[line - 1]
    for step in (1, -1):
        moved = None
        for k in range(line - 1, 0, -1):
            term = terms[line - 1 + step * k]
            if moved is not None:
                term = (term.astype(jnp.float32) + moved.astype(jnp.float32)).astype(term.dtype)
            moved = shuffle(term, line_steps(line, plane, step, step * k))
        if moved is not None:
            total = total + moved.astype(jnp.float32)
    return total.astype(jnp.bfloat16)


def sum_quarters(quarter, rides, line, plane):
    total = quarter
    for ride in rides:
        total = total + ride.astype(jnp.float32)
    every = lax.all_gather(total.astype(jnp.bfloat16), "rows", axis=0, tiled=True)
    every = every.reshape((line, plane * quarter.shape[0]) + quarter.shape[1:])
    return jnp.sum(every.astype(jnp.float32), axis=0)


def per_device(node_features, weight, tile_values, tile_row, source_owner, source_block, labels):
    local_rows, width = node_features.shape
    n_tiles, block_size = tile_values.shape[:2]
    blocks = local_rows // block_size
    rows, cols = lax.axis_size("rows"), lax.axis_size("cols")
    plane = math.gcd(rows, LARGEST_PLANE)
    line = rows // plane
    halves = 2 if width % 256 == 0 else 1
    part_width = width // halves
    slots = -(-min(n_tiles, line * (2 * n_tiles // rows)) // cols)
    features = weight.shape[0]
    owners = source_owner[:, 0]

    index = lax.axis_index("rows")
    col = lax.axis_index("cols")
    z, q = index // plane, index % plane
    me = jnp.stack([z, q, col]).astype(jnp.int32)

    def other_cols(x):
        return [
            lax.ppermute(x, "cols", [((c + k) % cols, c) for c in range(cols)])
            for k in range(1, cols)
        ]

    lanes = [slice(h * part_width, (h + 1) * part_width) for h in range(halves)]
    node_parts = line_gather(node_features, line, plane, lanes)
    code = (
        owners % plane
        + (tile_row << DST_BIT)
        + ((owners // plane * blocks + source_block) << SRC_BIT)
    )
    wide = jnp.zeros((8, -(-n_tiles // 128) * 128), jnp.int32).at[0, :n_tiles].set(code)
    codes = lax.all_gather(wide, "rows", axis=0)[:, 0]
    packed = pack_tiles(me, owners, tile_values, plane, cols, slots)
    plan = plan_tiles(me, codes, plane, cols, slots, blocks, n_tiles)
    tile_parts = [tile_values]
    for k in range(1, plane):
        arrived = across_plane(packed[k - 1], k, line, plane)
        tile_parts += [arrived] + other_cols(arrived)

    first = col * width
    own_first = jnp.roll(weight, (-first, -first), (0, 1))
    own_labels = ((labels - first) % features)[:, None]
    plan, own_first, own_labels = lax.optimization_barrier((plan, own_first, own_labels))

    aggregated = []
    for h in range(halves):
        sums = forward_tiles(
            me, plan, tile_parts, node_parts[h], plane, pl.ds(h * part_width, part_width)
        )
        total = sums[0]
        for k in range(1, plane):
            total = total + across_plane(sums[k], k, line, plane).astype(jnp.float32)
        mine = total.astype(jnp.bfloat16)
        aggregated.append([mine] + other_cols(mine))
    parts = [aggregated[h][c] for c in range(cols) for h in range(halves)]

    outs = dense(me, own_labels, own_first, parts, halves, plane, local_rows * rows)
    activations, own_grads, quarter = outs[0], outs[1 : 1 + halves], outs[1 + halves]
    riding = outs[2 + halves :]

    feature_grads, rides = [], []
    for h in range(halves):
        if h > 0:
            riding, grads = lax.optimization_barrier((riding, grads))
        grads = [own_grads[h]]
        for k in range(1, plane):
            sent = riding[k - 1] if h == halves - 1 else own_grads[h]
            grads.append(across_plane(sent, k, line, plane))
        if h == halves - 1:
            height = quarter.shape[0]
            for grad in grads[1:]:
                pieces = [grad[local_rows + i * height :][:height] for i in range(halves)]
                rides.append(jnp.concatenate(pieces, axis=1))
        terms = spread_tiles(me, plan, tile_parts, grads, line)
        feature_grads.append(line_sum(terms, line, plane))
    weight_grad = jnp.roll(sum_quarters(quarter, rides, line, plane), first, 0)
    return activations, weight_grad, jnp.concatenate(feature_grads, axis=1)


def solution(mesh):
    return jax.shard_map(
        per_device,
        mesh=mesh,
        in_specs=(
            P("rows", "cols"),
            P(),
            P("rows", None, None),
            P("rows"),
            P("rows", None),
            P("rows"),
            P("rows"),
        ),
        out_specs=(P("rows", "cols"), P(None, "cols"), P("rows", "cols")),
        check_vma=False,
    )
```

```python
import functools
import math

import jax
import jax.numpy as jnp
from jax import lax
from jax.experimental import pallas as pl
from jax.experimental.pallas import tpu as pltpu
from jax.sharding import PartitionSpec as P

VMEM = pl.BlockSpec(memory_space=pltpu.VMEM)
SMEM = pl.BlockSpec(memory_space=pltpu.SMEM)
ANY = pl.BlockSpec(memory_space=pl.ANY)
SPARE_BYTES = 6 * 1024 * 1024
UNROLL = 8
LARGEST_PLANE = 4


def params(*shapes):
    room = SPARE_BYTES
    for shape in shapes:
        *lead, high, wide = shape.shape
        room += math.prod(lead) * high * (-(-wide // 128) * 128) * jnp.dtype(shape.dtype).itemsize
    return pltpu.CompilerParams(vmem_limit_bytes=room)


def shuffle(x, pairs):
    return lax.ppermute(x, "rows", pairs)


def across_plane(x, k, line, plane):
    return shuffle(x, [(r, r ^ k) for r in range(line * plane)])


def pack_kernel(plane, cols, me_ref, owner_ref, codes_ref, tiles_ref, out_ref, list_ref, slot_ref):
    place, col = me_ref[1], me_ref[2]
    slots = out_ref.shape[1] - 1
    spare = plane * slots
    for k in range(plane):
        slot_ref[k] = 0
    for i in range(spare):
        list_ref[i] = 0

    def step(t, carry):
        to = lax.rem(owner_ref[t], plane)
        slot = slot_ref[to]
        slot_ref[to] = slot + 1
        sent = lax.rem(slot, cols) == col
        list_ref[jnp.where(sent, to * slots + lax.div(slot, cols), spare)] = t
        return carry

    lax.fori_loop(0, tiles_ref.shape[0], step, 0, unroll=4)
    for to in range(plane):
        for slot in range(slots):
            out_ref[to, slot] = tiles_ref[list_ref[to * slots + slot]]
        out_ref[to, slots, : codes_ref.shape[0]] = codes_ref[...]


def pack_tiles(me, owners, codes, tile_values, plane, cols, slots):
    shape = jax.ShapeDtypeStruct((plane, slots + 1) + tile_values.shape[1:], tile_values.dtype)
    return pl.pallas_call(
        functools.partial(pack_kernel, plane, cols),
        out_shape=shape,
        in_specs=[SMEM, SMEM, VMEM, VMEM],
        out_specs=VMEM,
        scratch_shapes=[
            pltpu.SMEM((plane * slots + 1,), jnp.int32),
            pltpu.SMEM((plane,), jnp.int32),
        ],
        compiler_params=params(tile_values, shape),
        name="pack_tiles",
    )(me, owners, codes, tile_values)


DST_BIT, SRC_BIT = 10, 18


def plan_kernel(plane, cols, slots, blocks, tiles, me_ref, codes_ref, plan_ref, count_ref):
    place, col = me_ref[1], me_ref[2]
    found = jnp.int32(0)
    for k in range(plane):
        device = place ^ k

        def step(t, carry, k=k, device=device):
            at, slot = carry
            code = codes_ref[device, t]
            if k == 0:
                position = t
            else:
                column = lax.rem(slot + (cols - col), cols)
                position = tiles + ((k - 1) * cols + column) * slots + lax.div(slot, cols)
            plan_ref[at] = (code & (-1 << DST_BIT)) + (position + (k * blocks << DST_BIT))
            one = ((code & ((1 << DST_BIT) - 1)) == place).astype(jnp.int32)
            return at + one, slot + one

        found, _ = lax.fori_loop(0, tiles, step, (found, jnp.int32(0)), unroll=8)
    for i in range(UNROLL):
        plan_ref[found + i] = tiles + (plane - 1) * cols * slots
    count_ref[0] = lax.div(found + UNROLL - 1, UNROLL)


def plan_tiles(me, codes, plane, cols, slots, blocks, tiles):
    entries = tiles * plane + UNROLL
    return pl.pallas_call(
        functools.partial(plan_kernel, plane, cols, slots, blocks, tiles),
        out_shape=(
            jax.ShapeDtypeStruct((entries,), jnp.int32),
            jax.ShapeDtypeStruct((1,), jnp.int32),
        ),
        in_specs=[SMEM, SMEM],
        out_specs=(SMEM, SMEM),
        compiler_params=params(),
        name="plan_tiles",
    )(me, codes)


def planned(plan_ref, t):
    entry = plan_ref[t]
    position = entry & ((1 << DST_BIT) - 1)
    dst = (entry >> DST_BIT) & ((1 << (SRC_BIT - DST_BIT)) - 1)
    return position, dst, entry >> SRC_BIT


def load_tiles(place, tile_refs, tiles_ref, sems):
    own_ref, arrived_refs = tile_refs[0], tile_refs[1:]
    plane, slots = arrived_refs[0].shape[0], arrived_refs[0].shape[1] - 1
    first = own_ref.shape[0]
    moves = [(own_ref, 0, first)]
    for k in range(1, plane):
        for ref in arrived_refs:
            moves.append((ref.at[place ^ k, pl.ds(0, slots)], first, slots))
            first += slots
    copies = []
    for i, (ref, at, count) in enumerate(moves):
        copy = pltpu.make_async_copy(ref, tiles_ref.at[pl.ds(at, count)], sems.at[i])
        copy.start()
        copies.append(copy)
    tiles_ref[first] = jnp.zeros_like(tiles_ref[first])
    return copies


def tile_space(tile_parts):
    own, arrived = tile_parts[0], tile_parts[1:]
    plane, slots = arrived[0].shape[0], arrived[0].shape[1] - 1
    moves = (plane - 1) * len(arrived)
    space = pltpu.VMEM((own.shape[0] + moves * slots + 1,) + own.shape[1:], jnp.bfloat16)
    return space, pltpu.SemaphoreType.DMA((1 + moves,))


def block_rows(index, size):
    return pl.ds(pl.multiple_of(index * size, size), size)


def forward_kernel(line, n_tiles, lanes, me_ref, plan_ref, count_ref, *refs):
    tile_refs, refs = refs[:n_tiles], refs[n_tiles:]
    part_refs, refs = refs[: 2 * line - 1], refs[2 * line - 1 :]
    out_refs, (tiles_ref, nodes_ref, acc_ref, tile_sems, part_sems) = refs[:-5], refs[-5:]
    rows, width = part_refs[0].shape[0], nodes_ref.shape[1]
    size = tiles_ref.shape[1]
    mine = me_ref[0]

    def each_part(act):
        for i, ref in enumerate(part_refs):
            source = mine + i - (line - 1)

            @pl.when((source >= 0) & (source < line))
            def _():
                here = ref.at[:, lanes] if ref.shape != (rows, width) else ref
                act(
                    pltpu.make_async_copy(
                        here, nodes_ref.at[block_rows(source, rows)], part_sems.at[i]
                    )
                )

    copies = load_tiles(me_ref[1], tile_refs, tiles_ref, tile_sems)
    each_part(lambda copy: copy.start())
    acc_ref[...] = jnp.zeros_like(acc_ref)
    for copy in copies:
        copy.wait()
    each_part(lambda copy: copy.wait())

    def step(i, carry):
        for j in range(UNROLL):
            position, dst, src = planned(plan_ref, i * UNROLL + j)
            acc_ref[block_rows(dst, size)] += jnp.dot(
                tiles_ref[position],
                nodes_ref[block_rows(src, size)],
                preferred_element_type=jnp.float32,
            )
        return carry

    lax.fori_loop(0, count_ref[0], step, 0)
    for k, ref in enumerate(out_refs):
        ref[...] = acc_ref[k * rows : (k + 1) * rows].astype(ref.dtype)


def forward_tiles(me, plan, tile_parts, node_parts, plane, lanes):
    line = (len(node_parts) + 1) // 2
    rows, width = node_parts[0].shape[0], lanes.size
    space, tile_sems = tile_space(tile_parts)
    kinds = [jnp.float32] + [jnp.bfloat16] * (plane - 1)
    outs = tuple(jax.ShapeDtypeStruct((rows, width), kind) for kind in kinds)
    scratch = [
        space,
        pltpu.VMEM((line * rows, width), jnp.bfloat16),
        pltpu.VMEM((plane * rows, width), jnp.float32),
    ]
    return pl.pallas_call(
        functools.partial(forward_kernel, line, len(tile_parts), lanes),
        out_shape=outs,
        in_specs=[SMEM] * 3 + [ANY] * (len(tile_parts) + len(node_parts)),
        out_specs=(VMEM,) * plane,
        scratch_shapes=scratch
        + [
            tile_sems,
            pltpu.SemaphoreType.DMA((len(node_parts),)),
        ],
        compiler_params=params(*outs, *scratch),
        name="forward_tiles",
    )(me, *plan, *tile_parts, *node_parts)


def dense_kernel(scale, chunk, halves, plane, me_ref, labels_ref, weight_ref, *refs):
    parts, outs = refs[: -1 - halves - plane - 1], refs[-1 - halves - plane - 1 :]
    act_ref, grad_refs, rest = outs[0], outs[1 : 1 + halves], outs[1 + halves :]
    quarter_ref, ride_refs, wgrad_ref = rest[0], rest[1:-1], rest[-1]
    rows, part_width = parts[0].shape
    width = part_width * halves
    features = weight_ref.shape[0]
    size = labels_ref.shape[1]
    quarter = features // plane
    wgrad_ref[...] = jnp.zeros_like(wgrad_ref)

    def rows_step(i, carry):
        here = block_rows(i, chunk)
        agg = jnp.concatenate([part[here, :] for part in parts], axis=1)
        hidden = jnp.dot(agg, weight_ref[...], preferred_element_type=jnp.float32)
        sigmoid = jax.nn.sigmoid(hidden)
        activated = hidden * sigmoid
        act_ref[here, :] = activated[:, :width].astype(act_ref.dtype)
        slopes = sigmoid * (1.0 + hidden * (1.0 - sigmoid))
        named = []
        for b in range(chunk // size):
            across = labels_ref[pl.ds(i * (chunk // size) + b, 1), :]
            named.append(jnp.broadcast_to(across, (size, size)).T)
        named = jnp.concatenate(named, axis=0)
        ids = lax.broadcasted_iota(jnp.int32, (chunk, size), 1).astype(jnp.float32)
        target = jnp.concatenate(
            [(named == ids + f * size).astype(jnp.float32) for f in range(features // size)],
            axis=1,
        )
        out_grad = ((activated - target) * slopes).astype(jnp.bfloat16)
        agg_grad = lax.dot_general(
            out_grad,
            weight_ref[:width, :],
            (((1,), (1,)), ((), ())),
            preferred_element_type=jnp.float32,
        ).astype(jnp.bfloat16)
        for h, ref in enumerate(grad_refs):
            ref[here, :] = agg_grad[:, h * part_width : (h + 1) * part_width]
        for ref in ride_refs:
            ref[here, :] = agg_grad[:, width - part_width :]
        wgrad_ref[...] += lax.dot_general(
            agg,
            out_grad[:, :width],
            (((0,), (0,)), ((), ())),
            preferred_element_type=jnp.float32,
        )
        return carry

    lax.fori_loop(0, rows // chunk, rows_step, 0)
    place = me_ref[1]
    quarter_ref[...] = wgrad_ref[block_rows(place, quarter)] * scale
    for k, ref in enumerate(ride_refs, 1):
        sent = (wgrad_ref[block_rows(place ^ k, quarter)] * scale).astype(ref.dtype)
        for h in range(halves):
            first = rows + h * quarter
            ref[first : first + quarter] = sent[:, h * part_width : (h + 1) * part_width]


def dense(me, labels, weight, parts, halves, plane, node_total):
    rows, part_width = parts[0].shape
    width = part_width * halves
    chunk = math.gcd(rows, 256)
    features = weight.shape[0]
    quarter = features // plane
    outs = (
        (jax.ShapeDtypeStruct((rows, width), jnp.bfloat16),)
        + (jax.ShapeDtypeStruct((rows, part_width), jnp.bfloat16),) * halves
        + (jax.ShapeDtypeStruct((quarter, width), jnp.float32),)
        + (jax.ShapeDtypeStruct((rows + halves * quarter, part_width), jnp.bfloat16),)
        * (plane - 1)
    )
    terms = pltpu.VMEM((features, width), jnp.float32)
    return pl.pallas_call(
        functools.partial(dense_kernel, 1.0 / math.sqrt(node_total), chunk, halves, plane),
        out_shape=outs,
        in_specs=[SMEM] + [VMEM] * (2 + len(parts)),
        out_specs=(VMEM,) * (1 + halves + plane),
        scratch_shapes=[terms],
        compiler_params=params(labels, weight, *parts, *outs, terms),
        name="dense",
    )(me, labels, weight, *parts)


def spread_kernel(line, n_tiles, plane, me_ref, plan_ref, count_ref, *refs):
    tile_refs, refs = refs[:n_tiles], refs[n_tiles:]
    grad_refs, refs = refs[:plane], refs[plane:]
    out_refs, (tiles_ref, grads_ref, acc_ref, tile_sems, grad_sems) = refs[:-5], refs[-5:]
    rows = grad_refs[0].shape[0]
    size = tiles_ref.shape[1]
    mine = me_ref[0]
    copies = load_tiles(me_ref[1], tile_refs, tiles_ref, tile_sems)
    for k, ref in enumerate(grad_refs):
        copy = pltpu.make_async_copy(
            ref.at[pl.ds(0, rows)], grads_ref.at[pl.ds(k * rows, rows)], grad_sems.at[k]
        )
        copy.start()
        copies.append(copy)
    acc_ref[...] = jnp.zeros_like(acc_ref)
    for copy in copies:
        copy.wait()

    def step(i, carry):
        for j in range(UNROLL):
            position, dst, src = planned(plan_ref, i * UNROLL + j)
            acc_ref[block_rows(src, size)] += lax.dot_general(
                tiles_ref[position],
                grads_ref[block_rows(dst, size)],
                (((0,), (0,)), ((), ())),
                preferred_element_type=jnp.float32,
            )
        return carry

    lax.fori_loop(0, count_ref[0], step, 0)
    for i, ref in enumerate(out_refs):
        target = mine + i - (line - 1)

        @pl.when((target >= 0) & (target < line))
        def _():
            ref[...] = acc_ref[block_rows(target, rows)].astype(ref.dtype)


def spread_tiles(me, plan, tile_parts, grads, line):
    plane = len(grads)
    rows, width = grads[0].shape
    space, tile_sems = tile_space(tile_parts)
    kinds = [jnp.float32 if i == line - 1 else jnp.bfloat16 for i in range(2 * line - 1)]
    outs = tuple(jax.ShapeDtypeStruct((rows, width), kind) for kind in kinds)
    scratch = [
        space,
        pltpu.VMEM((plane * rows, width), jnp.bfloat16),
        pltpu.VMEM((line * rows, width), jnp.float32),
    ]
    return pl.pallas_call(
        functools.partial(spread_kernel, line, len(tile_parts), plane),
        out_shape=outs,
        in_specs=[SMEM] * 3 + [ANY] * (len(tile_parts) + plane),
        out_specs=(VMEM,) * (2 * line - 1),
        scratch_shapes=scratch
        + [
            tile_sems,
            pltpu.SemaphoreType.DMA((plane,)),
        ],
        compiler_params=params(*outs, *scratch),
        name="spread_tiles",
    )(me, *plan, *tile_parts, *grads)


def line_steps(line, plane, step, reach):
    return [
        (z * plane + q, (z + step) * plane + q)
        for z in range(line)
        if 0 <= z + step < line and 0 <= z + reach < line
        for q in range(plane)
    ]


def line_gather(x, line, plane, lanes):
    far = line - 1
    up, down = [x], [x]
    for k in range(1, far - 1):
        up.append(shuffle(up[-1], line_steps(line, plane, 1, 1 - k)))
        down.append(shuffle(down[-1], line_steps(line, plane, -1, k - 1)))
    later, _ = lax.optimization_barrier((x, up[-1]))
    ends = [shuffle(later, line_steps(line, plane, step, step)) for step in (far, -far)]
    parts = []
    for part in lanes:
        low, high = up[:0:-1], down
        if far > 1:
            low = [shuffle(up[-1][:, part], line_steps(line, plane, 1, 2 - far))] + low
            high = high + [shuffle(down[-1][:, part], line_steps(line, plane, -1, far - 2))]
        parts.append([ends[0]] + low + high + [ends[1]])
    return parts


def line_sum(terms, line, plane):
    far = line - 1
    total = terms[far]
    for step in (1, -1):
        ending = shuffle(terms[far + step * far], line_steps(line, plane, step * far, step * far))
        moved = None
        for k in range(far - 1, 0, -1):
            term = terms[far + step * k]
            if moved is not None:
                term = (term.astype(jnp.float32) + moved.astype(jnp.float32)).astype(term.dtype)
            moved = shuffle(term, line_steps(line, plane, step, step * k))
        total = total + ending.astype(jnp.float32)
        if moved is not None:
            total = total + moved.astype(jnp.float32)
    return total.astype(jnp.bfloat16)


def sum_quarters(quarter, rides, z, q, line, plane):
    total = quarter
    for ride in rides:
        total = total + ride.astype(jnp.float32)
    k = 1
    while k < line:
        mine = total.astype(jnp.bfloat16)
        other = shuffle(mine, [(r, r ^ (k * plane)) for r in range(line * plane)])
        total = mine.astype(jnp.float32) + other.astype(jnp.float32)
        k *= 2
    k = 1
    while k < plane:
        other = across_plane(total, k, line, plane)
        lower = (q // k) % 2 == 0
        total = jnp.concatenate([jnp.where(lower, total, other), jnp.where(lower, other, total)])
        k *= 2
    return total


def per_device(node_features, weight, tile_values, tile_row, source_owner, source_block, labels):
    local_rows, width = node_features.shape
    n_tiles, block_size = tile_values.shape[:2]
    blocks = local_rows // block_size
    rows, cols = lax.axis_size("rows"), lax.axis_size("cols")
    plane = math.gcd(rows, LARGEST_PLANE)
    line = rows // plane
    halves = 2 if width % 256 == 0 else 1
    part_width = width // halves
    slots = -(-min(n_tiles, line * (2 * n_tiles // rows)) // cols)
    features = weight.shape[0]
    owners = source_owner[:, 0]

    index = lax.axis_index("rows")
    col = lax.axis_index("cols")
    z, q = index // plane, index % plane
    me = jnp.stack([z, q, col]).astype(jnp.int32)

    def other_cols(x):
        return [
            lax.ppermute(x, "cols", [((c + k) % cols, c) for c in range(cols)])
            for k in range(1, cols)
        ]

    lanes = [slice(h * part_width, (h + 1) * part_width) for h in range(halves)]
    node_parts = line_gather(node_features, line, plane, lanes)
    source = owners // plane * blocks + source_block
    codes = jnp.zeros((8, block_size), jnp.bfloat16)
    codes = codes.at[:3, :n_tiles].set(
        jnp.stack([owners % plane, tile_row, source]).astype(jnp.bfloat16)
    )
    packed = pack_tiles(me, owners, codes, tile_values, plane, cols, slots)
    planes = [[l * plane + p for p in range(plane)] for l in range(line)]
    arrived = lax.all_to_all(packed, "rows", 0, 0, axis_index_groups=planes, tiled=True)
    named = arrived[:, slots, :3, :n_tiles].astype(jnp.int32)
    code = named[:, 0] + (named[:, 1] << DST_BIT) + (named[:, 2] << SRC_BIT)
    plan = plan_tiles(me, code, plane, cols, slots, blocks, n_tiles)
    tile_parts = [tile_values, arrived] + other_cols(arrived)

    first = col * width
    own_first = jnp.roll(weight, (-first, -first), (0, 1))
    own_labels = ((labels - first) % features).reshape(blocks, block_size).astype(jnp.float32)
    plan, own_first, own_labels = lax.optimization_barrier((plan, own_first, own_labels))

    aggregated = []
    for h in range(halves):
        sums = forward_tiles(
            me, plan, tile_parts, node_parts[h], plane, pl.ds(h * part_width, part_width)
        )
        total = sums[0]
        for k in range(1, plane):
            total = total + across_plane(sums[k], k, line, plane).astype(jnp.float32)
        mine = total.astype(jnp.bfloat16)
        aggregated.append([mine] + other_cols(mine))
    parts = [aggregated[h][c] for c in range(cols) for h in range(halves)]

    outs = dense(me, own_labels, own_first, parts, halves, plane, local_rows * rows)
    activations, own_grads, quarter = outs[0], outs[1 : 1 + halves], outs[1 + halves]
    riding = outs[2 + halves :]

    feature_grads, rides = [], []
    for h in range(halves):
        if h > 0:
            riding, _ = lax.optimization_barrier((riding, grads[1]))
        grads = [own_grads[h]]
        for k in range(1, plane):
            sent = riding[k - 1] if h == halves - 1 else own_grads[h]
            grads.append(across_plane(sent, k, line, plane))
        if h == halves - 1:
            height = quarter.shape[0]
            for grad in grads[1:]:
                pieces = [grad[local_rows + i * height :][:height] for i in range(halves)]
                rides.append(jnp.concatenate(pieces, axis=1))
        terms = spread_tiles(me, plan, tile_parts, grads, line)
        feature_grads.append(line_sum(terms, line, plane))
    weight_grad = jnp.roll(sum_quarters(quarter, rides, z, q, line, plane), first, 0)
    return activations, weight_grad, jnp.concatenate(feature_grads, axis=1)


def solution(mesh):
    return jax.shard_map(
        per_device,
        mesh=mesh,
        in_specs=(
            P("rows", "cols"),
            P(),
            P("rows", None, None),
            P("rows"),
            P("rows", None),
            P("rows"),
            P("rows"),
        ),
        out_specs=(P("rows", "cols"), P(None, "cols"), P("rows", "cols")),
        check_vma=False,
    )
```

```python
import functools
import math

import jax
import jax.numpy as jnp
from jax import lax
from jax.experimental import pallas as pl
from jax.experimental.pallas import tpu as pltpu
from jax.sharding import PartitionSpec as P

VMEM = pl.BlockSpec(memory_space=pltpu.VMEM)
SMEM = pl.BlockSpec(memory_space=pltpu.SMEM)
ANY = pl.BlockSpec(memory_space=pl.ANY)
SPARE_BYTES = 6 * 1024 * 1024
UNROLL = 8
LARGEST_PLANE = 4


def params(*shapes):
    room = SPARE_BYTES
    for shape in shapes:
        *lead, high, wide = shape.shape
        room += math.prod(lead) * high * (-(-wide // 128) * 128) * jnp.dtype(shape.dtype).itemsize
    return pltpu.CompilerParams(vmem_limit_bytes=room)


def shuffle(x, pairs):
    return lax.ppermute(x, "rows", pairs)


def across_plane(x, k, line, plane):
    return shuffle(x, [(r, r ^ k) for r in range(line * plane)])


CODE_ROWS = 16


def pack_kernel(plane, cols, me_ref, owner_ref, owners_ref, row_ref, source_ref, tiles_ref, *refs):
    out_refs, (codes_ref, list_ref, slot_ref, rows_ref) = refs[: plane - 1], refs[plane - 1 :]
    place, col = me_ref[1], me_ref[2]
    slots = out_refs[0].shape[0] - 1
    spare = (plane - 1) * slots
    for k in range(plane):
        slot_ref[k] = 0
    for i in range(spare):
        list_ref[i] = 0

    def step(t, carry):
        k = lax.rem(owner_ref[t], plane) ^ place
        slot = slot_ref[k]
        slot_ref[k] = slot + 1
        sent = (k > 0) & (lax.rem(slot, cols) == col)
        list_ref[jnp.where(sent, (k - 1) * slots + lax.div(slot, cols), spare)] = t
        return carry

    tiles = tiles_ref.shape[0]
    lax.fori_loop(0, tiles, step, 0, unroll=4)
    rows_ref[...] = jnp.zeros_like(rows_ref)
    owners = owners_ref[...]
    group = lax.div(owners, plane)
    rows_ref[0:1, :tiles] = (owners - group * plane).astype(jnp.float32)
    rows_ref[1:2, :tiles] = row_ref[...].astype(jnp.float32)
    rows_ref[2:3, :tiles] = source_ref[...].astype(jnp.float32)
    rows_ref[3:4, :tiles] = group.astype(jnp.float32)
    codes = rows_ref[...].astype(codes_ref.dtype)
    codes_ref[...] = codes
    for k, out_ref in enumerate(out_refs):
        for slot in range(slots):
            out_ref[slot] = tiles_ref[list_ref[k * slots + slot]]
        out_ref[slots, :CODE_ROWS] = codes


def pack_tiles(me, owners, tile_row, source_block, tile_values, plane, cols, slots):
    tiles, block = tile_values.shape[0], tile_values.shape[1:]
    shape = jax.ShapeDtypeStruct((slots + 1,) + block, tile_values.dtype)
    codes = jax.ShapeDtypeStruct((CODE_ROWS, block[1]), tile_values.dtype)
    along = [x.reshape(1, tiles) for x in (owners, tile_row, source_block)]
    return pl.pallas_call(
        functools.partial(pack_kernel, plane, cols),
        out_shape=(shape,) * (plane - 1) + (codes,),
        in_specs=[SMEM, SMEM] + [VMEM] * 4,
        out_specs=(VMEM,) * plane,
        scratch_shapes=[
            pltpu.SMEM(((plane - 1) * slots + 1,), jnp.int32),
            pltpu.SMEM((plane,), jnp.int32),
            pltpu.VMEM((CODE_ROWS, block[1]), jnp.float32),
        ],
        compiler_params=params(tile_values, *(shape,) * (plane - 1)),
        name="pack_tiles",
    )(me, owners, *along, tile_values)


SRC_BIT = 12
PLACE_BIT = 24


def collect_kernel(plane, cols, slots, blocks, tiles, me_ref, own_ref, *refs):
    tile_refs, refs = refs[: 1 + (plane - 1) * cols], refs[1 + (plane - 1) * cols :]
    out_ref, turned_ref, plan_ref, count_ref, *scratch = refs
    rows_ref, words_ref, codes_ref, spots_ref, buffer_ref, row_sems, word_sem, tile_sems = scratch
    place, col = me_ref[1], me_ref[2]
    copies, first = [], 0
    for i, ref in enumerate(tile_refs):
        size = tiles if i == 0 else slots
        copy = pltpu.make_async_copy(
            ref.at[pl.ds(0, size)], buffer_ref.at[pl.ds(first, size)], tile_sems.at[i]
        )
        copy.start()
        copies.append(copy)
        first += size
    looks = []
    for k in range(plane):
        ref = own_ref if k == 0 else tile_refs[1 + (k - 1) * cols].at[slots, pl.ds(0, CODE_ROWS)]
        copy = pltpu.make_async_copy(ref, rows_ref.at[k], row_sems.at[k])
        copy.start()
        looks.append(copy)
    words_ref[...] = jnp.zeros_like(words_ref)
    for k, copy in enumerate(looks):
        copy.wait()
        rows = rows_ref[k].astype(jnp.float32).astype(jnp.int32)
        source = rows[3:4] * blocks + rows[2:3]
        word = (rows[0:1] << PLACE_BIT) + (source << SRC_BIT) + (rows[1:2] + k * blocks)
        words_ref[k : k + 1] = word
    copy = pltpu.make_async_copy(words_ref, codes_ref, word_sem)
    copy.start()
    copy.wait()
    found = jnp.int32(0)
    for k in range(plane):

        def step(t, carry, k=k):
            at, slot = carry
            code = codes_ref[k, t]
            if k == 0:
                spot = t
            else:
                column = lax.rem(slot + (cols - col), cols)
                spot = tiles + ((k - 1) * cols + column) * slots + lax.div(slot, cols)
            plan_ref[at] = code & ((1 << PLACE_BIT) - 1)
            spots_ref[at] = spot
            one = ((code >> PLACE_BIT) == place).astype(jnp.int32)
            return at + one, slot + one

        found, _ = lax.fori_loop(0, tiles, step, (found, jnp.int32(0)), unroll=8)
    for i in range(UNROLL):
        plan_ref[found + i] = 0
        spots_ref[found + i] = 0
    count = lax.div(found + UNROLL - 1, UNROLL)
    count_ref[0] = count
    for copy in copies:
        copy.wait()

    def lay(i, carry):
        for j in range(UNROLL):
            tile = buffer_ref[spots_ref[i * UNROLL + j]]
            out_ref[i * UNROLL + j] = tile
            turned_ref[i * UNROLL + j] = tile.T
        return carry

    lax.fori_loop(0, count, lay, 0)
    for i in range(UNROLL):
        out_ref[found + i] = jnp.zeros_like(out_ref[found + i])
        turned_ref[found + i] = jnp.zeros_like(turned_ref[found + i])


def collect_tiles(me, codes, tile_parts, plane, cols, slots, blocks, most):
    tiles, block = tile_parts[0].shape[0], tile_parts[0].shape[1:]
    entries = plane * tiles + UNROLL
    laid = jax.ShapeDtypeStruct((most + 2 * UNROLL,) + block, jnp.bfloat16)
    buffer = pltpu.VMEM((tiles + (plane - 1) * cols * slots,) + block, jnp.bfloat16)
    high = -(-plane // 8) * 8
    return pl.pallas_call(
        functools.partial(collect_kernel, plane, cols, slots, blocks, tiles),
        out_shape=(
            laid,
            laid,
            jax.ShapeDtypeStruct((entries,), jnp.int32),
            jax.ShapeDtypeStruct((1,), jnp.int32),
        ),
        in_specs=[SMEM] + [ANY] * (1 + len(tile_parts)),
        out_specs=(VMEM, VMEM, SMEM, SMEM),
        scratch_shapes=[
            pltpu.VMEM((plane, CODE_ROWS, block[1]), jnp.bfloat16),
            pltpu.VMEM((high, block[1]), jnp.int32),
            pltpu.SMEM((high, block[1]), jnp.int32),
            pltpu.SMEM((entries,), jnp.int32),
            buffer,
            pltpu.SemaphoreType.DMA((plane,)),
            pltpu.SemaphoreType.DMA,
            pltpu.SemaphoreType.DMA((len(tile_parts),)),
        ],
        compiler_params=params(laid, laid, buffer),
        name="collect_tiles",
    )(me, codes, *tile_parts)


def planned(plan_ref, t):
    entry = plan_ref[t]
    return entry & ((1 << SRC_BIT) - 1), entry >> SRC_BIT


def block_rows(index, size):
    return pl.ds(pl.multiple_of(index * size, size), size)


def forward_kernel(line, lanes, me_ref, plan_ref, count_ref, tiles_ref, *refs):
    part_refs, refs = refs[: 2 * line - 1], refs[2 * line - 1 :]
    out_refs, (nodes_ref, acc_ref, part_sems) = refs[:-3], refs[-3:]
    rows, width = part_refs[0].shape[0], nodes_ref.shape[1]
    size = tiles_ref.shape[1]
    mine = me_ref[0]

    def each_part(act):
        for i, ref in enumerate(part_refs):
            source = mine + i - (line - 1)

            @pl.when((source >= 0) & (source < line))
            def _():
                here = ref.at[:, lanes] if ref.shape != (rows, width) else ref
                act(
                    pltpu.make_async_copy(
                        here, nodes_ref.at[block_rows(source, rows)], part_sems.at[i]
                    )
                )

    each_part(lambda copy: copy.start())
    acc_ref[...] = jnp.zeros_like(acc_ref)
    each_part(lambda copy: copy.wait())

    def step(i, carry):
        for j in range(UNROLL):
            t = i * UNROLL + j
            dst, src = planned(plan_ref, t)
            acc_ref[block_rows(dst, size)] += jnp.dot(
                tiles_ref[t],
                nodes_ref[block_rows(src, size)],
                preferred_element_type=jnp.float32,
            )
        return carry

    lax.fori_loop(0, count_ref[0], step, 0)
    for k, ref in enumerate(out_refs):
        ref[...] = acc_ref[k * rows : (k + 1) * rows].astype(ref.dtype)


def forward_tiles(me, plan, count, tiles, node_parts, plane, lanes):
    line = (len(node_parts) + 1) // 2
    rows, width = node_parts[0].shape[0], lanes.size
    kinds = [jnp.float32] + [jnp.bfloat16] * (plane - 1)
    outs = tuple(jax.ShapeDtypeStruct((rows, width), kind) for kind in kinds)
    scratch = [
        pltpu.VMEM((line * rows, width), jnp.bfloat16),
        pltpu.VMEM((plane * rows, width), jnp.float32),
    ]
    return pl.pallas_call(
        functools.partial(forward_kernel, line, lanes),
        out_shape=outs,
        in_specs=[SMEM] * 3 + [VMEM] + [ANY] * len(node_parts),
        out_specs=(VMEM,) * plane,
        scratch_shapes=scratch + [pltpu.SemaphoreType.DMA((len(node_parts),))],
        compiler_params=params(tiles, *outs, *scratch),
        name="forward_tiles",
    )(me, plan, count, tiles, *node_parts)


def dense_kernel(chunk, halves, labels_ref, weight_ref, *refs):
    parts, (act_ref, out_grad_ref, agg_grad_ref) = refs[:-3], refs[-3:]
    rows, part_width = parts[0].shape
    width = part_width * halves
    features = weight_ref.shape[0]
    size = labels_ref.shape[1]

    def rows_step(i, carry):
        here = block_rows(i, chunk)
        agg = jnp.concatenate([part[here, :] for part in parts], axis=1)
        hidden = jnp.dot(agg, weight_ref[...], preferred_element_type=jnp.float32)
        sigmoid = jax.nn.sigmoid(hidden)
        activated = hidden * sigmoid
        act_ref[here, :] = activated[:, :width].astype(act_ref.dtype)
        slopes = sigmoid * (1.0 + hidden * (1.0 - sigmoid))
        named = []
        for b in range(chunk // size):
            across = labels_ref[pl.ds(i * (chunk // size) + b, 1), :]
            named.append(jnp.broadcast_to(across, (size, size)).T)
        named = jnp.concatenate(named, axis=0)
        ids = lax.broadcasted_iota(jnp.int32, (chunk, size), 1).astype(jnp.float32)
        target = jnp.concatenate(
            [(named == ids + f * size).astype(jnp.float32) for f in range(features // size)],
            axis=1,
        )
        out_grad = ((activated - target) * slopes).astype(jnp.bfloat16)
        out_grad_ref[here, :] = out_grad
        agg_grad_ref[here, :] = lax.dot_general(
            out_grad,
            weight_ref[:part_width, :],
            (((1,), (1,)), ((), ())),
            preferred_element_type=jnp.float32,
        ).astype(agg_grad_ref.dtype)
        return carry

    lax.fori_loop(0, rows // chunk, rows_step, 0)


def dense(labels, weight, parts, halves):
    rows, part_width = parts[0].shape
    chunk = math.gcd(rows, 256)
    outs = tuple(
        jax.ShapeDtypeStruct((rows, width), jnp.bfloat16)
        for width in (part_width * halves, weight.shape[0], part_width)
    )
    return pl.pallas_call(
        functools.partial(dense_kernel, chunk, halves),
        out_shape=outs,
        in_specs=[VMEM] * (2 + len(parts)),
        out_specs=(VMEM,) * 3,
        compiler_params=params(labels, weight, *parts, *outs),
        name="dense",
    )(labels, weight, *parts)


def grads_kernel(scale, halves, weight_ref, out_grad_ref, *refs):
    parts, (terms_ref, *agg_grad_refs) = refs[: -halves], refs[-halves:]
    part_width = parts[0].shape[1]
    for h, ref in enumerate(agg_grad_refs, 1):
        ref[...] = lax.dot_general(
            out_grad_ref[...],
            weight_ref[h * part_width : (h + 1) * part_width, :],
            (((1,), (1,)), ((), ())),
            preferred_element_type=jnp.float32,
        ).astype(ref.dtype)
    for i, part in enumerate(parts):
        terms = lax.dot_general(
            part[...],
            out_grad_ref[:, : part_width * halves],
            (((0,), (0,)), ((), ())),
            preferred_element_type=jnp.float32,
        )
        terms_ref[i * part_width : (i + 1) * part_width] = (terms * scale).astype(terms_ref.dtype)


def grads(weight, out_grad, parts, halves, node_total):
    rows, part_width = parts[0].shape
    outs = (jax.ShapeDtypeStruct((weight.shape[0], part_width * halves), jnp.bfloat16),) + (
        jax.ShapeDtypeStruct((rows, part_width), jnp.bfloat16),
    ) * (halves - 1)
    return pl.pallas_call(
        functools.partial(grads_kernel, 1.0 / math.sqrt(node_total), halves),
        out_shape=outs,
        in_specs=[VMEM] * (2 + len(parts)),
        out_specs=(VMEM,) * halves,
        compiler_params=params(weight, out_grad, *parts, *outs),
        name="grads",
    )(weight, out_grad, *parts)


def spread_kernel(line, plane, me_ref, plan_ref, count_ref, tiles_ref, *refs):
    grad_refs, refs = refs[:plane], refs[plane:]
    out_refs, (grads_ref, acc_ref, grad_sems) = refs[:-3], refs[-3:]
    rows = grad_refs[0].shape[0]
    size = tiles_ref.shape[1]
    mine = me_ref[0]
    copies = []
    for k, ref in enumerate(grad_refs):
        copy = pltpu.make_async_copy(ref, grads_ref.at[pl.ds(k * rows, rows)], grad_sems.at[k])
        copy.start()
        copies.append(copy)
    acc_ref[...] = jnp.zeros_like(acc_ref)
    for copy in copies:
        copy.wait()

    def step(i, carry):
        for j in range(UNROLL):
            t = i * UNROLL + j
            dst, src = planned(plan_ref, t)
            acc_ref[block_rows(src, size)] += jnp.dot(
                tiles_ref[t],
                grads_ref[block_rows(dst, size)],
                preferred_element_type=jnp.float32,
            )
        return carry

    lax.fori_loop(0, count_ref[0], step, 0)
    for i, ref in enumerate(out_refs):
        target = mine + i - (line - 1)

        @pl.when((target >= 0) & (target < line))
        def _():
            ref[...] = acc_ref[block_rows(target, rows)].astype(ref.dtype)


def spread_tiles(me, plan, count, tiles, grad_parts, line):
    plane = len(grad_parts)
    rows, width = grad_parts[0].shape
    kinds = [jnp.float32 if i == line - 1 else jnp.bfloat16 for i in range(2 * line - 1)]
    outs = tuple(jax.ShapeDtypeStruct((rows, width), kind) for kind in kinds)
    scratch = [
        pltpu.VMEM((plane * rows, width), jnp.bfloat16),
        pltpu.VMEM((line * rows, width), jnp.float32),
    ]
    return pl.pallas_call(
        functools.partial(spread_kernel, line, plane),
        out_shape=outs,
        in_specs=[SMEM] * 3 + [VMEM] + [ANY] * plane,
        out_specs=(VMEM,) * (2 * line - 1),
        scratch_shapes=scratch + [pltpu.SemaphoreType.DMA((plane,))],
        compiler_params=params(tiles, *outs, *scratch),
        name="spread_tiles",
    )(me, plan, count, tiles, *grad_parts)


def line_steps(line, plane, step, reach):
    return [
        (z * plane + q, (z + step) * plane + q)
        for z in range(line)
        if 0 <= z + step < line and 0 <= z + reach < line
        for q in range(plane)
    ]


def line_gather(x, line, plane, lanes):
    up, down = [x], [x]
    for k in range(1, line - 1):
        up.append(shuffle(up[-1], line_steps(line, plane, 1, 1 - k)))
        down.append(shuffle(down[-1], line_steps(line, plane, -1, k - 1)))
    parts = []
    for part in lanes:
        first = shuffle(up[-1][:, part], line_steps(line, plane, 1, 2 - line))
        last = shuffle(down[-1][:, part], line_steps(line, plane, -1, line - 2))
        parts.append([first] + up[:0:-1] + down + [last])
    return parts


def line_sum(terms, line, plane):
    total = terms[line - 1]
    for step in (1, -1):
        moved = None
        for k in range(line - 1, 0, -1):
            term = terms[line - 1 + step * k]
            if moved is not None:
                term = (term.astype(jnp.float32) + moved.astype(jnp.float32)).astype(term.dtype)
            moved = shuffle(term, line_steps(line, plane, step, step * k))
        if moved is not None:
            total = total + moved.astype(jnp.float32)
    return total.astype(jnp.bfloat16)


def sum_rows(terms, rows):
    apart = rows
    steps = []
    while apart > 1:
        apart //= 2
        steps.append(apart)
    near = [k for k in steps if k >= LARGEST_PLANE]
    for k in near[::-1] + [k for k in steps if k < LARGEST_PLANE]:
        other = shuffle(terms, [(r, r ^ k) for r in range(rows)])
        total = terms.astype(jnp.float32) + other.astype(jnp.float32)
        terms = total.astype(terms.dtype)
    return total


def per_device(node_features, weight, tile_values, tile_row, source_owner, source_block, labels):
    local_rows, width = node_features.shape
    n_tiles, block_size = tile_values.shape[:2]
    blocks = local_rows // block_size
    rows, cols = lax.axis_size("rows"), lax.axis_size("cols")
    plane = math.gcd(rows, LARGEST_PLANE)
    line = rows // plane
    halves = 2 if width % 256 == 0 else 1
    part_width = width // halves
    slots = -(-min(n_tiles, line * (2 * n_tiles // rows)) // cols)
    features = weight.shape[0]
    owners = source_owner[:, 0]

    index = lax.axis_index("rows")
    col = lax.axis_index("cols")
    z, q = index // plane, index % plane
    me = jnp.stack([z, q, col]).astype(jnp.int32)

    def other_cols(x):
        return [
            lax.ppermute(x, "cols", [((c + k) % cols, c) for c in range(cols)])
            for k in range(1, cols)
        ]

    lanes = [slice(h * part_width, (h + 1) * part_width) for h in range(halves)]
    node_parts = line_gather(node_features, line, plane, lanes)
    *packed, codes = pack_tiles(
        me, owners, tile_row, source_block, tile_values, plane, cols, slots
    )
    tile_parts = [tile_values]
    for k in range(1, plane):
        arrived = across_plane(packed[k - 1], k, line, plane)
        tile_parts += [arrived] + other_cols(arrived)
    most = plane * min(n_tiles, line * (2 * n_tiles // rows))
    tiles, turned, plan, count = collect_tiles(
        me, codes, tile_parts, plane, cols, slots, blocks, most
    )

    first = col * width
    own_first = jnp.roll(weight, (-first, -first), (0, 1))
    own_labels = ((labels - first) % features).reshape(blocks, block_size).astype(jnp.float32)
    plan, own_first, own_labels = lax.optimization_barrier((plan, own_first, own_labels))

    aggregated = []
    for h in range(halves):
        here = pl.ds(h * part_width, part_width)
        sums = forward_tiles(me, plan, count, tiles, node_parts[h], plane, here)
        total = sums[0]
        for k in range(1, plane):
            total = total + across_plane(sums[k], k, line, plane).astype(jnp.float32)
        mine = total.astype(jnp.bfloat16)
        aggregated.append([mine] + other_cols(mine))
    parts = [aggregated[h][c] for c in range(cols) for h in range(halves)]

    activations, out_grad, agg_grad = dense(own_labels, own_first, parts, halves)
    weight_terms, *agg_grads = grads(own_first, out_grad, parts, halves, local_rows * rows)

    feature_grads = []
    for agg_grad in [agg_grad] + agg_grads:
        arrived = [agg_grad] + [across_plane(agg_grad, k, line, plane) for k in range(1, plane)]
        terms = spread_tiles(me, plan, count, turned, arrived, line)
        feature_grads.append(line_sum(terms, line, plane))
    weight_grad = jnp.roll(sum_rows(weight_terms, rows), first, 0)
    return activations, weight_grad, jnp.concatenate(feature_grads, axis=1)


def solution(mesh):
    return jax.shard_map(
        per_device,
        mesh=mesh,
        in_specs=(
            P("rows", "cols"),
            P(),
            P("rows", None, None),
            P("rows"),
            P("rows", None),
            P("rows"),
            P("rows"),
        ),
        out_specs=(P("rows", "cols"), P(None, "cols"), P("rows", "cols")),
        check_vma=False,
    )
```

```python
import functools
import math

import jax
import jax.numpy as jnp
from jax import lax
from jax.experimental import pallas as pl
from jax.experimental.pallas import tpu as pltpu
from jax.sharding import PartitionSpec as P

VMEM = pl.BlockSpec(memory_space=pltpu.VMEM)
SMEM = pl.BlockSpec(memory_space=pltpu.SMEM)
ANY = pl.BlockSpec(memory_space=pl.ANY)
HBM = pl.BlockSpec(memory_space=pltpu.HBM)
SPARE_BYTES = 6 * 1024 * 1024
PACK_BYTES = 56 * 1024 * 1024
UNROLL = 8
LARGEST_PLANE = 4


def params(*shapes):
    room = SPARE_BYTES
    for shape in shapes:
        *lead, high, wide = shape.shape
        room += math.prod(lead) * high * (-(-wide // 128) * 128) * jnp.dtype(shape.dtype).itemsize
    return pltpu.CompilerParams(vmem_limit_bytes=room)


def shuffle(x, pairs):
    return lax.ppermute(x, "rows", pairs)


def across_plane(x, k, line, plane):
    return shuffle(x, [(r, r ^ k) for r in range(line * plane)])


CODE_ROWS = 16


def pack_kernel(plane, cols, me_ref, owner_ref, row_ref, source_ref, tiles_ref, *refs):
    out_refs, (codes_ref, *scratch) = refs[: plane - 1], refs[plane - 1 :]
    list_ref, slot_ref, owners_ref, along_ref, rows_ref, small_sems, tile_sems = scratch
    place, col = me_ref[1], me_ref[2]
    tiles = tiles_ref.shape[0]
    slots = out_refs[0].shape[0] - 1
    spare = (plane - 1) * slots
    looks = [pltpu.make_async_copy(owner_ref, owners_ref, small_sems.at[0])]
    for i, ref in enumerate((owner_ref, row_ref, source_ref)):
        looks.append(pltpu.make_async_copy(ref, along_ref.at[i], small_sems.at[1 + i]))
    for look in looks:
        look.start()
    for k in range(plane):
        slot_ref[k] = 0
    for i in range(spare):
        list_ref[i] = 0
    rows_ref[...] = jnp.zeros_like(rows_ref)
    for look in looks:
        look.wait()

    def step(t, carry):
        k = lax.rem(owners_ref[0, t], plane) ^ place
        slot = slot_ref[k]
        slot_ref[k] = slot + 1
        sent = (k > 0) & (lax.rem(slot, cols) == col)
        list_ref[jnp.where(sent, (k - 1) * slots + lax.div(slot, cols), spare)] = t
        return carry

    lax.fori_loop(0, tiles, step, 0, unroll=4)
    copies = []
    for k, out_ref in enumerate(out_refs):
        for slot in range(slots):
            at = k * slots + slot
            copy = pltpu.make_async_copy(
                tiles_ref.at[list_ref[at]], out_ref.at[slot], tile_sems.at[at]
            )
            copy.start()
            copies.append(copy)
    owners = along_ref[0]
    group = lax.div(owners, plane)
    rows_ref[0:1, :tiles] = (owners - group * plane).astype(jnp.float32)
    rows_ref[1:2, :tiles] = along_ref[1].astype(jnp.float32)
    rows_ref[2:3, :tiles] = along_ref[2].astype(jnp.float32)
    rows_ref[3:4, :tiles] = group.astype(jnp.float32)
    codes = rows_ref[...].astype(codes_ref.dtype)
    codes_ref[...] = codes
    for out_ref in out_refs:
        out_ref[slots, :CODE_ROWS] = codes
    for copy in copies:
        copy.wait()


def pack_tiles(me, owners, tile_row, source_block, tile_values, plane, cols, slots):
    tiles, block = tile_values.shape[0], tile_values.shape[1:]
    shape = jax.ShapeDtypeStruct((slots + 1,) + block, tile_values.dtype)
    codes = jax.ShapeDtypeStruct((CODE_ROWS, block[1]), tile_values.dtype)
    along = [x.reshape(1, tiles) for x in (owners, tile_row, source_block)]
    return pl.pallas_call(
        functools.partial(pack_kernel, plane, cols),
        out_shape=(shape,) * (plane - 1) + (codes,),
        in_specs=[SMEM] + [HBM] * 4,
        out_specs=(VMEM,) * plane,
        scratch_shapes=[
            pltpu.SMEM(((plane - 1) * slots + 1,), jnp.int32),
            pltpu.SMEM((plane,), jnp.int32),
            pltpu.SMEM((1, tiles), jnp.int32),
            pltpu.VMEM((3, 1, tiles), jnp.int32),
            pltpu.VMEM((CODE_ROWS, block[1]), jnp.float32),
            pltpu.SemaphoreType.DMA((4,)),
            pltpu.SemaphoreType.DMA(((plane - 1) * slots,)),
        ],
        compiler_params=pltpu.CompilerParams(vmem_limit_bytes=PACK_BYTES),
        name="pack_tiles",
    )(me, *along, tile_values)


DST_BIT, SRC_BIT, PLACE_BIT = 10, 16, 24


def collect_kernel(plane, cols, slots, blocks, tiles, me_ref, own_ref, *refs):
    tile_refs, refs = refs[: 1 + (plane - 1) * cols], refs[1 + (plane - 1) * cols :]
    out_ref, plan_ref, count_ref, *scratch = refs
    rows_ref, words_ref, codes_ref, row_sems, word_sem, tile_sems = scratch
    place, col = me_ref[1], me_ref[2]
    looks = []
    for k in range(plane):
        ref = own_ref if k == 0 else tile_refs[1 + (k - 1) * cols].at[slots, pl.ds(0, CODE_ROWS)]
        copy = pltpu.make_async_copy(ref, rows_ref.at[k], row_sems.at[k])
        copy.start()
        looks.append(copy)
    copies, first = [], 0
    for i, ref in enumerate(tile_refs):
        size = tiles if i == 0 else slots
        copy = pltpu.make_async_copy(
            ref.at[pl.ds(0, size)], out_ref.at[pl.ds(first, size)], tile_sems.at[i]
        )
        copy.start()
        copies.append(copy)
        first += size
    out_ref[first] = jnp.zeros_like(out_ref[first])
    words_ref[...] = jnp.zeros_like(words_ref)
    for k, copy in enumerate(looks):
        copy.wait()
        rows = rows_ref[k].astype(jnp.float32).astype(jnp.int32)
        source = rows[3:4] * blocks + rows[2:3]
        word = (rows[0:1] << PLACE_BIT) + (source << SRC_BIT)
        words_ref[k : k + 1] = word + ((rows[1:2] + k * blocks) << DST_BIT)
    copy = pltpu.make_async_copy(words_ref, codes_ref, word_sem)
    copy.start()
    copy.wait()
    found = jnp.int32(0)
    for k in range(plane):

        def step(t, carry, k=k):
            at, slot = carry
            code = codes_ref[k, t]
            if k == 0:
                spot = t
            else:
                column = lax.rem(slot + (cols - col), cols)
                spot = tiles + ((k - 1) * cols + column) * slots + lax.div(slot, cols)
            plan_ref[at] = (code & ((1 << PLACE_BIT) - 1)) + spot
            one = ((code >> PLACE_BIT) == place).astype(jnp.int32)
            return at + one, slot + one

        found, _ = lax.fori_loop(0, tiles, step, (found, jnp.int32(0)), unroll=8)
    for i in range(UNROLL):
        plan_ref[found + i] = first
    count_ref[0] = lax.div(found + UNROLL - 1, UNROLL)
    for copy in copies:
        copy.wait()


def collect_tiles(me, codes, tile_parts, plane, cols, slots, blocks):
    tiles, block = tile_parts[0].shape[0], tile_parts[0].shape[1:]
    entries = plane * tiles + UNROLL
    spots = tiles + (plane - 1) * cols * slots + 1
    laid = jax.ShapeDtypeStruct((spots,) + block, jnp.bfloat16)
    high = -(-plane // 8) * 8
    return pl.pallas_call(
        functools.partial(collect_kernel, plane, cols, slots, blocks, tiles),
        out_shape=(
            laid,
            jax.ShapeDtypeStruct((entries,), jnp.int32),
            jax.ShapeDtypeStruct((1,), jnp.int32),
        ),
        in_specs=[SMEM] + [ANY] * (1 + len(tile_parts)),
        out_specs=(VMEM, SMEM, SMEM),
        scratch_shapes=[
            pltpu.VMEM((plane, CODE_ROWS, block[1]), jnp.bfloat16),
            pltpu.VMEM((high, block[1]), jnp.int32),
            pltpu.SMEM((high, block[1]), jnp.int32),
            pltpu.SemaphoreType.DMA((plane,)),
            pltpu.SemaphoreType.DMA,
            pltpu.SemaphoreType.DMA((len(tile_parts),)),
        ],
        compiler_params=params(laid),
        name="collect_tiles",
    )(me, codes, *tile_parts)


def planned(plan_ref, t):
    entry = plan_ref[t]
    spot = entry & ((1 << DST_BIT) - 1)
    return spot, (entry >> DST_BIT) & ((1 << (SRC_BIT - DST_BIT)) - 1), entry >> SRC_BIT


def turn_kernel(plan_ref, count_ref, tiles_ref, out_ref):
    def step(i, carry):
        for j in range(UNROLL):
            t = i * UNROLL + j
            out_ref[t] = tiles_ref[planned(plan_ref, t)[0]].T
        return carry

    lax.fori_loop(0, count_ref[0], step, 0)


def turn_tiles(plan, count, tiles, most):
    turned = jax.ShapeDtypeStruct((most + UNROLL,) + tiles.shape[1:], tiles.dtype)
    return pl.pallas_call(
        turn_kernel,
        out_shape=turned,
        in_specs=[SMEM, SMEM, VMEM],
        out_specs=VMEM,
        compiler_params=params(tiles, turned),
        name="turn_tiles",
    )(plan, count, tiles)


def block_rows(index, size):
    return pl.ds(pl.multiple_of(index * size, size), size)


def forward_kernel(line, lanes, me_ref, plan_ref, count_ref, tiles_ref, *refs):
    part_refs, refs = refs[: 2 * line - 1], refs[2 * line - 1 :]
    out_refs, (nodes_ref, acc_ref, part_sems) = refs[:-3], refs[-3:]
    rows, width = part_refs[0].shape[0], nodes_ref.shape[1]
    size = tiles_ref.shape[1]
    mine = me_ref[0]

    def each_part(act):
        for i, ref in enumerate(part_refs):
            source = mine + i - (line - 1)

            @pl.when((source >= 0) & (source < line))
            def _():
                here = ref.at[:, lanes] if ref.shape != (rows, width) else ref
                act(
                    pltpu.make_async_copy(
                        here, nodes_ref.at[block_rows(source, rows)], part_sems.at[i]
                    )
                )

    each_part(lambda copy: copy.start())
    acc_ref[...] = jnp.zeros_like(acc_ref)
    each_part(lambda copy: copy.wait())

    def step(i, carry):
        for j in range(UNROLL):
            spot, dst, src = planned(plan_ref, i * UNROLL + j)
            acc_ref[block_rows(dst, size)] += jnp.dot(
                tiles_ref[spot],
                nodes_ref[block_rows(src, size)],
                preferred_element_type=jnp.float32,
            )
        return carry

    lax.fori_loop(0, count_ref[0], step, 0)
    for k, ref in enumerate(out_refs):
        ref[...] = acc_ref[k * rows : (k + 1) * rows].astype(ref.dtype)


def forward_tiles(me, plan, count, tiles, node_parts, plane, lanes):
    line = (len(node_parts) + 1) // 2
    rows, width = node_parts[0].shape[0], lanes.size
    kinds = [jnp.float32] + [jnp.bfloat16] * (plane - 1)
    outs = tuple(jax.ShapeDtypeStruct((rows, width), kind) for kind in kinds)
    scratch = [
        pltpu.VMEM((line * rows, width), jnp.bfloat16),
        pltpu.VMEM((plane * rows, width), jnp.float32),
    ]
    return pl.pallas_call(
        functools.partial(forward_kernel, line, lanes),
        out_shape=outs,
        in_specs=[SMEM] * 3 + [VMEM] + [ANY] * len(node_parts),
        out_specs=(VMEM,) * plane,
        scratch_shapes=scratch + [pltpu.SemaphoreType.DMA((len(node_parts),))],
        compiler_params=params(tiles, *outs, *scratch),
        name="forward_tiles",
    )(me, plan, count, tiles, *node_parts)


def dense_kernel(chunk, halves, labels_ref, weight_ref, *refs):
    parts, (act_ref, out_grad_ref, agg_grad_ref) = refs[:-3], refs[-3:]
    rows, part_width = parts[0].shape
    width = part_width * halves
    features = weight_ref.shape[0]
    size = labels_ref.shape[1]

    def rows_step(i, carry):
        here = block_rows(i, chunk)
        agg = jnp.concatenate([part[here, :] for part in parts], axis=1)
        hidden = jnp.dot(agg, weight_ref[...], preferred_element_type=jnp.float32)
        sigmoid = jax.nn.sigmoid(hidden)
        activated = hidden * sigmoid
        act_ref[here, :] = activated[:, :width].astype(act_ref.dtype)
        slopes = sigmoid * (1.0 + hidden * (1.0 - sigmoid))
        named = []
        for b in range(chunk // size):
            across = labels_ref[pl.ds(i * (chunk // size) + b, 1), :]
            named.append(jnp.broadcast_to(across, (size, size)).T)
        named = jnp.concatenate(named, axis=0)
        ids = lax.broadcasted_iota(jnp.int32, (chunk, size), 1).astype(jnp.float32)
        target = jnp.concatenate(
            [(named == ids + f * size).astype(jnp.float32) for f in range(features // size)],
            axis=1,
        )
        out_grad = ((activated - target) * slopes).astype(jnp.bfloat16)
        out_grad_ref[here, :] = out_grad
        agg_grad_ref[here, :] = lax.dot_general(
            out_grad,
            weight_ref[:part_width, :],
            (((1,), (1,)), ((), ())),
            preferred_element_type=jnp.float32,
        ).astype(agg_grad_ref.dtype)
        return carry

    lax.fori_loop(0, rows // chunk, rows_step, 0)


def dense(labels, weight, parts, halves):
    rows, part_width = parts[0].shape
    chunk = math.gcd(rows, 256)
    outs = tuple(
        jax.ShapeDtypeStruct((rows, width), jnp.bfloat16)
        for width in (part_width * halves, weight.shape[0], part_width)
    )
    return pl.pallas_call(
        functools.partial(dense_kernel, chunk, halves),
        out_shape=outs,
        in_specs=[VMEM] * (2 + len(parts)),
        out_specs=(VMEM,) * 3,
        compiler_params=params(labels, weight, *parts, *outs),
        name="dense",
    )(labels, weight, *parts)


def grads_kernel(scale, halves, weight_ref, out_grad_ref, *refs):
    parts, (terms_ref, *agg_grad_refs) = refs[: -halves], refs[-halves:]
    part_width = parts[0].shape[1]
    for h, ref in enumerate(agg_grad_refs, 1):
        ref[...] = lax.dot_general(
            out_grad_ref[...],
            weight_ref[h * part_width : (h + 1) * part_width, :],
            (((1,), (1,)), ((), ())),
            preferred_element_type=jnp.float32,
        ).astype(ref.dtype)
    for i, part in enumerate(parts):
        terms = lax.dot_general(
            part[...],
            out_grad_ref[:, : part_width * halves],
            (((0,), (0,)), ((), ())),
            preferred_element_type=jnp.float32,
        )
        terms_ref[i * part_width : (i + 1) * part_width] = (terms * scale).astype(terms_ref.dtype)


def grads(weight, out_grad, parts, halves, node_total):
    rows, part_width = parts[0].shape
    outs = (jax.ShapeDtypeStruct((weight.shape[0], part_width * halves), jnp.bfloat16),) + (
        jax.ShapeDtypeStruct((rows, part_width), jnp.bfloat16),
    ) * (halves - 1)
    return pl.pallas_call(
        functools.partial(grads_kernel, 1.0 / math.sqrt(node_total), halves),
        out_shape=outs,
        in_specs=[VMEM] * (2 + len(parts)),
        out_specs=(VMEM,) * halves,
        compiler_params=params(weight, out_grad, *parts, *outs),
        name="grads",
    )(weight, out_grad, *parts)


def spread_kernel(line, plane, me_ref, plan_ref, count_ref, tiles_ref, *refs):
    grad_refs, refs = refs[:plane], refs[plane:]
    out_refs, (grads_ref, acc_ref, grad_sems) = refs[:-3], refs[-3:]
    rows = grad_refs[0].shape[0]
    size = tiles_ref.shape[1]
    mine = me_ref[0]
    copies = []
    for k, ref in enumerate(grad_refs):
        copy = pltpu.make_async_copy(ref, grads_ref.at[pl.ds(k * rows, rows)], grad_sems.at[k])
        copy.start()
        copies.append(copy)
    acc_ref[...] = jnp.zeros_like(acc_ref)
    for copy in copies:
        copy.wait()

    def step(i, carry):
        for j in range(UNROLL):
            t = i * UNROLL + j
            _, dst, src = planned(plan_ref, t)
            acc_ref[block_rows(src, size)] += jnp.dot(
                tiles_ref[t],
                grads_ref[block_rows(dst, size)],
                preferred_element_type=jnp.float32,
            )
        return carry

    lax.fori_loop(0, count_ref[0], step, 0)
    for i, ref in enumerate(out_refs):
        target = mine + i - (line - 1)

        @pl.when((target >= 0) & (target < line))
        def _():
            ref[...] = acc_ref[block_rows(target, rows)].astype(ref.dtype)


def spread_tiles(me, plan, count, tiles, grad_parts, line):
    plane = len(grad_parts)
    rows, width = grad_parts[0].shape
    kinds = [jnp.float32 if i == line - 1 else jnp.bfloat16 for i in range(2 * line - 1)]
    outs = tuple(jax.ShapeDtypeStruct((rows, width), kind) for kind in kinds)
    scratch = [
        pltpu.VMEM((plane * rows, width), jnp.bfloat16),
        pltpu.VMEM((line * rows, width), jnp.float32),
    ]
    return pl.pallas_call(
        functools.partial(spread_kernel, line, plane),
        out_shape=outs,
        in_specs=[SMEM] * 3 + [VMEM] + [ANY] * plane,
        out_specs=(VMEM,) * (2 * line - 1),
        scratch_shapes=scratch + [pltpu.SemaphoreType.DMA((plane,))],
        compiler_params=params(tiles, *outs, *scratch),
        name="spread_tiles",
    )(me, plan, count, tiles, *grad_parts)


def line_steps(line, plane, step, reach):
    return [
        (z * plane + q, (z + step) * plane + q)
        for z in range(line)
        if 0 <= z + step < line and 0 <= z + reach < line
        for q in range(plane)
    ]


def line_gather(x, line, plane, lanes):
    up, down = [x], [x]
    for k in range(1, line - 1):
        up.append(shuffle(up[-1], line_steps(line, plane, 1, 1 - k)))
        down.append(shuffle(down[-1], line_steps(line, plane, -1, k - 1)))
    parts = []
    for part in lanes:
        first = shuffle(up[-1][:, part], line_steps(line, plane, 1, 2 - line))
        last = shuffle(down[-1][:, part], line_steps(line, plane, -1, line - 2))
        parts.append([first] + up[:0:-1] + down + [last])
    return parts


def line_sum(terms, line, plane):
    pieces, early, late = [terms[line - 1]], [], []
    for step in (1, -1):
        moved = None
        for k in range(line - 1, 0, -1):
            term = terms[line - 1 + step * k]
            if moved is not None:
                term = (term.astype(jnp.float32) + moved.astype(jnp.float32)).astype(term.dtype)
            moved = shuffle(term, line_steps(line, plane, step, step * k))
            if k == line - 1:
                late.append(moved)
            if k == line - 2:
                early.append(term)
        pieces.append(moved)
    return pieces, early, late


def finish_kernel(halves, *refs):
    out_ref, refs = refs[-1], refs[:-1]
    each = len(refs) // halves
    width = refs[0].shape[1]
    for h in range(halves):
        total = refs[h * each][...]
        for ref in refs[h * each + 1 : (h + 1) * each]:
            total += ref[...].astype(jnp.float32)
        out_ref[:, h * width : (h + 1) * width] = total.astype(out_ref.dtype)


def finish(pieces):
    flat = [piece for half in pieces for piece in half]
    rows, width = flat[0].shape
    out = jax.ShapeDtypeStruct((rows, width * len(pieces)), jnp.bfloat16)
    return pl.pallas_call(
        functools.partial(finish_kernel, len(pieces)),
        out_shape=out,
        in_specs=[VMEM] * len(flat),
        out_specs=VMEM,
        compiler_params=params(out, *flat),
        name="finish",
    )(*flat)


def sum_apart(terms, first, end, rows):
    while first < end:
        other = shuffle(terms, [(r, r ^ first) for r in range(rows)])
        total = terms.astype(jnp.float32) + other.astype(jnp.float32)
        terms = total.astype(terms.dtype)
        first *= 2
    return total


def per_device(node_features, weight, tile_values, tile_row, source_owner, source_block, labels):
    local_rows, width = node_features.shape
    n_tiles, block_size = tile_values.shape[:2]
    blocks = local_rows // block_size
    rows, cols = lax.axis_size("rows"), lax.axis_size("cols")
    plane = math.gcd(rows, LARGEST_PLANE)
    line = rows // plane
    halves = 2 if width % 256 == 0 else 1
    part_width = width // halves
    slots = -(-min(n_tiles, line * (2 * n_tiles // rows)) // cols)
    features = weight.shape[0]
    owners = source_owner[:, 0]

    index = lax.axis_index("rows")
    col = lax.axis_index("cols")
    z, q = index // plane, index % plane
    me = jnp.stack([z, q, col]).astype(jnp.int32)

    def other_cols(x):
        return [
            lax.ppermute(x, "cols", [((c + k) % cols, c) for c in range(cols)])
            for k in range(1, cols)
        ]

    lanes = [slice(h * part_width, (h + 1) * part_width) for h in range(halves)]
    *packed, codes = pack_tiles(
        me, owners, tile_row, source_block, tile_values, plane, cols, slots
    )
    node_features, _ = lax.optimization_barrier((node_features, packed))
    node_parts = line_gather(node_features, line, plane, lanes)
    tile_parts = [tile_values]
    for k in range(1, plane):
        arrived = across_plane(packed[k - 1], k, line, plane)
        tile_parts += [arrived] + other_cols(arrived)
    most = plane * min(n_tiles, line * (2 * n_tiles // rows))
    tiles, plan, count = collect_tiles(me, codes, tile_parts, plane, cols, slots, blocks)

    first = col * width
    own_first = jnp.roll(weight, (-first, -first), (0, 1))
    own_labels = ((labels - first) % features).reshape(blocks, block_size).astype(jnp.float32)
    plan, own_first, own_labels = lax.optimization_barrier((plan, own_first, own_labels))

    aggregated = []
    for h in range(halves):
        here = pl.ds(h * part_width, part_width)
        sums = forward_tiles(me, plan, count, tiles, node_parts[h], plane, here)
        total = sums[0]
        for k in range(1, plane):
            total = total + across_plane(sums[k], k, line, plane).astype(jnp.float32)
        mine = total.astype(jnp.bfloat16)
        aggregated.append([mine] + other_cols(mine))
    parts = [aggregated[h][c] for c in range(cols) for h in range(halves)]

    later, _ = lax.optimization_barrier((tiles, sums[0]))
    turned = turn_tiles(plan, count, later, most)
    own_labels, turned = lax.optimization_barrier((own_labels, turned))

    activations, out_grad, agg_grad = dense(own_labels, own_first, parts, halves)
    weight_terms, *agg_grads = grads(own_first, out_grad, parts, halves, local_rows * rows)

    pieces = []
    for i, agg_grad in enumerate(agg_grads[::-1] + [agg_grad]):
        arrived = [agg_grad] + [across_plane(agg_grad, k, line, plane) for k in range(1, plane)]
        terms = spread_tiles(me, plan, count, turned, arrived, line)
        half, early, late = line_sum(terms, line, plane)
        pieces.append(half)
        if i == 0:
            weight_terms = sum_apart(weight_terms, plane, 2 * plane, rows).astype(jnp.bfloat16)
            weight_terms, _ = lax.optimization_barrier((weight_terms, early))
    if line > 2:
        weight_terms = sum_apart(weight_terms, 2 * plane, rows, rows).astype(jnp.bfloat16)
    weight_terms, _ = lax.optimization_barrier((weight_terms, late))
    weight_terms = sum_apart(weight_terms, 1, plane, rows)
    weight_grad = jnp.roll(weight_terms, first, 0)
    return activations, weight_grad, finish(pieces[::-1])


def solution(mesh):
    return jax.shard_map(
        per_device,
        mesh=mesh,
        in_specs=(
            P("rows", "cols"),
            P(),
            P("rows", None, None),
            P("rows"),
            P("rows", None),
            P("rows"),
            P("rows"),
        ),
        out_specs=(P("rows", "cols"), P(None, "cols"), P("rows", "cols")),
        check_vma=False,
    )
```

```python
import functools
import math

import jax
import jax.numpy as jnp
from jax import lax
from jax.experimental import pallas as pl
from jax.experimental.pallas import tpu as pltpu
from jax.sharding import PartitionSpec as P

VMEM = pl.BlockSpec(memory_space=pltpu.VMEM)
SMEM = pl.BlockSpec(memory_space=pltpu.SMEM)
ANY = pl.BlockSpec(memory_space=pl.ANY)
HBM = pl.BlockSpec(memory_space=pltpu.HBM)
SPARE_BYTES = 6 * 1024 * 1024
PACK_BYTES = 56 * 1024 * 1024
UNROLL = 8
LARGEST_PLANE = 4


def params(*shapes):
    room = SPARE_BYTES
    for shape in shapes:
        *lead, high, wide = shape.shape
        room += math.prod(lead) * high * (-(-wide // 128) * 128) * jnp.dtype(shape.dtype).itemsize
    return pltpu.CompilerParams(vmem_limit_bytes=room)


def quotient(x, n):
    return x >> (n.bit_length() - 1) if n & (n - 1) == 0 else lax.div(x, n)


def remainder(x, n):
    return x & (n - 1) if n & (n - 1) == 0 else lax.rem(x, n)


def shuffle(x, pairs):
    return lax.ppermute(x, "rows", pairs)


def across_plane(x, k, line, plane):
    return shuffle(x, [(r, r ^ k) for r in range(line * plane)])


CODE_ROWS = 16


def pack_kernel(plane, cols, me_ref, owner_ref, row_ref, source_ref, tiles_ref, *refs):
    out_refs, (codes_ref, *scratch) = refs[: plane - 1], refs[plane - 1 :]
    list_ref, slot_ref, owners_ref, along_ref, rows_ref, held_ref, small_sems, held_sem = scratch
    place, col = me_ref[1], me_ref[2]
    tiles, size = tiles_ref.shape[:2]
    slots = (out_refs[0].shape[0] - CODE_ROWS) // size
    spare = (plane - 1) * slots
    looks = [pltpu.make_async_copy(owner_ref, owners_ref, small_sems.at[0])]
    for i, ref in enumerate((owner_ref, row_ref, source_ref)):
        looks.append(pltpu.make_async_copy(ref, along_ref.at[i], small_sems.at[1 + i]))
    for look in looks:
        look.start()
    bulk = pltpu.make_async_copy(tiles_ref, held_ref, held_sem)
    bulk.start()
    for k in range(plane):
        slot_ref[k] = 0
    for i in range(spare):
        list_ref[i] = 0
    rows_ref[...] = jnp.zeros_like(rows_ref)
    for look in looks:
        look.wait()

    def step(t, carry):
        k = remainder(owners_ref[0, t], plane) ^ place
        slot = slot_ref[k]
        slot_ref[k] = slot + 1
        sent = (k > 0) & (remainder(slot, cols) == col)
        list_ref[jnp.where(sent, (k - 1) * slots + quotient(slot, cols), spare)] = t
        return carry

    lax.fori_loop(0, tiles, step, 0, unroll=4)
    owners = along_ref[0]
    rows_ref[0:1, :tiles] = remainder(owners, plane).astype(jnp.float32)
    rows_ref[1:2, :tiles] = along_ref[1].astype(jnp.float32)
    rows_ref[2:3, :tiles] = along_ref[2].astype(jnp.float32)
    rows_ref[3:4, :tiles] = quotient(owners, plane).astype(jnp.float32)
    codes = rows_ref[...].astype(codes_ref.dtype)
    codes_ref[...] = codes
    bulk.wait()
    for k, out_ref in enumerate(out_refs):
        for slot in range(slots):
            out_ref[slot * size : (slot + 1) * size] = held_ref[list_ref[k * slots + slot]]
        out_ref[slots * size :] = codes


def pack_tiles(me, owners, tile_row, source_block, tile_values, plane, cols, slots):
    tiles, size, wide = tile_values.shape
    shape = jax.ShapeDtypeStruct((slots * size + CODE_ROWS, wide), tile_values.dtype)
    codes = jax.ShapeDtypeStruct((CODE_ROWS, wide), tile_values.dtype)
    along = [x.reshape(1, tiles) for x in (owners, tile_row, source_block)]
    return pl.pallas_call(
        functools.partial(pack_kernel, plane, cols),
        out_shape=(shape,) * (plane - 1) + (codes,),
        in_specs=[SMEM] + [HBM] * 4,
        out_specs=(VMEM,) * plane,
        scratch_shapes=[
            pltpu.SMEM(((plane - 1) * slots + 1,), jnp.int32),
            pltpu.SMEM((plane,), jnp.int32),
            pltpu.SMEM((1, tiles), jnp.int32),
            pltpu.VMEM((3, 1, tiles), jnp.int32),
            pltpu.VMEM((CODE_ROWS, wide), jnp.float32),
            pltpu.VMEM((tiles, size, wide), tile_values.dtype),
            pltpu.SemaphoreType.DMA((4,)),
            pltpu.SemaphoreType.DMA,
        ],
        compiler_params=pltpu.CompilerParams(vmem_limit_bytes=PACK_BYTES),
        name="pack_tiles",
    )(me, *along, tile_values)


DST_BIT, SRC_BIT, PLACE_BIT = 10, 16, 24


def collect_kernel(plane, cols, slots, blocks, me_ref, own_ref, *refs):
    tile_refs, refs = refs[: 1 + (plane - 1) * cols], refs[1 + (plane - 1) * cols :]
    out_ref, plan_ref, count_ref, *scratch = refs
    rows_ref, words_ref, codes_ref, row_sems, word_sem, tile_sems = scratch
    place, col = me_ref[1], me_ref[2]
    size = out_ref.shape[1]
    tiles = tile_refs[0].shape[0] // size
    looks = []
    for k in range(plane):
        ref = own_ref
        if k > 0:
            ref = tile_refs[1 + (k - 1) * cols].at[pl.ds(slots * size, CODE_ROWS)]
        copy = pltpu.make_async_copy(ref, rows_ref.at[k], row_sems.at[k])
        copy.start()
        looks.append(copy)
    copies, first = [], 0
    for i, ref in enumerate(tile_refs):
        for at in range(tiles if i == 0 else slots):
            copy = pltpu.make_async_copy(
                ref.at[pl.ds(at * size, size)], out_ref.at[first], tile_sems.at[first]
            )
            copies.append(copy)
            first += 1
    for copy in copies:
        copy.start()
    out_ref[first] = jnp.zeros_like(out_ref[first])
    words_ref[...] = jnp.zeros_like(words_ref)
    for k, copy in enumerate(looks):
        copy.wait()
        rows = rows_ref[k].astype(jnp.float32).astype(jnp.int32)
        source = rows[3:4] * blocks + rows[2:3]
        word = (rows[0:1] << PLACE_BIT) + (source << SRC_BIT)
        words_ref[k : k + 1] = word + ((rows[1:2] + k * blocks) << DST_BIT)
    copy = pltpu.make_async_copy(words_ref, codes_ref, word_sem)
    copy.start()
    copy.wait()
    found = jnp.int32(0)
    for k in range(plane):

        def step(t, carry, k=k):
            at, slot = carry
            code = codes_ref[k, t]
            if k == 0:
                spot = t
            else:
                column = remainder(slot + (cols - col), cols)
                spot = tiles + ((k - 1) * cols + column) * slots + quotient(slot, cols)
            plan_ref[at] = (code & ((1 << PLACE_BIT) - 1)) + spot
            one = ((code >> PLACE_BIT) == place).astype(jnp.int32)
            return at + one, slot + one

        found, _ = lax.fori_loop(0, tiles, step, (found, jnp.int32(0)), unroll=8)
    for i in range(UNROLL):
        plan_ref[found + i] = first
    count_ref[0] = quotient(found + UNROLL - 1, UNROLL)
    for copy in copies:
        copy.wait()


def collect_tiles(me, codes, tile_parts, plane, cols, slots, blocks):
    wide = tile_parts[0].shape[1]
    tiles = tile_parts[0].shape[0] // wide
    entries = plane * tiles + UNROLL
    spots = tiles + (plane - 1) * cols * slots + 1
    laid = jax.ShapeDtypeStruct((spots, wide, wide), jnp.bfloat16)
    high = -(-plane // 8) * 8
    return pl.pallas_call(
        functools.partial(collect_kernel, plane, cols, slots, blocks),
        out_shape=(
            laid,
            jax.ShapeDtypeStruct((entries,), jnp.int32),
            jax.ShapeDtypeStruct((1,), jnp.int32),
        ),
        in_specs=[SMEM] + [ANY] * (1 + len(tile_parts)),
        out_specs=(VMEM, SMEM, SMEM),
        scratch_shapes=[
            pltpu.VMEM((plane, CODE_ROWS, wide), jnp.bfloat16),
            pltpu.VMEM((high, wide), jnp.int32),
            pltpu.SMEM((high, wide), jnp.int32),
            pltpu.SemaphoreType.DMA((plane,)),
            pltpu.SemaphoreType.DMA,
            pltpu.SemaphoreType.DMA((spots - 1,)),
        ],
        compiler_params=params(laid),
        name="collect_tiles",
    )(me, codes, *tile_parts)


def planned(plan_ref, t):
    entry = plan_ref[t]
    spot = entry & ((1 << DST_BIT) - 1)
    return spot, (entry >> DST_BIT) & ((1 << (SRC_BIT - DST_BIT)) - 1), entry >> SRC_BIT


def turn_kernel(plan_ref, count_ref, tiles_ref, out_ref):
    def step(i, carry):
        for j in range(UNROLL):
            t = i * UNROLL + j
            out_ref[t] = tiles_ref[planned(plan_ref, t)[0]].T
        return carry

    lax.fori_loop(0, count_ref[0], step, 0)


def turn_tiles(plan, count, tiles, most):
    turned = jax.ShapeDtypeStruct((most + UNROLL,) + tiles.shape[1:], tiles.dtype)
    return pl.pallas_call(
        turn_kernel,
        out_shape=turned,
        in_specs=[SMEM, SMEM, VMEM],
        out_specs=VMEM,
        compiler_params=params(tiles, turned),
        name="turn_tiles",
    )(plan, count, tiles)


def block_rows(index, size):
    return pl.ds(pl.multiple_of(index * size, size), size)


def forward_kernel(line, lanes, me_ref, plan_ref, count_ref, tiles_ref, *refs):
    part_refs, refs = refs[: 2 * line - 1], refs[2 * line - 1 :]
    out_refs, (nodes_ref, acc_ref, part_sems) = refs[:-3], refs[-3:]
    rows, width = part_refs[0].shape[0], nodes_ref.shape[1]
    size = tiles_ref.shape[1]
    mine = me_ref[0]

    def each_part(act):
        for i, ref in enumerate(part_refs):
            source = mine + i - (line - 1)

            @pl.when((source >= 0) & (source < line))
            def _():
                here = ref.at[:, lanes] if ref.shape != (rows, width) else ref
                act(
                    pltpu.make_async_copy(
                        here, nodes_ref.at[block_rows(source, rows)], part_sems.at[i]
                    )
                )

    each_part(lambda copy: copy.start())
    acc_ref[...] = jnp.zeros_like(acc_ref)
    each_part(lambda copy: copy.wait())

    def step(i, carry):
        for j in range(UNROLL):
            spot, dst, src = planned(plan_ref, i * UNROLL + j)
            acc_ref[block_rows(dst, size)] += jnp.dot(
                tiles_ref[spot],
                nodes_ref[block_rows(src, size)],
                preferred_element_type=jnp.float32,
            )
        return carry

    lax.fori_loop(0, count_ref[0], step, 0)
    for k, ref in enumerate(out_refs):
        ref[...] = acc_ref[k * rows : (k + 1) * rows].astype(ref.dtype)


def forward_tiles(me, plan, count, tiles, node_parts, plane, lanes):
    line = (len(node_parts) + 1) // 2
    rows, width = node_parts[0].shape[0], lanes.size
    kinds = [jnp.float32] + [jnp.bfloat16] * (plane - 1)
    outs = tuple(jax.ShapeDtypeStruct((rows, width), kind) for kind in kinds)
    scratch = [
        pltpu.VMEM((line * rows, width), jnp.bfloat16),
        pltpu.VMEM((plane * rows, width), jnp.float32),
    ]
    return pl.pallas_call(
        functools.partial(forward_kernel, line, lanes),
        out_shape=outs,
        in_specs=[SMEM] * 3 + [VMEM] + [ANY] * len(node_parts),
        out_specs=(VMEM,) * plane,
        scratch_shapes=scratch + [pltpu.SemaphoreType.DMA((len(node_parts),))],
        compiler_params=params(tiles, *outs, *scratch),
        name="forward_tiles",
    )(me, plan, count, tiles, *node_parts)


def dense_kernel(chunk, halves, labels_ref, weight_ref, *refs):
    parts, (act_ref, out_grad_ref, agg_grad_ref) = refs[:-3], refs[-3:]
    rows, part_width = parts[0].shape
    width = part_width * halves
    features = weight_ref.shape[0]
    size = labels_ref.shape[1]

    def rows_step(i, carry):
        here = block_rows(i, chunk)
        agg = jnp.concatenate([part[here, :] for part in parts], axis=1)
        hidden = jnp.dot(agg, weight_ref[...], preferred_element_type=jnp.float32)
        sigmoid = jax.nn.sigmoid(hidden)
        activated = hidden * sigmoid
        act_ref[here, :] = activated[:, :width].astype(act_ref.dtype)
        slopes = sigmoid * (1.0 + hidden * (1.0 - sigmoid))
        named = []
        for b in range(chunk // size):
            across = labels_ref[pl.ds(i * (chunk // size) + b, 1), :]
            named.append(jnp.broadcast_to(across, (size, size)).T)
        named = jnp.concatenate(named, axis=0)
        ids = lax.broadcasted_iota(jnp.int32, (chunk, size), 1).astype(jnp.float32)
        target = jnp.concatenate(
            [(named == ids + f * size).astype(jnp.float32) for f in range(features // size)],
            axis=1,
        )
        out_grad = ((activated - target) * slopes).astype(jnp.bfloat16)
        out_grad_ref[here, :] = out_grad
        agg_grad_ref[here, :] = lax.dot_general(
            out_grad,
            weight_ref[:part_width, :],
            (((1,), (1,)), ((), ())),
            preferred_element_type=jnp.float32,
        ).astype(agg_grad_ref.dtype)
        return carry

    lax.fori_loop(0, rows // chunk, rows_step, 0)


def dense(labels, weight, parts, halves):
    rows, part_width = parts[0].shape
    chunk = math.gcd(rows, 256)
    outs = tuple(
        jax.ShapeDtypeStruct((rows, width), jnp.bfloat16)
        for width in (part_width * halves, weight.shape[0], part_width)
    )
    return pl.pallas_call(
        functools.partial(dense_kernel, chunk, halves),
        out_shape=outs,
        in_specs=[VMEM] * (2 + len(parts)),
        out_specs=(VMEM,) * 3,
        compiler_params=params(labels, weight, *parts, *outs),
        name="dense",
    )(labels, weight, *parts)


def grads_kernel(scale, halves, weight_ref, out_grad_ref, *refs):
    parts, (terms_ref, *agg_grad_refs) = refs[: -halves], refs[-halves:]
    part_width = parts[0].shape[1]
    for h, ref in enumerate(agg_grad_refs, 1):
        ref[...] = lax.dot_general(
            out_grad_ref[...],
            weight_ref[h * part_width : (h + 1) * part_width, :],
            (((1,), (1,)), ((), ())),
            preferred_element_type=jnp.float32,
        ).astype(ref.dtype)
    for i, part in enumerate(parts):
        terms = lax.dot_general(
            part[...],
            out_grad_ref[:, : part_width * halves],
            (((0,), (0,)), ((), ())),
            preferred_element_type=jnp.float32,
        )
        terms_ref[i * part_width : (i + 1) * part_width] = (terms * scale).astype(terms_ref.dtype)


def grads(weight, out_grad, parts, halves, node_total):
    rows, part_width = parts[0].shape
    outs = (jax.ShapeDtypeStruct((weight.shape[0], part_width * halves), jnp.bfloat16),) + (
        jax.ShapeDtypeStruct((rows, part_width), jnp.bfloat16),
    ) * (halves - 1)
    return pl.pallas_call(
        functools.partial(grads_kernel, 1.0 / math.sqrt(node_total), halves),
        out_shape=outs,
        in_specs=[VMEM] * (2 + len(parts)),
        out_specs=(VMEM,) * halves,
        compiler_params=params(weight, out_grad, *parts, *outs),
        name="grads",
    )(weight, out_grad, *parts)


def spread_kernel(line, plane, me_ref, plan_ref, count_ref, tiles_ref, *refs):
    grad_refs, refs = refs[:plane], refs[plane:]
    out_refs, (grads_ref, acc_ref, grad_sems) = refs[:-3], refs[-3:]
    rows = grad_refs[0].shape[0]
    size = tiles_ref.shape[1]
    mine = me_ref[0]
    copies = []
    for k, ref in enumerate(grad_refs):
        copy = pltpu.make_async_copy(ref, grads_ref.at[pl.ds(k * rows, rows)], grad_sems.at[k])
        copy.start()
        copies.append(copy)
    acc_ref[...] = jnp.zeros_like(acc_ref)
    for copy in copies:
        copy.wait()

    def step(i, carry):
        for j in range(UNROLL):
            t = i * UNROLL + j
            _, dst, src = planned(plan_ref, t)
            acc_ref[block_rows(src, size)] += jnp.dot(
                tiles_ref[t],
                grads_ref[block_rows(dst, size)],
                preferred_element_type=jnp.float32,
            )
        return carry

    lax.fori_loop(0, count_ref[0], step, 0)
    for i, ref in enumerate(out_refs):
        target = mine + i - (line - 1)

        @pl.when((target >= 0) & (target < line))
        def _():
            ref[...] = acc_ref[block_rows(target, rows)].astype(ref.dtype)


def spread_tiles(me, plan, count, tiles, grad_parts, line):
    plane = len(grad_parts)
    rows, width = grad_parts[0].shape
    kinds = [jnp.float32 if i == line - 1 else jnp.bfloat16 for i in range(2 * line - 1)]
    outs = tuple(jax.ShapeDtypeStruct((rows, width), kind) for kind in kinds)
    scratch = [
        pltpu.VMEM((plane * rows, width), jnp.bfloat16),
        pltpu.VMEM((line * rows, width), jnp.float32),
    ]
    return pl.pallas_call(
        functools.partial(spread_kernel, line, plane),
        out_shape=outs,
        in_specs=[SMEM] * 3 + [VMEM] + [ANY] * plane,
        out_specs=(VMEM,) * (2 * line - 1),
        scratch_shapes=scratch + [pltpu.SemaphoreType.DMA((plane,))],
        compiler_params=params(tiles, *outs, *scratch),
        name="spread_tiles",
    )(me, plan, count, tiles, *grad_parts)


def line_steps(line, plane, step, reach):
    return [
        (z * plane + q, (z + step) * plane + q)
        for z in range(line)
        if 0 <= z + step < line and 0 <= z + reach < line
        for q in range(plane)
    ]


def line_gather(x, line, plane, lanes):
    up, down = [x], [x]
    for k in range(1, line - 1):
        up.append(shuffle(up[-1], line_steps(line, plane, 1, 1 - k)))
        down.append(shuffle(down[-1], line_steps(line, plane, -1, k - 1)))
    parts = []
    for part in lanes:
        first = shuffle(up[-1][:, part], line_steps(line, plane, 1, 2 - line))
        last = shuffle(down[-1][:, part], line_steps(line, plane, -1, line - 2))
        parts.append([first] + up[:0:-1] + down + [last])
    return parts


def line_sum(terms, line, plane, beside):
    moved = {1: None, -1: None}
    for k in range(line - 1, 0, -1):
        for step in moved:
            term = terms[line - 1 + step * k]
            if moved[step] is not None:
                total = term.astype(jnp.float32) + moved[step].astype(jnp.float32)
                term = total.astype(term.dtype)
            moved[step] = shuffle(term, line_steps(line, plane, step, step * k))
        if k == line - 1:
            moved, beside = lax.optimization_barrier((moved, beside))
    return [terms[line - 1], moved[1], moved[-1]], beside


def finish_kernel(halves, *refs):
    out_ref, refs = refs[-1], refs[:-1]
    each = len(refs) // halves
    width = refs[0].shape[1]
    for h in range(halves):
        total = refs[h * each][...]
        for ref in refs[h * each + 1 : (h + 1) * each]:
            total += ref[...].astype(jnp.float32)
        out_ref[:, h * width : (h + 1) * width] = total.astype(out_ref.dtype)


def finish(pieces):
    flat = [piece for half in pieces for piece in half]
    rows, width = flat[0].shape
    out = jax.ShapeDtypeStruct((rows, width * len(pieces)), jnp.bfloat16)
    return pl.pallas_call(
        functools.partial(finish_kernel, len(pieces)),
        out_shape=out,
        in_specs=[VMEM] * len(flat),
        out_specs=VMEM,
        compiler_params=params(out, *flat),
        name="finish",
    )(*flat)


def sum_apart(terms, first, end, rows):
    total = terms.astype(jnp.float32)
    while first < end:
        other = shuffle(terms, [(r, r ^ first) for r in range(rows)])
        total = terms.astype(jnp.float32) + other.astype(jnp.float32)
        terms = total.astype(terms.dtype)
        first *= 2
    return total


def per_device(node_features, weight, tile_values, tile_row, source_owner, source_block, labels):
    local_rows, width = node_features.shape
    n_tiles, block_size = tile_values.shape[:2]
    blocks = local_rows // block_size
    rows, cols = lax.axis_size("rows"), lax.axis_size("cols")
    plane = math.gcd(rows, LARGEST_PLANE)
    line = rows // plane
    halves = 2 if width % 256 == 0 else 1
    part_width = width // halves
    slots = -(-min(n_tiles, line * (2 * n_tiles // rows)) // cols)
    features = weight.shape[0]
    owners = source_owner[:, 0]

    index = lax.axis_index("rows")
    col = lax.axis_index("cols")
    z, q = index // plane, index % plane
    me = jnp.stack([z, q, col]).astype(jnp.int32)

    def other_cols(x):
        return [
            lax.ppermute(x, "cols", [((c + k) % cols, c) for c in range(cols)])
            for k in range(1, cols)
        ]

    lanes = [slice(h * part_width, (h + 1) * part_width) for h in range(halves)]
    *packed, codes = pack_tiles(
        me, owners, tile_row, source_block, tile_values, plane, cols, slots
    )
    node_parts = line_gather(node_features, line, plane, lanes)
    tile_parts = [tile_values.reshape(n_tiles * block_size, block_size)]
    for k in range(1, plane):
        arrived = across_plane(packed[k - 1], k, line, plane)
        tile_parts += [arrived] + other_cols(arrived)
    most = plane * min(n_tiles, line * (2 * n_tiles // rows))
    tiles, plan, count = collect_tiles(me, codes, tile_parts, plane, cols, slots, blocks)

    first = col * width
    own_first = jnp.roll(weight, (-first, -first), (0, 1))
    own_labels = ((labels - first) % features).reshape(blocks, block_size).astype(jnp.float32)
    plan, own_first, own_labels = lax.optimization_barrier((plan, own_first, own_labels))

    aggregated = []
    for h in range(halves):
        here = pl.ds(h * part_width, part_width)
        sums = forward_tiles(me, plan, count, tiles, node_parts[h], plane, here)
        total = sums[0]
        for k in range(1, plane):
            total = total + across_plane(sums[k], k, line, plane).astype(jnp.float32)
        mine = total.astype(jnp.bfloat16)
        aggregated.append([mine] + other_cols(mine))
    parts = [aggregated[h][c] for c in range(cols) for h in range(halves)]

    later, _ = lax.optimization_barrier((tiles, sums[0]))
    turned = turn_tiles(plan, count, later, most)
    own_labels, turned = lax.optimization_barrier((own_labels, turned))

    activations, out_grad, agg_grad = dense(own_labels, own_first, parts, halves)
    weight_terms, *agg_grads = grads(own_first, out_grad, parts, halves, local_rows * rows)

    pieces = []
    for i, agg_grad in enumerate(agg_grads[::-1] + [agg_grad]):
        arrived = [agg_grad] + [across_plane(agg_grad, k, line, plane) for k in range(1, plane)]
        if i == 0:
            weight_terms = sum_apart(weight_terms, plane, 2 * plane, rows).astype(jnp.bfloat16)
            arrived, weight_terms = lax.optimization_barrier((arrived, weight_terms))
            weight_terms = sum_apart(weight_terms, 2 * plane, rows, rows).astype(jnp.bfloat16)
        terms = spread_tiles(me, plan, count, turned, arrived, line)
        half, weight_terms = line_sum(terms, line, plane, weight_terms)
        pieces.append(half)
    weight_terms = sum_apart(weight_terms, 1, plane, rows)
    weight_grad = jnp.roll(weight_terms, first, 0)
    return activations, weight_grad, finish(pieces[::-1])


def solution(mesh):
    return jax.shard_map(
        per_device,
        mesh=mesh,
        in_specs=(
            P("rows", "cols"),
            P(),
            P("rows", None, None),
            P("rows"),
            P("rows", None),
            P("rows"),
            P("rows"),
        ),
        out_specs=(P("rows", "cols"), P(None, "cols"), P("rows", "cols")),
        check_vma=False,
    )
```

```python
import functools
import math

import jax
import jax.numpy as jnp
from jax import lax
from jax.experimental import pallas as pl
from jax.experimental.pallas import tpu as pltpu
from jax.sharding import PartitionSpec as P

VMEM = pl.BlockSpec(memory_space=pltpu.VMEM)
SMEM = pl.BlockSpec(memory_space=pltpu.SMEM)
ANY = pl.BlockSpec(memory_space=pl.ANY)
HBM = pl.BlockSpec(memory_space=pltpu.HBM)
SPARE_BYTES = 2 * 1024 * 1024
PACK_BYTES = 56 * 1024 * 1024
UNROLL = 8
LARGEST_PLANE = 4


def params(*shapes):
    room = SPARE_BYTES
    for shape in shapes:
        *lead, high, wide = shape.shape
        room += math.prod(lead) * high * (-(-wide // 128) * 128) * jnp.dtype(shape.dtype).itemsize
    return pltpu.CompilerParams(vmem_limit_bytes=room)


def quotient(x, n):
    return x >> (n.bit_length() - 1) if n & (n - 1) == 0 else lax.div(x, n)


def remainder(x, n):
    return x & (n - 1) if n & (n - 1) == 0 else lax.rem(x, n)


def shuffle(x, pairs):
    return lax.ppermute(x, "rows", pairs)


def across_plane(x, k, line, plane):
    return shuffle(x, [(r, r ^ k) for r in range(line * plane)])


CODE_ROWS = 16


def pack_kernel(plane, cols, me_ref, owner_ref, row_ref, source_ref, tiles_ref, *refs):
    out_refs, (codes_ref, *scratch) = refs[: plane - 1], refs[plane - 1 :]
    list_ref, slot_ref, owners_ref, along_ref, rows_ref, held_ref, small_sems, held_sem = scratch
    place, col = me_ref[1], me_ref[2]
    tiles, size = tiles_ref.shape[:2]
    slots = (out_refs[0].shape[0] - CODE_ROWS) // size
    spare = (plane - 1) * slots
    looks = [pltpu.make_async_copy(owner_ref, owners_ref, small_sems.at[0])]
    for i, ref in enumerate((owner_ref, row_ref, source_ref)):
        looks.append(pltpu.make_async_copy(ref, along_ref.at[i], small_sems.at[1 + i]))
    for look in looks:
        look.start()
    bulk = pltpu.make_async_copy(tiles_ref, held_ref, held_sem)
    bulk.start()
    for k in range(plane):
        slot_ref[k] = 0
    for i in range(spare):
        list_ref[i] = 0
    rows_ref[...] = jnp.zeros_like(rows_ref)
    for look in looks:
        look.wait()

    def step(t, carry):
        k = remainder(owners_ref[0, t], plane) ^ place
        slot = slot_ref[k]
        slot_ref[k] = slot + 1
        sent = (k > 0) & (remainder(slot, cols) == col)
        list_ref[jnp.where(sent, (k - 1) * slots + quotient(slot, cols), spare)] = t
        return carry

    lax.fori_loop(0, tiles, step, 0, unroll=4)
    owners = along_ref[0]
    rows_ref[0:1, :tiles] = remainder(owners, plane).astype(jnp.float32)
    rows_ref[1:2, :tiles] = along_ref[1].astype(jnp.float32)
    rows_ref[2:3, :tiles] = along_ref[2].astype(jnp.float32)
    rows_ref[3:4, :tiles] = quotient(owners, plane).astype(jnp.float32)
    codes = rows_ref[...].astype(codes_ref.dtype)
    codes_ref[...] = codes
    bulk.wait()
    for k, out_ref in enumerate(out_refs):
        for slot in range(slots):
            out_ref[slot * size : (slot + 1) * size] = held_ref[list_ref[k * slots + slot]]
        out_ref[slots * size :] = codes


def pack_tiles(me, owners, tile_row, source_block, tile_values, plane, cols, slots):
    tiles, size, wide = tile_values.shape
    shape = jax.ShapeDtypeStruct((slots * size + CODE_ROWS, wide), tile_values.dtype)
    codes = jax.ShapeDtypeStruct((CODE_ROWS, wide), tile_values.dtype)
    along = [x.reshape(1, tiles) for x in (owners, tile_row, source_block)]
    return pl.pallas_call(
        functools.partial(pack_kernel, plane, cols),
        out_shape=(shape,) * (plane - 1) + (codes,),
        in_specs=[SMEM] + [HBM] * 4,
        out_specs=(VMEM,) * plane,
        scratch_shapes=[
            pltpu.SMEM(((plane - 1) * slots + 1,), jnp.int32),
            pltpu.SMEM((plane,), jnp.int32),
            pltpu.SMEM((1, tiles), jnp.int32),
            pltpu.VMEM((3, 1, tiles), jnp.int32),
            pltpu.VMEM((CODE_ROWS, wide), jnp.float32),
            pltpu.VMEM((tiles, size, wide), tile_values.dtype),
            pltpu.SemaphoreType.DMA((4,)),
            pltpu.SemaphoreType.DMA,
        ],
        compiler_params=pltpu.CompilerParams(vmem_limit_bytes=PACK_BYTES),
        name="pack_tiles",
    )(me, *along, tile_values)


DST_BIT, SRC_BIT, PLACE_BIT = 10, 16, 24


def collect_kernel(plane, cols, slots, blocks, me_ref, own_ref, *refs):
    tile_refs, refs = refs[: 1 + (plane - 1) * cols], refs[1 + (plane - 1) * cols :]
    out_ref, plan_ref, count_ref, *scratch = refs
    rows_ref, words_ref, codes_ref, row_sems, word_sem, tile_sems = scratch
    place, col = me_ref[1], me_ref[2]
    size = out_ref.shape[1]
    tiles = tile_refs[0].shape[0] // size
    looks = []
    for k in range(plane):
        ref = own_ref
        if k > 0:
            ref = tile_refs[1 + (k - 1) * cols].at[pl.ds(slots * size, CODE_ROWS)]
        copy = pltpu.make_async_copy(ref, rows_ref.at[k], row_sems.at[k])
        copy.start()
        looks.append(copy)
    copies, first = [], 0
    for i, ref in enumerate(tile_refs):
        rows = (tiles if i == 0 else slots) * size
        copy = pltpu.make_async_copy(
            ref.at[pl.ds(0, rows)], out_ref.at[pl.ds(first, rows)], tile_sems.at[i]
        )
        copy.start()
        copies.append(copy)
        first += rows
    out_ref[first:] = jnp.zeros_like(out_ref[first:])
    first //= size
    words_ref[...] = jnp.zeros_like(words_ref)
    for k, copy in enumerate(looks):
        copy.wait()
        rows = rows_ref[k].astype(jnp.float32).astype(jnp.int32)
        source = rows[3:4] * blocks + rows[2:3]
        word = (rows[0:1] << PLACE_BIT) + (source << SRC_BIT)
        words_ref[k : k + 1] = word + ((rows[1:2] + k * blocks) << DST_BIT)
    copy = pltpu.make_async_copy(words_ref, codes_ref, word_sem)
    copy.start()
    copy.wait()
    found = jnp.int32(0)
    for k in range(plane):

        def step(t, carry, k=k):
            at, slot = carry
            code = codes_ref[k, t]
            if k == 0:
                spot = t
            else:
                column = remainder(slot + (cols - col), cols)
                spot = tiles + ((k - 1) * cols + column) * slots + quotient(slot, cols)
            plan_ref[at] = (code & ((1 << PLACE_BIT) - 1)) + spot
            one = ((code >> PLACE_BIT) == place).astype(jnp.int32)
            return at + one, slot + one

        found, _ = lax.fori_loop(0, tiles, step, (found, jnp.int32(0)), unroll=8)
    for i in range(UNROLL):
        plan_ref[found + i] = first
    count_ref[0] = quotient(found + UNROLL - 1, UNROLL)
    for copy in copies:
        copy.wait()


def collect_tiles(me, codes, tile_parts, plane, cols, slots, blocks):
    wide = tile_parts[0].shape[1]
    tiles = tile_parts[0].shape[0] // wide
    entries = plane * tiles + UNROLL
    spots = tiles + (plane - 1) * cols * slots + 1
    laid = jax.ShapeDtypeStruct((spots * wide, wide), jnp.bfloat16)
    high = -(-plane // 8) * 8
    return pl.pallas_call(
        functools.partial(collect_kernel, plane, cols, slots, blocks),
        out_shape=(
            laid,
            jax.ShapeDtypeStruct((entries,), jnp.int32),
            jax.ShapeDtypeStruct((1,), jnp.int32),
        ),
        in_specs=[SMEM] + [ANY] * (1 + len(tile_parts)),
        out_specs=(VMEM, SMEM, SMEM),
        scratch_shapes=[
            pltpu.VMEM((plane, CODE_ROWS, wide), jnp.bfloat16),
            pltpu.VMEM((high, wide), jnp.int32),
            pltpu.SMEM((high, wide), jnp.int32),
            pltpu.SemaphoreType.DMA((plane,)),
            pltpu.SemaphoreType.DMA,
            pltpu.SemaphoreType.DMA((len(tile_parts),)),
        ],
        compiler_params=params(laid),
        name="collect_tiles",
    )(me, codes, *tile_parts)


def planned(plan_ref, t):
    entry = plan_ref[t]
    spot = entry & ((1 << DST_BIT) - 1)
    return spot, (entry >> DST_BIT) & ((1 << (SRC_BIT - DST_BIT)) - 1), entry >> SRC_BIT


def block_rows(index, size):
    return pl.ds(pl.multiple_of(index * size, size), size)


def forward_kernel(line, lanes, me_ref, plan_ref, count_ref, tiles_ref, *refs):
    part_refs, refs = refs[: 2 * line - 1], refs[2 * line - 1 :]
    out_refs, (nodes_ref, acc_ref, part_sems) = refs[:-3], refs[-3:]
    rows, width = part_refs[0].shape[0], nodes_ref.shape[1]
    size = tiles_ref.shape[1]
    mine = me_ref[0]

    def each_part(act):
        for i, ref in enumerate(part_refs):
            source = mine + i - (line - 1)

            @pl.when((source >= 0) & (source < line))
            def _():
                here = ref.at[:, lanes] if ref.shape != (rows, width) else ref
                act(
                    pltpu.make_async_copy(
                        here, nodes_ref.at[block_rows(source, rows)], part_sems.at[i]
                    )
                )

    each_part(lambda copy: copy.start())
    acc_ref[...] = jnp.zeros_like(acc_ref)
    each_part(lambda copy: copy.wait())

    def step(i, carry):
        for j in range(UNROLL):
            spot, dst, src = planned(plan_ref, i * UNROLL + j)
            acc_ref[block_rows(dst, size)] += jnp.dot(
                tiles_ref[block_rows(spot, size)],
                nodes_ref[block_rows(src, size)],
                preferred_element_type=jnp.float32,
            )
        return carry

    lax.fori_loop(0, count_ref[0], step, 0)
    for k, ref in enumerate(out_refs):
        ref[...] = acc_ref[k * rows : (k + 1) * rows].astype(ref.dtype)


def forward_tiles(me, plan, count, tiles, node_parts, plane, lanes):
    line = (len(node_parts) + 1) // 2
    rows, width = node_parts[0].shape[0], lanes.size
    kinds = [jnp.float32] + [jnp.bfloat16] * (plane - 1)
    outs = tuple(jax.ShapeDtypeStruct((rows, width), kind) for kind in kinds)
    scratch = [
        pltpu.VMEM((line * rows, width), jnp.bfloat16),
        pltpu.VMEM((plane * rows, width), jnp.float32),
    ]
    return pl.pallas_call(
        functools.partial(forward_kernel, line, lanes),
        out_shape=outs,
        in_specs=[SMEM] * 3 + [VMEM] + [ANY] * len(node_parts),
        out_specs=(VMEM,) * plane,
        scratch_shapes=scratch + [pltpu.SemaphoreType.DMA((len(node_parts),))],
        compiler_params=params(tiles, *outs, *scratch),
        name="forward_tiles",
    )(me, plan, count, tiles, *node_parts)


def dense_kernel(chunk, halves, labels_ref, weight_ref, *refs):
    parts, (act_ref, out_grad_ref, agg_grad_ref) = refs[:-3], refs[-3:]
    rows, part_width = parts[0].shape
    width = part_width * halves
    features = weight_ref.shape[0]
    size = labels_ref.shape[1]

    def rows_step(i, carry):
        here = block_rows(i, chunk)
        agg = jnp.concatenate([part[here, :] for part in parts], axis=1)
        hidden = jnp.dot(agg, weight_ref[...], preferred_element_type=jnp.float32)
        sigmoid = jax.nn.sigmoid(hidden)
        activated = hidden * sigmoid
        act_ref[here, :] = activated[:, :width].astype(act_ref.dtype)
        slopes = sigmoid * (1.0 + hidden * (1.0 - sigmoid))
        named = []
        for b in range(chunk // size):
            across = labels_ref[pl.ds(i * (chunk // size) + b, 1), :]
            named.append(jnp.broadcast_to(across, (size, size)).T)
        named = jnp.concatenate(named, axis=0)
        ids = lax.broadcasted_iota(jnp.int32, (chunk, size), 1).astype(jnp.float32)
        target = jnp.concatenate(
            [(named == ids + f * size).astype(jnp.float32) for f in range(features // size)],
            axis=1,
        )
        out_grad = ((activated - target) * slopes).astype(jnp.bfloat16)
        out_grad_ref[here, :] = out_grad
        agg_grad_ref[here, :] = lax.dot_general(
            out_grad,
            weight_ref[:part_width, :],
            (((1,), (1,)), ((), ())),
            preferred_element_type=jnp.float32,
        ).astype(agg_grad_ref.dtype)
        return carry

    lax.fori_loop(0, rows // chunk, rows_step, 0)


def dense(labels, weight, parts, halves):
    rows, part_width = parts[0].shape
    chunk = math.gcd(rows, 256)
    outs = tuple(
        jax.ShapeDtypeStruct((rows, width), jnp.bfloat16)
        for width in (part_width * halves, weight.shape[0], part_width)
    )
    return pl.pallas_call(
        functools.partial(dense_kernel, chunk, halves),
        out_shape=outs,
        in_specs=[VMEM] * (2 + len(parts)),
        out_specs=(VMEM,) * 3,
        compiler_params=params(labels, weight, *parts, *outs),
        name="dense",
    )(labels, weight, *parts)


def grads_kernel(scale, halves, weight_ref, out_grad_ref, *refs):
    parts, (terms_ref, *agg_grad_refs) = refs[: -halves], refs[-halves:]
    part_width = parts[0].shape[1]
    for h, ref in enumerate(agg_grad_refs, 1):
        ref[...] = lax.dot_general(
            out_grad_ref[...],
            weight_ref[h * part_width : (h + 1) * part_width, :],
            (((1,), (1,)), ((), ())),
            preferred_element_type=jnp.float32,
        ).astype(ref.dtype)
    for i, part in enumerate(parts):
        terms = lax.dot_general(
            part[...],
            out_grad_ref[:, : part_width * halves],
            (((0,), (0,)), ((), ())),
            preferred_element_type=jnp.float32,
        )
        terms_ref[i * part_width : (i + 1) * part_width] = (terms * scale).astype(terms_ref.dtype)


def grads(weight, out_grad, parts, halves, node_total):
    rows, part_width = parts[0].shape
    outs = (jax.ShapeDtypeStruct((weight.shape[0], part_width * halves), jnp.bfloat16),) + (
        jax.ShapeDtypeStruct((rows, part_width), jnp.bfloat16),
    ) * (halves - 1)
    return pl.pallas_call(
        functools.partial(grads_kernel, 1.0 / math.sqrt(node_total), halves),
        out_shape=outs,
        in_specs=[VMEM] * (2 + len(parts)),
        out_specs=(VMEM,) * halves,
        compiler_params=params(weight, out_grad, *parts, *outs),
        name="grads",
    )(weight, out_grad, *parts)


def spread_kernel(line, plane, me_ref, plan_ref, count_ref, tiles_ref, *refs):
    grad_refs, refs = refs[:plane], refs[plane:]
    out_refs, (grads_ref, acc_ref, grad_sems) = refs[:-3], refs[-3:]
    rows = grad_refs[0].shape[0]
    size = tiles_ref.shape[1]
    mine = me_ref[0]
    copies = []
    for k, ref in enumerate(grad_refs):
        copy = pltpu.make_async_copy(ref, grads_ref.at[pl.ds(k * rows, rows)], grad_sems.at[k])
        copy.start()
        copies.append(copy)
    acc_ref[...] = jnp.zeros_like(acc_ref)
    for copy in copies:
        copy.wait()

    def step(i, carry):
        for j in range(UNROLL):
            spot, dst, src = planned(plan_ref, i * UNROLL + j)
            acc_ref[block_rows(src, size)] += lax.dot_general(
                tiles_ref[block_rows(spot, size)],
                grads_ref[block_rows(dst, size)],
                (((0,), (0,)), ((), ())),
                preferred_element_type=jnp.float32,
            )
        return carry

    lax.fori_loop(0, count_ref[0], step, 0)
    for i, ref in enumerate(out_refs):
        target = mine + i - (line - 1)

        @pl.when((target >= 0) & (target < line))
        def _():
            ref[...] = acc_ref[block_rows(target, rows)].astype(ref.dtype)


def spread_tiles(me, plan, count, tiles, grad_parts, line):
    plane = len(grad_parts)
    rows, width = grad_parts[0].shape
    kinds = [jnp.float32 if i == line - 1 else jnp.bfloat16 for i in range(2 * line - 1)]
    outs = tuple(jax.ShapeDtypeStruct((rows, width), kind) for kind in kinds)
    scratch = [
        pltpu.VMEM((plane * rows, width), jnp.bfloat16),
        pltpu.VMEM((line * rows, width), jnp.float32),
    ]
    return pl.pallas_call(
        functools.partial(spread_kernel, line, plane),
        out_shape=outs,
        in_specs=[SMEM] * 3 + [VMEM] + [ANY] * plane,
        out_specs=(VMEM,) * (2 * line - 1),
        scratch_shapes=scratch + [pltpu.SemaphoreType.DMA((plane,))],
        compiler_params=params(tiles, *outs, *scratch),
        name="spread_tiles",
    )(me, plan, count, tiles, *grad_parts)


def line_steps(line, plane, step, reach):
    return [
        (z * plane + q, (z + step) * plane + q)
        for z in range(line)
        if 0 <= z + step < line and 0 <= z + reach < line
        for q in range(plane)
    ]


def line_gather(x, line, plane, lanes):
    up, down = [x], [x]
    for k in range(1, line - 1):
        up.append(shuffle(up[-1], line_steps(line, plane, 1, 1 - k)))
        down.append(shuffle(down[-1], line_steps(line, plane, -1, k - 1)))
    parts = []
    for part in lanes:
        first = shuffle(up[-1][:, part], line_steps(line, plane, 1, 2 - line))
        last = shuffle(down[-1][:, part], line_steps(line, plane, -1, line - 2))
        parts.append([first] + up[:0:-1] + down + [last])
    return parts


def line_sum(terms, line, plane, beside):
    moved = {1: None, -1: None}
    for k in range(line - 1, 0, -1):
        for step in moved:
            term = terms[line - 1 + step * k]
            if moved[step] is not None:
                total = term.astype(jnp.float32) + moved[step].astype(jnp.float32)
                term = total.astype(term.dtype)
            moved[step] = shuffle(term, line_steps(line, plane, step, step * k))
        if k == line - 1:
            moved, beside = lax.optimization_barrier((moved, beside))
    return [terms[line - 1], moved[1], moved[-1]], beside


def finish_kernel(halves, *refs):
    out_ref, refs = refs[-1], refs[:-1]
    each = len(refs) // halves
    width = refs[0].shape[1]
    for h in range(halves):
        total = refs[h * each][...]
        for ref in refs[h * each + 1 : (h + 1) * each]:
            total += ref[...].astype(jnp.float32)
        out_ref[:, h * width : (h + 1) * width] = total.astype(out_ref.dtype)


def finish(pieces):
    flat = [piece for half in pieces for piece in half]
    rows, width = flat[0].shape
    out = jax.ShapeDtypeStruct((rows, width * len(pieces)), jnp.bfloat16)
    return pl.pallas_call(
        functools.partial(finish_kernel, len(pieces)),
        out_shape=out,
        in_specs=[VMEM] * len(flat),
        out_specs=VMEM,
        compiler_params=params(out, *flat),
        name="finish",
    )(*flat)


def sum_apart(terms, first, end, rows):
    total = terms.astype(jnp.float32)
    while first < end:
        other = shuffle(terms, [(r, r ^ first) for r in range(rows)])
        total = terms.astype(jnp.float32) + other.astype(jnp.float32)
        terms = total.astype(terms.dtype)
        first *= 2
    return total


def per_device(node_features, weight, tile_values, tile_row, source_owner, source_block, labels):
    local_rows, width = node_features.shape
    n_tiles, block_size = tile_values.shape[:2]
    blocks = local_rows // block_size
    rows, cols = lax.axis_size("rows"), lax.axis_size("cols")
    plane = math.gcd(rows, LARGEST_PLANE)
    line = rows // plane
    halves = 2 if width % 256 == 0 else 1
    part_width = width // halves
    slots = -(-min(n_tiles, line * (2 * n_tiles // rows)) // cols)
    features = weight.shape[0]
    owners = source_owner[:, 0]

    index = lax.axis_index("rows")
    col = lax.axis_index("cols")
    z, q = index // plane, index % plane
    me = jnp.stack([z, q, col]).astype(jnp.int32)

    def other_cols(x):
        return [
            lax.ppermute(x, "cols", [((c + k) % cols, c) for c in range(cols)])
            for k in range(1, cols)
        ]

    lanes = [slice(h * part_width, (h + 1) * part_width) for h in range(halves)]
    *packed, codes = pack_tiles(
        me, owners, tile_row, source_block, tile_values, plane, cols, slots
    )
    node_parts = line_gather(node_features, line, plane, lanes)
    tile_parts = [tile_values.reshape(n_tiles * block_size, block_size)]
    for k in range(1, plane):
        arrived = across_plane(packed[k - 1], k, line, plane)
        tile_parts += [arrived] + other_cols(arrived)
    tiles, plan, count = collect_tiles(me, codes, tile_parts, plane, cols, slots, blocks)

    first = col * width
    own_first = jnp.roll(weight, (-first, -first), (0, 1))
    own_labels = ((labels - first) % features).reshape(blocks, block_size).astype(jnp.float32)
    plan, own_first, own_labels = lax.optimization_barrier((plan, own_first, own_labels))

    aggregated = []
    for h in range(halves):
        here = pl.ds(h * part_width, part_width)
        sums = forward_tiles(me, plan, count, tiles, node_parts[h], plane, here)
        total = sums[0]
        for k in range(1, plane):
            total = total + across_plane(sums[k], k, line, plane).astype(jnp.float32)
        mine = total.astype(jnp.bfloat16)
        aggregated.append([mine] + other_cols(mine))
    parts = [aggregated[h][c] for c in range(cols) for h in range(halves)]

    activations, out_grad, agg_grad = dense(own_labels, own_first, parts, halves)
    weight_terms, *agg_grads = grads(own_first, out_grad, parts, halves, local_rows * rows)

    pieces = []
    for i, agg_grad in enumerate(agg_grads[::-1] + [agg_grad]):
        arrived = [agg_grad] + [across_plane(agg_grad, k, line, plane) for k in range(1, plane)]
        if i == 0:
            weight_terms = sum_apart(weight_terms, plane, 2 * plane, rows).astype(jnp.bfloat16)
            arrived, weight_terms = lax.optimization_barrier((arrived, weight_terms))
            weight_terms = sum_apart(weight_terms, 2 * plane, rows, rows).astype(jnp.bfloat16)
        terms = spread_tiles(me, plan, count, tiles, arrived, line)
        half, weight_terms = line_sum(terms, line, plane, weight_terms)
        pieces.append(half)
    weight_terms = sum_apart(weight_terms, 1, plane, rows)
    weight_grad = jnp.roll(weight_terms, first, 0)
    return activations, weight_grad, finish(pieces[::-1])


def solution(mesh):
    return jax.shard_map(
        per_device,
        mesh=mesh,
        in_specs=(
            P("rows", "cols"),
            P(),
            P("rows", None, None),
            P("rows"),
            P("rows", None),
            P("rows"),
            P("rows"),
        ),
        out_specs=(P("rows", "cols"), P(None, "cols"), P("rows", "cols")),
        check_vma=False,
    )
```

```python
import functools
import math

import jax
import jax.numpy as jnp
from jax import lax
from jax.experimental import pallas as pl
from jax.experimental.pallas import tpu as pltpu
from jax.sharding import PartitionSpec as P

VMEM = pl.BlockSpec(memory_space=pltpu.VMEM)
SMEM = pl.BlockSpec(memory_space=pltpu.SMEM)
ANY = pl.BlockSpec(memory_space=pl.ANY)
HBM = pl.BlockSpec(memory_space=pltpu.HBM)
SPARE_BYTES = 2 * 1024 * 1024
PACK_BYTES = 56 * 1024 * 1024
UNROLL = 8
LARGEST_PLANE = 4


def params(*shapes):
    room = SPARE_BYTES
    for shape in shapes:
        *lead, high, wide = shape.shape
        room += math.prod(lead) * high * (-(-wide // 128) * 128) * jnp.dtype(shape.dtype).itemsize
    return pltpu.CompilerParams(vmem_limit_bytes=room)


def quotient(x, n):
    return x >> (n.bit_length() - 1) if n & (n - 1) == 0 else lax.div(x, n)


def remainder(x, n):
    return x & (n - 1) if n & (n - 1) == 0 else lax.rem(x, n)


def position(plane):
    index, col = lax.axis_index("rows"), lax.axis_index("cols")
    return quotient(index, plane), remainder(index, plane), col, 1 - 2 * (col & 1)


def shuffle(x, pairs):
    return lax.ppermute(x, "rows", pairs)


def across_plane(x, k, line, plane):
    return shuffle(x, [(r, r ^ k) for r in range(line * plane)])


CODE_ROWS = 16


def pack_kernel(plane, cols, owner_ref, row_ref, source_ref, tiles_ref, *refs):
    out_refs, (codes_ref, *scratch) = refs[: plane - 1], refs[plane - 1 :]
    list_ref, slot_ref, owners_ref, along_ref, rows_ref, held_ref, small_sems, held_sem = scratch
    _, place, col, _ = position(plane)
    tiles, size = tiles_ref.shape[:2]
    slots = (out_refs[0].shape[0] - CODE_ROWS) // size
    spare = (plane - 1) * slots
    looks = [pltpu.make_async_copy(owner_ref, owners_ref, small_sems.at[0])]
    for i, ref in enumerate((owner_ref, row_ref, source_ref)):
        looks.append(pltpu.make_async_copy(ref, along_ref.at[i], small_sems.at[1 + i]))
    for look in looks:
        look.start()
    bulk = pltpu.make_async_copy(tiles_ref, held_ref, held_sem)
    bulk.start()
    for k in range(plane):
        slot_ref[k] = 0
    for i in range(spare):
        list_ref[i] = 0
    rows_ref[...] = jnp.zeros_like(rows_ref)
    for look in looks:
        look.wait()

    def step(t, carry):
        k = remainder(owners_ref[0, t], plane) ^ place
        slot = slot_ref[k]
        slot_ref[k] = slot + 1
        sent = (k > 0) & (remainder(slot, cols) == col)
        list_ref[jnp.where(sent, (k - 1) * slots + quotient(slot, cols), spare)] = t
        return carry

    lax.fori_loop(0, tiles, step, 0, unroll=4)
    owners = along_ref[0]
    rows_ref[0:1, :tiles] = remainder(owners, plane).astype(jnp.float32)
    rows_ref[1:2, :tiles] = along_ref[1].astype(jnp.float32)
    rows_ref[2:3, :tiles] = along_ref[2].astype(jnp.float32)
    rows_ref[3:4, :tiles] = quotient(owners, plane).astype(jnp.float32)
    codes = rows_ref[...].astype(codes_ref.dtype)
    codes_ref[...] = codes
    bulk.wait()
    for k, out_ref in enumerate(out_refs):
        for slot in range(slots):
            out_ref[slot * size : (slot + 1) * size] = held_ref[list_ref[k * slots + slot]]
        out_ref[slots * size :] = codes


def pack_tiles(owners, tile_row, source_block, tile_values, plane, cols, slots):
    tiles, size, wide = tile_values.shape
    shape = jax.ShapeDtypeStruct((slots * size + CODE_ROWS, wide), tile_values.dtype)
    codes = jax.ShapeDtypeStruct((CODE_ROWS, wide), tile_values.dtype)
    along = [x.reshape(1, tiles) for x in (owners, tile_row, source_block)]
    return pl.pallas_call(
        functools.partial(pack_kernel, plane, cols),
        out_shape=(shape,) * (plane - 1) + (codes,),
        in_specs=[HBM] * 4,
        out_specs=(VMEM,) * plane,
        scratch_shapes=[
            pltpu.SMEM(((plane - 1) * slots + 1,), jnp.int32),
            pltpu.SMEM((plane,), jnp.int32),
            pltpu.SMEM((1, tiles), jnp.int32),
            pltpu.VMEM((3, 1, tiles), jnp.int32),
            pltpu.VMEM((CODE_ROWS, wide), jnp.float32),
            pltpu.VMEM((tiles, size, wide), tile_values.dtype),
            pltpu.SemaphoreType.DMA((4,)),
            pltpu.SemaphoreType.DMA,
        ],
        compiler_params=pltpu.CompilerParams(vmem_limit_bytes=PACK_BYTES),
        name="pack_tiles",
    )(*along, tile_values)


DST_BIT, SRC_BIT, PLACE_BIT = 10, 16, 24


def collect_kernel(plane, cols, slots, blocks, own_ref, *refs):
    tile_refs, refs = refs[: 1 + (plane - 1) * cols], refs[1 + (plane - 1) * cols :]
    out_ref, plan_ref, count_ref, *scratch = refs
    rows_ref, words_ref, codes_ref, row_sems, word_sem, tile_sems = scratch
    _, place, col, _ = position(plane)
    size = out_ref.shape[1]
    tiles = tile_refs[0].shape[0] // size
    looks = []
    for k in range(plane):
        ref = own_ref
        if k > 0:
            ref = tile_refs[1 + (k - 1) * cols].at[pl.ds(slots * size, CODE_ROWS)]
        copy = pltpu.make_async_copy(ref, rows_ref.at[k], row_sems.at[k])
        copy.start()
        looks.append(copy)
    copies, first = [], 0
    for i, ref in enumerate(tile_refs):
        rows = (tiles if i == 0 else slots) * size
        copy = pltpu.make_async_copy(
            ref.at[pl.ds(0, rows)], out_ref.at[pl.ds(first, rows)], tile_sems.at[i]
        )
        copy.start()
        copies.append(copy)
        first += rows
    out_ref[first:] = jnp.zeros_like(out_ref[first:])
    first //= size
    words_ref[...] = jnp.zeros_like(words_ref)
    for k, copy in enumerate(looks):
        copy.wait()
        rows = rows_ref[k].astype(jnp.float32).astype(jnp.int32)
        source = rows[3:4] * blocks + rows[2:3]
        word = (rows[0:1] << PLACE_BIT) + (source << SRC_BIT)
        words_ref[k : k + 1] = word + ((rows[1:2] + k * blocks) << DST_BIT)
    copy = pltpu.make_async_copy(words_ref, codes_ref, word_sem)
    copy.start()
    copy.wait()
    found = jnp.int32(0)
    for k in range(plane):

        def step(t, carry, k=k):
            at, slot = carry
            code = codes_ref[k, t]
            if k == 0:
                spot = t
            else:
                column = remainder(slot + (cols - col), cols)
                spot = tiles + ((k - 1) * cols + column) * slots + quotient(slot, cols)
            plan_ref[at] = (code & ((1 << PLACE_BIT) - 1)) + spot
            one = ((code >> PLACE_BIT) == place).astype(jnp.int32)
            return at + one, slot + one

        found, _ = lax.fori_loop(0, tiles, step, (found, jnp.int32(0)), unroll=8)
    for i in range(UNROLL):
        plan_ref[found + i] = first
    count_ref[0] = quotient(found + UNROLL - 1, UNROLL)
    for copy in copies:
        copy.wait()


def collect_tiles(codes, tile_parts, plane, cols, slots, blocks):
    wide = tile_parts[0].shape[1]
    tiles = tile_parts[0].shape[0] // wide
    entries = plane * tiles + UNROLL
    spots = tiles + (plane - 1) * cols * slots + 1
    laid = jax.ShapeDtypeStruct((spots * wide, wide), jnp.bfloat16)
    high = -(-plane // 8) * 8
    return pl.pallas_call(
        functools.partial(collect_kernel, plane, cols, slots, blocks),
        out_shape=(
            laid,
            jax.ShapeDtypeStruct((entries,), jnp.int32),
            jax.ShapeDtypeStruct((1,), jnp.int32),
        ),
        in_specs=[ANY] * (1 + len(tile_parts)),
        out_specs=(VMEM, SMEM, SMEM),
        scratch_shapes=[
            pltpu.VMEM((plane, CODE_ROWS, wide), jnp.bfloat16),
            pltpu.VMEM((high, wide), jnp.int32),
            pltpu.SMEM((high, wide), jnp.int32),
            pltpu.SemaphoreType.DMA((plane,)),
            pltpu.SemaphoreType.DMA,
            pltpu.SemaphoreType.DMA((len(tile_parts),)),
        ],
        compiler_params=params(laid),
        name="collect_tiles",
    )(codes, *tile_parts)


def planned(plan_ref, t):
    entry = plan_ref[t]
    spot = entry & ((1 << DST_BIT) - 1)
    return spot, (entry >> DST_BIT) & ((1 << (SRC_BIT - DST_BIT)) - 1), entry >> SRC_BIT


def block_rows(index, size):
    return pl.ds(pl.multiple_of(index * size, size), size)


def forward_kernel(line, lanes, plane, plan_ref, count_ref, tiles_ref, *refs):
    part_refs, refs = refs[: 2 * line - 1], refs[2 * line - 1 :]
    out_refs, (nodes_ref, acc_ref, part_sems) = refs[:-3], refs[-3:]
    rows, width = part_refs[0].shape[0], nodes_ref.shape[1]
    size = tiles_ref.shape[1]
    mine, _, _, way = position(plane)

    def each_part(act):
        for i, ref in enumerate(part_refs):
            source = mine + way * (i - (line - 1))

            @pl.when((source >= 0) & (source < line))
            def _():
                here = ref.at[:, lanes] if ref.shape != (rows, width) else ref
                act(
                    pltpu.make_async_copy(
                        here, nodes_ref.at[block_rows(source, rows)], part_sems.at[i]
                    )
                )

    each_part(lambda copy: copy.start())
    acc_ref[...] = jnp.zeros_like(acc_ref)
    each_part(lambda copy: copy.wait())

    def step(i, carry):
        for j in range(UNROLL):
            spot, dst, src = planned(plan_ref, i * UNROLL + j)
            acc_ref[block_rows(dst, size)] += jnp.dot(
                tiles_ref[block_rows(spot, size)],
                nodes_ref[block_rows(src, size)],
                preferred_element_type=jnp.float32,
            )
        return carry

    lax.fori_loop(0, count_ref[0], step, 0)
    for k, ref in enumerate(out_refs):
        ref[...] = acc_ref[k * rows : (k + 1) * rows].astype(ref.dtype)


def forward_tiles(plan, count, tiles, node_parts, plane, lanes):
    line = (len(node_parts) + 1) // 2
    rows, width = node_parts[0].shape[0], lanes.size
    kinds = [jnp.float32] + [jnp.bfloat16] * (plane - 1)
    outs = tuple(jax.ShapeDtypeStruct((rows, width), kind) for kind in kinds)
    scratch = [
        pltpu.VMEM((line * rows, width), jnp.bfloat16),
        pltpu.VMEM((plane * rows, width), jnp.float32),
    ]
    return pl.pallas_call(
        functools.partial(forward_kernel, line, lanes, plane),
        out_shape=outs,
        in_specs=[SMEM] * 2 + [VMEM] + [ANY] * len(node_parts),
        out_specs=(VMEM,) * plane,
        scratch_shapes=scratch + [pltpu.SemaphoreType.DMA((len(node_parts),))],
        compiler_params=params(tiles, *outs, *scratch),
        name="forward_tiles",
    )(plan, count, tiles, *node_parts)


def dense_kernel(chunk, halves, labels_ref, weight_ref, *refs):
    parts, (act_ref, out_grad_ref, agg_grad_ref) = refs[:-3], refs[-3:]
    rows, part_width = parts[0].shape
    width = part_width * halves
    features = weight_ref.shape[0]
    size = labels_ref.shape[1]

    def rows_step(i, carry):
        here = block_rows(i, chunk)
        agg = jnp.concatenate([part[here, :] for part in parts], axis=1)
        hidden = jnp.dot(agg, weight_ref[...], preferred_element_type=jnp.float32)
        sigmoid = jax.nn.sigmoid(hidden)
        activated = hidden * sigmoid
        act_ref[here, :] = activated[:, :width].astype(act_ref.dtype)
        slopes = sigmoid * (1.0 + hidden * (1.0 - sigmoid))
        named = []
        for b in range(chunk // size):
            across = labels_ref[pl.ds(i * (chunk // size) + b, 1), :]
            named.append(jnp.broadcast_to(across, (size, size)).T)
        named = jnp.concatenate(named, axis=0)
        ids = lax.broadcasted_iota(jnp.int32, (chunk, size), 1).astype(jnp.float32)
        target = jnp.concatenate(
            [(named == ids + f * size).astype(jnp.float32) for f in range(features // size)],
            axis=1,
        )
        out_grad = ((activated - target) * slopes).astype(jnp.bfloat16)
        out_grad_ref[here, :] = out_grad
        agg_grad_ref[here, :] = lax.dot_general(
            out_grad,
            weight_ref[:part_width, :],
            (((1,), (1,)), ((), ())),
            preferred_element_type=jnp.float32,
        ).astype(agg_grad_ref.dtype)
        return carry

    lax.fori_loop(0, rows // chunk, rows_step, 0)


def dense(labels, weight, parts, halves):
    rows, part_width = parts[0].shape
    chunk = math.gcd(rows, 256)
    outs = tuple(
        jax.ShapeDtypeStruct((rows, width), jnp.bfloat16)
        for width in (part_width * halves, weight.shape[0], part_width)
    )
    return pl.pallas_call(
        functools.partial(dense_kernel, chunk, halves),
        out_shape=outs,
        in_specs=[VMEM] * (2 + len(parts)),
        out_specs=(VMEM,) * 3,
        compiler_params=params(labels, weight, *parts, *outs),
        name="dense",
    )(labels, weight, *parts)


def grads_kernel(scale, halves, weight_ref, out_grad_ref, *refs):
    parts, (terms_ref, *agg_grad_refs) = refs[: -halves], refs[-halves:]
    part_width = parts[0].shape[1]
    for h, ref in enumerate(agg_grad_refs, 1):
        ref[...] = lax.dot_general(
            out_grad_ref[...],
            weight_ref[h * part_width : (h + 1) * part_width, :],
            (((1,), (1,)), ((), ())),
            preferred_element_type=jnp.float32,
        ).astype(ref.dtype)
    for i, part in enumerate(parts):
        terms = lax.dot_general(
            part[...],
            out_grad_ref[:, : part_width * halves],
            (((0,), (0,)), ((), ())),
            preferred_element_type=jnp.float32,
        )
        terms_ref[i * part_width : (i + 1) * part_width] = (terms * scale).astype(terms_ref.dtype)


def grads(weight, out_grad, parts, halves, node_total):
    rows, part_width = parts[0].shape
    outs = (jax.ShapeDtypeStruct((weight.shape[0], part_width * halves), jnp.bfloat16),) + (
        jax.ShapeDtypeStruct((rows, part_width), jnp.bfloat16),
    ) * (halves - 1)
    return pl.pallas_call(
        functools.partial(grads_kernel, 1.0 / math.sqrt(node_total), halves),
        out_shape=outs,
        in_specs=[VMEM] * (2 + len(parts)),
        out_specs=(VMEM,) * halves,
        compiler_params=params(weight, out_grad, *parts, *outs),
        name="grads",
    )(weight, out_grad, *parts)


def spread_kernel(line, plane, plan_ref, count_ref, tiles_ref, *refs):
    grad_refs, refs = refs[:plane], refs[plane:]
    out_refs, (grads_ref, acc_ref, grad_sems) = refs[:-3], refs[-3:]
    rows = grad_refs[0].shape[0]
    size = tiles_ref.shape[1]
    mine, _, _, way = position(plane)
    copies = []
    for k, ref in enumerate(grad_refs):
        copy = pltpu.make_async_copy(ref, grads_ref.at[pl.ds(k * rows, rows)], grad_sems.at[k])
        copy.start()
        copies.append(copy)
    acc_ref[...] = jnp.zeros_like(acc_ref)
    for copy in copies:
        copy.wait()

    def step(i, carry):
        for j in range(UNROLL):
            spot, dst, src = planned(plan_ref, i * UNROLL + j)
            acc_ref[block_rows(src, size)] += lax.dot_general(
                tiles_ref[block_rows(spot, size)],
                grads_ref[block_rows(dst, size)],
                (((0,), (0,)), ((), ())),
                preferred_element_type=jnp.float32,
            )
        return carry

    lax.fori_loop(0, count_ref[0], step, 0)
    for i, ref in enumerate(out_refs):
        target = mine + way * (i - (line - 1))

        @pl.when((target >= 0) & (target < line))
        def _():
            ref[...] = acc_ref[block_rows(target, rows)].astype(ref.dtype)


def spread_tiles(plan, count, tiles, grad_parts, line):
    plane = len(grad_parts)
    rows, width = grad_parts[0].shape
    kinds = [jnp.float32 if i == line - 1 else jnp.bfloat16 for i in range(2 * line - 1)]
    outs = tuple(jax.ShapeDtypeStruct((rows, width), kind) for kind in kinds)
    scratch = [
        pltpu.VMEM((plane * rows, width), jnp.bfloat16),
        pltpu.VMEM((line * rows, width), jnp.float32),
    ]
    return pl.pallas_call(
        functools.partial(spread_kernel, line, plane),
        out_shape=outs,
        in_specs=[SMEM] * 2 + [VMEM] + [ANY] * plane,
        out_specs=(VMEM,) * (2 * line - 1),
        scratch_shapes=scratch + [pltpu.SemaphoreType.DMA((plane,))],
        compiler_params=params(tiles, *outs, *scratch),
        name="spread_tiles",
    )(plan, count, tiles, *grad_parts)


def along_line(x, line, plane, cols, step, reach):
    pairs = []
    for z in range(line):
        for q in range(plane):
            for c in range(cols):
                way = 1 - 2 * (c & 1)
                to, end = z + way * step, z + way * reach
                if 0 <= to < line and 0 <= end < line:
                    pairs.append(((z * plane + q) * cols + c, (to * plane + q) * cols + c))
    return lax.ppermute(x, ("rows", "cols"), pairs)


def line_gather(x, line, plane, cols, lanes):
    move = lambda part, step, reach: along_line(part, line, plane, cols, step, reach)
    up, down = [x], [x]
    for k in range(1, line - 1):
        up.append(move(up[-1], 1, 1 - k))
        down.append(move(down[-1], -1, k - 1))
    parts, high, low = [], up[-1], down[-1]
    for part in lanes:
        first = move(high[:, part], 1, 2 - line)
        last = move(low[:, part], -1, line - 2)
        high, low, first = lax.optimization_barrier((high, low, first))
        parts.append([first] + up[:0:-1] + down + [last])
    return parts


def line_sum(terms, line, plane, cols, beside):
    moved = {1: None, -1: None}
    for k in range(line - 1, 0, -1):
        for step in moved:
            term = terms[line - 1 + step * k]
            if moved[step] is not None:
                total = term.astype(jnp.float32) + moved[step].astype(jnp.float32)
                term = total.astype(term.dtype)
            moved[step] = along_line(term, line, plane, cols, step, step * k)
        if k == line - 1:
            moved, beside = lax.optimization_barrier((moved, beside))
    return [terms[line - 1], moved[1], moved[-1]], beside


def finish_kernel(halves, *refs):
    out_ref, refs = refs[-1], refs[:-1]
    each = len(refs) // halves
    width = refs[0].shape[1]
    for h in range(halves):
        total = refs[h * each][...]
        for ref in refs[h * each + 1 : (h + 1) * each]:
            total += ref[...].astype(jnp.float32)
        out_ref[:, h * width : (h + 1) * width] = total.astype(out_ref.dtype)


def finish(pieces):
    flat = [piece for half in pieces for piece in half]
    rows, width = flat[0].shape
    out = jax.ShapeDtypeStruct((rows, width * len(pieces)), jnp.bfloat16)
    return pl.pallas_call(
        functools.partial(finish_kernel, len(pieces)),
        out_shape=out,
        in_specs=[VMEM] * len(flat),
        out_specs=VMEM,
        compiler_params=params(out, *flat),
        name="finish",
    )(*flat)


def sum_apart(terms, first, end, rows):
    while first < end:
        other = shuffle(terms, [(r, r ^ first) for r in range(rows)])
        total = terms.astype(jnp.float32) + other.astype(jnp.float32)
        terms = total.astype(terms.dtype)
        first *= 2
    return terms


def prepare_kernel(cols, labels_ref, weight_ref, own_labels_ref, own_first_ref, wide_ref):
    col = lax.axis_index("cols")
    features = weight_ref.shape[0]
    width = features // cols
    labels = labels_ref[...] - col * width
    own_labels_ref[...] = jnp.where(labels < 0, labels + features, labels).astype(jnp.float32)
    for c in range(cols):
        row = remainder(col + c, cols) * width
        rows = weight_ref[pl.ds(pl.multiple_of(row, width), width), :]
        wide_ref[c * width : (c + 1) * width] = rows.astype(jnp.float32)
    turned = pltpu.roll(wide_ref[...], remainder(cols - col, cols) * width, axis=1)
    own_first_ref[...] = turned.astype(own_first_ref.dtype)


def prepare(labels, weight, cols):
    outs = (jax.ShapeDtypeStruct(labels.shape, jnp.float32), weight)
    wide = pltpu.VMEM(weight.shape, jnp.float32)
    return pl.pallas_call(
        functools.partial(prepare_kernel, cols),
        out_shape=(outs[0], jax.ShapeDtypeStruct(weight.shape, weight.dtype)),
        in_specs=[VMEM, VMEM],
        out_specs=(VMEM, VMEM),
        scratch_shapes=[wide],
        compiler_params=params(weight, weight, wide, wide),
        name="prepare",
    )(labels, weight)


def weight_kernel(cols, mine_ref, other_ref, out_ref):
    col = lax.axis_index("cols")
    width = out_ref.shape[1]
    for c in range(cols):
        here = pl.ds(c * width, width)
        total = mine_ref[here].astype(jnp.float32) + other_ref[here].astype(jnp.float32)
        row = remainder(col + c, cols) * width
        out_ref[pl.ds(pl.multiple_of(row, width), width)] = total


def finish_weight(mine, other, cols):
    out = jax.ShapeDtypeStruct(mine.shape, jnp.float32)
    return pl.pallas_call(
        functools.partial(weight_kernel, cols),
        out_shape=out,
        in_specs=[VMEM, VMEM],
        out_specs=VMEM,
        compiler_params=params(mine, other, out),
        name="finish_weight",
    )(mine, other)


def per_device(node_features, weight, tile_values, tile_row, source_owner, source_block, labels):
    local_rows, width = node_features.shape
    n_tiles, block_size = tile_values.shape[:2]
    blocks = local_rows // block_size
    rows, cols = lax.axis_size("rows"), lax.axis_size("cols")
    plane = math.gcd(rows, LARGEST_PLANE)
    line = rows // plane
    halves = 2 if width % 256 == 0 else 1
    part_width = width // halves
    slots = -(-min(n_tiles, line * (2 * n_tiles // rows)) // cols)
    owners = source_owner[:, 0]

    def other_cols(x):
        return [
            lax.ppermute(x, "cols", [((c + k) % cols, c) for c in range(cols)])
            for k in range(1, cols)
        ]

    lanes = [slice(h * part_width, (h + 1) * part_width) for h in range(halves)]
    *packed, codes = pack_tiles(
        owners, tile_row, source_block, tile_values, plane, cols, slots
    )
    node_parts = line_gather(node_features, line, plane, cols, lanes)
    tile_parts = [tile_values.reshape(n_tiles * block_size, block_size)]
    for k in range(1, plane):
        arrived = across_plane(packed[k - 1], k, line, plane)
        tile_parts += [arrived] + other_cols(arrived)
    tiles, plan, count = collect_tiles(codes, tile_parts, plane, cols, slots, blocks)

    own_labels, own_first = prepare(labels.reshape(blocks, block_size), weight, cols)
    plan, own_first, own_labels = lax.optimization_barrier((plan, own_first, own_labels))

    aggregated = []
    for h in range(halves):
        here = pl.ds(h * part_width, part_width)
        sums = forward_tiles(plan, count, tiles, node_parts[h], plane, here)
        total = sums[0]
        for k in range(1, plane):
            total = total + across_plane(sums[k], k, line, plane).astype(jnp.float32)
        mine = total.astype(jnp.bfloat16)
        aggregated.append([mine] + other_cols(mine))
    parts = [aggregated[h][c] for c in range(cols) for h in range(halves)]

    activations, out_grad, agg_grad = dense(own_labels, own_first, parts, halves)
    weight_terms, *agg_grads = grads(own_first, out_grad, parts, halves, local_rows * rows)

    pieces = []
    for i, agg_grad in enumerate(agg_grads[::-1] + [agg_grad]):
        arrived = [agg_grad] + [across_plane(agg_grad, k, line, plane) for k in range(1, plane)]
        if i == 0:
            weight_terms = sum_apart(weight_terms, plane, 2 * plane, rows)
            arrived, weight_terms = lax.optimization_barrier((arrived, weight_terms))
            weight_terms = sum_apart(weight_terms, 2 * plane, rows, rows)
        terms = spread_tiles(plan, count, tiles, arrived, line)
        half, weight_terms = line_sum(terms, line, plane, cols, weight_terms)
        pieces.append(half)
    weight_terms = sum_apart(weight_terms, 1, plane // 2, rows)
    other = across_plane(weight_terms, plane // 2, line, plane)
    weight_grad = finish_weight(weight_terms, other, cols)
    return activations, weight_grad, finish(pieces[::-1])


def solution(mesh):
    return jax.shard_map(
        per_device,
        mesh=mesh,
        in_specs=(
            P("rows", "cols"),
            P(),
            P("rows", None, None),
            P("rows"),
            P("rows", None),
            P("rows"),
            P("rows"),
        ),
        out_specs=(P("rows", "cols"), P(None, "cols"), P("rows", "cols")),
        check_vma=False,
    )
```

```python
import functools
import math

import jax
import jax.numpy as jnp
from jax import lax
from jax.experimental import pallas as pl
from jax.experimental.pallas import tpu as pltpu
from jax.sharding import PartitionSpec as P

VMEM = pl.BlockSpec(memory_space=pltpu.VMEM)
SMEM = pl.BlockSpec(memory_space=pltpu.SMEM)
ANY = pl.BlockSpec(memory_space=pl.ANY)
HBM = pl.BlockSpec(memory_space=pltpu.HBM)
SPARE_BYTES = 2 * 1024 * 1024
PACK_BYTES = 56 * 1024 * 1024
UNROLL = 8
LARGEST_PLANE = 4


def params(*shapes):
    room = SPARE_BYTES
    for shape in shapes:
        *lead, high, wide = shape.shape
        room += math.prod(lead) * high * (-(-wide // 128) * 128) * jnp.dtype(shape.dtype).itemsize
    return pltpu.CompilerParams(vmem_limit_bytes=room)


def quotient(x, n):
    return x >> (n.bit_length() - 1) if n & (n - 1) == 0 else lax.div(x, n)


def remainder(x, n):
    return x & (n - 1) if n & (n - 1) == 0 else lax.rem(x, n)


def position(plane):
    index, col = lax.axis_index("rows"), lax.axis_index("cols")
    return quotient(index, plane), remainder(index, plane), col, 1 - 2 * (col & 1)


def shuffle(x, pairs):
    return lax.ppermute(x, "rows", pairs)


def across_plane(x, k, line, plane):
    return shuffle(x, [(r, r ^ k) for r in range(line * plane)])


CODE_ROWS = 16


def pack_kernel(plane, cols, owner_ref, row_ref, source_ref, tiles_ref, *refs):
    out_refs, (codes_ref, *scratch) = refs[: plane - 1], refs[plane - 1 :]
    list_ref, slot_ref, owners_ref, along_ref, rows_ref, held_ref, small_sems, held_sem = scratch
    _, place, col, _ = position(plane)
    tiles, size = tiles_ref.shape[:2]
    slots = (out_refs[0].shape[0] - CODE_ROWS) // size
    spare = (plane - 1) * slots
    looks = [pltpu.make_async_copy(owner_ref, owners_ref, small_sems.at[0])]
    for i, ref in enumerate((owner_ref, row_ref, source_ref)):
        looks.append(pltpu.make_async_copy(ref, along_ref.at[i], small_sems.at[1 + i]))
    for look in looks:
        look.start()
    bulk = pltpu.make_async_copy(tiles_ref, held_ref, held_sem)
    bulk.start()
    for k in range(plane):
        slot_ref[k] = 0
    for i in range(spare):
        list_ref[i] = 0
    rows_ref[...] = jnp.zeros_like(rows_ref)
    for look in looks:
        look.wait()

    def step(t, carry):
        k = remainder(owners_ref[0, t], plane) ^ place
        slot = slot_ref[k]
        slot_ref[k] = slot + 1
        sent = (k > 0) & (remainder(slot, cols) == col)
        list_ref[jnp.where(sent, (k - 1) * slots + quotient(slot, cols), spare)] = t
        return carry

    lax.fori_loop(0, tiles, step, 0, unroll=4)
    owners = along_ref[0]
    rows_ref[0:1, :tiles] = remainder(owners, plane).astype(jnp.float32)
    rows_ref[1:2, :tiles] = along_ref[1].astype(jnp.float32)
    rows_ref[2:3, :tiles] = along_ref[2].astype(jnp.float32)
    rows_ref[3:4, :tiles] = quotient(owners, plane).astype(jnp.float32)
    codes = rows_ref[...].astype(codes_ref.dtype)
    codes_ref[...] = codes
    bulk.wait()
    for k, out_ref in enumerate(out_refs):
        for slot in range(slots):
            out_ref[slot * size : (slot + 1) * size] = held_ref[list_ref[k * slots + slot]]
        out_ref[slots * size :] = codes


def pack_tiles(owners, tile_row, source_block, tile_values, plane, cols, slots):
    tiles, size, wide = tile_values.shape
    shape = jax.ShapeDtypeStruct((slots * size + CODE_ROWS, wide), tile_values.dtype)
    codes = jax.ShapeDtypeStruct((CODE_ROWS, wide), tile_values.dtype)
    along = [x.reshape(1, tiles) for x in (owners, tile_row, source_block)]
    return pl.pallas_call(
        functools.partial(pack_kernel, plane, cols),
        out_shape=(shape,) * (plane - 1) + (codes,),
        in_specs=[HBM] * 4,
        out_specs=(VMEM,) * plane,
        scratch_shapes=[
            pltpu.SMEM(((plane - 1) * slots + 1,), jnp.int32),
            pltpu.SMEM((plane,), jnp.int32),
            pltpu.SMEM((1, tiles), jnp.int32),
            pltpu.VMEM((3, 1, tiles), jnp.int32),
            pltpu.VMEM((CODE_ROWS, wide), jnp.float32),
            pltpu.VMEM((tiles, size, wide), tile_values.dtype),
            pltpu.SemaphoreType.DMA((4,)),
            pltpu.SemaphoreType.DMA,
        ],
        compiler_params=pltpu.CompilerParams(vmem_limit_bytes=PACK_BYTES),
        name="pack_tiles",
    )(*along, tile_values)


DST_BIT, SRC_BIT, PLACE_BIT = 10, 16, 24


def own_kernel(tiles_ref, codes_ref, out_ref, own_ref, sems):
    rows = tiles_ref.shape[0]
    moves = ((tiles_ref, out_ref.at[pl.ds(0, rows)]), (codes_ref, own_ref))
    copies = [pltpu.make_async_copy(*move, sems.at[i]) for i, move in enumerate(moves)]
    for copy in copies:
        copy.start()
    out_ref[out_ref.shape[0] - out_ref.shape[1] :] = jnp.zeros(
        (out_ref.shape[1], out_ref.shape[1]), out_ref.dtype
    )
    for copy in copies:
        copy.wait()


def own_tiles(tiles, codes, spots):
    wide = tiles.shape[1]
    laid = jax.ShapeDtypeStruct((spots * wide, wide), tiles.dtype)
    return pl.pallas_call(
        own_kernel,
        out_shape=(laid, jax.ShapeDtypeStruct(codes.shape, codes.dtype)),
        in_specs=[ANY, ANY],
        out_specs=(VMEM, VMEM),
        scratch_shapes=[pltpu.SemaphoreType.DMA((2,))],
        compiler_params=params(laid),
        name="own_tiles",
    )(tiles, codes)


def collect_kernel(plane, cols, slots, blocks, tiles, own_ref, laid_ref, *refs):
    tile_refs, refs = refs[: (plane - 1) * cols], refs[(plane - 1) * cols :]
    out_ref, plan_ref, count_ref, *scratch = refs
    rows_ref, words_ref, codes_ref, row_sems, word_sem, tile_sems = scratch
    _, place, col, _ = position(plane)
    size = out_ref.shape[1]
    looks = []
    for k in range(plane):
        ref = own_ref
        if k > 0:
            ref = tile_refs[(k - 1) * cols].at[pl.ds(slots * size, CODE_ROWS)]
        copy = pltpu.make_async_copy(ref, rows_ref.at[k], row_sems.at[k])
        copy.start()
        looks.append(copy)
    copies, first, rows = [], tiles * size, slots * size
    for i, ref in enumerate(tile_refs):
        copy = pltpu.make_async_copy(
            ref.at[pl.ds(0, rows)], out_ref.at[pl.ds(first, rows)], tile_sems.at[i]
        )
        copy.start()
        copies.append(copy)
        first += rows
    words_ref[...] = jnp.zeros_like(words_ref)
    for k, copy in enumerate(looks):
        copy.wait()
        rows = rows_ref[k].astype(jnp.float32).astype(jnp.int32)
        source = rows[3:4] * blocks + rows[2:3]
        word = (rows[0:1] << PLACE_BIT) + (source << SRC_BIT)
        words_ref[k : k + 1] = word + ((rows[1:2] + k * blocks) << DST_BIT)
    copy = pltpu.make_async_copy(words_ref, codes_ref, word_sem)
    copy.start()
    copy.wait()
    found = jnp.int32(0)
    for k in range(plane):

        def step(t, carry, k=k):
            at, slot = carry
            code = codes_ref[k, t]
            if k == 0:
                spot = t
            else:
                column = remainder(slot + (cols - col), cols)
                spot = tiles + ((k - 1) * cols + column) * slots + quotient(slot, cols)
            plan_ref[at] = (code & ((1 << PLACE_BIT) - 1)) + spot
            one = ((code >> PLACE_BIT) == place).astype(jnp.int32)
            return at + one, slot + one

        found, _ = lax.fori_loop(0, tiles, step, (found, jnp.int32(0)), unroll=8)
    for i in range(UNROLL):
        plan_ref[found + i] = first // size
    count_ref[0] = quotient(found + UNROLL - 1, UNROLL)
    for copy in copies:
        copy.wait()


def collect_tiles(codes, laid, tile_parts, plane, cols, slots, blocks, tiles):
    wide = laid.shape[1]
    entries = plane * tiles + UNROLL
    high = -(-plane // 8) * 8
    return pl.pallas_call(
        functools.partial(collect_kernel, plane, cols, slots, blocks, tiles),
        out_shape=(
            jax.ShapeDtypeStruct(laid.shape, laid.dtype),
            jax.ShapeDtypeStruct((entries,), jnp.int32),
            jax.ShapeDtypeStruct((1,), jnp.int32),
        ),
        in_specs=[ANY, VMEM] + [ANY] * len(tile_parts),
        out_specs=(VMEM, SMEM, SMEM),
        scratch_shapes=[
            pltpu.VMEM((plane, CODE_ROWS, wide), jnp.bfloat16),
            pltpu.VMEM((high, wide), jnp.int32),
            pltpu.SMEM((high, wide), jnp.int32),
            pltpu.SemaphoreType.DMA((plane,)),
            pltpu.SemaphoreType.DMA,
            pltpu.SemaphoreType.DMA((len(tile_parts),)),
        ],
        input_output_aliases={1: 0},
        compiler_params=params(laid),
        name="collect_tiles",
    )(codes, laid, *tile_parts)


def planned(plan_ref, t):
    entry = plan_ref[t]
    spot = entry & ((1 << DST_BIT) - 1)
    return spot, (entry >> DST_BIT) & ((1 << (SRC_BIT - DST_BIT)) - 1), entry >> SRC_BIT


def block_rows(index, size):
    return pl.ds(pl.multiple_of(index * size, size), size)


def forward_kernel(line, lanes, plane, plan_ref, count_ref, tiles_ref, *refs):
    part_refs, refs = refs[: 2 * line - 1], refs[2 * line - 1 :]
    out_refs, (nodes_ref, acc_ref, part_sems) = refs[:-3], refs[-3:]
    rows, width = part_refs[0].shape[0], nodes_ref.shape[1]
    size = tiles_ref.shape[1]
    mine, _, _, way = position(plane)

    def each_part(act):
        for i, ref in enumerate(part_refs):
            source = mine + way * (i - (line - 1))

            @pl.when((source >= 0) & (source < line))
            def _():
                here = ref.at[:, lanes] if ref.shape != (rows, width) else ref
                act(
                    pltpu.make_async_copy(
                        here, nodes_ref.at[block_rows(source, rows)], part_sems.at[i]
                    )
                )

    each_part(lambda copy: copy.start())
    acc_ref[...] = jnp.zeros_like(acc_ref)
    each_part(lambda copy: copy.wait())

    def step(i, carry):
        for j in range(UNROLL):
            spot, dst, src = planned(plan_ref, i * UNROLL + j)
            acc_ref[block_rows(dst, size)] += jnp.dot(
                tiles_ref[block_rows(spot, size)],
                nodes_ref[block_rows(src, size)],
                preferred_element_type=jnp.float32,
            )
        return carry

    lax.fori_loop(0, count_ref[0], step, 0)
    for k, ref in enumerate(out_refs):
        ref[...] = acc_ref[k * rows : (k + 1) * rows].astype(ref.dtype)


def forward_tiles(plan, count, tiles, node_parts, plane, lanes):
    line = (len(node_parts) + 1) // 2
    rows, width = node_parts[0].shape[0], lanes.size
    kinds = [jnp.float32] + [jnp.bfloat16] * (plane - 1)
    outs = tuple(jax.ShapeDtypeStruct((rows, width), kind) for kind in kinds)
    scratch = [
        pltpu.VMEM((line * rows, width), jnp.bfloat16),
        pltpu.VMEM((plane * rows, width), jnp.float32),
    ]
    return pl.pallas_call(
        functools.partial(forward_kernel, line, lanes, plane),
        out_shape=outs,
        in_specs=[SMEM] * 2 + [VMEM] + [ANY] * len(node_parts),
        out_specs=(VMEM,) * plane,
        scratch_shapes=scratch + [pltpu.SemaphoreType.DMA((len(node_parts),))],
        compiler_params=params(tiles, *outs, *scratch),
        name="forward_tiles",
    )(plan, count, tiles, *node_parts)


def dense_kernel(chunk, halves, labels_ref, weight_ref, *refs):
    parts, (act_ref, out_grad_ref, agg_grad_ref) = refs[:-3], refs[-3:]
    rows, part_width = parts[0].shape
    width = part_width * halves
    features = weight_ref.shape[0]
    size = labels_ref.shape[1]

    def rows_step(i, carry):
        here = block_rows(i, chunk)
        agg = jnp.concatenate([part[here, :] for part in parts], axis=1)
        hidden = jnp.dot(agg, weight_ref[...], preferred_element_type=jnp.float32)
        sigmoid = jax.nn.sigmoid(hidden)
        activated = hidden * sigmoid
        act_ref[here, :] = activated[:, :width].astype(act_ref.dtype)
        slopes = sigmoid * (1.0 + hidden * (1.0 - sigmoid))
        named = []
        for b in range(chunk // size):
            across = labels_ref[pl.ds(i * (chunk // size) + b, 1), :]
            named.append(jnp.broadcast_to(across, (size, size)).T)
        named = jnp.concatenate(named, axis=0)
        ids = lax.broadcasted_iota(jnp.int32, (chunk, size), 1).astype(jnp.float32)
        target = jnp.concatenate(
            [(named == ids + f * size).astype(jnp.float32) for f in range(features // size)],
            axis=1,
        )
        out_grad = ((activated - target) * slopes).astype(jnp.bfloat16)
        out_grad_ref[here, :] = out_grad
        agg_grad_ref[here, :] = lax.dot_general(
            out_grad,
            weight_ref[:part_width, :],
            (((1,), (1,)), ((), ())),
            preferred_element_type=jnp.float32,
        ).astype(agg_grad_ref.dtype)
        return carry

    lax.fori_loop(0, rows // chunk, rows_step, 0)


def dense(labels, weight, parts, halves):
    rows, part_width = parts[0].shape
    chunk = math.gcd(rows, 256)
    outs = tuple(
        jax.ShapeDtypeStruct((rows, width), jnp.bfloat16)
        for width in (part_width * halves, weight.shape[0], part_width)
    )
    return pl.pallas_call(
        functools.partial(dense_kernel, chunk, halves),
        out_shape=outs,
        in_specs=[VMEM] * (2 + len(parts)),
        out_specs=(VMEM,) * 3,
        compiler_params=params(labels, weight, *parts, *outs),
        name="dense",
    )(labels, weight, *parts)


def grads_kernel(scale, halves, weight_ref, out_grad_ref, *refs):
    parts, (terms_ref, *agg_grad_refs) = refs[: -halves], refs[-halves:]
    part_width = parts[0].shape[1]
    for h, ref in enumerate(agg_grad_refs, 1):
        ref[...] = lax.dot_general(
            out_grad_ref[...],
            weight_ref[h * part_width : (h + 1) * part_width, :],
            (((1,), (1,)), ((), ())),
            preferred_element_type=jnp.float32,
        ).astype(ref.dtype)
    for i, part in enumerate(parts):
        terms = lax.dot_general(
            part[...],
            out_grad_ref[:, : part_width * halves],
            (((0,), (0,)), ((), ())),
            preferred_element_type=jnp.float32,
        )
        terms_ref[i * part_width : (i + 1) * part_width] = (terms * scale).astype(terms_ref.dtype)


def grads(weight, out_grad, parts, halves, node_total):
    rows, part_width = parts[0].shape
    outs = (jax.ShapeDtypeStruct((weight.shape[0], part_width * halves), jnp.bfloat16),) + (
        jax.ShapeDtypeStruct((rows, part_width), jnp.bfloat16),
    ) * (halves - 1)
    return pl.pallas_call(
        functools.partial(grads_kernel, 1.0 / math.sqrt(node_total), halves),
        out_shape=outs,
        in_specs=[VMEM] * (2 + len(parts)),
        out_specs=(VMEM,) * halves,
        compiler_params=params(weight, out_grad, *parts, *outs),
        name="grads",
    )(weight, out_grad, *parts)


def spread_kernel(line, plane, plan_ref, count_ref, tiles_ref, *refs):
    grad_refs, refs = refs[:plane], refs[plane:]
    out_refs, (grads_ref, acc_ref, grad_sems) = refs[:-3], refs[-3:]
    rows = grad_refs[0].shape[0]
    size = tiles_ref.shape[1]
    mine, _, _, way = position(plane)
    copies = []
    for k, ref in enumerate(grad_refs):
        copy = pltpu.make_async_copy(ref, grads_ref.at[pl.ds(k * rows, rows)], grad_sems.at[k])
        copy.start()
        copies.append(copy)
    acc_ref[...] = jnp.zeros_like(acc_ref)
    for copy in copies:
        copy.wait()

    def step(i, carry):
        for j in range(UNROLL):
            spot, dst, src = planned(plan_ref, i * UNROLL + j)
            acc_ref[block_rows(src, size)] += lax.dot_general(
                tiles_ref[block_rows(spot, size)],
                grads_ref[block_rows(dst, size)],
                (((0,), (0,)), ((), ())),
                preferred_element_type=jnp.float32,
            )
        return carry

    lax.fori_loop(0, count_ref[0], step, 0)
    for i, ref in enumerate(out_refs):
        target = mine + way * (i - (line - 1))

        @pl.when((target >= 0) & (target < line))
        def _():
            ref[...] = acc_ref[block_rows(target, rows)].astype(ref.dtype)


def spread_tiles(plan, count, tiles, grad_parts, line):
    plane = len(grad_parts)
    rows, width = grad_parts[0].shape
    kinds = [jnp.float32 if i == line - 1 else jnp.bfloat16 for i in range(2 * line - 1)]
    outs = tuple(jax.ShapeDtypeStruct((rows, width), kind) for kind in kinds)
    scratch = [
        pltpu.VMEM((plane * rows, width), jnp.bfloat16),
        pltpu.VMEM((line * rows, width), jnp.float32),
    ]
    return pl.pallas_call(
        functools.partial(spread_kernel, line, plane),
        out_shape=outs,
        in_specs=[SMEM] * 2 + [VMEM] + [ANY] * plane,
        out_specs=(VMEM,) * (2 * line - 1),
        scratch_shapes=scratch + [pltpu.SemaphoreType.DMA((plane,))],
        compiler_params=params(tiles, *outs, *scratch),
        name="spread_tiles",
    )(plan, count, tiles, *grad_parts)


def along_line(x, line, plane, cols, step, reach):
    pairs = []
    for z in range(line):
        for q in range(plane):
            for c in range(cols):
                way = 1 - 2 * (c & 1)
                to, end = z + way * step, z + way * reach
                if 0 <= to < line and 0 <= end < line:
                    pairs.append(((z * plane + q) * cols + c, (to * plane + q) * cols + c))
    return lax.ppermute(x, ("rows", "cols"), pairs)


def line_gather(x, after, line, plane, cols, lanes):
    move = lambda part, step, reach: along_line(part, line, plane, cols, step, reach)
    later, _ = lax.optimization_barrier((x, after))
    up, down = [x], [later]
    for k in range(1, line - 1):
        up.append(move(up[-1], 1, 1 - k))
        down.append(move(down[-1], -1, k - 1))
    parts, high, low = [], up[-1], down[-1]
    for part in lanes:
        first = move(high[:, part], 1, 2 - line)
        last = move(low[:, part], -1, line - 2)
        high, low, first = lax.optimization_barrier((high, low, first))
        parts.append([first] + up[:0:-1] + down + [last])
    return parts


def line_sum(terms, line, plane, cols, beside):
    moved, late = {1: None, -1: None}, None
    for k in range(line - 1, 0, -1):
        for step in moved:
            term = terms[line - 1 + step * k]
            if moved[step] is not None:
                total = term.astype(jnp.float32) + moved[step].astype(jnp.float32)
                term = total.astype(term.dtype)
            moved[step] = along_line(term, line, plane, cols, step, step * k)
        if k == line - 1 and beside is not None:
            moved, beside = lax.optimization_barrier((moved, beside))
        if k > 1:
            late = tuple(moved.values())
    return [terms[line - 1], moved[1], moved[-1]], beside, late


def finish_kernel(halves, *refs):
    out_ref, refs = refs[-1], refs[:-1]
    each = len(refs) // halves
    width = refs[0].shape[1]
    for h in range(halves):
        total = refs[h * each][...]
        for ref in refs[h * each + 1 : (h + 1) * each]:
            total += ref[...].astype(jnp.float32)
        out_ref[:, h * width : (h + 1) * width] = total.astype(out_ref.dtype)


def finish(pieces):
    flat = [piece for half in pieces for piece in half]
    rows, width = flat[0].shape
    out = jax.ShapeDtypeStruct((rows, width * len(pieces)), jnp.bfloat16)
    return pl.pallas_call(
        functools.partial(finish_kernel, len(pieces)),
        out_shape=out,
        in_specs=[VMEM] * len(flat),
        out_specs=VMEM,
        compiler_params=params(out, *flat),
        name="finish",
    )(*flat)


def sum_apart(terms, first, end, rows):
    while first < end:
        other = shuffle(terms, [(r, r ^ first) for r in range(rows)])
        total = terms.astype(jnp.float32) + other.astype(jnp.float32)
        terms = total.astype(terms.dtype)
        first *= 2
    return terms


def prepare_kernel(cols, labels_ref, weight_ref, own_labels_ref, own_first_ref, wide_ref):
    col = lax.axis_index("cols")
    features = weight_ref.shape[0]
    width = features // cols
    labels = labels_ref[...] - col * width
    own_labels_ref[...] = jnp.where(labels < 0, labels + features, labels).astype(jnp.float32)
    for c in range(cols):
        row = remainder(col + c, cols) * width
        rows = weight_ref[pl.ds(pl.multiple_of(row, width), width), :]
        wide_ref[c * width : (c + 1) * width] = rows.astype(jnp.float32)
    turned = pltpu.roll(wide_ref[...], remainder(cols - col, cols) * width, axis=1)
    own_first_ref[...] = turned.astype(own_first_ref.dtype)


def prepare(labels, weight, cols):
    outs = (jax.ShapeDtypeStruct(labels.shape, jnp.float32), weight)
    wide = pltpu.VMEM(weight.shape, jnp.float32)
    return pl.pallas_call(
        functools.partial(prepare_kernel, cols),
        out_shape=(outs[0], jax.ShapeDtypeStruct(weight.shape, weight.dtype)),
        in_specs=[VMEM, VMEM],
        out_specs=(VMEM, VMEM),
        scratch_shapes=[wide],
        compiler_params=params(weight, weight, wide, wide),
        name="prepare",
    )(labels, weight)


def weight_kernel(cols, mine_ref, other_ref, out_ref):
    col = lax.axis_index("cols")
    width = out_ref.shape[1]
    for c in range(cols):
        here = pl.ds(c * width, width)
        total = mine_ref[here].astype(jnp.float32) + other_ref[here].astype(jnp.float32)
        row = remainder(col + c, cols) * width
        out_ref[pl.ds(pl.multiple_of(row, width), width)] = total


def finish_weight(mine, other, cols):
    out = jax.ShapeDtypeStruct(mine.shape, jnp.float32)
    return pl.pallas_call(
        functools.partial(weight_kernel, cols),
        out_shape=out,
        in_specs=[VMEM, VMEM],
        out_specs=VMEM,
        compiler_params=params(mine, other, out),
        name="finish_weight",
    )(mine, other)


def per_device(node_features, weight, tile_values, tile_row, source_owner, source_block, labels):
    local_rows, width = node_features.shape
    n_tiles, block_size = tile_values.shape[:2]
    blocks = local_rows // block_size
    rows, cols = lax.axis_size("rows"), lax.axis_size("cols")
    plane = math.gcd(rows, LARGEST_PLANE)
    line = rows // plane
    halves = 2 if width % 256 == 0 else 1
    part_width = width // halves
    slots = -(-min(n_tiles, line * (2 * n_tiles // rows)) // cols)
    owners = source_owner[:, 0]

    def other_cols(x):
        return [
            lax.ppermute(x, "cols", [((c + k) % cols, c) for c in range(cols)])
            for k in range(1, cols)
        ]

    lanes = [slice(h * part_width, (h + 1) * part_width) for h in range(halves)]
    *packed, codes = pack_tiles(
        owners, tile_row, source_block, tile_values, plane, cols, slots
    )
    node_parts = line_gather(node_features, packed, line, plane, cols, lanes)
    spots = n_tiles + (plane - 1) * cols * slots + 1
    flat = tile_values.reshape(n_tiles * block_size, block_size)
    early = own_tiles(flat, codes, spots) + prepare(labels.reshape(blocks, block_size), weight, cols)
    tile_parts = []
    for k in range(1, plane):
        arrived = across_plane(packed[k - 1], k, line, plane)
        if k == 1:
            arrived, early = lax.optimization_barrier((arrived, early))
        tile_parts += [arrived] + other_cols(arrived)
    laid, codes, own_labels, own_first = early
    tiles, plan, count = collect_tiles(
        codes, laid, tile_parts, plane, cols, slots, blocks, n_tiles
    )

    aggregated = []
    for h in range(halves):
        here = pl.ds(h * part_width, part_width)
        sums = forward_tiles(plan, count, tiles, node_parts[h], plane, here)
        total = sums[0]
        for k in range(1, plane):
            total = total + across_plane(sums[k], k, line, plane).astype(jnp.float32)
        mine = total.astype(jnp.bfloat16)
        aggregated.append([mine] + other_cols(mine))
    parts = [aggregated[h][c] for c in range(cols) for h in range(halves)]

    activations, out_grad, agg_grad = dense(own_labels, own_first, parts, halves)
    weight_terms, *agg_grads = grads(own_first, out_grad, parts, halves, local_rows * rows)

    pieces = []
    for i, agg_grad in enumerate([agg_grad] + agg_grads):
        arrived = [agg_grad] + [across_plane(agg_grad, k, line, plane) for k in range(1, plane)]
        if i == 0:
            weight_terms = sum_apart(weight_terms, plane, 2 * plane, rows)
            arrived, weight_terms = lax.optimization_barrier((arrived, weight_terms))
            weight_terms = sum_apart(weight_terms, 2 * plane, rows, rows)
        terms = spread_tiles(plan, count, tiles, arrived, line)
        beside = weight_terms if i == 0 else None
        half, beside, late = line_sum(terms, line, plane, cols, beside)
        if i == 0:
            weight_terms, _ = lax.optimization_barrier((beside, late))
        pieces.append(half)
    weight_terms = sum_apart(weight_terms, 1, plane // 2, rows)
    weight_terms, _ = lax.optimization_barrier((weight_terms, late))
    other = across_plane(weight_terms, plane // 2, line, plane)
    weight_grad = finish_weight(weight_terms, other, cols)
    return activations, weight_grad, finish(pieces)


def solution(mesh):
    return jax.shard_map(
        per_device,
        mesh=mesh,
        in_specs=(
            P("rows", "cols"),
            P(),
            P("rows", None, None),
            P("rows"),
            P("rows", None),
            P("rows"),
            P("rows"),
        ),
        out_specs=(P("rows", "cols"), P(None, "cols"), P("rows", "cols")),
        check_vma=False,
    )
```

```python
import functools
import math

import jax
import jax.numpy as jnp
from jax import lax
from jax.experimental import pallas as pl
from jax.experimental.pallas import tpu as pltpu
from jax.sharding import PartitionSpec as P

VMEM = pl.BlockSpec(memory_space=pltpu.VMEM)
SMEM = pl.BlockSpec(memory_space=pltpu.SMEM)
ANY = pl.BlockSpec(memory_space=pl.ANY)
HBM = pl.BlockSpec(memory_space=pltpu.HBM)
SPARE_BYTES = 2 * 1024 * 1024
PACK_BYTES = 56 * 1024 * 1024
UNROLL = 8
LARGEST_PLANE = 4


def params(*shapes):
    room = SPARE_BYTES
    for shape in shapes:
        *lead, high, wide = shape.shape
        room += math.prod(lead) * high * (-(-wide // 128) * 128) * jnp.dtype(shape.dtype).itemsize
    return pltpu.CompilerParams(vmem_limit_bytes=room)


def quotient(x, n):
    return x >> (n.bit_length() - 1) if n & (n - 1) == 0 else lax.div(x, n)


def remainder(x, n):
    return x & (n - 1) if n & (n - 1) == 0 else lax.rem(x, n)


def position(plane):
    index, col = lax.axis_index("rows"), lax.axis_index("cols")
    return quotient(index, plane), remainder(index, plane), col, 1 - 2 * (col & 1)


def shuffle(x, pairs):
    return lax.ppermute(x, "rows", pairs)


def across_plane(x, k, line, plane):
    return shuffle(x, [(r, r ^ k) for r in range(line * plane)])


CODE_ROWS = 16


def plane_gather(x, line, plane):
    if plane != 4:
        return [(x, 0)] + [
            (across_plane(x, k, line, plane), k * x.shape[0]) for k in range(1, plane)
        ]
    rows = x.shape[0]
    near = [across_plane(x, k, line, plane) for k in (1, 2)]
    pieces = [(x, 0), (near[0], rows), (near[1], 2 * rows)]
    handed = (near[0][: rows // 2], near[1][rows // 2 :])
    for i, part in enumerate(handed):
        arrived = across_plane(part, 2 - i, line, plane)
        pieces.append((arrived, 3 * rows + i * (rows // 2)))
    return pieces


def pack_kernel(plane, cols, owner_ref, row_ref, source_ref, tiles_ref, *refs):
    out_refs, (codes_ref, *scratch) = refs[: plane - 1], refs[plane - 1 :]
    list_ref, slot_ref, owners_ref, along_ref, rows_ref, held_ref, small_sems, held_sem = scratch
    _, place, col, _ = position(plane)
    tiles, size = tiles_ref.shape[:2]
    slots = (out_refs[0].shape[0] - CODE_ROWS) // size
    spare = (plane - 1) * slots
    looks = [pltpu.make_async_copy(owner_ref, owners_ref, small_sems.at[0])]
    for i, ref in enumerate((owner_ref, row_ref, source_ref)):
        looks.append(pltpu.make_async_copy(ref, along_ref.at[i], small_sems.at[1 + i]))
    for look in looks:
        look.start()
    bulk = pltpu.make_async_copy(tiles_ref, held_ref, held_sem)
    bulk.start()
    for k in range(plane):
        slot_ref[k] = 0
    for i in range(spare):
        list_ref[i] = 0
    rows_ref[...] = jnp.zeros_like(rows_ref)
    for look in looks:
        look.wait()

    def step(t, carry):
        k = remainder(owners_ref[0, t], plane) ^ place
        slot = slot_ref[k]
        slot_ref[k] = slot + 1
        sent = (k > 0) & (remainder(slot, cols) == col)
        list_ref[jnp.where(sent, (k - 1) * slots + quotient(slot, cols), spare)] = t
        return carry

    lax.fori_loop(0, tiles, step, 0, unroll=4)
    owners = along_ref[0]
    rows_ref[0:1, :tiles] = remainder(owners, plane).astype(jnp.float32)
    rows_ref[1:2, :tiles] = along_ref[1].astype(jnp.float32)
    rows_ref[2:3, :tiles] = along_ref[2].astype(jnp.float32)
    rows_ref[3:4, :tiles] = quotient(owners, plane).astype(jnp.float32)
    codes = rows_ref[...].astype(codes_ref.dtype)
    codes_ref[...] = codes
    bulk.wait()
    for k, out_ref in enumerate(out_refs):
        for slot in range(slots):
            out_ref[slot * size : (slot + 1) * size] = held_ref[list_ref[k * slots + slot]]
        out_ref[slots * size :] = codes


def pack_tiles(owners, tile_row, source_block, tile_values, plane, cols, slots):
    tiles, size, wide = tile_values.shape
    shape = jax.ShapeDtypeStruct((slots * size + CODE_ROWS, wide), tile_values.dtype)
    codes = jax.ShapeDtypeStruct((CODE_ROWS, wide), tile_values.dtype)
    along = [x.reshape(1, tiles) for x in (owners, tile_row, source_block)]
    return pl.pallas_call(
        functools.partial(pack_kernel, plane, cols),
        out_shape=(shape,) * (plane - 1) + (codes,),
        in_specs=[HBM] * 4,
        out_specs=(VMEM,) * plane,
        scratch_shapes=[
            pltpu.SMEM(((plane - 1) * slots + 1,), jnp.int32),
            pltpu.SMEM((plane,), jnp.int32),
            pltpu.SMEM((1, tiles), jnp.int32),
            pltpu.VMEM((3, 1, tiles), jnp.int32),
            pltpu.VMEM((CODE_ROWS, wide), jnp.float32),
            pltpu.VMEM((tiles, size, wide), tile_values.dtype),
            pltpu.SemaphoreType.DMA((4,)),
            pltpu.SemaphoreType.DMA,
        ],
        compiler_params=pltpu.CompilerParams(vmem_limit_bytes=PACK_BYTES),
        name="pack_tiles",
    )(*along, tile_values)


DST_BIT, SRC_BIT, PLACE_BIT = 10, 16, 24


def own_kernel(tiles_ref, codes_ref, out_ref, own_ref, sems):
    rows = tiles_ref.shape[0]
    moves = ((tiles_ref, out_ref.at[pl.ds(0, rows)]), (codes_ref, own_ref))
    copies = [pltpu.make_async_copy(*move, sems.at[i]) for i, move in enumerate(moves)]
    for copy in copies:
        copy.start()
    out_ref[out_ref.shape[0] - out_ref.shape[1] :] = jnp.zeros(
        (out_ref.shape[1], out_ref.shape[1]), out_ref.dtype
    )
    for copy in copies:
        copy.wait()


def own_tiles(tiles, codes, spots):
    wide = tiles.shape[1]
    laid = jax.ShapeDtypeStruct((spots * wide, wide), tiles.dtype)
    return pl.pallas_call(
        own_kernel,
        out_shape=(laid, jax.ShapeDtypeStruct(codes.shape, codes.dtype)),
        in_specs=[ANY, ANY],
        out_specs=(VMEM, VMEM),
        scratch_shapes=[pltpu.SemaphoreType.DMA((2,))],
        compiler_params=params(laid),
        name="own_tiles",
    )(tiles, codes)


def collect_kernel(plane, cols, slots, blocks, tiles, own_ref, laid_ref, *refs):
    tile_refs, refs = refs[: (plane - 1) * cols], refs[(plane - 1) * cols :]
    out_ref, plan_ref, count_ref, *scratch = refs
    rows_ref, words_ref, codes_ref, row_sems, word_sem, tile_sems = scratch
    _, place, col, _ = position(plane)
    size = out_ref.shape[1]
    looks = []
    for k in range(plane):
        ref = own_ref
        if k > 0:
            ref = tile_refs[(k - 1) * cols].at[pl.ds(slots * size, CODE_ROWS)]
        copy = pltpu.make_async_copy(ref, rows_ref.at[k], row_sems.at[k])
        copy.start()
        looks.append(copy)
    copies, first, rows = [], tiles * size, slots * size
    for i, ref in enumerate(tile_refs):
        copy = pltpu.make_async_copy(
            ref.at[pl.ds(0, rows)], out_ref.at[pl.ds(first, rows)], tile_sems.at[i]
        )
        copy.start()
        copies.append(copy)
        first += rows
    words_ref[...] = jnp.zeros_like(words_ref)
    for k, copy in enumerate(looks):
        copy.wait()
        rows = rows_ref[k].astype(jnp.float32).astype(jnp.int32)
        source = rows[3:4] * blocks + rows[2:3]
        word = (rows[0:1] << PLACE_BIT) + (source << SRC_BIT)
        words_ref[k : k + 1] = word + ((rows[1:2] + k * blocks) << DST_BIT)
    copy = pltpu.make_async_copy(words_ref, codes_ref, word_sem)
    copy.start()
    copy.wait()
    found = jnp.int32(0)
    for k in range(plane):

        def step(t, carry, k=k):
            at, slot = carry
            code = codes_ref[k, t]
            if k == 0:
                spot = t
            else:
                column = remainder(slot + (cols - col), cols)
                spot = tiles + ((k - 1) * cols + column) * slots + quotient(slot, cols)
            plan_ref[at] = (code & ((1 << PLACE_BIT) - 1)) + spot
            one = ((code >> PLACE_BIT) == place).astype(jnp.int32)
            return at + one, slot + one

        found, _ = lax.fori_loop(0, tiles, step, (found, jnp.int32(0)), unroll=8)
    for i in range(UNROLL):
        plan_ref[found + i] = first // size
    count_ref[0] = quotient(found + UNROLL - 1, UNROLL)
    for copy in copies:
        copy.wait()


def collect_tiles(codes, laid, tile_parts, plane, cols, slots, blocks, tiles):
    wide = laid.shape[1]
    entries = plane * tiles + UNROLL
    high = -(-plane // 8) * 8
    return pl.pallas_call(
        functools.partial(collect_kernel, plane, cols, slots, blocks, tiles),
        out_shape=(
            jax.ShapeDtypeStruct(laid.shape, laid.dtype),
            jax.ShapeDtypeStruct((entries,), jnp.int32),
            jax.ShapeDtypeStruct((1,), jnp.int32),
        ),
        in_specs=[ANY, VMEM] + [ANY] * len(tile_parts),
        out_specs=(VMEM, SMEM, SMEM),
        scratch_shapes=[
            pltpu.VMEM((plane, CODE_ROWS, wide), jnp.bfloat16),
            pltpu.VMEM((high, wide), jnp.int32),
            pltpu.SMEM((high, wide), jnp.int32),
            pltpu.SemaphoreType.DMA((plane,)),
            pltpu.SemaphoreType.DMA,
            pltpu.SemaphoreType.DMA((len(tile_parts),)),
        ],
        input_output_aliases={1: 0},
        compiler_params=params(laid),
        name="collect_tiles",
    )(codes, laid, *tile_parts)


def planned(plan_ref, t):
    entry = plan_ref[t]
    spot = entry & ((1 << DST_BIT) - 1)
    return spot, (entry >> DST_BIT) & ((1 << (SRC_BIT - DST_BIT)) - 1), entry >> SRC_BIT


def block_rows(index, size):
    return pl.ds(pl.multiple_of(index * size, size), size)


def forward_kernel(line, lanes, plane, plan_ref, count_ref, tiles_ref, *refs):
    part_refs, refs = refs[: 2 * line - 1], refs[2 * line - 1 :]
    out_refs, (nodes_ref, acc_ref, part_sems) = refs[:-3], refs[-3:]
    rows, width = part_refs[0].shape[0], nodes_ref.shape[1]
    size = tiles_ref.shape[1]
    mine, _, _, way = position(plane)

    def each_part(act):
        for i, ref in enumerate(part_refs):
            source = mine + way * (i - (line - 1))

            @pl.when((source >= 0) & (source < line))
            def _():
                here = ref.at[:, lanes] if ref.shape != (rows, width) else ref
                act(
                    pltpu.make_async_copy(
                        here, nodes_ref.at[block_rows(source, rows)], part_sems.at[i]
                    )
                )

    each_part(lambda copy: copy.start())
    acc_ref[...] = jnp.zeros_like(acc_ref)
    each_part(lambda copy: copy.wait())

    def step(i, carry):
        for j in range(UNROLL):
            spot, dst, src = planned(plan_ref, i * UNROLL + j)
            acc_ref[block_rows(dst, size)] += jnp.dot(
                tiles_ref[block_rows(spot, size)],
                nodes_ref[block_rows(src, size)],
                preferred_element_type=jnp.float32,
            )
        return carry

    lax.fori_loop(0, count_ref[0], step, 0)
    for k, ref in enumerate(out_refs):
        ref[...] = acc_ref[k * rows : (k + 1) * rows].astype(ref.dtype)


def forward_tiles(plan, count, tiles, node_parts, plane, lanes):
    line = (len(node_parts) + 1) // 2
    rows, width = node_parts[0].shape[0], lanes.size
    kinds = [jnp.float32] + [jnp.bfloat16] * (plane - 1)
    outs = tuple(jax.ShapeDtypeStruct((rows, width), kind) for kind in kinds)
    scratch = [
        pltpu.VMEM((line * rows, width), jnp.bfloat16),
        pltpu.VMEM((plane * rows, width), jnp.float32),
    ]
    return pl.pallas_call(
        functools.partial(forward_kernel, line, lanes, plane),
        out_shape=outs,
        in_specs=[SMEM] * 2 + [VMEM] + [ANY] * len(node_parts),
        out_specs=(VMEM,) * plane,
        scratch_shapes=scratch + [pltpu.SemaphoreType.DMA((len(node_parts),))],
        compiler_params=params(tiles, *outs, *scratch),
        name="forward_tiles",
    )(plan, count, tiles, *node_parts)


def dense_kernel(chunk, halves, labels_ref, weight_ref, *refs):
    parts, (act_ref, out_grad_ref, agg_grad_ref) = refs[:-3], refs[-3:]
    rows, part_width = parts[0].shape
    width = part_width * halves
    features = weight_ref.shape[0]
    size = labels_ref.shape[1]

    def rows_step(i, carry):
        here = block_rows(i, chunk)
        agg = jnp.concatenate([part[here, :] for part in parts], axis=1)
        hidden = jnp.dot(agg, weight_ref[...], preferred_element_type=jnp.float32)
        sigmoid = jax.nn.sigmoid(hidden)
        activated = hidden * sigmoid
        act_ref[here, :] = activated[:, :width].astype(act_ref.dtype)
        slopes = sigmoid * (1.0 + hidden * (1.0 - sigmoid))
        named = []
        for b in range(chunk // size):
            across = labels_ref[pl.ds(i * (chunk // size) + b, 1), :]
            named.append(jnp.broadcast_to(across, (size, size)).T)
        named = jnp.concatenate(named, axis=0)
        ids = lax.broadcasted_iota(jnp.int32, (chunk, size), 1).astype(jnp.float32)
        target = jnp.concatenate(
            [(named == ids + f * size).astype(jnp.float32) for f in range(features // size)],
            axis=1,
        )
        out_grad = ((activated - target) * slopes).astype(jnp.bfloat16)
        out_grad_ref[here, :] = out_grad
        agg_grad_ref[here, :] = lax.dot_general(
            out_grad,
            weight_ref[:part_width, :],
            (((1,), (1,)), ((), ())),
            preferred_element_type=jnp.float32,
        ).astype(agg_grad_ref.dtype)
        return carry

    lax.fori_loop(0, rows // chunk, rows_step, 0)


def dense(labels, weight, parts, halves):
    rows, part_width = parts[0].shape
    chunk = math.gcd(rows, 256)
    outs = tuple(
        jax.ShapeDtypeStruct((rows, width), jnp.bfloat16)
        for width in (part_width * halves, weight.shape[0], part_width)
    )
    return pl.pallas_call(
        functools.partial(dense_kernel, chunk, halves),
        out_shape=outs,
        in_specs=[VMEM] * (2 + len(parts)),
        out_specs=(VMEM,) * 3,
        compiler_params=params(labels, weight, *parts, *outs),
        name="dense",
    )(labels, weight, *parts)


def grads_kernel(scale, halves, weight_ref, out_grad_ref, *refs):
    parts, (terms_ref, *agg_grad_refs) = refs[: -halves], refs[-halves:]
    part_width = parts[0].shape[1]
    for h, ref in enumerate(agg_grad_refs, 1):
        ref[...] = lax.dot_general(
            out_grad_ref[...],
            weight_ref[h * part_width : (h + 1) * part_width, :],
            (((1,), (1,)), ((), ())),
            preferred_element_type=jnp.float32,
        ).astype(ref.dtype)
    for i, part in enumerate(parts):
        terms = lax.dot_general(
            part[...],
            out_grad_ref[:, : part_width * halves],
            (((0,), (0,)), ((), ())),
            preferred_element_type=jnp.float32,
        )
        terms_ref[i * part_width : (i + 1) * part_width] = (terms * scale).astype(terms_ref.dtype)


def grads(weight, out_grad, parts, halves, node_total):
    rows, part_width = parts[0].shape
    outs = (jax.ShapeDtypeStruct((weight.shape[0], part_width * halves), jnp.bfloat16),) + (
        jax.ShapeDtypeStruct((rows, part_width), jnp.bfloat16),
    ) * (halves - 1)
    return pl.pallas_call(
        functools.partial(grads_kernel, 1.0 / math.sqrt(node_total), halves),
        out_shape=outs,
        in_specs=[VMEM] * (2 + len(parts)),
        out_specs=(VMEM,) * halves,
        compiler_params=params(weight, out_grad, *parts, *outs),
        name="grads",
    )(weight, out_grad, *parts)


def spread_kernel(line, plane, places, plan_ref, count_ref, tiles_ref, *refs):
    grad_refs, refs = refs[: len(places)], refs[len(places) :]
    out_refs, (grads_ref, acc_ref, grad_sems) = refs[:-3], refs[-3:]
    rows = grad_refs[0].shape[0]
    size = tiles_ref.shape[1]
    mine, _, _, way = position(plane)
    copies = []
    for k, (ref, at) in enumerate(zip(grad_refs, places)):
        here = grads_ref.at[pl.ds(at, ref.shape[0])]
        copy = pltpu.make_async_copy(ref, here, grad_sems.at[k])
        copy.start()
        copies.append(copy)
    acc_ref[...] = jnp.zeros_like(acc_ref)
    for copy in copies:
        copy.wait()

    def step(i, carry):
        for j in range(UNROLL):
            spot, dst, src = planned(plan_ref, i * UNROLL + j)
            acc_ref[block_rows(src, size)] += lax.dot_general(
                tiles_ref[block_rows(spot, size)],
                grads_ref[block_rows(dst, size)],
                (((0,), (0,)), ((), ())),
                preferred_element_type=jnp.float32,
            )
        return carry

    lax.fori_loop(0, count_ref[0], step, 0)
    for i, ref in enumerate(out_refs):
        target = mine + way * (i - (line - 1))

        @pl.when((target >= 0) & (target < line))
        def _():
            ref[...] = acc_ref[block_rows(target, rows)].astype(ref.dtype)


def spread_tiles(plan, count, tiles, pieces, line, plane):
    grad_parts, places = zip(*pieces)
    rows, width = grad_parts[0].shape
    kinds = [jnp.float32 if i == line - 1 else jnp.bfloat16 for i in range(2 * line - 1)]
    outs = tuple(jax.ShapeDtypeStruct((rows, width), kind) for kind in kinds)
    scratch = [
        pltpu.VMEM((plane * rows, width), jnp.bfloat16),
        pltpu.VMEM((line * rows, width), jnp.float32),
    ]
    return pl.pallas_call(
        functools.partial(spread_kernel, line, plane, places),
        out_shape=outs,
        in_specs=[SMEM] * 2 + [VMEM] + [ANY] * len(places),
        out_specs=(VMEM,) * (2 * line - 1),
        scratch_shapes=scratch + [pltpu.SemaphoreType.DMA((len(places),))],
        compiler_params=params(tiles, *outs, *scratch),
        name="spread_tiles",
    )(plan, count, tiles, *grad_parts)


def along_line(x, line, plane, cols, step, reach):
    pairs = []
    for z in range(line):
        for q in range(plane):
            for c in range(cols):
                way = 1 - 2 * (c & 1)
                to, end = z + way * step, z + way * reach
                if 0 <= to < line and 0 <= end < line:
                    pairs.append(((z * plane + q) * cols + c, (to * plane + q) * cols + c))
    return lax.ppermute(x, ("rows", "cols"), pairs)


def line_gather(x, after, line, plane, cols, lanes):
    move = lambda part, step, reach: along_line(part, line, plane, cols, step, reach)
    later, _ = lax.optimization_barrier((x, after))
    up, down = [x], [later]
    for k in range(1, line - 1):
        up.append(move(up[-1], 1, 1 - k))
        down.append(move(down[-1], -1, k - 1))
    parts, high, low = [], up[-1], down[-1]
    for part in lanes:
        first = move(high[:, part], 1, 2 - line)
        last = move(low[:, part], -1, line - 2)
        parts.append([first] + up[:0:-1] + down + [last])
    return parts


def line_sum(terms, line, plane, cols, beside):
    moved, late = {1: None, -1: None}, None
    for k in range(line - 1, 0, -1):
        for step in moved:
            term = terms[line - 1 + step * k]
            if moved[step] is not None:
                total = term.astype(jnp.float32) + moved[step].astype(jnp.float32)
                term = total.astype(term.dtype)
            moved[step] = along_line(term, line, plane, cols, step, step * k)
        if k == line - 1 and beside is not None:
            moved, beside = lax.optimization_barrier((moved, beside))
        if k > 1:
            late = tuple(moved.values())
    return [terms[line - 1], moved[1], moved[-1]], beside, late


def finish_kernel(halves, *refs):
    out_ref, refs = refs[-1], refs[:-1]
    each = len(refs) // halves
    width = refs[0].shape[1]
    for h in range(halves):
        total = refs[h * each][...]
        for ref in refs[h * each + 1 : (h + 1) * each]:
            total += ref[...].astype(jnp.float32)
        out_ref[:, h * width : (h + 1) * width] = total.astype(out_ref.dtype)


def finish(pieces):
    flat = [piece for half in pieces for piece in half]
    rows, width = flat[0].shape
    out = jax.ShapeDtypeStruct((rows, width * len(pieces)), jnp.bfloat16)
    return pl.pallas_call(
        functools.partial(finish_kernel, len(pieces)),
        out_shape=out,
        in_specs=[VMEM] * len(flat),
        out_specs=VMEM,
        compiler_params=params(out, *flat),
        name="finish",
    )(*flat)


def sum_apart(terms, first, end, rows):
    while first < end:
        other = shuffle(terms, [(r, r ^ first) for r in range(rows)])
        total = terms.astype(jnp.float32) + other.astype(jnp.float32)
        terms = total.astype(terms.dtype)
        first *= 2
    return terms


def prepare_kernel(cols, labels_ref, weight_ref, own_labels_ref, own_first_ref, wide_ref):
    col = lax.axis_index("cols")
    features = weight_ref.shape[0]
    width = features // cols
    labels = labels_ref[...] - col * width
    own_labels_ref[...] = jnp.where(labels < 0, labels + features, labels).astype(jnp.float32)
    for c in range(cols):
        row = remainder(col + c, cols) * width
        rows = weight_ref[pl.ds(pl.multiple_of(row, width), width), :]
        wide_ref[c * width : (c + 1) * width] = rows.astype(jnp.float32)
    turned = pltpu.roll(wide_ref[...], remainder(cols - col, cols) * width, axis=1)
    own_first_ref[...] = turned.astype(own_first_ref.dtype)


def prepare(labels, weight, cols):
    outs = (jax.ShapeDtypeStruct(labels.shape, jnp.float32), weight)
    wide = pltpu.VMEM(weight.shape, jnp.float32)
    return pl.pallas_call(
        functools.partial(prepare_kernel, cols),
        out_shape=(outs[0], jax.ShapeDtypeStruct(weight.shape, weight.dtype)),
        in_specs=[VMEM, VMEM],
        out_specs=(VMEM, VMEM),
        scratch_shapes=[wide],
        compiler_params=params(weight, weight, wide, wide),
        name="prepare",
    )(labels, weight)


def weight_kernel(cols, mine_ref, other_ref, out_ref):
    col = lax.axis_index("cols")
    width = out_ref.shape[1]
    for c in range(cols):
        here = pl.ds(c * width, width)
        total = mine_ref[here].astype(jnp.float32) + other_ref[here].astype(jnp.float32)
        row = remainder(col + c, cols) * width
        out_ref[pl.ds(pl.multiple_of(row, width), width)] = total


def finish_weight(mine, other, cols):
    out = jax.ShapeDtypeStruct(mine.shape, jnp.float32)
    return pl.pallas_call(
        functools.partial(weight_kernel, cols),
        out_shape=out,
        in_specs=[VMEM, VMEM],
        out_specs=VMEM,
        compiler_params=params(mine, other, out),
        name="finish_weight",
    )(mine, other)


def per_device(node_features, weight, tile_values, tile_row, source_owner, source_block, labels):
    local_rows, width = node_features.shape
    n_tiles, block_size = tile_values.shape[:2]
    blocks = local_rows // block_size
    rows, cols = lax.axis_size("rows"), lax.axis_size("cols")
    plane = math.gcd(rows, LARGEST_PLANE)
    line = rows // plane
    halves = 2 if width % 256 == 0 else 1
    part_width = width // halves
    slots = -(-min(n_tiles, line * (2 * n_tiles // rows)) // cols)
    owners = source_owner[:, 0]

    def other_cols(x):
        return [
            lax.ppermute(x, "cols", [((c + k) % cols, c) for c in range(cols)])
            for k in range(1, cols)
        ]

    lanes = [slice(h * part_width, (h + 1) * part_width) for h in range(halves)]
    *packed, codes = pack_tiles(
        owners, tile_row, source_block, tile_values, plane, cols, slots
    )
    node_parts = line_gather(node_features, packed, line, plane, cols, lanes)
    spots = n_tiles + (plane - 1) * cols * slots + 1
    flat = tile_values.reshape(n_tiles * block_size, block_size)
    early = own_tiles(flat, codes, spots) + prepare(labels.reshape(blocks, block_size), weight, cols)
    tile_parts = []
    for k in range(1, plane):
        arrived = across_plane(packed[k - 1], k, line, plane)
        if k == 1:
            arrived, early = lax.optimization_barrier((arrived, early))
        tile_parts += [arrived] + other_cols(arrived)
    laid, codes, own_labels, own_first = early
    tiles, plan, count = collect_tiles(
        codes, laid, tile_parts, plane, cols, slots, blocks, n_tiles
    )

    aggregated = []
    for h in range(halves):
        here = pl.ds(h * part_width, part_width)
        sums = forward_tiles(plan, count, tiles, node_parts[h], plane, here)
        total = sums[0]
        for k in range(1, plane):
            total = total + across_plane(sums[k], k, line, plane).astype(jnp.float32)
        mine = total.astype(jnp.bfloat16)
        aggregated.append([mine] + other_cols(mine))
    parts = [aggregated[h][c] for c in range(cols) for h in range(halves)]

    activations, out_grad, agg_grad = dense(own_labels, own_first, parts, halves)
    weight_terms, *agg_grads = grads(own_first, out_grad, parts, halves, local_rows * rows)

    pieces = []
    for i, agg_grad in enumerate([agg_grad] + agg_grads):
        arrived, places = zip(*plane_gather(agg_grad, line, plane))
        if i == 0:
            weight_terms = sum_apart(weight_terms, plane, 2 * plane, rows)
            arrived, weight_terms = lax.optimization_barrier((arrived, weight_terms))
            weight_terms = sum_apart(weight_terms, 2 * plane, rows, rows)
        terms = spread_tiles(plan, count, tiles, list(zip(arrived, places)), line, plane)
        beside = weight_terms if i == 0 else None
        half, beside, late = line_sum(terms, line, plane, cols, beside)
        if i == 0:
            weight_terms, _ = lax.optimization_barrier((beside, late))
        pieces.append(half)
    weight_terms = sum_apart(weight_terms, 1, plane // 2, rows)
    weight_terms, _ = lax.optimization_barrier((weight_terms, late))
    other = across_plane(weight_terms, plane // 2, line, plane)
    weight_grad = finish_weight(weight_terms, other, cols)
    return activations, weight_grad, finish(pieces)


def solution(mesh):
    return jax.shard_map(
        per_device,
        mesh=mesh,
        in_specs=(
            P("rows", "cols"),
            P(),
            P("rows", None, None),
            P("rows"),
            P("rows", None),
            P("rows"),
            P("rows"),
        ),
        out_specs=(P("rows", "cols"), P(None, "cols"), P("rows", "cols")),
        check_vma=False,
    )
```

```python
import functools
import math

import jax
import jax.numpy as jnp
from jax import lax
from jax.experimental import pallas as pl
from jax.experimental.pallas import tpu as pltpu
from jax.sharding import PartitionSpec as P

VMEM = pl.BlockSpec(memory_space=pltpu.VMEM)
SMEM = pl.BlockSpec(memory_space=pltpu.SMEM)
ANY = pl.BlockSpec(memory_space=pl.ANY)
HBM = pl.BlockSpec(memory_space=pltpu.HBM)
SPARE_BYTES = 2 * 1024 * 1024
PACK_BYTES = 56 * 1024 * 1024
UNROLL = 8
LARGEST_PLANE = 4


def params(*shapes):
    room = SPARE_BYTES
    for shape in shapes:
        *lead, high, wide = shape.shape
        room += math.prod(lead) * high * (-(-wide // 128) * 128) * jnp.dtype(shape.dtype).itemsize
    return pltpu.CompilerParams(vmem_limit_bytes=room)


def quotient(x, n):
    return x >> (n.bit_length() - 1) if n & (n - 1) == 0 else lax.div(x, n)


def remainder(x, n):
    return x & (n - 1) if n & (n - 1) == 0 else lax.rem(x, n)


def position(plane):
    index, col = lax.axis_index("rows"), lax.axis_index("cols")
    return quotient(index, plane), remainder(index, plane), col, 1 - 2 * (col & 1)


def shuffle(x, pairs):
    return lax.ppermute(x, "rows", pairs)


def across_plane(x, k, line, plane):
    return shuffle(x, [(r, r ^ k) for r in range(line * plane)])


CODE_ROWS = 16


def plane_gather(x, line, plane, after):
    if plane != 4:
        parts = [x] + [across_plane(x, k, line, plane) for k in range(1, plane)]
        return parts, [k * x.shape[0] for k in range(plane)]
    rows = x.shape[0]
    near = [across_plane(x, k, line, plane) for k in (1, 2)]
    handed = (near[0][: rows // 2], near[1][rows // 2 :])
    handed, _ = lax.optimization_barrier((handed, after))
    far = [across_plane(part, 2 - i, line, plane) for i, part in enumerate(handed)]
    return [x] + near + far, [0, rows, 2 * rows, 3 * rows, 3 * rows + rows // 2]


def pack_kernel(plane, cols, owner_ref, row_ref, source_ref, tiles_ref, *refs):
    out_refs, (codes_ref, *scratch) = refs[: plane - 1], refs[plane - 1 :]
    list_ref, slot_ref, owners_ref, along_ref, rows_ref, held_ref, small_sems, held_sem = scratch
    _, place, col, _ = position(plane)
    tiles, size = tiles_ref.shape[:2]
    slots = (out_refs[0].shape[0] - CODE_ROWS) // size
    spare = (plane - 1) * slots
    looks = [pltpu.make_async_copy(owner_ref, owners_ref, small_sems.at[0])]
    for i, ref in enumerate((owner_ref, row_ref, source_ref)):
        looks.append(pltpu.make_async_copy(ref, along_ref.at[i], small_sems.at[1 + i]))
    for look in looks:
        look.start()
    bulk = pltpu.make_async_copy(tiles_ref, held_ref, held_sem)
    bulk.start()
    for k in range(plane):
        slot_ref[k] = 0
    for i in range(spare):
        list_ref[i] = 0
    rows_ref[...] = jnp.zeros_like(rows_ref)
    for look in looks:
        look.wait()

    def step(t, carry):
        k = remainder(owners_ref[0, t], plane) ^ place
        slot = slot_ref[k]
        slot_ref[k] = slot + 1
        sent = (k > 0) & (remainder(slot, cols) == col)
        list_ref[jnp.where(sent, (k - 1) * slots + quotient(slot, cols), spare)] = t
        return carry

    lax.fori_loop(0, tiles, step, 0, unroll=4)
    owners = along_ref[0]
    rows_ref[0:1, :tiles] = remainder(owners, plane).astype(jnp.float32)
    rows_ref[1:2, :tiles] = along_ref[1].astype(jnp.float32)
    rows_ref[2:3, :tiles] = along_ref[2].astype(jnp.float32)
    rows_ref[3:4, :tiles] = quotient(owners, plane).astype(jnp.float32)
    codes = rows_ref[...].astype(codes_ref.dtype)
    codes_ref[...] = codes
    bulk.wait()
    for k, out_ref in enumerate(out_refs):
        for slot in range(slots):
            out_ref[slot * size : (slot + 1) * size] = held_ref[list_ref[k * slots + slot]]
        out_ref[slots * size :] = codes


def pack_tiles(owners, tile_row, source_block, tile_values, plane, cols, slots):
    tiles, size, wide = tile_values.shape
    shape = jax.ShapeDtypeStruct((slots * size + CODE_ROWS, wide), tile_values.dtype)
    codes = jax.ShapeDtypeStruct((CODE_ROWS, wide), tile_values.dtype)
    along = [x.reshape(1, tiles) for x in (owners, tile_row, source_block)]
    return pl.pallas_call(
        functools.partial(pack_kernel, plane, cols),
        out_shape=(shape,) * (plane - 1) + (codes,),
        in_specs=[HBM] * 4,
        out_specs=(VMEM,) * plane,
        scratch_shapes=[
            pltpu.SMEM(((plane - 1) * slots + 1,), jnp.int32),
            pltpu.SMEM((plane,), jnp.int32),
            pltpu.SMEM((1, tiles), jnp.int32),
            pltpu.VMEM((3, 1, tiles), jnp.int32),
            pltpu.VMEM((CODE_ROWS, wide), jnp.float32),
            pltpu.VMEM((tiles, size, wide), tile_values.dtype),
            pltpu.SemaphoreType.DMA((4,)),
            pltpu.SemaphoreType.DMA,
        ],
        compiler_params=pltpu.CompilerParams(vmem_limit_bytes=PACK_BYTES),
        name="pack_tiles",
    )(*along, tile_values)


DST_BIT, SRC_BIT, PLACE_BIT = 10, 16, 24


def own_kernel(tiles_ref, codes_ref, out_ref, own_ref, sems):
    rows = tiles_ref.shape[0]
    moves = ((tiles_ref, out_ref.at[pl.ds(0, rows)]), (codes_ref, own_ref))
    copies = [pltpu.make_async_copy(*move, sems.at[i]) for i, move in enumerate(moves)]
    for copy in copies:
        copy.start()
    out_ref[out_ref.shape[0] - out_ref.shape[1] :] = jnp.zeros(
        (out_ref.shape[1], out_ref.shape[1]), out_ref.dtype
    )
    for copy in copies:
        copy.wait()


def own_tiles(tiles, codes, spots):
    wide = tiles.shape[1]
    laid = jax.ShapeDtypeStruct((spots * wide, wide), tiles.dtype)
    return pl.pallas_call(
        own_kernel,
        out_shape=(laid, jax.ShapeDtypeStruct(codes.shape, codes.dtype)),
        in_specs=[ANY, ANY],
        out_specs=(VMEM, VMEM),
        scratch_shapes=[pltpu.SemaphoreType.DMA((2,))],
        compiler_params=params(laid),
        name="own_tiles",
    )(tiles, codes)


def collect_kernel(plane, cols, slots, blocks, tiles, own_ref, laid_ref, *refs):
    tile_refs, refs = refs[: (plane - 1) * cols], refs[(plane - 1) * cols :]
    out_ref, plan_ref, count_ref, *scratch = refs
    rows_ref, words_ref, codes_ref, row_sems, word_sem, tile_sems = scratch
    _, place, col, _ = position(plane)
    size = out_ref.shape[1]
    looks = []
    for k in range(plane):
        ref = own_ref
        if k > 0:
            ref = tile_refs[(k - 1) * cols].at[pl.ds(slots * size, CODE_ROWS)]
        copy = pltpu.make_async_copy(ref, rows_ref.at[k], row_sems.at[k])
        copy.start()
        looks.append(copy)
    copies, first, rows = [], tiles * size, slots * size
    for i, ref in enumerate(tile_refs):
        copy = pltpu.make_async_copy(
            ref.at[pl.ds(0, rows)], out_ref.at[pl.ds(first, rows)], tile_sems.at[i]
        )
        copy.start()
        copies.append(copy)
        first += rows
    words_ref[...] = jnp.zeros_like(words_ref)
    for k, copy in enumerate(looks):
        copy.wait()
        rows = rows_ref[k].astype(jnp.float32).astype(jnp.int32)
        source = rows[3:4] * blocks + rows[2:3]
        word = (rows[0:1] << PLACE_BIT) + (source << SRC_BIT)
        words_ref[k : k + 1] = word + ((rows[1:2] + k * blocks) << DST_BIT)
    copy = pltpu.make_async_copy(words_ref, codes_ref, word_sem)
    copy.start()
    copy.wait()
    found = jnp.int32(0)
    for k in range(plane):

        def step(t, carry, k=k):
            at, slot = carry
            code = codes_ref[k, t]
            if k == 0:
                spot = t
            else:
                column = remainder(slot + (cols - col), cols)
                spot = tiles + ((k - 1) * cols + column) * slots + quotient(slot, cols)
            plan_ref[at] = (code & ((1 << PLACE_BIT) - 1)) + spot
            one = ((code >> PLACE_BIT) == place).astype(jnp.int32)
            return at + one, slot + one

        found, _ = lax.fori_loop(0, tiles, step, (found, jnp.int32(0)), unroll=8)
    for i in range(UNROLL):
        plan_ref[found + i] = first // size
    count_ref[0] = quotient(found + UNROLL - 1, UNROLL)
    for copy in copies:
        copy.wait()


def collect_tiles(codes, laid, tile_parts, plane, cols, slots, blocks, tiles):
    wide = laid.shape[1]
    entries = plane * tiles + UNROLL
    high = -(-plane // 8) * 8
    return pl.pallas_call(
        functools.partial(collect_kernel, plane, cols, slots, blocks, tiles),
        out_shape=(
            jax.ShapeDtypeStruct(laid.shape, laid.dtype),
            jax.ShapeDtypeStruct((entries,), jnp.int32),
            jax.ShapeDtypeStruct((1,), jnp.int32),
        ),
        in_specs=[ANY, VMEM] + [ANY] * len(tile_parts),
        out_specs=(VMEM, SMEM, SMEM),
        scratch_shapes=[
            pltpu.VMEM((plane, CODE_ROWS, wide), jnp.bfloat16),
            pltpu.VMEM((high, wide), jnp.int32),
            pltpu.SMEM((high, wide), jnp.int32),
            pltpu.SemaphoreType.DMA((plane,)),
            pltpu.SemaphoreType.DMA,
            pltpu.SemaphoreType.DMA((len(tile_parts),)),
        ],
        input_output_aliases={1: 0},
        compiler_params=params(laid),
        name="collect_tiles",
    )(codes, laid, *tile_parts)


def planned(plan_ref, t):
    entry = plan_ref[t]
    spot = entry & ((1 << DST_BIT) - 1)
    return spot, (entry >> DST_BIT) & ((1 << (SRC_BIT - DST_BIT)) - 1), entry >> SRC_BIT


def block_rows(index, size):
    return pl.ds(pl.multiple_of(index * size, size), size)


def forward_kernel(line, lanes, plane, plan_ref, count_ref, tiles_ref, *refs):
    part_refs, refs = refs[: 2 * line - 1], refs[2 * line - 1 :]
    out_refs, (nodes_ref, acc_ref, more_ref, part_sems) = refs[:-4], refs[-4:]
    rows, width = part_refs[0].shape[0], nodes_ref.shape[1]
    size = tiles_ref.shape[1]
    mine, _, _, way = position(plane)

    def each_part(act):
        for i, ref in enumerate(part_refs):
            source = mine + way * (i - (line - 1))

            @pl.when((source >= 0) & (source < line))
            def _():
                here = ref.at[:, lanes] if ref.shape != (rows, width) else ref
                act(
                    pltpu.make_async_copy(
                        here, nodes_ref.at[block_rows(source, rows)], part_sems.at[i]
                    )
                )

    each_part(lambda copy: copy.start())
    acc_ref[...] = jnp.zeros_like(acc_ref)
    more_ref[...] = jnp.zeros_like(more_ref)
    each_part(lambda copy: copy.wait())

    def step(i, carry):
        for j in range(UNROLL):
            spot, dst, src = planned(plan_ref, i * UNROLL + j)
            into_ref = more_ref if j % 2 else acc_ref
            into_ref[block_rows(dst, size)] += jnp.dot(
                tiles_ref[block_rows(spot, size)],
                nodes_ref[block_rows(src, size)],
                preferred_element_type=jnp.float32,
            )
        return carry

    lax.fori_loop(0, count_ref[0], step, 0)
    for k, ref in enumerate(out_refs):
        here = pl.ds(k * rows, rows)
        ref[...] = (acc_ref[here] + more_ref[here]).astype(ref.dtype)


def forward_tiles(plan, count, tiles, node_parts, plane, lanes):
    line = (len(node_parts) + 1) // 2
    rows, width = node_parts[0].shape[0], lanes.size
    kinds = [jnp.float32] + [jnp.bfloat16] * (plane - 1)
    outs = tuple(jax.ShapeDtypeStruct((rows, width), kind) for kind in kinds)
    scratch = [
        pltpu.VMEM((line * rows, width), jnp.bfloat16),
        pltpu.VMEM((plane * rows, width), jnp.float32),
        pltpu.VMEM((plane * rows, width), jnp.float32),
    ]
    return pl.pallas_call(
        functools.partial(forward_kernel, line, lanes, plane),
        out_shape=outs,
        in_specs=[SMEM] * 2 + [VMEM] + [ANY] * len(node_parts),
        out_specs=(VMEM,) * plane,
        scratch_shapes=scratch + [pltpu.SemaphoreType.DMA((len(node_parts),))],
        compiler_params=params(tiles, *outs, *scratch),
        name="forward_tiles",
    )(plan, count, tiles, *node_parts)


def dense_kernel(chunk, halves, labels_ref, weight_ref, *refs):
    parts, (act_ref, out_grad_ref, agg_grad_ref) = refs[:-3], refs[-3:]
    rows, part_width = parts[0].shape
    width = part_width * halves
    features = weight_ref.shape[0]
    size = labels_ref.shape[1]

    def rows_step(i, carry):
        here = block_rows(i, chunk)
        agg = jnp.concatenate([part[here, :] for part in parts], axis=1)
        hidden = jnp.dot(agg, weight_ref[...], preferred_element_type=jnp.float32)
        sigmoid = jax.nn.sigmoid(hidden)
        activated = hidden * sigmoid
        act_ref[here, :] = activated[:, :width].astype(act_ref.dtype)
        slopes = sigmoid * (1.0 + hidden * (1.0 - sigmoid))
        named = []
        for b in range(chunk // size):
            across = labels_ref[pl.ds(i * (chunk // size) + b, 1), :]
            named.append(jnp.broadcast_to(across, (size, size)).T)
        named = jnp.concatenate(named, axis=0)
        ids = lax.broadcasted_iota(jnp.int32, (chunk, size), 1).astype(jnp.float32)
        target = jnp.concatenate(
            [(named == ids + f * size).astype(jnp.float32) for f in range(features // size)],
            axis=1,
        )
        out_grad = ((activated - target) * slopes).astype(jnp.bfloat16)
        out_grad_ref[here, :] = out_grad
        agg_grad_ref[here, :] = lax.dot_general(
            out_grad,
            weight_ref[:part_width, :],
            (((1,), (1,)), ((), ())),
            preferred_element_type=jnp.float32,
        ).astype(agg_grad_ref.dtype)
        return carry

    lax.fori_loop(0, rows // chunk, rows_step, 0)


def dense(labels, weight, parts, halves):
    rows, part_width = parts[0].shape
    chunk = math.gcd(rows, 256)
    outs = tuple(
        jax.ShapeDtypeStruct((rows, width), jnp.bfloat16)
        for width in (part_width * halves, weight.shape[0], part_width)
    )
    return pl.pallas_call(
        functools.partial(dense_kernel, chunk, halves),
        out_shape=outs,
        in_specs=[VMEM] * (2 + len(parts)),
        out_specs=(VMEM,) * 3,
        compiler_params=params(labels, weight, *parts, *outs),
        name="dense",
    )(labels, weight, *parts)


def grads_kernel(scale, halves, weight_ref, out_grad_ref, *refs):
    parts, (terms_ref, *agg_grad_refs) = refs[: -halves], refs[-halves:]
    part_width = parts[0].shape[1]
    for h, ref in enumerate(agg_grad_refs, 1):
        ref[...] = lax.dot_general(
            out_grad_ref[...],
            weight_ref[h * part_width : (h + 1) * part_width, :],
            (((1,), (1,)), ((), ())),
            preferred_element_type=jnp.float32,
        ).astype(ref.dtype)
    for i, part in enumerate(parts):
        terms = lax.dot_general(
            part[...],
            out_grad_ref[:, : part_width * halves],
            (((0,), (0,)), ((), ())),
            preferred_element_type=jnp.float32,
        )
        terms_ref[i * part_width : (i + 1) * part_width] = (terms * scale).astype(terms_ref.dtype)


def grads(weight, out_grad, parts, halves, node_total):
    rows, part_width = parts[0].shape
    outs = (jax.ShapeDtypeStruct((weight.shape[0], part_width * halves), jnp.bfloat16),) + (
        jax.ShapeDtypeStruct((rows, part_width), jnp.bfloat16),
    ) * (halves - 1)
    return pl.pallas_call(
        functools.partial(grads_kernel, 1.0 / math.sqrt(node_total), halves),
        out_shape=outs,
        in_specs=[VMEM] * (2 + len(parts)),
        out_specs=(VMEM,) * halves,
        compiler_params=params(weight, out_grad, *parts, *outs),
        name="grads",
    )(weight, out_grad, *parts)


def spread_kernel(line, plane, places, plan_ref, count_ref, tiles_ref, *refs):
    grad_refs, refs = refs[: len(places)], refs[len(places) :]
    out_refs, (grads_ref, acc_ref, more_ref, grad_sems) = refs[:-4], refs[-4:]
    rows = grad_refs[0].shape[0]
    size = tiles_ref.shape[1]
    mine, _, _, way = position(plane)
    copies = []
    for k, (ref, at) in enumerate(zip(grad_refs, places)):
        here = grads_ref.at[pl.ds(at, ref.shape[0])]
        copy = pltpu.make_async_copy(ref, here, grad_sems.at[k])
        copy.start()
        copies.append(copy)
    acc_ref[...] = jnp.zeros_like(acc_ref)
    more_ref[...] = jnp.zeros_like(more_ref)
    for copy in copies:
        copy.wait()

    def step(i, carry):
        for j in range(UNROLL):
            spot, dst, src = planned(plan_ref, i * UNROLL + j)
            into_ref = more_ref if j % 2 else acc_ref
            into_ref[block_rows(src, size)] += lax.dot_general(
                tiles_ref[block_rows(spot, size)],
                grads_ref[block_rows(dst, size)],
                (((0,), (0,)), ((), ())),
                preferred_element_type=jnp.float32,
            )
        return carry

    lax.fori_loop(0, count_ref[0], step, 0)
    for i, ref in enumerate(out_refs):
        target = mine + way * (i - (line - 1))

        @pl.when((target >= 0) & (target < line))
        def _():
            here = block_rows(target, rows)
            ref[...] = (acc_ref[here] + more_ref[here]).astype(ref.dtype)


def spread_tiles(plan, count, tiles, pieces, line, plane):
    grad_parts, places = zip(*pieces)
    rows, width = grad_parts[0].shape
    kinds = [jnp.float32 if i == line - 1 else jnp.bfloat16 for i in range(2 * line - 1)]
    outs = tuple(jax.ShapeDtypeStruct((rows, width), kind) for kind in kinds)
    scratch = [
        pltpu.VMEM((plane * rows, width), jnp.bfloat16),
        pltpu.VMEM((line * rows, width), jnp.float32),
        pltpu.VMEM((line * rows, width), jnp.float32),
    ]
    return pl.pallas_call(
        functools.partial(spread_kernel, line, plane, places),
        out_shape=outs,
        in_specs=[SMEM] * 2 + [VMEM] + [ANY] * len(places),
        out_specs=(VMEM,) * (2 * line - 1),
        scratch_shapes=scratch + [pltpu.SemaphoreType.DMA((len(places),))],
        compiler_params=params(tiles, *outs, *scratch),
        name="spread_tiles",
    )(plan, count, tiles, *grad_parts)


def along_line(x, line, plane, cols, step, reach):
    pairs = []
    for z in range(line):
        for q in range(plane):
            for c in range(cols):
                way = 1 - 2 * (c & 1)
                to, end = z + way * step, z + way * reach
                if 0 <= to < line and 0 <= end < line:
                    pairs.append(((z * plane + q) * cols + c, (to * plane + q) * cols + c))
    return lax.ppermute(x, ("rows", "cols"), pairs)


def line_gather(x, after, line, plane, cols, lanes):
    move = lambda part, step, reach: along_line(part, line, plane, cols, step, reach)
    later, _ = lax.optimization_barrier((x, after))
    up, down = [x], [later]
    for k in range(1, line - 1):
        up.append(move(up[-1], 1, 1 - k))
        down.append(move(down[-1], -1, k - 1))
    parts, high, low = [], up[-1], down[-1]
    for part in lanes:
        first = move(high[:, part], 1, 2 - line)
        last = move(low[:, part], -1, line - 2)
        parts.append([first] + up[:0:-1] + down + [last])
    return parts


def line_sum(terms, line, plane, cols, beside):
    moved, late = {1: None, -1: None}, None
    for k in range(line - 1, 0, -1):
        for step in moved:
            term = terms[line - 1 + step * k]
            if moved[step] is not None:
                total = term.astype(jnp.float32) + moved[step].astype(jnp.float32)
                term = total.astype(term.dtype)
            moved[step] = along_line(term, line, plane, cols, step, step * k)
        if k == line - 1 and beside is not None:
            moved, beside = lax.optimization_barrier((moved, beside))
        if k > 1:
            late = tuple(moved.values())
    return [terms[line - 1], moved[1], moved[-1]], beside, late


def finish_kernel(halves, *refs):
    out_ref, refs = refs[-1], refs[:-1]
    each = len(refs) // halves
    width = refs[0].shape[1]
    for h in range(halves):
        total = refs[h * each][...]
        for ref in refs[h * each + 1 : (h + 1) * each]:
            total += ref[...].astype(jnp.float32)
        out_ref[:, h * width : (h + 1) * width] = total.astype(out_ref.dtype)


def finish(pieces):
    flat = [piece for half in pieces for piece in half]
    rows, width = flat[0].shape
    out = jax.ShapeDtypeStruct((rows, width * len(pieces)), jnp.bfloat16)
    return pl.pallas_call(
        functools.partial(finish_kernel, len(pieces)),
        out_shape=out,
        in_specs=[VMEM] * len(flat),
        out_specs=VMEM,
        compiler_params=params(out, *flat),
        name="finish",
    )(*flat)


def sum_apart(terms, far, near, rows, most=None):
    steps = []
    while far >= near:
        steps.append(far)
        far //= 2
    for apart in steps[:most]:
        other = shuffle(terms, [(r, r ^ apart) for r in range(rows)])
        total = terms.astype(jnp.float32) + other.astype(jnp.float32)
        terms = total.astype(terms.dtype)
    return terms


def prepare_kernel(cols, labels_ref, weight_ref, own_labels_ref, own_first_ref, wide_ref):
    col = lax.axis_index("cols")
    features = weight_ref.shape[0]
    width = features // cols
    labels = labels_ref[...] - col * width
    own_labels_ref[...] = jnp.where(labels < 0, labels + features, labels).astype(jnp.float32)
    for c in range(cols):
        row = remainder(col + c, cols) * width
        rows = weight_ref[pl.ds(pl.multiple_of(row, width), width), :]
        wide_ref[c * width : (c + 1) * width] = rows.astype(jnp.float32)
    turned = pltpu.roll(wide_ref[...], remainder(cols - col, cols) * width, axis=1)
    own_first_ref[...] = turned.astype(own_first_ref.dtype)


def prepare(labels, weight, cols):
    outs = (jax.ShapeDtypeStruct(labels.shape, jnp.float32), weight)
    wide = pltpu.VMEM(weight.shape, jnp.float32)
    return pl.pallas_call(
        functools.partial(prepare_kernel, cols),
        out_shape=(outs[0], jax.ShapeDtypeStruct(weight.shape, weight.dtype)),
        in_specs=[VMEM, VMEM],
        out_specs=(VMEM, VMEM),
        scratch_shapes=[wide],
        compiler_params=params(weight, weight, wide, wide),
        name="prepare",
    )(labels, weight)


def weight_kernel(cols, mine_ref, other_ref, out_ref):
    col = lax.axis_index("cols")
    width = out_ref.shape[1]
    for c in range(cols):
        here = pl.ds(c * width, width)
        total = mine_ref[here].astype(jnp.float32) + other_ref[here].astype(jnp.float32)
        row = remainder(col + c, cols) * width
        out_ref[pl.ds(pl.multiple_of(row, width), width)] = total


def finish_weight(mine, other, cols):
    out = jax.ShapeDtypeStruct(mine.shape, jnp.float32)
    return pl.pallas_call(
        functools.partial(weight_kernel, cols),
        out_shape=out,
        in_specs=[VMEM, VMEM],
        out_specs=VMEM,
        compiler_params=params(mine, other, out),
        name="finish_weight",
    )(mine, other)


def per_device(node_features, weight, tile_values, tile_row, source_owner, source_block, labels):
    local_rows, width = node_features.shape
    n_tiles, block_size = tile_values.shape[:2]
    blocks = local_rows // block_size
    rows, cols = lax.axis_size("rows"), lax.axis_size("cols")
    plane = math.gcd(rows, LARGEST_PLANE)
    line = rows // plane
    halves = 2 if width % 256 == 0 else 1
    part_width = width // halves
    slots = -(-min(n_tiles, line * (2 * n_tiles // rows)) // cols)
    owners = source_owner[:, 0]

    def other_cols(x):
        return [
            lax.ppermute(x, "cols", [((c + k) % cols, c) for c in range(cols)])
            for k in range(1, cols)
        ]

    lanes = [slice(h * part_width, (h + 1) * part_width) for h in range(halves)]
    *packed, codes = pack_tiles(
        owners, tile_row, source_block, tile_values, plane, cols, slots
    )
    node_parts = line_gather(node_features, packed, line, plane, cols, lanes)
    spots = n_tiles + (plane - 1) * cols * slots + 1
    flat = tile_values.reshape(n_tiles * block_size, block_size)
    early = own_tiles(flat, codes, spots) + prepare(labels.reshape(blocks, block_size), weight, cols)
    tile_parts = []
    for k in range(1, plane):
        arrived = across_plane(packed[k - 1], k, line, plane)
        if k == 1:
            arrived, early = lax.optimization_barrier((arrived, early))
        tile_parts += [arrived] + other_cols(arrived)
    laid, codes, own_labels, own_first = early
    tiles, plan, count = collect_tiles(
        codes, laid, tile_parts, plane, cols, slots, blocks, n_tiles
    )

    aggregated = []
    for h in range(halves):
        here = pl.ds(h * part_width, part_width)
        sums = forward_tiles(plan, count, tiles, node_parts[h], plane, here)
        total = sums[0]
        for k in range(1, plane):
            total = total + across_plane(sums[k], k, line, plane).astype(jnp.float32)
        mine = total.astype(jnp.bfloat16)
        aggregated.append([mine] + other_cols(mine))
    parts = [aggregated[h][c] for c in range(cols) for h in range(halves)]

    activations, out_grad, agg_grad = dense(own_labels, own_first, parts, halves)
    weight_terms, *agg_grads = grads(own_first, out_grad, parts, halves, local_rows * rows)

    pieces, after = [], None
    for i, agg_grad in enumerate([agg_grad] + agg_grads):
        arrived, places = plane_gather(agg_grad, line, plane, after)
        if i == 0:
            weight_terms = sum_apart(weight_terms, rows // 2, plane, rows, 1)
            arrived, weight_terms = lax.optimization_barrier((arrived, weight_terms))
            weight_terms = sum_apart(weight_terms, rows // 4, plane, rows)
        terms = spread_tiles(plan, count, tiles, list(zip(arrived, places)), line, plane)
        after = terms[0]
        beside = weight_terms if i == 0 else None
        half, beside, late = line_sum(terms, line, plane, cols, beside)
        if i == 0:
            weight_terms, _ = lax.optimization_barrier((beside, late))
        pieces.append(half)
    weight_terms = sum_apart(weight_terms, plane // 2, 2, rows)
    weight_terms, _ = lax.optimization_barrier((weight_terms, late))
    other = across_plane(weight_terms, 1, line, plane)
    weight_grad = finish_weight(weight_terms, other, cols)
    return activations, weight_grad, finish(pieces)


def solution(mesh):
    return jax.shard_map(
        per_device,
        mesh=mesh,
        in_specs=(
            P("rows", "cols"),
            P(),
            P("rows", None, None),
            P("rows"),
            P("rows", None),
            P("rows"),
            P("rows"),
        ),
        out_specs=(P("rows", "cols"), P(None, "cols"), P("rows", "cols")),
        check_vma=False,
    )
```

```python
import functools
import math

import jax
import jax.numpy as jnp
from jax import lax
from jax.experimental import pallas as pl
from jax.experimental.pallas import tpu as pltpu
from jax.sharding import PartitionSpec as P

VMEM = pl.BlockSpec(memory_space=pltpu.VMEM)
SMEM = pl.BlockSpec(memory_space=pltpu.SMEM)
ANY = pl.BlockSpec(memory_space=pl.ANY)
HBM = pl.BlockSpec(memory_space=pltpu.HBM)
SPARE_BYTES = 2 * 1024 * 1024
PACK_BYTES = 56 * 1024 * 1024
UNROLL = 8
LARGEST_PLANE = 4


def params(*shapes):
    room = SPARE_BYTES
    for shape in shapes:
        *lead, high, wide = shape.shape
        room += math.prod(lead) * high * (-(-wide // 128) * 128) * jnp.dtype(shape.dtype).itemsize
    return pltpu.CompilerParams(vmem_limit_bytes=room)


def quotient(x, n):
    return x >> (n.bit_length() - 1) if n & (n - 1) == 0 else lax.div(x, n)


def remainder(x, n):
    return x & (n - 1) if n & (n - 1) == 0 else lax.rem(x, n)


def position(plane):
    index, col = lax.axis_index("rows"), lax.axis_index("cols")
    return quotient(index, plane), remainder(index, plane), col, 1 - 2 * (col & 1)


def shuffle(x, pairs):
    return lax.ppermute(x, "rows", pairs)


def across_plane(x, k, line, plane):
    return shuffle(x, [(r, r ^ k) for r in range(line * plane)])


CODE_ROWS = 16


def pack_kernel(plane, cols, owner_ref, row_ref, source_ref, tiles_ref, *refs):
    out_refs, (codes_ref, *scratch) = refs[: plane - 1], refs[plane - 1 :]
    list_ref, slot_ref, owners_ref, along_ref, rows_ref, held_ref, small_sems, held_sem = scratch
    _, place, col, _ = position(plane)
    tiles, size = tiles_ref.shape[:2]
    slots = (out_refs[0].shape[0] - CODE_ROWS) // size
    spare = (plane - 1) * slots
    looks = [pltpu.make_async_copy(owner_ref, owners_ref, small_sems.at[0])]
    for i, ref in enumerate((owner_ref, row_ref, source_ref)):
        looks.append(pltpu.make_async_copy(ref, along_ref.at[i], small_sems.at[1 + i]))
    for look in looks:
        look.start()
    bulk = pltpu.make_async_copy(tiles_ref, held_ref, held_sem)
    bulk.start()
    for k in range(plane):
        slot_ref[k] = 0
    for i in range(spare):
        list_ref[i] = 0
    rows_ref[...] = jnp.zeros_like(rows_ref)
    for look in looks:
        look.wait()

    def step(t, carry):
        k = remainder(owners_ref[0, t], plane) ^ place
        slot = slot_ref[k]
        slot_ref[k] = slot + 1
        sent = (k > 0) & (remainder(slot, cols) == col)
        list_ref[jnp.where(sent, (k - 1) * slots + quotient(slot, cols), spare)] = t
        return carry

    lax.fori_loop(0, tiles, step, 0, unroll=4)
    owners = along_ref[0]
    rows_ref[0:1, :tiles] = remainder(owners, plane).astype(jnp.float32)
    rows_ref[1:2, :tiles] = along_ref[1].astype(jnp.float32)
    rows_ref[2:3, :tiles] = along_ref[2].astype(jnp.float32)
    rows_ref[3:4, :tiles] = quotient(owners, plane).astype(jnp.float32)
    codes = rows_ref[...].astype(codes_ref.dtype)
    codes_ref[...] = codes
    bulk.wait()
    for k, out_ref in enumerate(out_refs):
        for slot in range(slots):
            out_ref[slot * size : (slot + 1) * size] = held_ref[list_ref[k * slots + slot]]
        out_ref[slots * size :] = codes


def pack_tiles(owners, tile_row, source_block, tile_values, plane, cols, slots):
    tiles, size, wide = tile_values.shape
    shape = jax.ShapeDtypeStruct((slots * size + CODE_ROWS, wide), tile_values.dtype)
    codes = jax.ShapeDtypeStruct((CODE_ROWS, wide), tile_values.dtype)
    along = [x.reshape(1, tiles) for x in (owners, tile_row, source_block)]
    return pl.pallas_call(
        functools.partial(pack_kernel, plane, cols),
        out_shape=(shape,) * (plane - 1) + (codes,),
        in_specs=[HBM] * 4,
        out_specs=(VMEM,) * plane,
        scratch_shapes=[
            pltpu.SMEM(((plane - 1) * slots + 1,), jnp.int32),
            pltpu.SMEM((plane,), jnp.int32),
            pltpu.SMEM((1, tiles), jnp.int32),
            pltpu.VMEM((3, 1, tiles), jnp.int32),
            pltpu.VMEM((CODE_ROWS, wide), jnp.float32),
            pltpu.VMEM((tiles, size, wide), tile_values.dtype),
            pltpu.SemaphoreType.DMA((4,)),
            pltpu.SemaphoreType.DMA,
        ],
        compiler_params=pltpu.CompilerParams(vmem_limit_bytes=PACK_BYTES),
        name="pack_tiles",
    )(*along, tile_values)


DST_BIT, SRC_BIT, PLACE_BIT = 10, 16, 24


def own_kernel(tiles_ref, codes_ref, out_ref, own_ref, sems):
    rows = tiles_ref.shape[0]
    moves = ((tiles_ref, out_ref.at[pl.ds(0, rows)]), (codes_ref, own_ref))
    copies = [pltpu.make_async_copy(*move, sems.at[i]) for i, move in enumerate(moves)]
    for copy in copies:
        copy.start()
    out_ref[out_ref.shape[0] - out_ref.shape[1] :] = jnp.zeros(
        (out_ref.shape[1], out_ref.shape[1]), out_ref.dtype
    )
    for copy in copies:
        copy.wait()


def own_tiles(tiles, codes, spots):
    wide = tiles.shape[1]
    laid = jax.ShapeDtypeStruct((spots * wide, wide), tiles.dtype)
    return pl.pallas_call(
        own_kernel,
        out_shape=(laid, jax.ShapeDtypeStruct(codes.shape, codes.dtype)),
        in_specs=[ANY, ANY],
        out_specs=(VMEM, VMEM),
        scratch_shapes=[pltpu.SemaphoreType.DMA((2,))],
        compiler_params=params(laid),
        name="own_tiles",
    )(tiles, codes)


def collect_kernel(plane, cols, slots, blocks, tiles, own_ref, laid_ref, *refs):
    tile_refs, refs = refs[: (plane - 1) * cols], refs[(plane - 1) * cols :]
    out_ref, plan_ref, count_ref, *scratch = refs
    rows_ref, words_ref, codes_ref, row_sems, word_sem, tile_sems = scratch
    _, place, col, _ = position(plane)
    size = out_ref.shape[1]
    looks = []
    for k in range(plane):
        ref = own_ref
        if k > 0:
            ref = tile_refs[(k - 1) * cols].at[pl.ds(slots * size, CODE_ROWS)]
        copy = pltpu.make_async_copy(ref, rows_ref.at[k], row_sems.at[k])
        copy.start()
        looks.append(copy)
    copies, first, rows = [], tiles * size, slots * size
    for i, ref in enumerate(tile_refs):
        copy = pltpu.make_async_copy(
            ref.at[pl.ds(0, rows)], out_ref.at[pl.ds(first, rows)], tile_sems.at[i]
        )
        copy.start()
        copies.append(copy)
        first += rows
    words_ref[...] = jnp.zeros_like(words_ref)
    for k, copy in enumerate(looks):
        copy.wait()
        rows = rows_ref[k].astype(jnp.float32).astype(jnp.int32)
        source = rows[3:4] * blocks + rows[2:3]
        word = (rows[0:1] << PLACE_BIT) + (source << SRC_BIT)
        words_ref[k : k + 1] = word + ((rows[1:2] + k * blocks) << DST_BIT)
    copy = pltpu.make_async_copy(words_ref, codes_ref, word_sem)
    copy.start()
    copy.wait()
    found = jnp.int32(0)
    for k in range(plane):

        def step(t, carry, k=k):
            at, slot = carry
            code = codes_ref[k, t]
            if k == 0:
                spot = t
            else:
                column = remainder(slot + (cols - col), cols)
                spot = tiles + ((k - 1) * cols + column) * slots + quotient(slot, cols)
            plan_ref[at] = (code & ((1 << PLACE_BIT) - 1)) + spot
            one = ((code >> PLACE_BIT) == place).astype(jnp.int32)
            return at + one, slot + one

        found, _ = lax.fori_loop(0, tiles, step, (found, jnp.int32(0)), unroll=8)
    for i in range(UNROLL):
        plan_ref[found + i] = first // size
    count_ref[0] = quotient(found + UNROLL - 1, UNROLL)
    for copy in copies:
        copy.wait()


def collect_tiles(codes, laid, tile_parts, plane, cols, slots, blocks, tiles):
    wide = laid.shape[1]
    entries = plane * tiles + UNROLL
    high = -(-plane // 8) * 8
    return pl.pallas_call(
        functools.partial(collect_kernel, plane, cols, slots, blocks, tiles),
        out_shape=(
            jax.ShapeDtypeStruct(laid.shape, laid.dtype),
            jax.ShapeDtypeStruct((entries,), jnp.int32),
            jax.ShapeDtypeStruct((1,), jnp.int32),
        ),
        in_specs=[ANY, VMEM] + [ANY] * len(tile_parts),
        out_specs=(VMEM, SMEM, SMEM),
        scratch_shapes=[
            pltpu.VMEM((plane, CODE_ROWS, wide), jnp.bfloat16),
            pltpu.VMEM((high, wide), jnp.int32),
            pltpu.SMEM((high, wide), jnp.int32),
            pltpu.SemaphoreType.DMA((plane,)),
            pltpu.SemaphoreType.DMA,
            pltpu.SemaphoreType.DMA((len(tile_parts),)),
        ],
        input_output_aliases={1: 0},
        compiler_params=params(laid),
        name="collect_tiles",
    )(codes, laid, *tile_parts)


def planned(plan_ref, t):
    entry = plan_ref[t]
    spot = entry & ((1 << DST_BIT) - 1)
    return spot, (entry >> DST_BIT) & ((1 << (SRC_BIT - DST_BIT)) - 1), entry >> SRC_BIT


def block_rows(index, size):
    return pl.ds(pl.multiple_of(index * size, size), size)


def forward_kernel(line, lanes, plane, plan_ref, count_ref, tiles_ref, *refs):
    part_refs, refs = refs[: 2 * line - 1], refs[2 * line - 1 :]
    out_refs, (nodes_ref, acc_ref, part_sems) = refs[:-3], refs[-3:]
    rows, width = part_refs[0].shape[0], nodes_ref.shape[1]
    size = tiles_ref.shape[1]
    mine, _, _, way = position(plane)

    def each_part(act):
        for i, ref in enumerate(part_refs):
            source = mine + way * (i - (line - 1))

            @pl.when((source >= 0) & (source < line))
            def _():
                here = ref.at[:, lanes] if ref.shape != (rows, width) else ref
                act(
                    pltpu.make_async_copy(
                        here, nodes_ref.at[block_rows(source, rows)], part_sems.at[i]
                    )
                )

    each_part(lambda copy: copy.start())
    acc_ref[...] = jnp.zeros_like(acc_ref)
    each_part(lambda copy: copy.wait())

    def step(i, carry):
        ready = None
        for spot, dst, src in [planned(plan_ref, i * UNROLL + j) for j in range(UNROLL)]:
            product = jnp.dot(
                tiles_ref[block_rows(spot, size)],
                nodes_ref[block_rows(src, size)],
                preferred_element_type=jnp.float32,
            )
            if ready is not None:
                acc_ref[ready[0]] += ready[1]
            ready = block_rows(dst, size), product
        acc_ref[ready[0]] += ready[1]
        return carry

    lax.fori_loop(0, count_ref[0], step, 0)
    for k, ref in enumerate(out_refs):
        ref[...] = acc_ref[k * rows : (k + 1) * rows].astype(ref.dtype)


def forward_tiles(plan, count, tiles, node_parts, plane, lanes):
    line = (len(node_parts) + 1) // 2
    rows, width = node_parts[0].shape[0], lanes.size
    kinds = [jnp.float32] + [jnp.bfloat16] * (plane - 1)
    outs = tuple(jax.ShapeDtypeStruct((rows, width), kind) for kind in kinds)
    scratch = [
        pltpu.VMEM((line * rows, width), jnp.bfloat16),
        pltpu.VMEM((plane * rows, width), jnp.float32),
    ]
    return pl.pallas_call(
        functools.partial(forward_kernel, line, lanes, plane),
        out_shape=outs,
        in_specs=[SMEM] * 2 + [VMEM] + [ANY] * len(node_parts),
        out_specs=(VMEM,) * plane,
        scratch_shapes=scratch + [pltpu.SemaphoreType.DMA((len(node_parts),))],
        compiler_params=params(tiles, *outs, *scratch),
        name="forward_tiles",
    )(plan, count, tiles, *node_parts)


def dense_kernel(chunk, halves, labels_ref, weight_ref, *refs):
    parts, (act_ref, out_grad_ref, agg_grad_ref) = refs[:-3], refs[-3:]
    rows, part_width = parts[0].shape
    width = part_width * halves
    features = weight_ref.shape[0]
    size = labels_ref.shape[1]

    def rows_step(i, carry):
        here = block_rows(i, chunk)
        agg = jnp.concatenate([part[here, :] for part in parts], axis=1)
        hidden = jnp.dot(agg, weight_ref[...], preferred_element_type=jnp.float32)
        sigmoid = jax.nn.sigmoid(hidden)
        activated = hidden * sigmoid
        act_ref[here, :] = activated[:, :width].astype(act_ref.dtype)
        slopes = sigmoid * (1.0 + hidden * (1.0 - sigmoid))
        named = []
        for b in range(chunk // size):
            across = labels_ref[pl.ds(i * (chunk // size) + b, 1), :]
            named.append(jnp.broadcast_to(across, (size, size)).T)
        named = jnp.concatenate(named, axis=0)
        ids = lax.broadcasted_iota(jnp.int32, (chunk, size), 1).astype(jnp.float32)
        target = jnp.concatenate(
            [(named == ids + f * size).astype(jnp.float32) for f in range(features // size)],
            axis=1,
        )
        out_grad = ((activated - target) * slopes).astype(jnp.bfloat16)
        out_grad_ref[here, :] = out_grad
        agg_grad_ref[here, :] = lax.dot_general(
            out_grad,
            weight_ref[:part_width, :],
            (((1,), (1,)), ((), ())),
            preferred_element_type=jnp.float32,
        ).astype(agg_grad_ref.dtype)
        return carry

    lax.fori_loop(0, rows // chunk, rows_step, 0)


def dense(labels, weight, parts, halves):
    rows, part_width = parts[0].shape
    chunk = math.gcd(rows, 256)
    outs = tuple(
        jax.ShapeDtypeStruct((rows, width), jnp.bfloat16)
        for width in (part_width * halves, weight.shape[0], part_width)
    )
    return pl.pallas_call(
        functools.partial(dense_kernel, chunk, halves),
        out_shape=outs,
        in_specs=[VMEM] * (2 + len(parts)),
        out_specs=(VMEM,) * 3,
        compiler_params=params(labels, weight, *parts, *outs),
        name="dense",
    )(labels, weight, *parts)


def grads_kernel(scale, halves, weight_ref, out_grad_ref, *refs):
    parts, (terms_ref, *agg_grad_refs) = refs[: -halves], refs[-halves:]
    part_width = parts[0].shape[1]
    for h, ref in enumerate(agg_grad_refs, 1):
        ref[...] = lax.dot_general(
            out_grad_ref[...],
            weight_ref[h * part_width : (h + 1) * part_width, :],
            (((1,), (1,)), ((), ())),
            preferred_element_type=jnp.float32,
        ).astype(ref.dtype)
    for i, part in enumerate(parts):
        terms = lax.dot_general(
            part[...],
            out_grad_ref[:, : part_width * halves],
            (((0,), (0,)), ((), ())),
            preferred_element_type=jnp.float32,
        )
        terms_ref[i * part_width : (i + 1) * part_width] = (terms * scale).astype(terms_ref.dtype)


def grads(weight, out_grad, parts, halves, node_total):
    rows, part_width = parts[0].shape
    outs = (jax.ShapeDtypeStruct((weight.shape[0], part_width * halves), jnp.bfloat16),) + (
        jax.ShapeDtypeStruct((rows, part_width), jnp.bfloat16),
    ) * (halves - 1)
    return pl.pallas_call(
        functools.partial(grads_kernel, 1.0 / math.sqrt(node_total), halves),
        out_shape=outs,
        in_specs=[VMEM] * (2 + len(parts)),
        out_specs=(VMEM,) * halves,
        compiler_params=params(weight, out_grad, *parts, *outs),
        name="grads",
    )(weight, out_grad, *parts)


def spread_kernel(line, plane, plan_ref, count_ref, tiles_ref, *refs):
    grad_refs, refs = refs[:plane], refs[plane:]
    out_refs, (grads_ref, acc_ref, grad_sems) = refs[:-3], refs[-3:]
    rows = grad_refs[0].shape[0]
    size = tiles_ref.shape[1]
    mine, _, _, way = position(plane)
    copies = []
    for k, ref in enumerate(grad_refs):
        copy = pltpu.make_async_copy(ref, grads_ref.at[pl.ds(k * rows, rows)], grad_sems.at[k])
        copy.start()
        copies.append(copy)
    acc_ref[...] = jnp.zeros_like(acc_ref)
    for copy in copies:
        copy.wait()

    def step(i, carry):
        ready = None
        for spot, dst, src in [planned(plan_ref, i * UNROLL + j) for j in range(UNROLL)]:
            product = lax.dot_general(
                tiles_ref[block_rows(spot, size)],
                grads_ref[block_rows(dst, size)],
                (((0,), (0,)), ((), ())),
                preferred_element_type=jnp.float32,
            )
            if ready is not None:
                acc_ref[ready[0]] += ready[1]
            ready = block_rows(src, size), product
        acc_ref[ready[0]] += ready[1]
        return carry

    lax.fori_loop(0, count_ref[0], step, 0)
    for i, ref in enumerate(out_refs):
        target = mine + way * (i - (line - 1))

        @pl.when((target >= 0) & (target < line))
        def _():
            ref[...] = acc_ref[block_rows(target, rows)].astype(ref.dtype)


def spread_tiles(plan, count, tiles, grad_parts, line):
    plane = len(grad_parts)
    rows, width = grad_parts[0].shape
    kinds = [jnp.float32 if i == line - 1 else jnp.bfloat16 for i in range(2 * line - 1)]
    outs = tuple(jax.ShapeDtypeStruct((rows, width), kind) for kind in kinds)
    scratch = [
        pltpu.VMEM((plane * rows, width), jnp.bfloat16),
        pltpu.VMEM((line * rows, width), jnp.float32),
    ]
    return pl.pallas_call(
        functools.partial(spread_kernel, line, plane),
        out_shape=outs,
        in_specs=[SMEM] * 2 + [VMEM] + [ANY] * plane,
        out_specs=(VMEM,) * (2 * line - 1),
        scratch_shapes=scratch + [pltpu.SemaphoreType.DMA((plane,))],
        compiler_params=params(tiles, *outs, *scratch),
        name="spread_tiles",
    )(plan, count, tiles, *grad_parts)


def along_line(x, line, plane, cols, step, reach):
    pairs = []
    for z in range(line):
        for q in range(plane):
            for c in range(cols):
                way = 1 - 2 * (c & 1)
                to, end = z + way * step, z + way * reach
                if 0 <= to < line and 0 <= end < line:
                    pairs.append(((z * plane + q) * cols + c, (to * plane + q) * cols + c))
    return lax.ppermute(x, ("rows", "cols"), pairs)


def line_gather(x, after, line, plane, cols, lanes):
    move = lambda part, step, reach: along_line(part, line, plane, cols, step, reach)
    later, _ = lax.optimization_barrier((x, after))
    up, down = [x], [later]
    for k in range(1, line - 1):
        up.append(move(up[-1], 1, 1 - k))
        down.append(move(down[-1], -1, k - 1))
    parts, high, low = [], up[-1], down[-1]
    for part in lanes:
        first = move(high[:, part], 1, 2 - line)
        last = move(low[:, part], -1, line - 2)
        parts.append([first] + up[:0:-1] + down + [last])
    return parts


def line_sum(terms, line, plane, cols, beside):
    moved, late = {1: None, -1: None}, None
    for k in range(line - 1, 0, -1):
        for step in moved:
            term = terms[line - 1 + step * k]
            if moved[step] is not None:
                total = term.astype(jnp.float32) + moved[step].astype(jnp.float32)
                term = total.astype(term.dtype)
            moved[step] = along_line(term, line, plane, cols, step, step * k)
        if k == line - 1 and beside is not None:
            moved, beside = lax.optimization_barrier((moved, beside))
        if k > 1:
            late = tuple(moved.values())
    return [terms[line - 1], moved[1], moved[-1]], beside, late


def finish_kernel(halves, *refs):
    out_ref, refs = refs[-1], refs[:-1]
    each = len(refs) // halves
    width = refs[0].shape[1]
    for h in range(halves):
        total = refs[h * each][...]
        for ref in refs[h * each + 1 : (h + 1) * each]:
            total += ref[...].astype(jnp.float32)
        out_ref[:, h * width : (h + 1) * width] = total.astype(out_ref.dtype)


def finish(pieces):
    flat = [piece for half in pieces for piece in half]
    rows, width = flat[0].shape
    out = jax.ShapeDtypeStruct((rows, width * len(pieces)), jnp.bfloat16)
    return pl.pallas_call(
        functools.partial(finish_kernel, len(pieces)),
        out_shape=out,
        in_specs=[VMEM] * len(flat),
        out_specs=VMEM,
        compiler_params=params(out, *flat),
        name="finish",
    )(*flat)


def sum_apart(terms, first, end, rows):
    while first < end:
        other = shuffle(terms, [(r, r ^ first) for r in range(rows)])
        total = terms.astype(jnp.float32) + other.astype(jnp.float32)
        terms = total.astype(terms.dtype)
        first *= 2
    return terms


def prepare_kernel(cols, labels_ref, weight_ref, own_labels_ref, own_first_ref, wide_ref):
    col = lax.axis_index("cols")
    features = weight_ref.shape[0]
    width = features // cols
    labels = labels_ref[...] - col * width
    own_labels_ref[...] = jnp.where(labels < 0, labels + features, labels).astype(jnp.float32)
    for c in range(cols):
        row = remainder(col + c, cols) * width
        rows = weight_ref[pl.ds(pl.multiple_of(row, width), width), :]
        wide_ref[c * width : (c + 1) * width] = rows.astype(jnp.float32)
    turned = pltpu.roll(wide_ref[...], remainder(cols - col, cols) * width, axis=1)
    own_first_ref[...] = turned.astype(own_first_ref.dtype)


def prepare(labels, weight, cols):
    outs = (jax.ShapeDtypeStruct(labels.shape, jnp.float32), weight)
    wide = pltpu.VMEM(weight.shape, jnp.float32)
    return pl.pallas_call(
        functools.partial(prepare_kernel, cols),
        out_shape=(outs[0], jax.ShapeDtypeStruct(weight.shape, weight.dtype)),
        in_specs=[VMEM, VMEM],
        out_specs=(VMEM, VMEM),
        scratch_shapes=[wide],
        compiler_params=params(weight, weight, wide, wide),
        name="prepare",
    )(labels, weight)


def weight_kernel(cols, mine_ref, other_ref, out_ref):
    col = lax.axis_index("cols")
    width = out_ref.shape[1]
    for c in range(cols):
        here = pl.ds(c * width, width)
        total = mine_ref[here].astype(jnp.float32) + other_ref[here].astype(jnp.float32)
        row = remainder(col + c, cols) * width
        out_ref[pl.ds(pl.multiple_of(row, width), width)] = total


def finish_weight(mine, other, cols):
    out = jax.ShapeDtypeStruct(mine.shape, jnp.float32)
    return pl.pallas_call(
        functools.partial(weight_kernel, cols),
        out_shape=out,
        in_specs=[VMEM, VMEM],
        out_specs=VMEM,
        compiler_params=params(mine, other, out),
        name="finish_weight",
    )(mine, other)


def per_device(node_features, weight, tile_values, tile_row, source_owner, source_block, labels):
    local_rows, width = node_features.shape
    n_tiles, block_size = tile_values.shape[:2]
    blocks = local_rows // block_size
    rows, cols = lax.axis_size("rows"), lax.axis_size("cols")
    plane = math.gcd(rows, LARGEST_PLANE)
    line = rows // plane
    halves = 2 if width % 256 == 0 else 1
    part_width = width // halves
    slots = -(-min(n_tiles, line * (2 * n_tiles // rows)) // cols)
    owners = source_owner[:, 0]

    def other_cols(x):
        return [
            lax.ppermute(x, "cols", [((c + k) % cols, c) for c in range(cols)])
            for k in range(1, cols)
        ]

    lanes = [slice(h * part_width, (h + 1) * part_width) for h in range(halves)]
    *packed, codes = pack_tiles(
        owners, tile_row, source_block, tile_values, plane, cols, slots
    )
    node_parts = line_gather(node_features, packed, line, plane, cols, lanes)
    spots = n_tiles + (plane - 1) * cols * slots + 1
    flat = tile_values.reshape(n_tiles * block_size, block_size)
    early = own_tiles(flat, codes, spots) + prepare(labels.reshape(blocks, block_size), weight, cols)
    tile_parts = []
    for k in range(1, plane):
        arrived = across_plane(packed[k - 1], k, line, plane)
        if k == 1:
            arrived, early = lax.optimization_barrier((arrived, early))
        tile_parts += [arrived] + other_cols(arrived)
    laid, codes, own_labels, own_first = early
    tiles, plan, count = collect_tiles(
        codes, laid, tile_parts, plane, cols, slots, blocks, n_tiles
    )

    aggregated = []
    for h in range(halves):
        here = pl.ds(h * part_width, part_width)
        sums = forward_tiles(plan, count, tiles, node_parts[h], plane, here)
        total = sums[0]
        for k in range(1, plane):
            total = total + across_plane(sums[k], k, line, plane).astype(jnp.float32)
        mine = total.astype(jnp.bfloat16)
        aggregated.append([mine] + other_cols(mine))
    parts = [aggregated[h][c] for c in range(cols) for h in range(halves)]

    activations, out_grad, agg_grad = dense(own_labels, own_first, parts, halves)
    weight_terms, *agg_grads = grads(own_first, out_grad, parts, halves, local_rows * rows)

    pieces = []
    for i, agg_grad in enumerate([agg_grad] + agg_grads):
        arrived = [agg_grad] + [across_plane(agg_grad, k, line, plane) for k in range(1, plane)]
        if i == 0:
            weight_terms = sum_apart(weight_terms, plane, 2 * plane, rows)
            arrived, weight_terms = lax.optimization_barrier((arrived, weight_terms))
            weight_terms = sum_apart(weight_terms, 2 * plane, rows, rows)
        terms = spread_tiles(plan, count, tiles, arrived, line)
        beside = weight_terms if i == 0 else None
        half, beside, late = line_sum(terms, line, plane, cols, beside)
        if i == 0:
            weight_terms, _ = lax.optimization_barrier((beside, late))
        pieces.append(half)
    weight_terms = sum_apart(weight_terms, 1, plane // 2, rows)
    weight_terms, _ = lax.optimization_barrier((weight_terms, late))
    other = across_plane(weight_terms, plane // 2, line, plane)
    weight_grad = finish_weight(weight_terms, other, cols)
    return activations, weight_grad, finish(pieces)


def solution(mesh):
    return jax.shard_map(
        per_device,
        mesh=mesh,
        in_specs=(
            P("rows", "cols"),
            P(),
            P("rows", None, None),
            P("rows"),
            P("rows", None),
            P("rows"),
            P("rows"),
        ),
        out_specs=(P("rows", "cols"), P(None, "cols"), P("rows", "cols")),
        check_vma=False,
    )
```

```python
import functools
import math

import jax
import jax.numpy as jnp
from jax import lax
from jax.experimental import pallas as pl
from jax.experimental.pallas import tpu as pltpu
from jax.sharding import PartitionSpec as P

VMEM = pl.BlockSpec(memory_space=pltpu.VMEM)
SMEM = pl.BlockSpec(memory_space=pltpu.SMEM)
ANY = pl.BlockSpec(memory_space=pl.ANY)
HBM = pl.BlockSpec(memory_space=pltpu.HBM)
SPARE_BYTES = 2 * 1024 * 1024
PACK_BYTES = 56 * 1024 * 1024
UNROLL = 8
LARGEST_PLANE = 4


def params(*shapes):
    room = SPARE_BYTES
    for shape in shapes:
        *lead, high, wide = shape.shape
        room += math.prod(lead) * high * (-(-wide // 128) * 128) * jnp.dtype(shape.dtype).itemsize
    return pltpu.CompilerParams(vmem_limit_bytes=room)


def quotient(x, n):
    return x >> (n.bit_length() - 1) if n & (n - 1) == 0 else lax.div(x, n)


def remainder(x, n):
    return x & (n - 1) if n & (n - 1) == 0 else lax.rem(x, n)


def position(plane):
    index, col = lax.axis_index("rows"), lax.axis_index("cols")
    return quotient(index, plane), remainder(index, plane), col, 1 - 2 * (col & 1)


def shuffle(x, pairs):
    return lax.ppermute(x, "rows", pairs)


def across_plane(x, k, line, plane):
    return shuffle(x, [(r, r ^ k) for r in range(line * plane)])


CODE_ROWS = 16


def pack_kernel(plane, cols, owner_ref, row_ref, source_ref, tiles_ref, *refs):
    out_refs, (codes_ref, *scratch) = refs[: plane - 1], refs[plane - 1 :]
    list_ref, slot_ref, owners_ref, along_ref, rows_ref, held_ref, small_sems, held_sem = scratch
    _, place, col, _ = position(plane)
    tiles, size = tiles_ref.shape[:2]
    slots = (out_refs[0].shape[0] - CODE_ROWS) // size
    spare = (plane - 1) * slots
    looks = [pltpu.make_async_copy(owner_ref, owners_ref, small_sems.at[0])]
    for i, ref in enumerate((owner_ref, row_ref, source_ref)):
        looks.append(pltpu.make_async_copy(ref, along_ref.at[i], small_sems.at[1 + i]))
    for look in looks:
        look.start()
    bulk = pltpu.make_async_copy(tiles_ref, held_ref, held_sem)
    bulk.start()
    for k in range(plane):
        slot_ref[k] = 0
    for i in range(spare):
        list_ref[i] = 0
    rows_ref[...] = jnp.zeros_like(rows_ref)
    for look in looks:
        look.wait()

    def step(t, carry):
        k = remainder(owners_ref[0, t], plane) ^ place
        slot = slot_ref[k]
        slot_ref[k] = slot + 1
        sent = (k > 0) & (remainder(slot, cols) == col)
        list_ref[jnp.where(sent, (k - 1) * slots + quotient(slot, cols), spare)] = t
        return carry

    lax.fori_loop(0, tiles, step, 0, unroll=4)
    owners = along_ref[0]
    rows_ref[0:1, :tiles] = remainder(owners, plane).astype(jnp.float32)
    rows_ref[1:2, :tiles] = along_ref[1].astype(jnp.float32)
    rows_ref[2:3, :tiles] = along_ref[2].astype(jnp.float32)
    rows_ref[3:4, :tiles] = quotient(owners, plane).astype(jnp.float32)
    codes = rows_ref[...].astype(codes_ref.dtype)
    codes_ref[...] = codes
    bulk.wait()
    for k, out_ref in enumerate(out_refs):
        for slot in range(slots):
            out_ref[slot * size : (slot + 1) * size] = held_ref[list_ref[k * slots + slot]]
        out_ref[slots * size :] = codes


def pack_tiles(owners, tile_row, source_block, tile_values, plane, cols, slots):
    tiles, size, wide = tile_values.shape
    shape = jax.ShapeDtypeStruct((slots * size + CODE_ROWS, wide), tile_values.dtype)
    codes = jax.ShapeDtypeStruct((CODE_ROWS, wide), tile_values.dtype)
    along = [x.reshape(1, tiles) for x in (owners, tile_row, source_block)]
    return pl.pallas_call(
        functools.partial(pack_kernel, plane, cols),
        out_shape=(shape,) * (plane - 1) + (codes,),
        in_specs=[HBM] * 4,
        out_specs=(VMEM,) * plane,
        scratch_shapes=[
            pltpu.SMEM(((plane - 1) * slots + 1,), jnp.int32),
            pltpu.SMEM((plane,), jnp.int32),
            pltpu.SMEM((1, tiles), jnp.int32),
            pltpu.VMEM((3, 1, tiles), jnp.int32),
            pltpu.VMEM((CODE_ROWS, wide), jnp.float32),
            pltpu.VMEM((tiles, size, wide), tile_values.dtype),
            pltpu.SemaphoreType.DMA((4,)),
            pltpu.SemaphoreType.DMA,
        ],
        compiler_params=pltpu.CompilerParams(vmem_limit_bytes=PACK_BYTES),
        name="pack_tiles",
    )(*along, tile_values)


DST_BIT, SRC_BIT, PLACE_BIT = 10, 16, 24


def own_kernel(tiles_ref, codes_ref, out_ref, own_ref, sems):
    rows = tiles_ref.shape[0]
    moves = ((tiles_ref, out_ref.at[pl.ds(0, rows)]), (codes_ref, own_ref))
    copies = [pltpu.make_async_copy(*move, sems.at[i]) for i, move in enumerate(moves)]
    for copy in copies:
        copy.start()
    out_ref[out_ref.shape[0] - out_ref.shape[1] :] = jnp.zeros(
        (out_ref.shape[1], out_ref.shape[1]), out_ref.dtype
    )
    for copy in copies:
        copy.wait()


def own_tiles(tiles, codes, spots):
    wide = tiles.shape[1]
    laid = jax.ShapeDtypeStruct((spots * wide, wide), tiles.dtype)
    return pl.pallas_call(
        own_kernel,
        out_shape=(laid, jax.ShapeDtypeStruct(codes.shape, codes.dtype)),
        in_specs=[ANY, ANY],
        out_specs=(VMEM, VMEM),
        scratch_shapes=[pltpu.SemaphoreType.DMA((2,))],
        compiler_params=params(laid),
        name="own_tiles",
    )(tiles, codes)


def collect_kernel(plane, cols, slots, blocks, tiles, own_ref, laid_ref, *refs):
    tile_refs, refs = refs[: (plane - 1) * cols], refs[(plane - 1) * cols :]
    out_ref, plan_ref, count_ref, *scratch = refs
    rows_ref, words_ref, codes_ref, row_sems, word_sem, tile_sems = scratch
    _, place, col, _ = position(plane)
    size = out_ref.shape[1]
    looks = []
    for k in range(plane):
        ref = own_ref
        if k > 0:
            ref = tile_refs[(k - 1) * cols].at[pl.ds(slots * size, CODE_ROWS)]
        copy = pltpu.make_async_copy(ref, rows_ref.at[k], row_sems.at[k])
        copy.start()
        looks.append(copy)
    copies, first, rows = [], tiles * size, slots * size
    for i, ref in enumerate(tile_refs):
        copy = pltpu.make_async_copy(
            ref.at[pl.ds(0, rows)], out_ref.at[pl.ds(first, rows)], tile_sems.at[i]
        )
        copy.start()
        copies.append(copy)
        first += rows
    words_ref[...] = jnp.zeros_like(words_ref)
    for k, copy in enumerate(looks):
        copy.wait()
        rows = rows_ref[k].astype(jnp.float32).astype(jnp.int32)
        source = rows[3:4] * blocks + rows[2:3]
        word = (rows[0:1] << PLACE_BIT) + (source << SRC_BIT)
        words_ref[k : k + 1] = word + ((rows[1:2] + k * blocks) << DST_BIT)
    copy = pltpu.make_async_copy(words_ref, codes_ref, word_sem)
    copy.start()
    copy.wait()
    found = jnp.int32(0)
    for k in range(plane):

        def step(t, carry, k=k):
            at, slot = carry
            code = codes_ref[k, t]
            if k == 0:
                spot = t
            else:
                column = remainder(slot + (cols - col), cols)
                spot = tiles + ((k - 1) * cols + column) * slots + quotient(slot, cols)
            plan_ref[at] = (code & ((1 << PLACE_BIT) - 1)) + spot
            one = ((code >> PLACE_BIT) == place).astype(jnp.int32)
            return at + one, slot + one

        found, _ = lax.fori_loop(0, tiles, step, (found, jnp.int32(0)), unroll=8)
    for i in range(UNROLL):
        plan_ref[found + i] = first // size
    count_ref[0] = quotient(found + UNROLL - 1, UNROLL)
    for copy in copies:
        copy.wait()


def collect_tiles(codes, laid, tile_parts, plane, cols, slots, blocks, tiles):
    wide = laid.shape[1]
    entries = plane * tiles + UNROLL
    high = -(-plane // 8) * 8
    return pl.pallas_call(
        functools.partial(collect_kernel, plane, cols, slots, blocks, tiles),
        out_shape=(
            jax.ShapeDtypeStruct(laid.shape, laid.dtype),
            jax.ShapeDtypeStruct((entries,), jnp.int32),
            jax.ShapeDtypeStruct((1,), jnp.int32),
        ),
        in_specs=[ANY, VMEM] + [ANY] * len(tile_parts),
        out_specs=(VMEM, SMEM, SMEM),
        scratch_shapes=[
            pltpu.VMEM((plane, CODE_ROWS, wide), jnp.bfloat16),
            pltpu.VMEM((high, wide), jnp.int32),
            pltpu.SMEM((high, wide), jnp.int32),
            pltpu.SemaphoreType.DMA((plane,)),
            pltpu.SemaphoreType.DMA,
            pltpu.SemaphoreType.DMA((len(tile_parts),)),
        ],
        input_output_aliases={1: 0},
        compiler_params=params(laid),
        name="collect_tiles",
    )(codes, laid, *tile_parts)


def planned(plan_ref, t):
    entry = plan_ref[t]
    spot = entry & ((1 << DST_BIT) - 1)
    return spot, (entry >> DST_BIT) & ((1 << (SRC_BIT - DST_BIT)) - 1), entry >> SRC_BIT


def block_rows(index, size):
    return pl.ds(pl.multiple_of(index * size, size), size)


def forward_kernel(line, lanes, plane, plan_ref, count_ref, tiles_ref, *refs):
    part_refs, refs = refs[: 2 * line - 1], refs[2 * line - 1 :]
    out_refs, (nodes_ref, acc_ref, part_sems) = refs[:-3], refs[-3:]
    rows, width = part_refs[0].shape[0], nodes_ref.shape[1]
    size = tiles_ref.shape[1]
    mine, _, _, way = position(plane)

    def each_part(act):
        for i, ref in enumerate(part_refs):
            source = mine + way * (i - (line - 1))

            @pl.when((source >= 0) & (source < line))
            def _():
                here = ref.at[:, lanes] if ref.shape != (rows, width) else ref
                act(
                    pltpu.make_async_copy(
                        here, nodes_ref.at[block_rows(source, rows)], part_sems.at[i]
                    )
                )

    each_part(lambda copy: copy.start())
    acc_ref[...] = jnp.zeros_like(acc_ref)
    each_part(lambda copy: copy.wait())

    def step(i, carry):
        ready = None
        for spot, dst, src in [planned(plan_ref, i * UNROLL + j) for j in range(UNROLL)]:
            product = jnp.dot(
                tiles_ref[block_rows(spot, size)],
                nodes_ref[block_rows(src, size)],
                preferred_element_type=jnp.float32,
            )
            if ready is not None:
                acc_ref[ready[0]] += ready[1]
            ready = block_rows(dst, size), product
        acc_ref[ready[0]] += ready[1]
        return carry

    lax.fori_loop(0, count_ref[0], step, 0)
    for k, ref in enumerate(out_refs):
        ref[...] = acc_ref[k * rows : (k + 1) * rows].astype(ref.dtype)


def forward_tiles(plan, count, tiles, node_parts, plane, lanes):
    line = (len(node_parts) + 1) // 2
    rows, width = node_parts[0].shape[0], lanes.size
    kinds = [jnp.float32] + [jnp.bfloat16] * (plane - 1)
    outs = tuple(jax.ShapeDtypeStruct((rows, width), kind) for kind in kinds)
    scratch = [
        pltpu.VMEM((line * rows, width), jnp.bfloat16),
        pltpu.VMEM((plane * rows, width), jnp.float32),
    ]
    return pl.pallas_call(
        functools.partial(forward_kernel, line, lanes, plane),
        out_shape=outs,
        in_specs=[SMEM] * 2 + [VMEM] + [ANY] * len(node_parts),
        out_specs=(VMEM,) * plane,
        scratch_shapes=scratch + [pltpu.SemaphoreType.DMA((len(node_parts),))],
        compiler_params=params(tiles, *outs, *scratch),
        name="forward_tiles",
    )(plan, count, tiles, *node_parts)


def dense_kernel(chunk, halves, labels_ref, weight_ref, *refs):
    parts, (act_ref, out_grad_ref, agg_grad_ref) = refs[:-3], refs[-3:]
    rows, part_width = parts[0].shape
    width = part_width * halves
    features = weight_ref.shape[0]
    size = labels_ref.shape[1]

    def rows_step(i, carry):
        here = block_rows(i, chunk)
        agg = jnp.concatenate([part[here, :] for part in parts], axis=1)
        hidden = jnp.dot(agg, weight_ref[...], preferred_element_type=jnp.float32)
        sigmoid = jax.nn.sigmoid(hidden)
        activated = hidden * sigmoid
        act_ref[here, :] = activated[:, :width].astype(act_ref.dtype)
        slopes = sigmoid * (1.0 + hidden * (1.0 - sigmoid))
        named = []
        for b in range(chunk // size):
            across = labels_ref[pl.ds(i * (chunk // size) + b, 1), :]
            named.append(jnp.broadcast_to(across, (size, size)).T)
        named = jnp.concatenate(named, axis=0)
        ids = lax.broadcasted_iota(jnp.int32, (chunk, size), 1).astype(jnp.float32)
        target = jnp.concatenate(
            [(named == ids + f * size).astype(jnp.float32) for f in range(features // size)],
            axis=1,
        )
        out_grad = ((activated - target) * slopes).astype(jnp.bfloat16)
        out_grad_ref[here, :] = out_grad
        agg_grad_ref[here, :] = lax.dot_general(
            out_grad,
            weight_ref[:part_width, :],
            (((1,), (1,)), ((), ())),
            preferred_element_type=jnp.float32,
        ).astype(agg_grad_ref.dtype)
        return carry

    lax.fori_loop(0, rows // chunk, rows_step, 0)


def dense(labels, weight, parts, halves):
    rows, part_width = parts[0].shape
    chunk = math.gcd(rows, 256)
    outs = tuple(
        jax.ShapeDtypeStruct((rows, width), jnp.bfloat16)
        for width in (part_width * halves, weight.shape[0], part_width)
    )
    return pl.pallas_call(
        functools.partial(dense_kernel, chunk, halves),
        out_shape=outs,
        in_specs=[VMEM] * (2 + len(parts)),
        out_specs=(VMEM,) * 3,
        compiler_params=params(labels, weight, *parts, *outs),
        name="dense",
    )(labels, weight, *parts)


def grads_kernel(scale, halves, weight_ref, out_grad_ref, *refs):
    parts, (terms_ref, *agg_grad_refs) = refs[: -halves], refs[-halves:]
    part_width = parts[0].shape[1]
    for h, ref in enumerate(agg_grad_refs, 1):
        ref[...] = lax.dot_general(
            out_grad_ref[...],
            weight_ref[h * part_width : (h + 1) * part_width, :],
            (((1,), (1,)), ((), ())),
            preferred_element_type=jnp.float32,
        ).astype(ref.dtype)
    for i, part in enumerate(parts):
        terms = lax.dot_general(
            part[...],
            out_grad_ref[:, : part_width * halves],
            (((0,), (0,)), ((), ())),
            preferred_element_type=jnp.float32,
        )
        terms_ref[i * part_width : (i + 1) * part_width] = (terms * scale).astype(terms_ref.dtype)


def grads(weight, out_grad, parts, halves, node_total):
    rows, part_width = parts[0].shape
    outs = (jax.ShapeDtypeStruct((weight.shape[0], part_width * halves), jnp.bfloat16),) + (
        jax.ShapeDtypeStruct((rows, part_width), jnp.bfloat16),
    ) * (halves - 1)
    return pl.pallas_call(
        functools.partial(grads_kernel, 1.0 / math.sqrt(node_total), halves),
        out_shape=outs,
        in_specs=[VMEM] * (2 + len(parts)),
        out_specs=(VMEM,) * halves,
        compiler_params=params(weight, out_grad, *parts, *outs),
        name="grads",
    )(weight, out_grad, *parts)


def spread_kernel(line, plane, plan_ref, count_ref, tiles_ref, *refs):
    grad_refs, refs = refs[:plane], refs[plane:]
    out_refs, (grads_ref, acc_ref, grad_sems) = refs[:-3], refs[-3:]
    rows = grad_refs[0].shape[0]
    size = tiles_ref.shape[1]
    mine, _, _, way = position(plane)
    copies = []
    for k, ref in enumerate(grad_refs):
        copy = pltpu.make_async_copy(ref, grads_ref.at[pl.ds(k * rows, rows)], grad_sems.at[k])
        copy.start()
        copies.append(copy)
    acc_ref[...] = jnp.zeros_like(acc_ref)
    for copy in copies:
        copy.wait()

    def step(i, carry):
        ready = None
        for spot, dst, src in [planned(plan_ref, i * UNROLL + j) for j in range(UNROLL)]:
            product = lax.dot_general(
                tiles_ref[block_rows(spot, size)],
                grads_ref[block_rows(dst, size)],
                (((0,), (0,)), ((), ())),
                preferred_element_type=jnp.float32,
            )
            if ready is not None:
                acc_ref[ready[0]] += ready[1]
            ready = block_rows(src, size), product
        acc_ref[ready[0]] += ready[1]
        return carry

    lax.fori_loop(0, count_ref[0], step, 0)
    for i, ref in enumerate(out_refs):
        target = mine + way * (i - (line - 1))

        @pl.when((target >= 0) & (target < line))
        def _():
            ref[...] = acc_ref[block_rows(target, rows)].astype(ref.dtype)


def spread_tiles(plan, count, tiles, grad_parts, line):
    plane = len(grad_parts)
    rows, width = grad_parts[0].shape
    kinds = [jnp.float32 if i == line - 1 else jnp.bfloat16 for i in range(2 * line - 1)]
    outs = tuple(jax.ShapeDtypeStruct((rows, width), kind) for kind in kinds)
    scratch = [
        pltpu.VMEM((plane * rows, width), jnp.bfloat16),
        pltpu.VMEM((line * rows, width), jnp.float32),
    ]
    return pl.pallas_call(
        functools.partial(spread_kernel, line, plane),
        out_shape=outs,
        in_specs=[SMEM] * 2 + [VMEM] + [ANY] * plane,
        out_specs=(VMEM,) * (2 * line - 1),
        scratch_shapes=scratch + [pltpu.SemaphoreType.DMA((plane,))],
        compiler_params=params(tiles, *outs, *scratch),
        name="spread_tiles",
    )(plan, count, tiles, *grad_parts)


def along_line(x, line, plane, cols, step, reach):
    pairs = []
    for z in range(line):
        for q in range(plane):
            for c in range(cols):
                way = 1 - 2 * (c & 1)
                to, end = z + way * step, z + way * reach
                if 0 <= to < line and 0 <= end < line:
                    pairs.append(((z * plane + q) * cols + c, (to * plane + q) * cols + c))
    return lax.ppermute(x, ("rows", "cols"), pairs)


def line_gather(x, after, line, plane, cols, lanes):
    move = lambda part, step, reach: along_line(part, line, plane, cols, step, reach)
    later, _ = lax.optimization_barrier((x, after))
    up, down = [x], [later]
    for k in range(1, line - 1):
        up.append(move(up[-1], 1, 1 - k))
        down.append(move(down[-1], -1, k - 1))
    parts, high, low = [], up[-1], down[-1]
    for part in lanes:
        first = move(high[:, part], 1, 2 - line)
        last = move(low[:, part], -1, line - 2)
        parts.append([first] + up[:0:-1] + down + [last])
    return parts


def line_sum(terms, line, plane, cols, beside):
    moved, late = {1: None, -1: None}, None
    for k in range(line - 1, 0, -1):
        for step in moved:
            term = terms[line - 1 + step * k]
            if moved[step] is not None:
                total = term.astype(jnp.float32) + moved[step].astype(jnp.float32)
                term = total.astype(term.dtype)
            moved[step] = along_line(term, line, plane, cols, step, step * k)
        if k == line - 1 and beside is not None:
            moved, beside = lax.optimization_barrier((moved, beside))
        if k > 1:
            late = tuple(moved.values())
    return [terms[line - 1], moved[1], moved[-1]], beside, late


def finish_kernel(halves, *refs):
    out_ref, refs = refs[-1], refs[:-1]
    each = len(refs) // halves
    width = refs[0].shape[1]
    for h in range(halves):
        total = refs[h * each][...]
        for ref in refs[h * each + 1 : (h + 1) * each]:
            total += ref[...].astype(jnp.float32)
        out_ref[:, h * width : (h + 1) * width] = total.astype(out_ref.dtype)


def finish(pieces):
    flat = [piece for half in pieces for piece in half]
    rows, width = flat[0].shape
    out = jax.ShapeDtypeStruct((rows, width * len(pieces)), jnp.bfloat16)
    return pl.pallas_call(
        functools.partial(finish_kernel, len(pieces)),
        out_shape=out,
        in_specs=[VMEM] * len(flat),
        out_specs=VMEM,
        compiler_params=params(out, *flat),
        name="finish",
    )(*flat)


def sum_apart(terms, far, near, rows, most=None):
    steps = []
    while far >= near:
        steps.append(far)
        far //= 2
    for apart in steps[:most]:
        other = shuffle(terms, [(r, r ^ apart) for r in range(rows)])
        total = terms.astype(jnp.float32) + other.astype(jnp.float32)
        terms = total.astype(terms.dtype)
    return terms


def prepare_kernel(cols, labels_ref, weight_ref, own_labels_ref, own_first_ref, wide_ref):
    col = lax.axis_index("cols")
    features = weight_ref.shape[0]
    width = features // cols
    labels = labels_ref[...] - col * width
    own_labels_ref[...] = jnp.where(labels < 0, labels + features, labels).astype(jnp.float32)
    for c in range(cols):
        row = remainder(col + c, cols) * width
        rows = weight_ref[pl.ds(pl.multiple_of(row, width), width), :]
        wide_ref[c * width : (c + 1) * width] = rows.astype(jnp.float32)
    turned = pltpu.roll(wide_ref[...], remainder(cols - col, cols) * width, axis=1)
    own_first_ref[...] = turned.astype(own_first_ref.dtype)


def prepare(labels, weight, cols):
    outs = (jax.ShapeDtypeStruct(labels.shape, jnp.float32), weight)
    wide = pltpu.VMEM(weight.shape, jnp.float32)
    return pl.pallas_call(
        functools.partial(prepare_kernel, cols),
        out_shape=(outs[0], jax.ShapeDtypeStruct(weight.shape, weight.dtype)),
        in_specs=[VMEM, VMEM],
        out_specs=(VMEM, VMEM),
        scratch_shapes=[wide],
        compiler_params=params(weight, weight, wide, wide),
        name="prepare",
    )(labels, weight)


def weight_kernel(cols, mine_ref, other_ref, out_ref):
    col = lax.axis_index("cols")
    width = out_ref.shape[1]
    for c in range(cols):
        here = pl.ds(c * width, width)
        total = mine_ref[here].astype(jnp.float32) + other_ref[here].astype(jnp.float32)
        row = remainder(col + c, cols) * width
        out_ref[pl.ds(pl.multiple_of(row, width), width)] = total


def finish_weight(mine, other, cols):
    out = jax.ShapeDtypeStruct(mine.shape, jnp.float32)
    return pl.pallas_call(
        functools.partial(weight_kernel, cols),
        out_shape=out,
        in_specs=[VMEM, VMEM],
        out_specs=VMEM,
        compiler_params=params(mine, other, out),
        name="finish_weight",
    )(mine, other)


def per_device(node_features, weight, tile_values, tile_row, source_owner, source_block, labels):
    local_rows, width = node_features.shape
    n_tiles, block_size = tile_values.shape[:2]
    blocks = local_rows // block_size
    rows, cols = lax.axis_size("rows"), lax.axis_size("cols")
    plane = math.gcd(rows, LARGEST_PLANE)
    line = rows // plane
    halves = 2 if width % 256 == 0 else 1
    part_width = width // halves
    slots = -(-min(n_tiles, line * (2 * n_tiles // rows)) // cols)
    owners = source_owner[:, 0]

    def other_cols(x):
        return [
            lax.ppermute(x, "cols", [((c + k) % cols, c) for c in range(cols)])
            for k in range(1, cols)
        ]

    lanes = [slice(h * part_width, (h + 1) * part_width) for h in range(halves)]
    *packed, codes = pack_tiles(
        owners, tile_row, source_block, tile_values, plane, cols, slots
    )
    node_parts = line_gather(node_features, packed, line, plane, cols, lanes)
    spots = n_tiles + (plane - 1) * cols * slots + 1
    flat = tile_values.reshape(n_tiles * block_size, block_size)
    early = own_tiles(flat, codes, spots) + prepare(labels.reshape(blocks, block_size), weight, cols)
    tile_parts = []
    for k in range(1, plane):
        arrived = across_plane(packed[k - 1], k, line, plane)
        if k == 1:
            arrived, early = lax.optimization_barrier((arrived, early))
        tile_parts += [arrived] + other_cols(arrived)
    laid, codes, own_labels, own_first = early
    tiles, plan, count = collect_tiles(
        codes, laid, tile_parts, plane, cols, slots, blocks, n_tiles
    )

    aggregated = []
    for h in range(halves):
        here = pl.ds(h * part_width, part_width)
        sums = forward_tiles(plan, count, tiles, node_parts[h], plane, here)
        total = sums[0]
        for k in range(1, plane):
            total = total + across_plane(sums[k], k, line, plane).astype(jnp.float32)
        mine = total.astype(jnp.bfloat16)
        aggregated.append([mine] + other_cols(mine))
    parts = [aggregated[h][c] for c in range(cols) for h in range(halves)]

    activations, out_grad, agg_grad = dense(own_labels, own_first, parts, halves)
    weight_terms, *agg_grads = grads(own_first, out_grad, parts, halves, local_rows * rows)

    pieces = []
    for i, agg_grad in enumerate([agg_grad] + agg_grads):
        arrived = [agg_grad] + [across_plane(agg_grad, k, line, plane) for k in range(1, plane)]
        if i == 0:
            weight_terms = sum_apart(weight_terms, rows // 2, plane, rows, 1)
            arrived, weight_terms = lax.optimization_barrier((arrived, weight_terms))
            weight_terms = sum_apart(weight_terms, rows // 4, plane, rows)
        terms = spread_tiles(plan, count, tiles, arrived, line)
        half, _, late = line_sum(terms, line, plane, cols, None)
        if i == 0:
            weight_terms, _ = lax.optimization_barrier((weight_terms, late))
        pieces.append(half)
    weight_terms = sum_apart(weight_terms, plane // 2, 2, rows)
    weight_terms, _ = lax.optimization_barrier((weight_terms, late))
    other = across_plane(weight_terms, 1, line, plane)
    weight_grad = finish_weight(weight_terms, other, cols)
    return activations, weight_grad, finish(pieces)


def solution(mesh):
    return jax.shard_map(
        per_device,
        mesh=mesh,
        in_specs=(
            P("rows", "cols"),
            P(),
            P("rows", None, None),
            P("rows"),
            P("rows", None),
            P("rows"),
            P("rows"),
        ),
        out_specs=(P("rows", "cols"), P(None, "cols"), P("rows", "cols")),
        check_vma=False,
    )
```

```python
import functools
import math

import jax
import jax.numpy as jnp
from jax import lax
from jax.experimental import pallas as pl
from jax.experimental.pallas import tpu as pltpu
from jax.sharding import PartitionSpec as P

VMEM = pl.BlockSpec(memory_space=pltpu.VMEM)
SMEM = pl.BlockSpec(memory_space=pltpu.SMEM)
ANY = pl.BlockSpec(memory_space=pl.ANY)
HBM = pl.BlockSpec(memory_space=pltpu.HBM)
SPARE_BYTES = 2 * 1024 * 1024
PACK_BYTES = 56 * 1024 * 1024
UNROLL = 8
LARGEST_PLANE = 4


def params(*shapes):
    room = SPARE_BYTES
    for shape in shapes:
        *lead, high, wide = shape.shape
        room += math.prod(lead) * high * (-(-wide // 128) * 128) * jnp.dtype(shape.dtype).itemsize
    return pltpu.CompilerParams(vmem_limit_bytes=room)


def quotient(x, n):
    return x >> (n.bit_length() - 1) if n & (n - 1) == 0 else lax.div(x, n)


def remainder(x, n):
    return x & (n - 1) if n & (n - 1) == 0 else lax.rem(x, n)


def position(plane):
    index, col = lax.axis_index("rows"), lax.axis_index("cols")
    return quotient(index, plane), remainder(index, plane), col, 1 - 2 * (col & 1)


def shuffle(x, pairs):
    return lax.ppermute(x, "rows", pairs)


def across_plane(x, k, line, plane):
    return shuffle(x, [(r, r ^ k) for r in range(line * plane)])


CODE_ROWS = 16


def pack_kernel(plane, cols, owner_ref, row_ref, source_ref, tiles_ref, *refs):
    out_refs, (codes_ref, *scratch) = refs[: plane - 1], refs[plane - 1 :]
    list_ref, slot_ref, owners_ref, along_ref, rows_ref, held_ref, small_sems, held_sem = scratch
    _, place, col, _ = position(plane)
    tiles, size = tiles_ref.shape[:2]
    slots = (out_refs[0].shape[0] - CODE_ROWS) // size
    spare = (plane - 1) * slots
    looks = [pltpu.make_async_copy(owner_ref, owners_ref, small_sems.at[0])]
    for i, ref in enumerate((owner_ref, row_ref, source_ref)):
        looks.append(pltpu.make_async_copy(ref, along_ref.at[i], small_sems.at[1 + i]))
    for look in looks:
        look.start()
    bulk = pltpu.make_async_copy(tiles_ref, held_ref, held_sem)
    bulk.start()
    for k in range(plane):
        slot_ref[k] = 0
    for i in range(spare):
        list_ref[i] = 0
    rows_ref[...] = jnp.zeros_like(rows_ref)
    for look in looks:
        look.wait()

    def step(t, carry):
        k = remainder(owners_ref[0, t], plane) ^ place
        slot = slot_ref[k]
        slot_ref[k] = slot + 1
        sent = (k > 0) & (remainder(slot, cols) == col)
        list_ref[jnp.where(sent, (k - 1) * slots + quotient(slot, cols), spare)] = t
        return carry

    lax.fori_loop(0, tiles, step, 0, unroll=4)
    owners = along_ref[0]
    rows_ref[0:1, :tiles] = remainder(owners, plane).astype(jnp.float32)
    rows_ref[1:2, :tiles] = along_ref[1].astype(jnp.float32)
    rows_ref[2:3, :tiles] = along_ref[2].astype(jnp.float32)
    rows_ref[3:4, :tiles] = quotient(owners, plane).astype(jnp.float32)
    codes = rows_ref[...].astype(codes_ref.dtype)
    codes_ref[...] = codes
    bulk.wait()
    for k, out_ref in enumerate(out_refs):
        for slot in range(slots):
            out_ref[slot * size : (slot + 1) * size] = held_ref[list_ref[k * slots + slot]]
        out_ref[slots * size :] = codes


def pack_tiles(owners, tile_row, source_block, tile_values, plane, cols, slots):
    tiles, size, wide = tile_values.shape
    shape = jax.ShapeDtypeStruct((slots * size + CODE_ROWS, wide), tile_values.dtype)
    codes = jax.ShapeDtypeStruct((CODE_ROWS, wide), tile_values.dtype)
    along = [x.reshape(1, tiles) for x in (owners, tile_row, source_block)]
    return pl.pallas_call(
        functools.partial(pack_kernel, plane, cols),
        out_shape=(shape,) * (plane - 1) + (codes,),
        in_specs=[HBM] * 4,
        out_specs=(VMEM,) * plane,
        scratch_shapes=[
            pltpu.SMEM(((plane - 1) * slots + 1,), jnp.int32),
            pltpu.SMEM((plane,), jnp.int32),
            pltpu.SMEM((1, tiles), jnp.int32),
            pltpu.VMEM((3, 1, tiles), jnp.int32),
            pltpu.VMEM((CODE_ROWS, wide), jnp.float32),
            pltpu.VMEM((tiles, size, wide), tile_values.dtype),
            pltpu.SemaphoreType.DMA((4,)),
            pltpu.SemaphoreType.DMA,
        ],
        compiler_params=pltpu.CompilerParams(vmem_limit_bytes=PACK_BYTES),
        name="pack_tiles",
    )(*along, tile_values)


DST_BIT, SRC_BIT, PLACE_BIT = 10, 16, 24


def own_kernel(tiles_ref, codes_ref, out_ref, own_ref, sems):
    rows = tiles_ref.shape[0]
    moves = ((tiles_ref, out_ref.at[pl.ds(0, rows)]), (codes_ref, own_ref))
    copies = [pltpu.make_async_copy(*move, sems.at[i]) for i, move in enumerate(moves)]
    for copy in copies:
        copy.start()
    out_ref[out_ref.shape[0] - out_ref.shape[1] :] = jnp.zeros(
        (out_ref.shape[1], out_ref.shape[1]), out_ref.dtype
    )
    for copy in copies:
        copy.wait()


def own_tiles(tiles, codes, spots):
    wide = tiles.shape[1]
    laid = jax.ShapeDtypeStruct((spots * wide, wide), tiles.dtype)
    return pl.pallas_call(
        own_kernel,
        out_shape=(laid, jax.ShapeDtypeStruct(codes.shape, codes.dtype)),
        in_specs=[ANY, ANY],
        out_specs=(VMEM, VMEM),
        scratch_shapes=[pltpu.SemaphoreType.DMA((2,))],
        compiler_params=params(laid),
        name="own_tiles",
    )(tiles, codes)


def collect_kernel(plane, cols, slots, blocks, tiles, own_ref, laid_ref, *refs):
    tile_refs, refs = refs[: (plane - 1) * cols], refs[(plane - 1) * cols :]
    out_ref, plan_ref, count_ref, *scratch = refs
    rows_ref, words_ref, codes_ref, row_sems, word_sem, tile_sems = scratch
    _, place, col, _ = position(plane)
    size = out_ref.shape[1]
    looks = []
    for k in range(plane):
        ref = own_ref
        if k > 0:
            ref = tile_refs[(k - 1) * cols].at[pl.ds(slots * size, CODE_ROWS)]
        copy = pltpu.make_async_copy(ref, rows_ref.at[k], row_sems.at[k])
        copy.start()
        looks.append(copy)
    copies, first, rows = [], tiles * size, slots * size
    for i, ref in enumerate(tile_refs):
        copy = pltpu.make_async_copy(
            ref.at[pl.ds(0, rows)], out_ref.at[pl.ds(first, rows)], tile_sems.at[i]
        )
        copy.start()
        copies.append(copy)
        first += rows
    words_ref[...] = jnp.zeros_like(words_ref)
    for k, copy in enumerate(looks):
        copy.wait()
        rows = rows_ref[k].astype(jnp.float32).astype(jnp.int32)
        source = rows[3:4] * blocks + rows[2:3]
        word = (rows[0:1] << PLACE_BIT) + (source << SRC_BIT)
        words_ref[k : k + 1] = word + ((rows[1:2] + k * blocks) << DST_BIT)
    copy = pltpu.make_async_copy(words_ref, codes_ref, word_sem)
    copy.start()
    copy.wait()
    found = jnp.int32(0)
    for k in range(plane):

        def step(t, carry, k=k):
            at, slot = carry
            code = codes_ref[k, t]
            if k == 0:
                spot = t
            else:
                column = remainder(slot + (cols - col), cols)
                spot = tiles + ((k - 1) * cols + column) * slots + quotient(slot, cols)
            plan_ref[at] = (code & ((1 << PLACE_BIT) - 1)) + spot
            one = ((code >> PLACE_BIT) == place).astype(jnp.int32)
            return at + one, slot + one

        found, _ = lax.fori_loop(0, tiles, step, (found, jnp.int32(0)), unroll=8)
    for i in range(UNROLL):
        plan_ref[found + i] = first // size
    count_ref[0] = quotient(found + UNROLL - 1, UNROLL)
    for copy in copies:
        copy.wait()


def collect_tiles(codes, laid, tile_parts, plane, cols, slots, blocks, tiles):
    wide = laid.shape[1]
    entries = plane * tiles + UNROLL
    high = -(-plane // 8) * 8
    return pl.pallas_call(
        functools.partial(collect_kernel, plane, cols, slots, blocks, tiles),
        out_shape=(
            jax.ShapeDtypeStruct(laid.shape, laid.dtype),
            jax.ShapeDtypeStruct((entries,), jnp.int32),
            jax.ShapeDtypeStruct((1,), jnp.int32),
        ),
        in_specs=[ANY, VMEM] + [ANY] * len(tile_parts),
        out_specs=(VMEM, SMEM, SMEM),
        scratch_shapes=[
            pltpu.VMEM((plane, CODE_ROWS, wide), jnp.bfloat16),
            pltpu.VMEM((high, wide), jnp.int32),
            pltpu.SMEM((high, wide), jnp.int32),
            pltpu.SemaphoreType.DMA((plane,)),
            pltpu.SemaphoreType.DMA,
            pltpu.SemaphoreType.DMA((len(tile_parts),)),
        ],
        input_output_aliases={1: 0},
        compiler_params=params(laid),
        name="collect_tiles",
    )(codes, laid, *tile_parts)


def planned(plan_ref, t):
    entry = plan_ref[t]
    spot = entry & ((1 << DST_BIT) - 1)
    return spot, (entry >> DST_BIT) & ((1 << (SRC_BIT - DST_BIT)) - 1), entry >> SRC_BIT


def block_rows(index, size):
    return pl.ds(pl.multiple_of(index * size, size), size)


def forward_kernel(line, lanes, plane, plan_ref, count_ref, tiles_ref, *refs):
    part_refs, refs = refs[: 2 * line - 1], refs[2 * line - 1 :]
    out_refs, (nodes_ref, acc_ref, part_sems) = refs[:-3], refs[-3:]
    rows, width = part_refs[0].shape[0], nodes_ref.shape[1]
    size = tiles_ref.shape[1]
    mine, _, _, way = position(plane)

    def each_part(act):
        for i, ref in enumerate(part_refs):
            source = mine + way * (i - (line - 1))

            @pl.when((source >= 0) & (source < line))
            def _():
                here = ref.at[:, lanes] if ref.shape != (rows, width) else ref
                act(
                    pltpu.make_async_copy(
                        here, nodes_ref.at[block_rows(source, rows)], part_sems.at[i]
                    )
                )

    each_part(lambda copy: copy.start())
    acc_ref[...] = jnp.zeros_like(acc_ref)
    each_part(lambda copy: copy.wait())

    def step(i, carry):
        ready = None
        for spot, dst, src in [planned(plan_ref, i * UNROLL + j) for j in range(UNROLL)]:
            product = jnp.dot(
                tiles_ref[block_rows(spot, size)],
                nodes_ref[block_rows(src, size)],
                preferred_element_type=jnp.float32,
            )
            if ready is not None:
                acc_ref[ready[0]] += ready[1]
            ready = block_rows(dst, size), product
        acc_ref[ready[0]] += ready[1]
        return carry

    lax.fori_loop(0, count_ref[0], step, 0)
    for k, ref in enumerate(out_refs):
        ref[...] = acc_ref[k * rows : (k + 1) * rows].astype(ref.dtype)


def forward_tiles(plan, count, tiles, node_parts, plane, lanes):
    line = (len(node_parts) + 1) // 2
    rows, width = node_parts[0].shape[0], lanes.size
    kinds = [jnp.float32] + [jnp.bfloat16] * (plane - 1)
    outs = tuple(jax.ShapeDtypeStruct((rows, width), kind) for kind in kinds)
    scratch = [
        pltpu.VMEM((line * rows, width), jnp.bfloat16),
        pltpu.VMEM((plane * rows, width), jnp.float32),
    ]
    return pl.pallas_call(
        functools.partial(forward_kernel, line, lanes, plane),
        out_shape=outs,
        in_specs=[SMEM] * 2 + [VMEM] + [ANY] * len(node_parts),
        out_specs=(VMEM,) * plane,
        scratch_shapes=scratch + [pltpu.SemaphoreType.DMA((len(node_parts),))],
        compiler_params=params(tiles, *outs, *scratch),
        name="forward_tiles",
    )(plan, count, tiles, *node_parts)


def dense_kernel(chunk, halves, labels_ref, weight_ref, *refs):
    parts, (act_ref, out_grad_ref, agg_grad_ref) = refs[:-3], refs[-3:]
    rows, part_width = parts[0].shape
    width = part_width * halves
    features = weight_ref.shape[0]
    size = labels_ref.shape[1]

    def rows_step(i, carry):
        here = block_rows(i, chunk)
        agg = jnp.concatenate([part[here, :] for part in parts], axis=1)
        hidden = jnp.dot(agg, weight_ref[...], preferred_element_type=jnp.float32)
        sigmoid = 0.5 * jnp.tanh(0.5 * hidden) + 0.5
        activated = hidden * sigmoid
        act_ref[here, :] = activated[:, :width].astype(act_ref.dtype)
        slopes = sigmoid * (1.0 + hidden * (1.0 - sigmoid))
        named = []
        for b in range(chunk // size):
            across = labels_ref[pl.ds(i * (chunk // size) + b, 1), :]
            named.append(jnp.broadcast_to(across, (size, size)).T)
        named = jnp.concatenate(named, axis=0)
        ids = lax.broadcasted_iota(jnp.int32, (chunk, size), 1).astype(jnp.float32)
        target = jnp.concatenate(
            [(named == ids + f * size).astype(jnp.float32) for f in range(features // size)],
            axis=1,
        )
        out_grad = ((activated - target) * slopes).astype(jnp.bfloat16)
        out_grad_ref[here, :] = out_grad
        agg_grad_ref[here, :] = lax.dot_general(
            out_grad,
            weight_ref[:part_width, :],
            (((1,), (1,)), ((), ())),
            preferred_element_type=jnp.float32,
        ).astype(agg_grad_ref.dtype)
        return carry

    lax.fori_loop(0, rows // chunk, rows_step, 0)


def dense(labels, weight, parts, halves):
    rows, part_width = parts[0].shape
    chunk = math.gcd(rows, 256)
    outs = tuple(
        jax.ShapeDtypeStruct((rows, width), jnp.bfloat16)
        for width in (part_width * halves, weight.shape[0], part_width)
    )
    return pl.pallas_call(
        functools.partial(dense_kernel, chunk, halves),
        out_shape=outs,
        in_specs=[VMEM] * (2 + len(parts)),
        out_specs=(VMEM,) * 3,
        compiler_params=params(labels, weight, *parts, *outs),
        name="dense",
    )(labels, weight, *parts)


def grads_kernel(scale, halves, weight_ref, out_grad_ref, *refs):
    parts, (terms_ref, *agg_grad_refs) = refs[: -halves], refs[-halves:]
    part_width = parts[0].shape[1]
    for h, ref in enumerate(agg_grad_refs, 1):
        ref[...] = lax.dot_general(
            out_grad_ref[...],
            weight_ref[h * part_width : (h + 1) * part_width, :],
            (((1,), (1,)), ((), ())),
            preferred_element_type=jnp.float32,
        ).astype(ref.dtype)
    for i, part in enumerate(parts):
        terms = lax.dot_general(
            part[...],
            out_grad_ref[:, : part_width * halves],
            (((0,), (0,)), ((), ())),
            preferred_element_type=jnp.float32,
        )
        terms_ref[i * part_width : (i + 1) * part_width] = (terms * scale).astype(terms_ref.dtype)


def grads(weight, out_grad, parts, halves, node_total):
    rows, part_width = parts[0].shape
    outs = (jax.ShapeDtypeStruct((weight.shape[0], part_width * halves), jnp.bfloat16),) + (
        jax.ShapeDtypeStruct((rows, part_width), jnp.bfloat16),
    ) * (halves - 1)
    return pl.pallas_call(
        functools.partial(grads_kernel, 1.0 / math.sqrt(node_total), halves),
        out_shape=outs,
        in_specs=[VMEM] * (2 + len(parts)),
        out_specs=(VMEM,) * halves,
        compiler_params=params(weight, out_grad, *parts, *outs),
        name="grads",
    )(weight, out_grad, *parts)


def spread_kernel(line, plane, plan_ref, count_ref, tiles_ref, *refs):
    grad_refs, refs = refs[:plane], refs[plane:]
    out_refs, (grads_ref, acc_ref, grad_sems) = refs[:-3], refs[-3:]
    rows = grad_refs[0].shape[0]
    size = tiles_ref.shape[1]
    mine, _, _, way = position(plane)
    copies = []
    for k, ref in enumerate(grad_refs):
        copy = pltpu.make_async_copy(ref, grads_ref.at[pl.ds(k * rows, rows)], grad_sems.at[k])
        copy.start()
        copies.append(copy)
    acc_ref[...] = jnp.zeros_like(acc_ref)
    for copy in copies:
        copy.wait()

    def step(i, carry):
        ready = None
        for spot, dst, src in [planned(plan_ref, i * UNROLL + j) for j in range(UNROLL)]:
            product = lax.dot_general(
                tiles_ref[block_rows(spot, size)],
                grads_ref[block_rows(dst, size)],
                (((0,), (0,)), ((), ())),
                preferred_element_type=jnp.float32,
            )
            if ready is not None:
                acc_ref[ready[0]] += ready[1]
            ready = block_rows(src, size), product
        acc_ref[ready[0]] += ready[1]
        return carry

    lax.fori_loop(0, count_ref[0], step, 0)
    for i, ref in enumerate(out_refs):
        target = mine + way * (i - (line - 1))

        @pl.when((target >= 0) & (target < line))
        def _():
            ref[...] = acc_ref[block_rows(target, rows)].astype(ref.dtype)


def spread_tiles(plan, count, tiles, grad_parts, line):
    plane = len(grad_parts)
    rows, width = grad_parts[0].shape
    kinds = [jnp.float32 if i == line - 1 else jnp.bfloat16 for i in range(2 * line - 1)]
    outs = tuple(jax.ShapeDtypeStruct((rows, width), kind) for kind in kinds)
    scratch = [
        pltpu.VMEM((plane * rows, width), jnp.bfloat16),
        pltpu.VMEM((line * rows, width), jnp.float32),
    ]
    return pl.pallas_call(
        functools.partial(spread_kernel, line, plane),
        out_shape=outs,
        in_specs=[SMEM] * 2 + [VMEM] + [ANY] * plane,
        out_specs=(VMEM,) * (2 * line - 1),
        scratch_shapes=scratch + [pltpu.SemaphoreType.DMA((plane,))],
        compiler_params=params(tiles, *outs, *scratch),
        name="spread_tiles",
    )(plan, count, tiles, *grad_parts)


def along_line(x, line, plane, cols, step, reach):
    pairs = []
    for z in range(line):
        for q in range(plane):
            for c in range(cols):
                way = 1 - 2 * (c & 1)
                to, end = z + way * step, z + way * reach
                if 0 <= to < line and 0 <= end < line:
                    pairs.append(((z * plane + q) * cols + c, (to * plane + q) * cols + c))
    return lax.ppermute(x, ("rows", "cols"), pairs)


def line_gather(x, after, line, plane, cols, lanes):
    move = lambda part, step, reach: along_line(part, line, plane, cols, step, reach)
    later, _ = lax.optimization_barrier((x, after))
    up, down = [x], [later]
    for k in range(1, line - 1):
        up.append(move(up[-1], 1, 1 - k))
        down.append(move(down[-1], -1, k - 1))
    parts, high, low = [], up[-1], down[-1]
    for part in lanes:
        first = move(high[:, part], 1, 2 - line)
        last = move(low[:, part], -1, line - 2)
        parts.append([first] + up[:0:-1] + down + [last])
    return parts


def line_sum(terms, line, plane, cols, beside):
    moved, late = {1: None, -1: None}, None
    for k in range(line - 1, 0, -1):
        for step in moved:
            term = terms[line - 1 + step * k]
            if moved[step] is not None:
                total = term.astype(jnp.float32) + moved[step].astype(jnp.float32)
                term = total.astype(term.dtype)
            moved[step] = along_line(term, line, plane, cols, step, step * k)
        if k == line - 1 and beside is not None:
            moved, beside = lax.optimization_barrier((moved, beside))
        if k > 1:
            late = tuple(moved.values())
    return [terms[line - 1], moved[1], moved[-1]], beside, late


def finish_kernel(halves, *refs):
    out_ref, refs = refs[-1], refs[:-1]
    each = len(refs) // halves
    width = refs[0].shape[1]
    for h in range(halves):
        total = refs[h * each][...]
        for ref in refs[h * each + 1 : (h + 1) * each]:
            total += ref[...].astype(jnp.float32)
        out_ref[:, h * width : (h + 1) * width] = total.astype(out_ref.dtype)


def finish(pieces):
    flat = [piece for half in pieces for piece in half]
    rows, width = flat[0].shape
    out = jax.ShapeDtypeStruct((rows, width * len(pieces)), jnp.bfloat16)
    return pl.pallas_call(
        functools.partial(finish_kernel, len(pieces)),
        out_shape=out,
        in_specs=[VMEM] * len(flat),
        out_specs=VMEM,
        compiler_params=params(out, *flat),
        name="finish",
    )(*flat)


def sum_apart(terms, first, end, rows):
    while first < end:
        other = shuffle(terms, [(r, r ^ first) for r in range(rows)])
        total = terms.astype(jnp.float32) + other.astype(jnp.float32)
        terms = total.astype(terms.dtype)
        first *= 2
    return terms


def prepare_kernel(cols, labels_ref, weight_ref, own_labels_ref, own_first_ref, wide_ref):
    col = lax.axis_index("cols")
    features = weight_ref.shape[0]
    width = features // cols
    labels = labels_ref[...] - col * width
    own_labels_ref[...] = jnp.where(labels < 0, labels + features, labels).astype(jnp.float32)
    for c in range(cols):
        row = remainder(col + c, cols) * width
        rows = weight_ref[pl.ds(pl.multiple_of(row, width), width), :]
        wide_ref[c * width : (c + 1) * width] = rows.astype(jnp.float32)
    turned = pltpu.roll(wide_ref[...], remainder(cols - col, cols) * width, axis=1)
    own_first_ref[...] = turned.astype(own_first_ref.dtype)


def prepare(labels, weight, cols):
    outs = (jax.ShapeDtypeStruct(labels.shape, jnp.float32), weight)
    wide = pltpu.VMEM(weight.shape, jnp.float32)
    return pl.pallas_call(
        functools.partial(prepare_kernel, cols),
        out_shape=(outs[0], jax.ShapeDtypeStruct(weight.shape, weight.dtype)),
        in_specs=[VMEM, VMEM],
        out_specs=(VMEM, VMEM),
        scratch_shapes=[wide],
        compiler_params=params(weight, weight, wide, wide),
        name="prepare",
    )(labels, weight)


def weight_kernel(cols, mine_ref, other_ref, out_ref):
    col = lax.axis_index("cols")
    width = out_ref.shape[1]
    for c in range(cols):
        here = pl.ds(c * width, width)
        total = mine_ref[here].astype(jnp.float32) + other_ref[here].astype(jnp.float32)
        row = remainder(col + c, cols) * width
        out_ref[pl.ds(pl.multiple_of(row, width), width)] = total


def finish_weight(mine, other, cols):
    out = jax.ShapeDtypeStruct(mine.shape, jnp.float32)
    return pl.pallas_call(
        functools.partial(weight_kernel, cols),
        out_shape=out,
        in_specs=[VMEM, VMEM],
        out_specs=VMEM,
        compiler_params=params(mine, other, out),
        name="finish_weight",
    )(mine, other)


def per_device(node_features, weight, tile_values, tile_row, source_owner, source_block, labels):
    local_rows, width = node_features.shape
    n_tiles, block_size = tile_values.shape[:2]
    blocks = local_rows // block_size
    rows, cols = lax.axis_size("rows"), lax.axis_size("cols")
    plane = math.gcd(rows, LARGEST_PLANE)
    line = rows // plane
    halves = 2 if width % 256 == 0 else 1
    part_width = width // halves
    slots = -(-min(n_tiles, line * (2 * n_tiles // rows)) // cols)
    owners = source_owner[:, 0]

    def other_cols(x):
        return [
            lax.ppermute(x, "cols", [((c + k) % cols, c) for c in range(cols)])
            for k in range(1, cols)
        ]

    lanes = [slice(h * part_width, (h + 1) * part_width) for h in range(halves)]
    *packed, codes = pack_tiles(
        owners, tile_row, source_block, tile_values, plane, cols, slots
    )
    node_parts = line_gather(node_features, packed, line, plane, cols, lanes)
    spots = n_tiles + (plane - 1) * cols * slots + 1
    flat = tile_values.reshape(n_tiles * block_size, block_size)
    early = own_tiles(flat, codes, spots) + prepare(labels.reshape(blocks, block_size), weight, cols)
    tile_parts = []
    for k in range(1, plane):
        arrived = across_plane(packed[k - 1], k, line, plane)
        if k == 1:
            arrived, early = lax.optimization_barrier((arrived, early))
        tile_parts += [arrived] + other_cols(arrived)
    laid, codes, own_labels, own_first = early
    tiles, plan, count = collect_tiles(
        codes, laid, tile_parts, plane, cols, slots, blocks, n_tiles
    )

    aggregated = []
    for h in range(halves):
        here = pl.ds(h * part_width, part_width)
        sums = forward_tiles(plan, count, tiles, node_parts[h], plane, here)
        total = sums[0]
        for k in range(1, plane):
            total = total + across_plane(sums[k], k, line, plane).astype(jnp.float32)
        mine = total.astype(jnp.bfloat16)
        aggregated.append([mine] + other_cols(mine))
    parts = [aggregated[h][c] for c in range(cols) for h in range(halves)]

    activations, out_grad, agg_grad = dense(own_labels, own_first, parts, halves)
    weight_terms, *agg_grads = grads(own_first, out_grad, parts, halves, local_rows * rows)

    pieces = []
    for i, agg_grad in enumerate([agg_grad] + agg_grads):
        arrived = [agg_grad] + [across_plane(agg_grad, k, line, plane) for k in range(1, plane)]
        if i == 0:
            weight_terms = sum_apart(weight_terms, plane, rows, rows)
        terms = spread_tiles(plan, count, tiles, arrived, line)
        beside = weight_terms if i == 0 else None
        half, beside, late = line_sum(terms, line, plane, cols, beside)
        if i == 0:
            weight_terms, _ = lax.optimization_barrier((beside, late))
        pieces.append(half)
    weight_terms = sum_apart(weight_terms, 1, plane // 2, rows)
    weight_terms, _ = lax.optimization_barrier((weight_terms, late))
    other = across_plane(weight_terms, plane // 2, line, plane)
    weight_grad = finish_weight(weight_terms, other, cols)
    pieces, weight_grad = lax.optimization_barrier((pieces, weight_grad))
    return activations, weight_grad, finish(pieces)


def solution(mesh):
    return jax.shard_map(
        per_device,
        mesh=mesh,
        in_specs=(
            P("rows", "cols"),
            P(),
            P("rows", None, None),
            P("rows"),
            P("rows", None),
            P("rows"),
            P("rows"),
        ),
        out_specs=(P("rows", "cols"), P(None, "cols"), P("rows", "cols")),
        check_vma=False,
    )
```

```python
import functools
import math

import jax
import jax.numpy as jnp
from jax import lax
from jax.experimental import pallas as pl
from jax.experimental.pallas import tpu as pltpu
from jax.sharding import PartitionSpec as P

VMEM = pl.BlockSpec(memory_space=pltpu.VMEM)
SMEM = pl.BlockSpec(memory_space=pltpu.SMEM)
ANY = pl.BlockSpec(memory_space=pl.ANY)
HBM = pl.BlockSpec(memory_space=pltpu.HBM)
SPARE_BYTES = 2 * 1024 * 1024
PACK_BYTES = 56 * 1024 * 1024
UNROLL = 8
LARGEST_PLANE = 4


def params(*shapes):
    room = SPARE_BYTES
    for shape in shapes:
        *lead, high, wide = shape.shape
        room += math.prod(lead) * high * (-(-wide // 128) * 128) * jnp.dtype(shape.dtype).itemsize
    return pltpu.CompilerParams(vmem_limit_bytes=room)


def quotient(x, n):
    return x >> (n.bit_length() - 1) if n & (n - 1) == 0 else lax.div(x, n)


def remainder(x, n):
    return x & (n - 1) if n & (n - 1) == 0 else lax.rem(x, n)


def position(plane):
    index, col = lax.axis_index("rows"), lax.axis_index("cols")
    return quotient(index, plane), remainder(index, plane), col, 1 - 2 * (col & 1)


def shuffle(x, pairs):
    return lax.ppermute(x, "rows", pairs)


def across_plane(x, k, line, plane):
    return shuffle(x, [(r, r ^ k) for r in range(line * plane)])


CODE_ROWS = 16


def pack_kernel(plane, cols, owner_ref, row_ref, source_ref, tiles_ref, *refs):
    out_refs, (codes_ref, *scratch) = refs[: plane - 1], refs[plane - 1 :]
    list_ref, slot_ref, owners_ref, along_ref, rows_ref, held_ref, small_sems, held_sem = scratch
    _, place, col, _ = position(plane)
    tiles, size = tiles_ref.shape[:2]
    slots = (out_refs[0].shape[0] - CODE_ROWS) // size
    spare = (plane - 1) * slots
    looks = [pltpu.make_async_copy(owner_ref, owners_ref, small_sems.at[0])]
    for i, ref in enumerate((owner_ref, row_ref, source_ref)):
        looks.append(pltpu.make_async_copy(ref, along_ref.at[i], small_sems.at[1 + i]))
    for look in looks:
        look.start()
    bulk = pltpu.make_async_copy(tiles_ref, held_ref, held_sem)
    bulk.start()
    for k in range(plane):
        slot_ref[k] = 0
    for i in range(spare):
        list_ref[i] = 0
    rows_ref[...] = jnp.zeros_like(rows_ref)
    for look in looks:
        look.wait()

    def step(t, carry):
        k = remainder(owners_ref[0, t], plane) ^ place
        slot = slot_ref[k]
        slot_ref[k] = slot + 1
        sent = (k > 0) & (remainder(slot, cols) == col)
        list_ref[jnp.where(sent, (k - 1) * slots + quotient(slot, cols), spare)] = t
        return carry

    lax.fori_loop(0, tiles, step, 0, unroll=4)
    owners = along_ref[0]
    rows_ref[0:1, :tiles] = remainder(owners, plane).astype(jnp.float32)
    rows_ref[1:2, :tiles] = along_ref[1].astype(jnp.float32)
    rows_ref[2:3, :tiles] = along_ref[2].astype(jnp.float32)
    rows_ref[3:4, :tiles] = quotient(owners, plane).astype(jnp.float32)
    codes = rows_ref[...].astype(codes_ref.dtype)
    codes_ref[...] = codes
    bulk.wait()
    for k, out_ref in enumerate(out_refs):
        for slot in range(slots):
            out_ref[slot * size : (slot + 1) * size] = held_ref[list_ref[k * slots + slot]]
        out_ref[slots * size :] = codes


def pack_tiles(owners, tile_row, source_block, tile_values, plane, cols, slots):
    tiles, size, wide = tile_values.shape
    shape = jax.ShapeDtypeStruct((slots * size + CODE_ROWS, wide), tile_values.dtype)
    codes = jax.ShapeDtypeStruct((CODE_ROWS, wide), tile_values.dtype)
    along = [x.reshape(1, tiles) for x in (owners, tile_row, source_block)]
    return pl.pallas_call(
        functools.partial(pack_kernel, plane, cols),
        out_shape=(shape,) * (plane - 1) + (codes,),
        in_specs=[HBM] * 4,
        out_specs=(VMEM,) * plane,
        scratch_shapes=[
            pltpu.SMEM(((plane - 1) * slots + 1,), jnp.int32),
            pltpu.SMEM((plane,), jnp.int32),
            pltpu.SMEM((1, tiles), jnp.int32),
            pltpu.VMEM((3, 1, tiles), jnp.int32),
            pltpu.VMEM((CODE_ROWS, wide), jnp.float32),
            pltpu.VMEM((tiles, size, wide), tile_values.dtype),
            pltpu.SemaphoreType.DMA((4,)),
            pltpu.SemaphoreType.DMA,
        ],
        compiler_params=pltpu.CompilerParams(vmem_limit_bytes=PACK_BYTES),
        name="pack_tiles",
    )(*along, tile_values)


DST_BIT, SRC_BIT, PLACE_BIT = 10, 16, 24


def own_kernel(tiles_ref, codes_ref, out_ref, own_ref, sems):
    rows = tiles_ref.shape[0]
    moves = ((tiles_ref, out_ref.at[pl.ds(0, rows)]), (codes_ref, own_ref))
    copies = [pltpu.make_async_copy(*move, sems.at[i]) for i, move in enumerate(moves)]
    for copy in copies:
        copy.start()
    out_ref[out_ref.shape[0] - out_ref.shape[1] :] = jnp.zeros(
        (out_ref.shape[1], out_ref.shape[1]), out_ref.dtype
    )
    for copy in copies:
        copy.wait()


def own_tiles(tiles, codes, spots):
    wide = tiles.shape[1]
    laid = jax.ShapeDtypeStruct((spots * wide, wide), tiles.dtype)
    return pl.pallas_call(
        own_kernel,
        out_shape=(laid, jax.ShapeDtypeStruct(codes.shape, codes.dtype)),
        in_specs=[ANY, ANY],
        out_specs=(VMEM, VMEM),
        scratch_shapes=[pltpu.SemaphoreType.DMA((2,))],
        compiler_params=params(laid),
        name="own_tiles",
    )(tiles, codes)


def collect_kernel(plane, cols, slots, blocks, tiles, own_ref, laid_ref, *refs):
    tile_refs, refs = refs[: (plane - 1) * cols], refs[(plane - 1) * cols :]
    out_ref, plan_ref, count_ref, *scratch = refs
    rows_ref, words_ref, codes_ref, row_sems, word_sem, tile_sems = scratch
    _, place, col, _ = position(plane)
    size = out_ref.shape[1]
    looks = []
    for k in range(plane):
        ref = own_ref
        if k > 0:
            ref = tile_refs[(k - 1) * cols].at[pl.ds(slots * size, CODE_ROWS)]
        copy = pltpu.make_async_copy(ref, rows_ref.at[k], row_sems.at[k])
        copy.start()
        looks.append(copy)
    copies, first, rows = [], tiles * size, slots * size
    for i, ref in enumerate(tile_refs):
        copy = pltpu.make_async_copy(
            ref.at[pl.ds(0, rows)], out_ref.at[pl.ds(first, rows)], tile_sems.at[i]
        )
        copy.start()
        copies.append(copy)
        first += rows
    words_ref[...] = jnp.zeros_like(words_ref)
    for k, copy in enumerate(looks):
        copy.wait()
        rows = rows_ref[k].astype(jnp.float32).astype(jnp.int32)
        source = rows[3:4] * blocks + rows[2:3]
        word = (rows[0:1] << PLACE_BIT) + (source << SRC_BIT)
        words_ref[k : k + 1] = word + ((rows[1:2] + k * blocks) << DST_BIT)
    copy = pltpu.make_async_copy(words_ref, codes_ref, word_sem)
    copy.start()
    copy.wait()
    found = jnp.int32(0)
    for k in range(plane):

        def step(t, carry, k=k):
            at, slot = carry
            code = codes_ref[k, t]
            if k == 0:
                spot = t
            else:
                column = remainder(slot + (cols - col), cols)
                spot = tiles + ((k - 1) * cols + column) * slots + quotient(slot, cols)
            plan_ref[at] = (code & ((1 << PLACE_BIT) - 1)) + spot
            one = ((code >> PLACE_BIT) == place).astype(jnp.int32)
            return at + one, slot + one

        found, _ = lax.fori_loop(0, tiles, step, (found, jnp.int32(0)), unroll=8)
    for i in range(UNROLL):
        plan_ref[found + i] = first // size
    count_ref[0] = quotient(found + UNROLL - 1, UNROLL)
    for copy in copies:
        copy.wait()


def collect_tiles(codes, laid, tile_parts, plane, cols, slots, blocks, tiles):
    wide = laid.shape[1]
    entries = plane * tiles + UNROLL
    high = -(-plane // 8) * 8
    return pl.pallas_call(
        functools.partial(collect_kernel, plane, cols, slots, blocks, tiles),
        out_shape=(
            jax.ShapeDtypeStruct(laid.shape, laid.dtype),
            jax.ShapeDtypeStruct((entries,), jnp.int32),
            jax.ShapeDtypeStruct((1,), jnp.int32),
        ),
        in_specs=[ANY, VMEM] + [ANY] * len(tile_parts),
        out_specs=(VMEM, SMEM, SMEM),
        scratch_shapes=[
            pltpu.VMEM((plane, CODE_ROWS, wide), jnp.bfloat16),
            pltpu.VMEM((high, wide), jnp.int32),
            pltpu.SMEM((high, wide), jnp.int32),
            pltpu.SemaphoreType.DMA((plane,)),
            pltpu.SemaphoreType.DMA,
            pltpu.SemaphoreType.DMA((len(tile_parts),)),
        ],
        input_output_aliases={1: 0},
        compiler_params=params(laid),
        name="collect_tiles",
    )(codes, laid, *tile_parts)


def planned(plan_ref, t):
    entry = plan_ref[t]
    spot = entry & ((1 << DST_BIT) - 1)
    return spot, (entry >> DST_BIT) & ((1 << (SRC_BIT - DST_BIT)) - 1), entry >> SRC_BIT


def block_rows(index, size):
    return pl.ds(pl.multiple_of(index * size, size), size)


def forward_kernel(line, lanes, plane, plan_ref, count_ref, tiles_ref, *refs):
    part_refs, refs = refs[: 2 * line - 1], refs[2 * line - 1 :]
    out_refs, (nodes_ref, acc_ref, part_sems) = refs[:-3], refs[-3:]
    rows, width = part_refs[0].shape[0], nodes_ref.shape[1]
    size = tiles_ref.shape[1]
    mine, _, _, way = position(plane)

    def each_part(act):
        for i, ref in enumerate(part_refs):
            source = mine + way * (i - (line - 1))

            @pl.when((source >= 0) & (source < line))
            def _():
                here = ref.at[:, lanes] if ref.shape != (rows, width) else ref
                act(
                    pltpu.make_async_copy(
                        here, nodes_ref.at[block_rows(source, rows)], part_sems.at[i]
                    )
                )

    each_part(lambda copy: copy.start())
    acc_ref[...] = jnp.zeros_like(acc_ref)
    each_part(lambda copy: copy.wait())

    def step(i, carry):
        ready = None
        for spot, dst, src in [planned(plan_ref, i * UNROLL + j) for j in range(UNROLL)]:
            product = jnp.dot(
                tiles_ref[block_rows(spot, size)],
                nodes_ref[block_rows(src, size)],
                preferred_element_type=jnp.float32,
            )
            if ready is not None:
                acc_ref[ready[0]] += ready[1]
            ready = block_rows(dst, size), product
        acc_ref[ready[0]] += ready[1]
        return carry

    lax.fori_loop(0, count_ref[0], step, 0)
    for k, ref in enumerate(out_refs):
        ref[...] = acc_ref[k * rows : (k + 1) * rows].astype(ref.dtype)


def forward_tiles(plan, count, tiles, node_parts, plane, lanes):
    line = (len(node_parts) + 1) // 2
    rows, width = node_parts[0].shape[0], lanes.size
    kinds = [jnp.float32] + [jnp.bfloat16] * (plane - 1)
    outs = tuple(jax.ShapeDtypeStruct((rows, width), kind) for kind in kinds)
    scratch = [
        pltpu.VMEM((line * rows, width), jnp.bfloat16),
        pltpu.VMEM((plane * rows, width), jnp.float32),
    ]
    return pl.pallas_call(
        functools.partial(forward_kernel, line, lanes, plane),
        out_shape=outs,
        in_specs=[SMEM] * 2 + [VMEM] + [ANY] * len(node_parts),
        out_specs=(VMEM,) * plane,
        scratch_shapes=scratch + [pltpu.SemaphoreType.DMA((len(node_parts),))],
        compiler_params=params(tiles, *outs, *scratch),
        name="forward_tiles",
    )(plan, count, tiles, *node_parts)


def dense_kernel(chunk, halves, labels_ref, weight_ref, *refs):
    parts, (act_ref, out_grad_ref, agg_grad_ref) = refs[:-3], refs[-3:]
    rows, part_width = parts[0].shape
    width = part_width * halves
    features = weight_ref.shape[0]
    size = labels_ref.shape[1]

    def rows_step(i, carry):
        here = block_rows(i, chunk)
        agg = jnp.concatenate([part[here, :] for part in parts], axis=1)
        hidden = jnp.dot(agg, weight_ref[...], preferred_element_type=jnp.float32)
        sigmoid = jax.nn.sigmoid(hidden)
        activated = hidden * sigmoid
        act_ref[here, :] = activated[:, :width].astype(act_ref.dtype)
        slopes = sigmoid * (1.0 + hidden * (1.0 - sigmoid))
        named = []
        for b in range(chunk // size):
            across = labels_ref[pl.ds(i * (chunk // size) + b, 1), :]
            named.append(jnp.broadcast_to(across, (size, size)).T)
        named = jnp.concatenate(named, axis=0)
        ids = lax.broadcasted_iota(jnp.int32, (chunk, size), 1).astype(jnp.float32)
        target = jnp.concatenate(
            [(named == ids + f * size).astype(jnp.float32) for f in range(features // size)],
            axis=1,
        )
        out_grad = ((activated - target) * slopes).astype(jnp.bfloat16)
        out_grad_ref[here, :] = out_grad
        agg_grad_ref[here, :] = lax.dot_general(
            out_grad,
            weight_ref[:part_width, :],
            (((1,), (1,)), ((), ())),
            preferred_element_type=jnp.float32,
        ).astype(agg_grad_ref.dtype)
        return carry

    lax.fori_loop(0, rows // chunk, rows_step, 0)


def dense(labels, weight, parts, halves):
    rows, part_width = parts[0].shape
    chunk = math.gcd(rows, 256)
    outs = tuple(
        jax.ShapeDtypeStruct((rows, width), jnp.bfloat16)
        for width in (part_width * halves, weight.shape[0], part_width)
    )
    return pl.pallas_call(
        functools.partial(dense_kernel, chunk, halves),
        out_shape=outs,
        in_specs=[VMEM] * (2 + len(parts)),
        out_specs=(VMEM,) * 3,
        compiler_params=params(labels, weight, *parts, *outs),
        name="dense",
    )(labels, weight, *parts)


def grads_kernel(scale, halves, weight_ref, out_grad_ref, *refs):
    parts, (terms_ref, *agg_grad_refs) = refs[: -halves], refs[-halves:]
    part_width = parts[0].shape[1]
    for h, ref in enumerate(agg_grad_refs, 1):
        ref[...] = lax.dot_general(
            out_grad_ref[...],
            weight_ref[h * part_width : (h + 1) * part_width, :],
            (((1,), (1,)), ((), ())),
            preferred_element_type=jnp.float32,
        ).astype(ref.dtype)
    for i, part in enumerate(parts):
        terms = lax.dot_general(
            part[...],
            out_grad_ref[:, : part_width * halves],
            (((0,), (0,)), ((), ())),
            preferred_element_type=jnp.float32,
        )
        terms_ref[i * part_width : (i + 1) * part_width] = (terms * scale).astype(terms_ref.dtype)


def grads(weight, out_grad, parts, halves, node_total):
    rows, part_width = parts[0].shape
    outs = (jax.ShapeDtypeStruct((weight.shape[0], part_width * halves), jnp.bfloat16),) + (
        jax.ShapeDtypeStruct((rows, part_width), jnp.bfloat16),
    ) * (halves - 1)
    return pl.pallas_call(
        functools.partial(grads_kernel, 1.0 / math.sqrt(node_total), halves),
        out_shape=outs,
        in_specs=[VMEM] * (2 + len(parts)),
        out_specs=(VMEM,) * halves,
        compiler_params=params(weight, out_grad, *parts, *outs),
        name="grads",
    )(weight, out_grad, *parts)


def spread_kernel(line, plane, plan_ref, count_ref, tiles_ref, *refs):
    grad_refs, refs = refs[:plane], refs[plane:]
    out_refs, (grads_ref, acc_ref, grad_sems) = refs[:-3], refs[-3:]
    rows = grad_refs[0].shape[0]
    size = tiles_ref.shape[1]
    mine, _, _, way = position(plane)
    copies = []
    for k, ref in enumerate(grad_refs):
        copy = pltpu.make_async_copy(ref, grads_ref.at[pl.ds(k * rows, rows)], grad_sems.at[k])
        copy.start()
        copies.append(copy)
    acc_ref[...] = jnp.zeros_like(acc_ref)
    for copy in copies:
        copy.wait()

    def step(i, carry):
        ready = None
        for spot, dst, src in [planned(plan_ref, i * UNROLL + j) for j in range(UNROLL)]:
            product = lax.dot_general(
                tiles_ref[block_rows(spot, size)],
                grads_ref[block_rows(dst, size)],
                (((0,), (0,)), ((), ())),
                preferred_element_type=jnp.float32,
            )
            if ready is not None:
                acc_ref[ready[0]] += ready[1]
            ready = block_rows(src, size), product
        acc_ref[ready[0]] += ready[1]
        return carry

    lax.fori_loop(0, count_ref[0], step, 0)
    for i, ref in enumerate(out_refs):
        target = mine + way * (i - (line - 1))

        @pl.when((target >= 0) & (target < line))
        def _():
            ref[...] = acc_ref[block_rows(target, rows)].astype(ref.dtype)


def spread_tiles(plan, count, tiles, grad_parts, line):
    plane = len(grad_parts)
    rows, width = grad_parts[0].shape
    kinds = [jnp.float32 if i == line - 1 else jnp.bfloat16 for i in range(2 * line - 1)]
    outs = tuple(jax.ShapeDtypeStruct((rows, width), kind) for kind in kinds)
    scratch = [
        pltpu.VMEM((plane * rows, width), jnp.bfloat16),
        pltpu.VMEM((line * rows, width), jnp.float32),
    ]
    return pl.pallas_call(
        functools.partial(spread_kernel, line, plane),
        out_shape=outs,
        in_specs=[SMEM] * 2 + [VMEM] + [ANY] * plane,
        out_specs=(VMEM,) * (2 * line - 1),
        scratch_shapes=scratch + [pltpu.SemaphoreType.DMA((plane,))],
        compiler_params=params(tiles, *outs, *scratch),
        name="spread_tiles",
    )(plan, count, tiles, *grad_parts)


def along_line(x, line, plane, cols, step, reach):
    pairs = []
    for z in range(line):
        for q in range(plane):
            for c in range(cols):
                way = 1 - 2 * (c & 1)
                to, end = z + way * step, z + way * reach
                if 0 <= to < line and 0 <= end < line:
                    pairs.append(((z * plane + q) * cols + c, (to * plane + q) * cols + c))
    return lax.ppermute(x, ("rows", "cols"), pairs)


def line_gather(x, after, line, plane, cols, lanes):
    move = lambda part, step, reach: along_line(part, line, plane, cols, step, reach)
    later, _ = lax.optimization_barrier((x, after))
    up, down = [x], [later]
    for k in range(1, line - 1):
        up.append(move(up[-1], 1, 1 - k))
        down.append(move(down[-1], -1, k - 1))
    parts, high, low = [], up[-1], down[-1]
    for part in lanes:
        first = move(high[:, part], 1, 2 - line)
        last = move(low[:, part], -1, line - 2)
        parts.append([first] + up[:0:-1] + down + [last])
    return parts


def line_sum(terms, line, plane, cols, beside):
    moved, late = {1: None, -1: None}, None
    for k in range(line - 1, 0, -1):
        for step in moved:
            term = terms[line - 1 + step * k]
            if moved[step] is not None:
                total = term.astype(jnp.float32) + moved[step].astype(jnp.float32)
                term = total.astype(term.dtype)
            moved[step] = along_line(term, line, plane, cols, step, step * k)
        if k == line - 1 and beside is not None:
            moved, beside = lax.optimization_barrier((moved, beside))
        if k > 1:
            late = tuple(moved.values())
    return [terms[line - 1], moved[1], moved[-1]], beside, late


def finish_kernel(halves, *refs):
    out_ref, refs = refs[-1], refs[:-1]
    each = len(refs) // halves
    width = refs[0].shape[1]
    for h in range(halves):
        total = refs[h * each][...]
        for ref in refs[h * each + 1 : (h + 1) * each]:
            total += ref[...].astype(jnp.float32)
        out_ref[:, h * width : (h + 1) * width] = total.astype(out_ref.dtype)


def finish(pieces):
    flat = [piece for half in pieces for piece in half]
    rows, width = flat[0].shape
    out = jax.ShapeDtypeStruct((rows, width * len(pieces)), jnp.bfloat16)
    return pl.pallas_call(
        functools.partial(finish_kernel, len(pieces)),
        out_shape=out,
        in_specs=[VMEM] * len(flat),
        out_specs=VMEM,
        compiler_params=params(out, *flat),
        name="finish",
    )(*flat)


def sum_apart(terms, first, end, rows):
    while first < end:
        other = shuffle(terms, [(r, r ^ first) for r in range(rows)])
        total = terms.astype(jnp.float32) + other.astype(jnp.float32)
        terms = total.astype(terms.dtype)
        first *= 2
    return terms


def prepare_kernel(cols, labels_ref, weight_ref, own_labels_ref, own_first_ref, wide_ref):
    col = lax.axis_index("cols")
    features = weight_ref.shape[0]
    width = features // cols
    labels = labels_ref[...] - col * width
    own_labels_ref[...] = jnp.where(labels < 0, labels + features, labels).astype(jnp.float32)
    for c in range(cols):
        row = remainder(col + c, cols) * width
        rows = weight_ref[pl.ds(pl.multiple_of(row, width), width), :]
        wide_ref[c * width : (c + 1) * width] = rows.astype(jnp.float32)
    turned = pltpu.roll(wide_ref[...], remainder(cols - col, cols) * width, axis=1)
    own_first_ref[...] = turned.astype(own_first_ref.dtype)


def prepare(labels, weight, cols):
    outs = (jax.ShapeDtypeStruct(labels.shape, jnp.float32), weight)
    wide = pltpu.VMEM(weight.shape, jnp.float32)
    return pl.pallas_call(
        functools.partial(prepare_kernel, cols),
        out_shape=(outs[0], jax.ShapeDtypeStruct(weight.shape, weight.dtype)),
        in_specs=[VMEM, VMEM],
        out_specs=(VMEM, VMEM),
        scratch_shapes=[wide],
        compiler_params=params(weight, weight, wide, wide),
        name="prepare",
    )(labels, weight)


def weight_kernel(cols, mine_ref, other_ref, out_ref):
    col = lax.axis_index("cols")
    width = out_ref.shape[1]
    for c in range(cols):
        here = pl.ds(c * width, width)
        total = mine_ref[here].astype(jnp.float32) + other_ref[here].astype(jnp.float32)
        row = remainder(col + c, cols) * width
        out_ref[pl.ds(pl.multiple_of(row, width), width)] = total


def finish_weight(mine, other, cols):
    out = jax.ShapeDtypeStruct(mine.shape, jnp.float32)
    return pl.pallas_call(
        functools.partial(weight_kernel, cols),
        out_shape=out,
        in_specs=[VMEM, VMEM],
        out_specs=VMEM,
        compiler_params=params(mine, other, out),
        name="finish_weight",
    )(mine, other)


def per_device(node_features, weight, tile_values, tile_row, source_owner, source_block, labels):
    local_rows, width = node_features.shape
    n_tiles, block_size = tile_values.shape[:2]
    blocks = local_rows // block_size
    rows, cols = lax.axis_size("rows"), lax.axis_size("cols")
    plane = math.gcd(rows, LARGEST_PLANE)
    line = rows // plane
    halves = 2 if width % 256 == 0 else 1
    part_width = width // halves
    slots = -(-min(n_tiles, line * (2 * n_tiles // rows)) // cols)
    owners = source_owner[:, 0]

    def other_cols(x):
        return [
            lax.ppermute(x, "cols", [((c + k) % cols, c) for c in range(cols)])
            for k in range(1, cols)
        ]

    lanes = [slice(h * part_width, (h + 1) * part_width) for h in range(halves)]
    *packed, codes = pack_tiles(
        owners, tile_row, source_block, tile_values, plane, cols, slots
    )
    node_parts = line_gather(node_features, packed, line, plane, cols, lanes)
    spots = n_tiles + (plane - 1) * cols * slots + 1
    flat = tile_values.reshape(n_tiles * block_size, block_size)
    early = own_tiles(flat, codes, spots) + prepare(labels.reshape(blocks, block_size), weight, cols)
    tile_parts = []
    for k in range(1, plane):
        arrived = across_plane(packed[k - 1], k, line, plane)
        if k == 1:
            arrived, early = lax.optimization_barrier((arrived, early))
        tile_parts += [arrived] + other_cols(arrived)
    laid, codes, own_labels, own_first = early
    tiles, plan, count = collect_tiles(
        codes, laid, tile_parts, plane, cols, slots, blocks, n_tiles
    )

    aggregated = []
    for h in range(halves):
        here = pl.ds(h * part_width, part_width)
        sums = forward_tiles(plan, count, tiles, node_parts[h], plane, here)
        total = sums[0]
        for k in range(1, plane):
            total = total + across_plane(sums[k], k, line, plane).astype(jnp.float32)
        mine = total.astype(jnp.bfloat16)
        aggregated.append([mine] + other_cols(mine))
    parts = [aggregated[h][c] for c in range(cols) for h in range(halves)]

    activations, out_grad, agg_grad = dense(own_labels, own_first, parts, halves)
    weight_terms, *agg_grads = grads(own_first, out_grad, parts, halves, local_rows * rows)

    pieces = []
    for i, agg_grad in enumerate([agg_grad] + agg_grads):
        if i > 0:
            agg_grad, _ = lax.optimization_barrier((agg_grad, before))
        arrived = [agg_grad] + [across_plane(agg_grad, k, line, plane) for k in range(1, plane)]
        before = arrived[1:]
        if i == 0:
            weight_terms = sum_apart(weight_terms, plane, rows, rows)
        terms = spread_tiles(plan, count, tiles, arrived, line)
        beside = weight_terms if i == 0 else None
        half, beside, late = line_sum(terms, line, plane, cols, beside)
        if i == 0:
            weight_terms, _ = lax.optimization_barrier((beside, late))
        pieces.append(half)
    weight_terms = sum_apart(weight_terms, 1, plane // 2, rows)
    weight_terms, _ = lax.optimization_barrier((weight_terms, late))
    other = across_plane(weight_terms, plane // 2, line, plane)
    weight_grad = finish_weight(weight_terms, other, cols)
    return activations, weight_grad, finish(pieces)


def solution(mesh):
    return jax.shard_map(
        per_device,
        mesh=mesh,
        in_specs=(
            P("rows", "cols"),
            P(),
            P("rows", None, None),
            P("rows"),
            P("rows", None),
            P("rows"),
            P("rows"),
        ),
        out_specs=(P("rows", "cols"), P(None, "cols"), P("rows", "cols")),
        check_vma=False,
    )
```

```python
import functools
import math

import jax
import jax.numpy as jnp
from jax import lax
from jax.experimental import pallas as pl
from jax.experimental.pallas import tpu as pltpu
from jax.sharding import PartitionSpec as P

VMEM = pl.BlockSpec(memory_space=pltpu.VMEM)
SMEM = pl.BlockSpec(memory_space=pltpu.SMEM)
ANY = pl.BlockSpec(memory_space=pl.ANY)
HBM = pl.BlockSpec(memory_space=pltpu.HBM)
SPARE_BYTES = 2 * 1024 * 1024
PACK_BYTES = 56 * 1024 * 1024
UNROLL = 8
LARGEST_PLANE = 4


def params(*shapes):
    room = SPARE_BYTES
    for shape in shapes:
        *lead, high, wide = shape.shape
        room += math.prod(lead) * high * (-(-wide // 128) * 128) * jnp.dtype(shape.dtype).itemsize
    return pltpu.CompilerParams(vmem_limit_bytes=room)


def quotient(x, n):
    return x >> (n.bit_length() - 1) if n & (n - 1) == 0 else lax.div(x, n)


def remainder(x, n):
    return x & (n - 1) if n & (n - 1) == 0 else lax.rem(x, n)


def position(plane):
    index, col = lax.axis_index("rows"), lax.axis_index("cols")
    return quotient(index, plane), remainder(index, plane), col, 1 - 2 * (col & 1)


def shuffle(x, pairs):
    return lax.ppermute(x, "rows", pairs)


def across_plane(x, k, line, plane):
    return shuffle(x, [(r, r ^ k) for r in range(line * plane)])


CODE_ROWS = 16


def pack_kernel(plane, cols, owner_ref, row_ref, source_ref, tiles_ref, *refs):
    out_refs, (codes_ref, *scratch) = refs[: plane - 1], refs[plane - 1 :]
    list_ref, slot_ref, owners_ref, along_ref, rows_ref, held_ref, small_sems, held_sem = scratch
    _, place, col, _ = position(plane)
    tiles, size = tiles_ref.shape[:2]
    slots = (out_refs[0].shape[0] - CODE_ROWS) // size
    spare = (plane - 1) * slots
    looks = [pltpu.make_async_copy(owner_ref, owners_ref, small_sems.at[0])]
    for i, ref in enumerate((owner_ref, row_ref, source_ref)):
        looks.append(pltpu.make_async_copy(ref, along_ref.at[i], small_sems.at[1 + i]))
    for look in looks:
        look.start()
    bulk = pltpu.make_async_copy(tiles_ref, held_ref, held_sem)
    bulk.start()
    for k in range(plane):
        slot_ref[k] = 0
    for i in range(spare):
        list_ref[i] = 0
    rows_ref[...] = jnp.zeros_like(rows_ref)
    for look in looks:
        look.wait()

    def step(t, carry):
        k = remainder(owners_ref[0, t], plane) ^ place
        slot = slot_ref[k]
        slot_ref[k] = slot + 1
        sent = (k > 0) & (remainder(slot, cols) == col)
        list_ref[jnp.where(sent, (k - 1) * slots + quotient(slot, cols), spare)] = t
        return carry

    lax.fori_loop(0, tiles, step, 0, unroll=4)
    owners = along_ref[0]
    rows_ref[0:1, :tiles] = remainder(owners, plane).astype(jnp.float32)
    rows_ref[1:2, :tiles] = along_ref[1].astype(jnp.float32)
    rows_ref[2:3, :tiles] = along_ref[2].astype(jnp.float32)
    rows_ref[3:4, :tiles] = quotient(owners, plane).astype(jnp.float32)
    codes = rows_ref[...].astype(codes_ref.dtype)
    codes_ref[...] = codes
    bulk.wait()
    for k, out_ref in enumerate(out_refs):
        for slot in range(slots):
            out_ref[slot * size : (slot + 1) * size] = held_ref[list_ref[k * slots + slot]]
        out_ref[slots * size :] = codes


def pack_tiles(owners, tile_row, source_block, tile_values, plane, cols, slots):
    tiles, size, wide = tile_values.shape
    shape = jax.ShapeDtypeStruct((slots * size + CODE_ROWS, wide), tile_values.dtype)
    codes = jax.ShapeDtypeStruct((CODE_ROWS, wide), tile_values.dtype)
    along = [x.reshape(1, tiles) for x in (owners, tile_row, source_block)]
    return pl.pallas_call(
        functools.partial(pack_kernel, plane, cols),
        out_shape=(shape,) * (plane - 1) + (codes,),
        in_specs=[HBM] * 4,
        out_specs=(VMEM,) * plane,
        scratch_shapes=[
            pltpu.SMEM(((plane - 1) * slots + 1,), jnp.int32),
            pltpu.SMEM((plane,), jnp.int32),
            pltpu.SMEM((1, tiles), jnp.int32),
            pltpu.VMEM((3, 1, tiles), jnp.int32),
            pltpu.VMEM((CODE_ROWS, wide), jnp.float32),
            pltpu.VMEM((tiles, size, wide), tile_values.dtype),
            pltpu.SemaphoreType.DMA((4,)),
            pltpu.SemaphoreType.DMA,
        ],
        compiler_params=pltpu.CompilerParams(vmem_limit_bytes=PACK_BYTES),
        name="pack_tiles",
    )(*along, tile_values)


DST_BIT, SRC_BIT, PLACE_BIT = 10, 16, 24


def own_kernel(tiles_ref, codes_ref, out_ref, own_ref, sems):
    rows = tiles_ref.shape[0]
    moves = ((tiles_ref, out_ref.at[pl.ds(0, rows)]), (codes_ref, own_ref))
    copies = [pltpu.make_async_copy(*move, sems.at[i]) for i, move in enumerate(moves)]
    for copy in copies:
        copy.start()
    out_ref[out_ref.shape[0] - out_ref.shape[1] :] = jnp.zeros(
        (out_ref.shape[1], out_ref.shape[1]), out_ref.dtype
    )
    for copy in copies:
        copy.wait()


def own_tiles(tiles, codes, spots):
    wide = tiles.shape[1]
    laid = jax.ShapeDtypeStruct((spots * wide, wide), tiles.dtype)
    return pl.pallas_call(
        own_kernel,
        out_shape=(laid, jax.ShapeDtypeStruct(codes.shape, codes.dtype)),
        in_specs=[ANY, ANY],
        out_specs=(VMEM, VMEM),
        scratch_shapes=[pltpu.SemaphoreType.DMA((2,))],
        compiler_params=params(laid),
        name="own_tiles",
    )(tiles, codes)


def collect_kernel(plane, cols, slots, blocks, tiles, own_ref, laid_ref, *refs):
    tile_refs, refs = refs[: (plane - 1) * cols], refs[(plane - 1) * cols :]
    out_ref, plan_ref, count_ref, *scratch = refs
    rows_ref, words_ref, codes_ref, row_sems, word_sem, tile_sems = scratch
    _, place, col, _ = position(plane)
    size = out_ref.shape[1]
    looks = []
    for k in range(plane):
        ref = own_ref
        if k > 0:
            ref = tile_refs[(k - 1) * cols].at[pl.ds(slots * size, CODE_ROWS)]
        copy = pltpu.make_async_copy(ref, rows_ref.at[k], row_sems.at[k])
        copy.start()
        looks.append(copy)
    copies, first, rows = [], tiles * size, slots * size
    for i, ref in enumerate(tile_refs):
        copy = pltpu.make_async_copy(
            ref.at[pl.ds(0, rows)], out_ref.at[pl.ds(first, rows)], tile_sems.at[i]
        )
        copy.start()
        copies.append(copy)
        first += rows
    words_ref[...] = jnp.zeros_like(words_ref)
    for k, copy in enumerate(looks):
        copy.wait()
        rows = rows_ref[k].astype(jnp.float32).astype(jnp.int32)
        source = rows[3:4] * blocks + rows[2:3]
        word = (rows[0:1] << PLACE_BIT) + (source << SRC_BIT)
        words_ref[k : k + 1] = word + ((rows[1:2] + k * blocks) << DST_BIT)
    copy = pltpu.make_async_copy(words_ref, codes_ref, word_sem)
    copy.start()
    copy.wait()
    found = jnp.int32(0)
    for k in range(plane):

        def step(t, carry, k=k):
            at, slot = carry
            code = codes_ref[k, t]
            if k == 0:
                spot = t
            else:
                column = remainder(slot + (cols - col), cols)
                spot = tiles + ((k - 1) * cols + column) * slots + quotient(slot, cols)
            plan_ref[at] = (code & ((1 << PLACE_BIT) - 1)) + spot
            one = ((code >> PLACE_BIT) == place).astype(jnp.int32)
            return at + one, slot + one

        found, _ = lax.fori_loop(0, tiles, step, (found, jnp.int32(0)), unroll=8)
    for i in range(UNROLL):
        plan_ref[found + i] = first // size
    count_ref[0] = quotient(found + UNROLL - 1, UNROLL)
    for copy in copies:
        copy.wait()


def collect_tiles(codes, laid, tile_parts, plane, cols, slots, blocks, tiles):
    wide = laid.shape[1]
    entries = plane * tiles + UNROLL
    high = -(-plane // 8) * 8
    return pl.pallas_call(
        functools.partial(collect_kernel, plane, cols, slots, blocks, tiles),
        out_shape=(
            jax.ShapeDtypeStruct(laid.shape, laid.dtype),
            jax.ShapeDtypeStruct((entries,), jnp.int32),
            jax.ShapeDtypeStruct((1,), jnp.int32),
        ),
        in_specs=[ANY, VMEM] + [ANY] * len(tile_parts),
        out_specs=(VMEM, SMEM, SMEM),
        scratch_shapes=[
            pltpu.VMEM((plane, CODE_ROWS, wide), jnp.bfloat16),
            pltpu.VMEM((high, wide), jnp.int32),
            pltpu.SMEM((high, wide), jnp.int32),
            pltpu.SemaphoreType.DMA((plane,)),
            pltpu.SemaphoreType.DMA,
            pltpu.SemaphoreType.DMA((len(tile_parts),)),
        ],
        input_output_aliases={1: 0},
        compiler_params=params(laid),
        name="collect_tiles",
    )(codes, laid, *tile_parts)


def planned(plan_ref, t):
    entry = plan_ref[t]
    spot = entry & ((1 << DST_BIT) - 1)
    return spot, (entry >> DST_BIT) & ((1 << (SRC_BIT - DST_BIT)) - 1), entry >> SRC_BIT


def block_rows(index, size):
    return pl.ds(pl.multiple_of(index * size, size), size)


def forward_kernel(line, lanes, plane, plan_ref, count_ref, tiles_ref, *refs):
    part_refs, refs = refs[: 2 * line - 1], refs[2 * line - 1 :]
    out_refs, (nodes_ref, acc_ref, part_sems) = refs[:-3], refs[-3:]
    rows, width = part_refs[0].shape[0], nodes_ref.shape[1]
    size = tiles_ref.shape[1]
    mine, _, _, way = position(plane)

    def each_part(act):
        for i, ref in enumerate(part_refs):
            source = mine + way * (i - (line - 1))

            @pl.when((source >= 0) & (source < line))
            def _():
                here = ref.at[:, lanes] if ref.shape != (rows, width) else ref
                act(
                    pltpu.make_async_copy(
                        here, nodes_ref.at[block_rows(source, rows)], part_sems.at[i]
                    )
                )

    each_part(lambda copy: copy.start())
    acc_ref[...] = jnp.zeros_like(acc_ref)
    each_part(lambda copy: copy.wait())

    def step(i, carry):
        ready = None
        for spot, dst, src in [planned(plan_ref, i * UNROLL + j) for j in range(UNROLL)]:
            product = jnp.dot(
                tiles_ref[block_rows(spot, size)],
                nodes_ref[block_rows(src, size)],
                preferred_element_type=jnp.float32,
            )
            if ready is not None:
                acc_ref[ready[0]] += ready[1]
            ready = block_rows(dst, size), product
        acc_ref[ready[0]] += ready[1]
        return carry

    lax.fori_loop(0, count_ref[0], step, 0)
    for k, ref in enumerate(out_refs):
        ref[...] = acc_ref[k * rows : (k + 1) * rows].astype(ref.dtype)


def forward_tiles(plan, count, tiles, node_parts, plane, lanes):
    line = (len(node_parts) + 1) // 2
    rows, width = node_parts[0].shape[0], lanes.size
    kinds = [jnp.float32] + [jnp.bfloat16] * (plane - 1)
    outs = tuple(jax.ShapeDtypeStruct((rows, width), kind) for kind in kinds)
    scratch = [
        pltpu.VMEM((line * rows, width), jnp.bfloat16),
        pltpu.VMEM((plane * rows, width), jnp.float32),
    ]
    return pl.pallas_call(
        functools.partial(forward_kernel, line, lanes, plane),
        out_shape=outs,
        in_specs=[SMEM] * 2 + [VMEM] + [ANY] * len(node_parts),
        out_specs=(VMEM,) * plane,
        scratch_shapes=scratch + [pltpu.SemaphoreType.DMA((len(node_parts),))],
        compiler_params=params(tiles, *outs, *scratch),
        name="forward_tiles",
    )(plan, count, tiles, *node_parts)


def dense_kernel(chunk, halves, labels_ref, weight_ref, *refs):
    parts, (act_ref, out_grad_ref, agg_grad_ref) = refs[:-3], refs[-3:]
    rows, part_width = parts[0].shape
    width = part_width * halves
    features = weight_ref.shape[0]
    size = labels_ref.shape[1]

    def rows_step(i, carry):
        here = block_rows(i, chunk)
        agg = jnp.concatenate([part[here, :] for part in parts], axis=1)
        hidden = jnp.dot(agg, weight_ref[...], preferred_element_type=jnp.float32)
        sigmoid = jax.nn.sigmoid(hidden)
        activated = hidden * sigmoid
        act_ref[here, :] = activated[:, :width].astype(act_ref.dtype)
        slopes = sigmoid * (1.0 + hidden * (1.0 - sigmoid))
        named = []
        for b in range(chunk // size):
            across = labels_ref[pl.ds(i * (chunk // size) + b, 1), :]
            named.append(jnp.broadcast_to(across, (size, size)).T)
        named = jnp.concatenate(named, axis=0)
        ids = lax.broadcasted_iota(jnp.int32, (chunk, size), 1).astype(jnp.float32)
        target = jnp.concatenate(
            [(named == ids + f * size).astype(jnp.float32) for f in range(features // size)],
            axis=1,
        )
        out_grad = ((activated - target) * slopes).astype(jnp.bfloat16)
        out_grad_ref[here, :] = out_grad
        agg_grad_ref[here, :] = lax.dot_general(
            out_grad,
            weight_ref[:part_width, :],
            (((1,), (1,)), ((), ())),
            preferred_element_type=jnp.float32,
        ).astype(agg_grad_ref.dtype)
        return carry

    lax.fori_loop(0, rows // chunk, rows_step, 0)


def dense(labels, weight, parts, halves):
    rows, part_width = parts[0].shape
    chunk = math.gcd(rows, 256)
    outs = tuple(
        jax.ShapeDtypeStruct((rows, width), jnp.bfloat16)
        for width in (part_width * halves, weight.shape[0], part_width)
    )
    return pl.pallas_call(
        functools.partial(dense_kernel, chunk, halves),
        out_shape=outs,
        in_specs=[VMEM] * (2 + len(parts)),
        out_specs=(VMEM,) * 3,
        compiler_params=params(labels, weight, *parts, *outs),
        name="dense",
    )(labels, weight, *parts)


def grads_kernel(scale, halves, weight_ref, out_grad_ref, *refs):
    parts, (terms_ref, *agg_grad_refs) = refs[: -halves], refs[-halves:]
    part_width = parts[0].shape[1]
    for h, ref in enumerate(agg_grad_refs, 1):
        ref[...] = lax.dot_general(
            out_grad_ref[...],
            weight_ref[h * part_width : (h + 1) * part_width, :],
            (((1,), (1,)), ((), ())),
            preferred_element_type=jnp.float32,
        ).astype(ref.dtype)
    for i, part in enumerate(parts):
        terms = lax.dot_general(
            part[...],
            out_grad_ref[:, : part_width * halves],
            (((0,), (0,)), ((), ())),
            preferred_element_type=jnp.float32,
        )
        terms_ref[i * part_width : (i + 1) * part_width] = (terms * scale).astype(terms_ref.dtype)


def grads(weight, out_grad, parts, halves, node_total):
    rows, part_width = parts[0].shape
    outs = (jax.ShapeDtypeStruct((weight.shape[0], part_width * halves), jnp.bfloat16),) + (
        jax.ShapeDtypeStruct((rows, part_width), jnp.bfloat16),
    ) * (halves - 1)
    return pl.pallas_call(
        functools.partial(grads_kernel, 1.0 / math.sqrt(node_total), halves),
        out_shape=outs,
        in_specs=[VMEM] * (2 + len(parts)),
        out_specs=(VMEM,) * halves,
        compiler_params=params(weight, out_grad, *parts, *outs),
        name="grads",
    )(weight, out_grad, *parts)


def spread_kernel(line, plane, plan_ref, count_ref, tiles_ref, *refs):
    grad_refs, refs = refs[:plane], refs[plane:]
    out_refs, (grads_ref, acc_ref, grad_sems) = refs[:-3], refs[-3:]
    rows = grad_refs[0].shape[0]
    size = tiles_ref.shape[1]
    mine, _, _, way = position(plane)
    copies = []
    for k, ref in enumerate(grad_refs):
        copy = pltpu.make_async_copy(ref, grads_ref.at[pl.ds(k * rows, rows)], grad_sems.at[k])
        copy.start()
        copies.append(copy)
    acc_ref[...] = jnp.zeros_like(acc_ref)
    for copy in copies:
        copy.wait()

    def step(i, carry):
        ready = None
        for spot, dst, src in [planned(plan_ref, i * UNROLL + j) for j in range(UNROLL)]:
            product = lax.dot_general(
                tiles_ref[block_rows(spot, size)],
                grads_ref[block_rows(dst, size)],
                (((0,), (0,)), ((), ())),
                preferred_element_type=jnp.float32,
            )
            if ready is not None:
                acc_ref[ready[0]] += ready[1]
            ready = block_rows(src, size), product
        acc_ref[ready[0]] += ready[1]
        return carry

    lax.fori_loop(0, count_ref[0], step, 0)
    for i, ref in enumerate(out_refs):
        target = mine + way * (i - (line - 1))

        @pl.when((target >= 0) & (target < line))
        def _():
            ref[...] = acc_ref[block_rows(target, rows)].astype(ref.dtype)


def spread_tiles(plan, count, tiles, grad_parts, line):
    plane = len(grad_parts)
    rows, width = grad_parts[0].shape
    kinds = [jnp.float32 if i == line - 1 else jnp.bfloat16 for i in range(2 * line - 1)]
    outs = tuple(jax.ShapeDtypeStruct((rows, width), kind) for kind in kinds)
    scratch = [
        pltpu.VMEM((plane * rows, width), jnp.bfloat16),
        pltpu.VMEM((line * rows, width), jnp.float32),
    ]
    return pl.pallas_call(
        functools.partial(spread_kernel, line, plane),
        out_shape=outs,
        in_specs=[SMEM] * 2 + [VMEM] + [ANY] * plane,
        out_specs=(VMEM,) * (2 * line - 1),
        scratch_shapes=scratch + [pltpu.SemaphoreType.DMA((plane,))],
        compiler_params=params(tiles, *outs, *scratch),
        name="spread_tiles",
    )(plan, count, tiles, *grad_parts)


def along_line(x, line, plane, cols, step, reach):
    pairs = []
    for z in range(line):
        for q in range(plane):
            for c in range(cols):
                way = 1 - 2 * (c & 1)
                to, end = z + way * step, z + way * reach
                if 0 <= to < line and 0 <= end < line:
                    pairs.append(((z * plane + q) * cols + c, (to * plane + q) * cols + c))
    return lax.ppermute(x, ("rows", "cols"), pairs)


def line_gather(x, after, line, plane, cols, lanes):
    move = lambda part, step, reach: along_line(part, line, plane, cols, step, reach)
    later, _ = lax.optimization_barrier((x, after))
    up, down = [x], [later]
    for k in range(1, line - 1):
        up.append(move(up[-1], 1, 1 - k))
        down.append(move(down[-1], -1, k - 1))
    def last(part, after):
        high, low = up[-1], down[-1]
        if after is not None:
            high, low, _ = lax.optimization_barrier((high, low, after))
        first = move(high[:, part], 1, 2 - line)
        final = move(low[:, part], -1, line - 2)
        return [first] + up[:0:-1] + down + [final]

    return last


def line_sum(terms, line, plane, cols, beside):
    moved, late = {1: None, -1: None}, None
    for k in range(line - 1, 0, -1):
        for step in moved:
            term = terms[line - 1 + step * k]
            if moved[step] is not None:
                total = term.astype(jnp.float32) + moved[step].astype(jnp.float32)
                term = total.astype(term.dtype)
            moved[step] = along_line(term, line, plane, cols, step, step * k)
        if k == line - 1 and beside is not None:
            moved, beside = lax.optimization_barrier((moved, beside))
        if k > 1:
            late = tuple(moved.values())
    return [terms[line - 1], moved[1], moved[-1]], beside, late


def finish_kernel(halves, cols, mine_ref, other_ref, *refs):
    (weight_ref, out_ref), refs = refs[-2:], refs[:-2]
    col = lax.axis_index("cols")
    wide = weight_ref.shape[1]
    for c in range(cols):
        here = pl.ds(c * wide, wide)
        total = mine_ref[here].astype(jnp.float32) + other_ref[here].astype(jnp.float32)
        row = remainder(col + c, cols) * wide
        weight_ref[pl.ds(pl.multiple_of(row, wide), wide)] = total
    each = len(refs) // halves
    width = refs[0].shape[1]
    for h in range(halves):
        total = refs[h * each][...]
        for ref in refs[h * each + 1 : (h + 1) * each]:
            total += ref[...].astype(jnp.float32)
        out_ref[:, h * width : (h + 1) * width] = total.astype(out_ref.dtype)


def finish(mine, other, pieces, cols):
    flat = [piece for half in pieces for piece in half]
    rows, width = flat[0].shape
    outs = (
        jax.ShapeDtypeStruct(mine.shape, jnp.float32),
        jax.ShapeDtypeStruct((rows, width * len(pieces)), jnp.bfloat16),
    )
    return pl.pallas_call(
        functools.partial(finish_kernel, len(pieces), cols),
        out_shape=outs,
        in_specs=[VMEM] * (2 + len(flat)),
        out_specs=(VMEM, VMEM),
        compiler_params=params(mine, other, *outs, *flat),
        name="finish",
    )(mine, other, *flat)


def sum_apart(terms, first, end, rows):
    while first < end:
        other = shuffle(terms, [(r, r ^ first) for r in range(rows)])
        total = terms.astype(jnp.float32) + other.astype(jnp.float32)
        terms = total.astype(terms.dtype)
        first *= 2
    return terms


def prepare_kernel(cols, labels_ref, weight_ref, own_labels_ref, own_first_ref, wide_ref):
    col = lax.axis_index("cols")
    features = weight_ref.shape[0]
    width = features // cols
    labels = labels_ref[...] - col * width
    own_labels_ref[...] = jnp.where(labels < 0, labels + features, labels).astype(jnp.float32)
    for c in range(cols):
        row = remainder(col + c, cols) * width
        rows = weight_ref[pl.ds(pl.multiple_of(row, width), width), :]
        wide_ref[c * width : (c + 1) * width] = rows.astype(jnp.float32)
    turned = pltpu.roll(wide_ref[...], remainder(cols - col, cols) * width, axis=1)
    own_first_ref[...] = turned.astype(own_first_ref.dtype)


def prepare(labels, weight, cols):
    outs = (jax.ShapeDtypeStruct(labels.shape, jnp.float32), weight)
    wide = pltpu.VMEM(weight.shape, jnp.float32)
    return pl.pallas_call(
        functools.partial(prepare_kernel, cols),
        out_shape=(outs[0], jax.ShapeDtypeStruct(weight.shape, weight.dtype)),
        in_specs=[VMEM, VMEM],
        out_specs=(VMEM, VMEM),
        scratch_shapes=[wide],
        compiler_params=params(weight, weight, wide, wide),
        name="prepare",
    )(labels, weight)


def per_device(node_features, weight, tile_values, tile_row, source_owner, source_block, labels):
    local_rows, width = node_features.shape
    n_tiles, block_size = tile_values.shape[:2]
    blocks = local_rows // block_size
    rows, cols = lax.axis_size("rows"), lax.axis_size("cols")
    plane = math.gcd(rows, LARGEST_PLANE)
    line = rows // plane
    halves = 2 if width % 256 == 0 else 1
    part_width = width // halves
    slots = -(-min(n_tiles, line * (2 * n_tiles // rows)) // cols)
    owners = source_owner[:, 0]

    def other_cols(x):
        return [
            lax.ppermute(x, "cols", [((c + k) % cols, c) for c in range(cols)])
            for k in range(1, cols)
        ]

    lanes = [slice(h * part_width, (h + 1) * part_width) for h in range(halves)]
    *packed, codes = pack_tiles(
        owners, tile_row, source_block, tile_values, plane, cols, slots
    )
    last_parts = line_gather(node_features, packed, line, plane, cols, lanes)
    spots = n_tiles + (plane - 1) * cols * slots + 1
    flat = tile_values.reshape(n_tiles * block_size, block_size)
    early = own_tiles(flat, codes, spots) + prepare(labels.reshape(blocks, block_size), weight, cols)
    tile_parts = []
    for k in range(1, plane):
        arrived = across_plane(packed[k - 1], k, line, plane)
        if k == 1:
            arrived, early = lax.optimization_barrier((arrived, early))
        tile_parts += [arrived] + other_cols(arrived)
    laid, codes, own_labels, own_first = early
    tiles, plan, count = collect_tiles(
        codes, laid, tile_parts, plane, cols, slots, blocks, n_tiles
    )

    aggregated = []
    for h in range(halves):
        here = pl.ds(h * part_width, part_width)
        node_parts = last_parts(lanes[h], sums[-1] if h else None)
        sums = forward_tiles(plan, count, tiles, node_parts, plane, here)
        total = sums[0]
        for k in range(1, plane):
            total = total + across_plane(sums[k], k, line, plane).astype(jnp.float32)
        mine = total.astype(jnp.bfloat16)
        aggregated.append([mine] + other_cols(mine))
    parts = [aggregated[h][c] for c in range(cols) for h in range(halves)]

    activations, out_grad, agg_grad = dense(own_labels, own_first, parts, halves)
    weight_terms, *agg_grads = grads(own_first, out_grad, parts, halves, local_rows * rows)

    pieces = []
    for i, agg_grad in enumerate([agg_grad] + agg_grads):
        arrived = [agg_grad] + [across_plane(agg_grad, k, line, plane) for k in range(1, plane)]
        if i == 0:
            weight_terms = sum_apart(weight_terms, plane, 2 * plane, rows)
            arrived, weight_terms = lax.optimization_barrier((arrived, weight_terms))
            weight_terms = sum_apart(weight_terms, 2 * plane, rows, rows)
        terms = spread_tiles(plan, count, tiles, arrived, line)
        beside = weight_terms if i == 0 else None
        half, beside, late = line_sum(terms, line, plane, cols, beside)
        if i == 0:
            weight_terms, _ = lax.optimization_barrier((beside, late))
        pieces.append(half)
    weight_terms = sum_apart(weight_terms, 1, plane // 2, rows)
    weight_terms, _ = lax.optimization_barrier((weight_terms, late))
    other = across_plane(weight_terms, plane // 2, line, plane)
    return (activations,) + tuple(finish(weight_terms, other, pieces, cols))


def solution(mesh):
    return jax.shard_map(
        per_device,
        mesh=mesh,
        in_specs=(
            P("rows", "cols"),
            P(),
            P("rows", None, None),
            P("rows"),
            P("rows", None),
            P("rows"),
            P("rows"),
        ),
        out_specs=(P("rows", "cols"), P(None, "cols"), P("rows", "cols")),
        check_vma=False,
    )
```

```python
import functools
import math

import jax
import jax.numpy as jnp
from jax import lax
from jax.experimental import pallas as pl
from jax.experimental.pallas import tpu as pltpu
from jax.sharding import PartitionSpec as P

VMEM = pl.BlockSpec(memory_space=pltpu.VMEM)
SMEM = pl.BlockSpec(memory_space=pltpu.SMEM)
ANY = pl.BlockSpec(memory_space=pl.ANY)
HBM = pl.BlockSpec(memory_space=pltpu.HBM)
SPARE_BYTES = 2 * 1024 * 1024
PACK_BYTES = 56 * 1024 * 1024
UNROLL = 8
LARGEST_PLANE = 4


def params(*shapes):
    room = SPARE_BYTES
    for shape in shapes:
        *lead, high, wide = shape.shape
        room += math.prod(lead) * high * (-(-wide // 128) * 128) * jnp.dtype(shape.dtype).itemsize
    return pltpu.CompilerParams(vmem_limit_bytes=room)


def quotient(x, n):
    return x >> (n.bit_length() - 1) if n & (n - 1) == 0 else lax.div(x, n)


def remainder(x, n):
    return x & (n - 1) if n & (n - 1) == 0 else lax.rem(x, n)


def position(plane):
    index, col = lax.axis_index("rows"), lax.axis_index("cols")
    return quotient(index, plane), remainder(index, plane), col, 1 - 2 * (col & 1)


def shuffle(x, pairs):
    return lax.ppermute(x, "rows", pairs)


def across_plane(x, k, line, plane):
    return shuffle(x, [(r, r ^ k) for r in range(line * plane)])


CODE_ROWS = 16


def pack_kernel(plane, cols, owner_ref, row_ref, source_ref, tiles_ref, *refs):
    out_refs, (codes_ref, *scratch) = refs[: plane - 1], refs[plane - 1 :]
    list_ref, slot_ref, owners_ref, along_ref, rows_ref, held_ref, small_sems, held_sem = scratch
    _, place, col, _ = position(plane)
    tiles, size = tiles_ref.shape[:2]
    slots = (out_refs[0].shape[0] - CODE_ROWS) // size
    spare = (plane - 1) * slots
    looks = [pltpu.make_async_copy(owner_ref, owners_ref, small_sems.at[0])]
    for i, ref in enumerate((owner_ref, row_ref, source_ref)):
        looks.append(pltpu.make_async_copy(ref, along_ref.at[i], small_sems.at[1 + i]))
    for look in looks:
        look.start()
    bulk = pltpu.make_async_copy(tiles_ref, held_ref, held_sem)
    bulk.start()
    for k in range(plane):
        slot_ref[k] = 0
    for i in range(spare):
        list_ref[i] = 0
    rows_ref[...] = jnp.zeros_like(rows_ref)
    for look in looks:
        look.wait()

    def step(t, carry):
        k = remainder(owners_ref[0, t], plane) ^ place
        slot = slot_ref[k]
        slot_ref[k] = slot + 1
        sent = (k > 0) & (remainder(slot, cols) == col)
        list_ref[jnp.where(sent, (k - 1) * slots + quotient(slot, cols), spare)] = t
        return carry

    lax.fori_loop(0, tiles, step, 0, unroll=4)
    owners = along_ref[0]
    rows_ref[0:1, :tiles] = remainder(owners, plane).astype(jnp.float32)
    rows_ref[1:2, :tiles] = along_ref[1].astype(jnp.float32)
    rows_ref[2:3, :tiles] = along_ref[2].astype(jnp.float32)
    rows_ref[3:4, :tiles] = quotient(owners, plane).astype(jnp.float32)
    codes = rows_ref[...].astype(codes_ref.dtype)
    codes_ref[...] = codes
    bulk.wait()
    for k, out_ref in enumerate(out_refs):
        for slot in range(slots):
            out_ref[slot * size : (slot + 1) * size] = held_ref[list_ref[k * slots + slot]]
        out_ref[slots * size :] = codes


def pack_tiles(owners, tile_row, source_block, tile_values, plane, cols, slots):
    tiles, size, wide = tile_values.shape
    shape = jax.ShapeDtypeStruct((slots * size + CODE_ROWS, wide), tile_values.dtype)
    codes = jax.ShapeDtypeStruct((CODE_ROWS, wide), tile_values.dtype)
    along = [x.reshape(1, tiles) for x in (owners, tile_row, source_block)]
    return pl.pallas_call(
        functools.partial(pack_kernel, plane, cols),
        out_shape=(shape,) * (plane - 1) + (codes,),
        in_specs=[HBM] * 4,
        out_specs=(VMEM,) * plane,
        scratch_shapes=[
            pltpu.SMEM(((plane - 1) * slots + 1,), jnp.int32),
            pltpu.SMEM((plane,), jnp.int32),
            pltpu.SMEM((1, tiles), jnp.int32),
            pltpu.VMEM((3, 1, tiles), jnp.int32),
            pltpu.VMEM((CODE_ROWS, wide), jnp.float32),
            pltpu.VMEM((tiles, size, wide), tile_values.dtype),
            pltpu.SemaphoreType.DMA((4,)),
            pltpu.SemaphoreType.DMA,
        ],
        compiler_params=pltpu.CompilerParams(vmem_limit_bytes=PACK_BYTES),
        name="pack_tiles",
    )(*along, tile_values)


DST_BIT, SRC_BIT, PLACE_BIT = 10, 16, 24


def own_kernel(tiles_ref, codes_ref, out_ref, own_ref, sems):
    rows = tiles_ref.shape[0]
    moves = ((tiles_ref, out_ref.at[pl.ds(0, rows)]), (codes_ref, own_ref))
    copies = [pltpu.make_async_copy(*move, sems.at[i]) for i, move in enumerate(moves)]
    for copy in copies:
        copy.start()
    out_ref[out_ref.shape[0] - out_ref.shape[1] :] = jnp.zeros(
        (out_ref.shape[1], out_ref.shape[1]), out_ref.dtype
    )
    for copy in copies:
        copy.wait()


def own_tiles(tiles, codes, spots):
    wide = tiles.shape[1]
    laid = jax.ShapeDtypeStruct((spots * wide, wide), tiles.dtype)
    return pl.pallas_call(
        own_kernel,
        out_shape=(laid, jax.ShapeDtypeStruct(codes.shape, codes.dtype)),
        in_specs=[ANY, ANY],
        out_specs=(VMEM, VMEM),
        scratch_shapes=[pltpu.SemaphoreType.DMA((2,))],
        compiler_params=params(laid),
        name="own_tiles",
    )(tiles, codes)


def collect_kernel(plane, cols, slots, blocks, tiles, own_ref, laid_ref, *refs):
    tile_refs, refs = refs[: (plane - 1) * cols], refs[(plane - 1) * cols :]
    out_ref, plan_ref, count_ref, *scratch = refs
    rows_ref, words_ref, codes_ref, row_sems, word_sem, tile_sems = scratch
    _, place, col, _ = position(plane)
    size = out_ref.shape[1]
    looks = []
    for k in range(plane):
        ref = own_ref
        if k > 0:
            ref = tile_refs[(k - 1) * cols].at[pl.ds(slots * size, CODE_ROWS)]
        copy = pltpu.make_async_copy(ref, rows_ref.at[k], row_sems.at[k])
        copy.start()
        looks.append(copy)
    copies, first, rows = [], tiles * size, slots * size
    for i, ref in enumerate(tile_refs):
        copy = pltpu.make_async_copy(
            ref.at[pl.ds(0, rows)], out_ref.at[pl.ds(first, rows)], tile_sems.at[i]
        )
        copy.start()
        copies.append(copy)
        first += rows
    words_ref[...] = jnp.zeros_like(words_ref)
    for k, copy in enumerate(looks):
        copy.wait()
        rows = rows_ref[k].astype(jnp.float32).astype(jnp.int32)
        source = rows[3:4] * blocks + rows[2:3]
        word = (rows[0:1] << PLACE_BIT) + (source << SRC_BIT)
        words_ref[k : k + 1] = word + ((rows[1:2] + k * blocks) << DST_BIT)
    copy = pltpu.make_async_copy(words_ref, codes_ref, word_sem)
    copy.start()
    copy.wait()
    found = jnp.int32(0)
    for k in range(plane):

        def step(t, carry, k=k):
            at, slot = carry
            code = codes_ref[k, t]
            if k == 0:
                spot = t
            else:
                column = remainder(slot + (cols - col), cols)
                spot = tiles + ((k - 1) * cols + column) * slots + quotient(slot, cols)
            plan_ref[at] = (code & ((1 << PLACE_BIT) - 1)) + spot
            one = ((code >> PLACE_BIT) == place).astype(jnp.int32)
            return at + one, slot + one

        found, _ = lax.fori_loop(0, tiles, step, (found, jnp.int32(0)), unroll=8)
    for i in range(UNROLL):
        plan_ref[found + i] = first // size
    count_ref[0] = quotient(found + UNROLL - 1, UNROLL)
    for copy in copies:
        copy.wait()


def collect_tiles(codes, laid, tile_parts, plane, cols, slots, blocks, tiles):
    wide = laid.shape[1]
    entries = plane * tiles + UNROLL
    high = -(-plane // 8) * 8
    return pl.pallas_call(
        functools.partial(collect_kernel, plane, cols, slots, blocks, tiles),
        out_shape=(
            jax.ShapeDtypeStruct(laid.shape, laid.dtype),
            jax.ShapeDtypeStruct((entries,), jnp.int32),
            jax.ShapeDtypeStruct((1,), jnp.int32),
        ),
        in_specs=[ANY, VMEM] + [ANY] * len(tile_parts),
        out_specs=(VMEM, SMEM, SMEM),
        scratch_shapes=[
            pltpu.VMEM((plane, CODE_ROWS, wide), jnp.bfloat16),
            pltpu.VMEM((high, wide), jnp.int32),
            pltpu.SMEM((high, wide), jnp.int32),
            pltpu.SemaphoreType.DMA((plane,)),
            pltpu.SemaphoreType.DMA,
            pltpu.SemaphoreType.DMA((len(tile_parts),)),
        ],
        input_output_aliases={1: 0},
        compiler_params=params(laid),
        name="collect_tiles",
    )(codes, laid, *tile_parts)


def planned(plan_ref, t):
    entry = plan_ref[t]
    spot = entry & ((1 << DST_BIT) - 1)
    return spot, (entry >> DST_BIT) & ((1 << (SRC_BIT - DST_BIT)) - 1), entry >> SRC_BIT


def block_rows(index, size):
    return pl.ds(pl.multiple_of(index * size, size), size)


def forward_kernel(line, lanes, plane, plan_ref, count_ref, tiles_ref, *refs):
    part_refs, refs = refs[: 2 * line - 1], refs[2 * line - 1 :]
    out_refs, (nodes_ref, acc_ref, part_sems) = refs[:-3], refs[-3:]
    rows, width = part_refs[0].shape[0], nodes_ref.shape[1]
    size = tiles_ref.shape[1]
    mine, _, _, way = position(plane)

    def each_part(act):
        for i, ref in enumerate(part_refs):
            source = mine + way * (i - (line - 1))

            @pl.when((source >= 0) & (source < line))
            def _():
                here = ref.at[:, lanes] if ref.shape != (rows, width) else ref
                act(
                    pltpu.make_async_copy(
                        here, nodes_ref.at[block_rows(source, rows)], part_sems.at[i]
                    )
                )

    each_part(lambda copy: copy.start())
    acc_ref[...] = jnp.zeros_like(acc_ref)
    each_part(lambda copy: copy.wait())

    def step(i, carry):
        ready = None
        for spot, dst, src in [planned(plan_ref, i * UNROLL + j) for j in range(UNROLL)]:
            product = jnp.dot(
                tiles_ref[block_rows(spot, size)],
                nodes_ref[block_rows(src, size)],
                preferred_element_type=jnp.float32,
            )
            if ready is not None:
                acc_ref[ready[0]] += ready[1]
            ready = block_rows(dst, size), product
        acc_ref[ready[0]] += ready[1]
        return carry

    lax.fori_loop(0, count_ref[0], step, 0)
    for k, ref in enumerate(out_refs):
        ref[...] = acc_ref[k * rows : (k + 1) * rows].astype(ref.dtype)


def forward_tiles(plan, count, tiles, node_parts, plane, lanes):
    line = (len(node_parts) + 1) // 2
    rows, width = node_parts[0].shape[0], lanes.size
    kinds = [jnp.float32] + [jnp.bfloat16] * (plane - 1)
    outs = tuple(jax.ShapeDtypeStruct((rows, width), kind) for kind in kinds)
    scratch = [
        pltpu.VMEM((line * rows, width), jnp.bfloat16),
        pltpu.VMEM((plane * rows, width), jnp.float32),
    ]
    return pl.pallas_call(
        functools.partial(forward_kernel, line, lanes, plane),
        out_shape=outs,
        in_specs=[SMEM] * 2 + [VMEM] + [ANY] * len(node_parts),
        out_specs=(VMEM,) * plane,
        scratch_shapes=scratch + [pltpu.SemaphoreType.DMA((len(node_parts),))],
        compiler_params=params(tiles, *outs, *scratch),
        name="forward_tiles",
    )(plan, count, tiles, *node_parts)


def dense_kernel(chunk, halves, labels_ref, weight_ref, *refs):
    parts, (act_ref, out_grad_ref, agg_grad_ref) = refs[:-3], refs[-3:]
    rows, part_width = parts[0].shape
    width = part_width * halves
    features = weight_ref.shape[0]
    size = labels_ref.shape[1]

    def rows_step(i, carry):
        here = block_rows(i, chunk)
        agg = jnp.concatenate([part[here, :] for part in parts], axis=1)
        hidden = jnp.dot(agg, weight_ref[...], preferred_element_type=jnp.float32)
        sigmoid = jax.nn.sigmoid(hidden)
        activated = hidden * sigmoid
        act_ref[here, :] = activated[:, :width].astype(act_ref.dtype)
        slopes = sigmoid * (1.0 + hidden * (1.0 - sigmoid))
        named = []
        for b in range(chunk // size):
            across = labels_ref[pl.ds(i * (chunk // size) + b, 1), :]
            named.append(jnp.broadcast_to(across, (size, size)).T)
        named = jnp.concatenate(named, axis=0)
        ids = lax.broadcasted_iota(jnp.int32, (chunk, size), 1).astype(jnp.float32)
        target = jnp.concatenate(
            [(named == ids + f * size).astype(jnp.float32) for f in range(features // size)],
            axis=1,
        )
        out_grad = ((activated - target) * slopes).astype(jnp.bfloat16)
        out_grad_ref[here, :] = out_grad
        agg_grad_ref[here, :] = lax.dot_general(
            out_grad,
            weight_ref[:part_width, :],
            (((1,), (1,)), ((), ())),
            preferred_element_type=jnp.float32,
        ).astype(agg_grad_ref.dtype)
        return carry

    lax.fori_loop(0, rows // chunk, rows_step, 0)


def dense(labels, weight, parts, halves):
    rows, part_width = parts[0].shape
    chunk = math.gcd(rows, 256)
    outs = tuple(
        jax.ShapeDtypeStruct((rows, width), jnp.bfloat16)
        for width in (part_width * halves, weight.shape[0], part_width)
    )
    return pl.pallas_call(
        functools.partial(dense_kernel, chunk, halves),
        out_shape=outs,
        in_specs=[VMEM] * (2 + len(parts)),
        out_specs=(VMEM,) * 3,
        compiler_params=params(labels, weight, *parts, *outs),
        name="dense",
    )(labels, weight, *parts)


def grads_kernel(scale, halves, weight_ref, out_grad_ref, *refs):
    parts, (terms_ref, *agg_grad_refs) = refs[: -halves], refs[-halves:]
    part_width = parts[0].shape[1]
    for h, ref in enumerate(agg_grad_refs, 1):
        ref[...] = lax.dot_general(
            out_grad_ref[...],
            weight_ref[h * part_width : (h + 1) * part_width, :],
            (((1,), (1,)), ((), ())),
            preferred_element_type=jnp.float32,
        ).astype(ref.dtype)
    for i, part in enumerate(parts):
        terms = lax.dot_general(
            part[...],
            out_grad_ref[:, : part_width * halves],
            (((0,), (0,)), ((), ())),
            preferred_element_type=jnp.float32,
        )
        terms_ref[i * part_width : (i + 1) * part_width] = (terms * scale).astype(terms_ref.dtype)


def grads(weight, out_grad, parts, halves, node_total):
    rows, part_width = parts[0].shape
    outs = (jax.ShapeDtypeStruct((weight.shape[0], part_width * halves), jnp.bfloat16),) + (
        jax.ShapeDtypeStruct((rows, part_width), jnp.bfloat16),
    ) * (halves - 1)
    return pl.pallas_call(
        functools.partial(grads_kernel, 1.0 / math.sqrt(node_total), halves),
        out_shape=outs,
        in_specs=[VMEM] * (2 + len(parts)),
        out_specs=(VMEM,) * halves,
        compiler_params=params(weight, out_grad, *parts, *outs),
        name="grads",
    )(weight, out_grad, *parts)


def spread_kernel(line, plane, plan_ref, count_ref, tiles_ref, *refs):
    grad_refs, refs = refs[:plane], refs[plane:]
    out_refs, (grads_ref, acc_ref, grad_sems) = refs[:-3], refs[-3:]
    rows = grad_refs[0].shape[0]
    size = tiles_ref.shape[1]
    mine, _, _, way = position(plane)
    copies = []
    for k, ref in enumerate(grad_refs):
        copy = pltpu.make_async_copy(ref, grads_ref.at[pl.ds(k * rows, rows)], grad_sems.at[k])
        copy.start()
        copies.append(copy)
    acc_ref[...] = jnp.zeros_like(acc_ref)
    for copy in copies:
        copy.wait()

    def step(i, carry):
        ready = None
        for spot, dst, src in [planned(plan_ref, i * UNROLL + j) for j in range(UNROLL)]:
            product = lax.dot_general(
                tiles_ref[block_rows(spot, size)],
                grads_ref[block_rows(dst, size)],
                (((0,), (0,)), ((), ())),
                preferred_element_type=jnp.float32,
            )
            if ready is not None:
                acc_ref[ready[0]] += ready[1]
            ready = block_rows(src, size), product
        acc_ref[ready[0]] += ready[1]
        return carry

    lax.fori_loop(0, count_ref[0], step, 0)
    for i, ref in enumerate(out_refs):
        target = mine + way * (i - (line - 1))

        @pl.when((target >= 0) & (target < line))
        def _():
            ref[...] = acc_ref[block_rows(target, rows)].astype(ref.dtype)


def spread_tiles(plan, count, tiles, grad_parts, line):
    plane = len(grad_parts)
    rows, width = grad_parts[0].shape
    kinds = [jnp.float32 if i == line - 1 else jnp.bfloat16 for i in range(2 * line - 1)]
    outs = tuple(jax.ShapeDtypeStruct((rows, width), kind) for kind in kinds)
    scratch = [
        pltpu.VMEM((plane * rows, width), jnp.bfloat16),
        pltpu.VMEM((line * rows, width), jnp.float32),
    ]
    return pl.pallas_call(
        functools.partial(spread_kernel, line, plane),
        out_shape=outs,
        in_specs=[SMEM] * 2 + [VMEM] + [ANY] * plane,
        out_specs=(VMEM,) * (2 * line - 1),
        scratch_shapes=scratch + [pltpu.SemaphoreType.DMA((plane,))],
        compiler_params=params(tiles, *outs, *scratch),
        name="spread_tiles",
    )(plan, count, tiles, *grad_parts)


def along_line(x, line, plane, cols, step, reach):
    pairs = []
    for z in range(line):
        for q in range(plane):
            for c in range(cols):
                way = 1 - 2 * (c & 1)
                to, end = z + way * step, z + way * reach
                if 0 <= to < line and 0 <= end < line:
                    pairs.append(((z * plane + q) * cols + c, (to * plane + q) * cols + c))
    return lax.ppermute(x, ("rows", "cols"), pairs)


def line_gather(x, after, line, plane, cols, lanes):
    move = lambda part, step, reach: along_line(part, line, plane, cols, step, reach)
    later, _ = lax.optimization_barrier((x, after))
    up, down = [x], [later]
    for k in range(1, line - 1):
        up.append(move(up[-1], 1, 1 - k))
        down.append(move(down[-1], -1, k - 1))
    parts, high, low = [], up[-1], down[-1]
    for part in lanes:
        first = move(high[:, part], 1, 2 - line)
        last = move(low[:, part], -1, line - 2)
        parts.append([first] + up[:0:-1] + down + [last])
    return parts


def line_sum(terms, line, plane, cols, beside):
    moved, late = {1: None, -1: None}, None
    for k in range(line - 1, 0, -1):
        for step in moved:
            term = terms[line - 1 + step * k]
            if moved[step] is not None:
                total = term.astype(jnp.float32) + moved[step].astype(jnp.float32)
                term = total.astype(term.dtype)
            moved[step] = along_line(term, line, plane, cols, step, step * k)
        if k == line - 1 and beside is not None:
            moved, beside = lax.optimization_barrier((moved, beside))
        if k > 1:
            late = tuple(moved.values())
    return [terms[line - 1], moved[1], moved[-1]], beside, late


def finish_kernel(halves, cols, mine_ref, other_ref, *refs):
    (weight_ref, out_ref), refs = refs[-2:], refs[:-2]
    col = lax.axis_index("cols")
    wide = weight_ref.shape[1]
    for c in range(cols):
        here = pl.ds(c * wide, wide)
        total = mine_ref[here].astype(jnp.float32) + other_ref[here].astype(jnp.float32)
        row = remainder(col + c, cols) * wide
        weight_ref[pl.ds(pl.multiple_of(row, wide), wide)] = total
    each = len(refs) // halves
    width = refs[0].shape[1]
    for h in range(halves):
        total = refs[h * each][...]
        for ref in refs[h * each + 1 : (h + 1) * each]:
            total += ref[...].astype(jnp.float32)
        out_ref[:, h * width : (h + 1) * width] = total.astype(out_ref.dtype)


def finish(mine, other, pieces, cols):
    flat = [piece for half in pieces for piece in half]
    rows, width = flat[0].shape
    outs = (
        jax.ShapeDtypeStruct(mine.shape, jnp.float32),
        jax.ShapeDtypeStruct((rows, width * len(pieces)), jnp.bfloat16),
    )
    return pl.pallas_call(
        functools.partial(finish_kernel, len(pieces), cols),
        out_shape=outs,
        in_specs=[VMEM] * (2 + len(flat)),
        out_specs=(VMEM, VMEM),
        compiler_params=params(mine, other, *outs, *flat),
        name="finish",
    )(mine, other, *flat)


def sum_apart(terms, first, end, rows):
    while first < end:
        other = shuffle(terms, [(r, r ^ first) for r in range(rows)])
        total = terms.astype(jnp.float32) + other.astype(jnp.float32)
        terms = total.astype(terms.dtype)
        first *= 2
    return terms


def prepare_kernel(cols, labels_ref, weight_ref, own_labels_ref, own_first_ref, wide_ref):
    col = lax.axis_index("cols")
    features = weight_ref.shape[0]
    width = features // cols
    labels = labels_ref[...] - col * width
    own_labels_ref[...] = jnp.where(labels < 0, labels + features, labels).astype(jnp.float32)
    for c in range(cols):
        row = remainder(col + c, cols) * width
        rows = weight_ref[pl.ds(pl.multiple_of(row, width), width), :]
        wide_ref[c * width : (c + 1) * width] = rows.astype(jnp.float32)
    turned = pltpu.roll(wide_ref[...], remainder(cols - col, cols) * width, axis=1)
    own_first_ref[...] = turned.astype(own_first_ref.dtype)


def prepare(labels, weight, cols):
    outs = (jax.ShapeDtypeStruct(labels.shape, jnp.float32), weight)
    wide = pltpu.VMEM(weight.shape, jnp.float32)
    return pl.pallas_call(
        functools.partial(prepare_kernel, cols),
        out_shape=(outs[0], jax.ShapeDtypeStruct(weight.shape, weight.dtype)),
        in_specs=[VMEM, VMEM],
        out_specs=(VMEM, VMEM),
        scratch_shapes=[wide],
        compiler_params=params(weight, weight, wide, wide),
        name="prepare",
    )(labels, weight)


def per_device(node_features, weight, tile_values, tile_row, source_owner, source_block, labels):
    local_rows, width = node_features.shape
    n_tiles, block_size = tile_values.shape[:2]
    blocks = local_rows // block_size
    rows, cols = lax.axis_size("rows"), lax.axis_size("cols")
    plane = math.gcd(rows, LARGEST_PLANE)
    line = rows // plane
    halves = 2 if width % 256 == 0 else 1
    part_width = width // halves
    slots = -(-min(n_tiles, line * (2 * n_tiles // rows)) // cols)
    owners = source_owner[:, 0]

    def other_cols(x):
        return [
            lax.ppermute(x, "cols", [((c + k) % cols, c) for c in range(cols)])
            for k in range(1, cols)
        ]

    lanes = [slice(h * part_width, (h + 1) * part_width) for h in range(halves)]
    *packed, codes = pack_tiles(
        owners, tile_row, source_block, tile_values, plane, cols, slots
    )
    node_parts = line_gather(node_features, packed, line, plane, cols, lanes)
    spots = n_tiles + (plane - 1) * cols * slots + 1
    flat = tile_values.reshape(n_tiles * block_size, block_size)
    early = own_tiles(flat, codes, spots) + prepare(labels.reshape(blocks, block_size), weight, cols)
    tile_parts = []
    for k in range(1, plane):
        arrived = across_plane(packed[k - 1], k, line, plane)
        if k == 1:
            arrived, early = lax.optimization_barrier((arrived, early))
        tile_parts += [arrived] + other_cols(arrived)
    laid, codes, own_labels, own_first = early
    tiles, plan, count = collect_tiles(
        codes, laid, tile_parts, plane, cols, slots, blocks, n_tiles
    )

    aggregated = []
    for h in range(halves):
        here = pl.ds(h * part_width, part_width)
        sums = forward_tiles(plan, count, tiles, node_parts[h], plane, here)
        total = sums[0]
        for k in range(1, plane):
            total = total + across_plane(sums[k], k, line, plane).astype(jnp.float32)
        mine = total.astype(jnp.bfloat16)
        aggregated.append([mine] + other_cols(mine))
    parts = [aggregated[h][c] for c in range(cols) for h in range(halves)]

    activations, out_grad, agg_grad = dense(own_labels, own_first, parts, halves)
    weight_terms, *agg_grads = grads(own_first, out_grad, parts, halves, local_rows * rows)

    pieces = []
    for i, agg_grad in enumerate([agg_grad] + agg_grads):
        arrived = [agg_grad] + [across_plane(agg_grad, k, line, plane) for k in range(1, plane)]
        if i == 0:
            weight_terms = sum_apart(weight_terms, plane, 2 * plane, rows)
            arrived, weight_terms = lax.optimization_barrier((arrived, weight_terms))
            weight_terms = sum_apart(weight_terms, 2 * plane, rows, rows)
        terms = spread_tiles(plan, count, tiles, arrived, line)
        beside = weight_terms if i == 0 else None
        half, beside, late = line_sum(terms, line, plane, cols, beside)
        if i == 0:
            weight_terms, _ = lax.optimization_barrier((beside, late))
        pieces.append(half)
    weight_terms = sum_apart(weight_terms, 1, plane // 2, rows)
    weight_terms, _ = lax.optimization_barrier((weight_terms, late))
    other = across_plane(weight_terms, plane // 2, line, plane)
    return (activations,) + tuple(finish(weight_terms, other, pieces, cols))


def solution(mesh):
    return jax.shard_map(
        per_device,
        mesh=mesh,
        in_specs=(
            P("rows", "cols"),
            P(),
            P("rows", None, None),
            P("rows"),
            P("rows", None),
            P("rows"),
            P("rows"),
        ),
        out_specs=(P("rows", "cols"), P(None, "cols"), P("rows", "cols")),
        check_vma=False,
    )
```

```python
import functools
import math

import jax
import jax.numpy as jnp
from jax import lax
from jax.experimental import pallas as pl
from jax.experimental.pallas import tpu as pltpu
from jax.sharding import PartitionSpec as P

VMEM = pl.BlockSpec(memory_space=pltpu.VMEM)
SMEM = pl.BlockSpec(memory_space=pltpu.SMEM)
ANY = pl.BlockSpec(memory_space=pl.ANY)
HBM = pl.BlockSpec(memory_space=pltpu.HBM)
SPARE_BYTES = 2 * 1024 * 1024
PACK_BYTES = 56 * 1024 * 1024
UNROLL = 8
LARGEST_PLANE = 4


def params(*shapes):
    room = SPARE_BYTES
    for shape in shapes:
        *lead, high, wide = shape.shape
        room += math.prod(lead) * high * (-(-wide // 128) * 128) * jnp.dtype(shape.dtype).itemsize
    return pltpu.CompilerParams(vmem_limit_bytes=room)


def quotient(x, n):
    return x >> (n.bit_length() - 1) if n & (n - 1) == 0 else lax.div(x, n)


def remainder(x, n):
    return x & (n - 1) if n & (n - 1) == 0 else lax.rem(x, n)


def position(plane):
    index, col = lax.axis_index("rows"), lax.axis_index("cols")
    return quotient(index, plane), remainder(index, plane), col, 1 - 2 * (col & 1)


def shuffle(x, pairs):
    return lax.ppermute(x, "rows", pairs)


def across_plane(x, k, line, plane):
    return shuffle(x, [(r, r ^ k) for r in range(line * plane)])


CODE_ROWS = 16


def pack_kernel(plane, cols, owner_ref, row_ref, source_ref, tiles_ref, *refs):
    out_refs, (codes_ref, *scratch) = refs[: plane - 1], refs[plane - 1 :]
    list_ref, slot_ref, owners_ref, along_ref, rows_ref, held_ref, small_sems, held_sem = scratch
    _, place, col, _ = position(plane)
    tiles, size = tiles_ref.shape[:2]
    slots = (out_refs[0].shape[0] - CODE_ROWS) // size
    spare = (plane - 1) * slots
    looks = [pltpu.make_async_copy(owner_ref, owners_ref, small_sems.at[0])]
    for i, ref in enumerate((owner_ref, row_ref, source_ref)):
        looks.append(pltpu.make_async_copy(ref, along_ref.at[i], small_sems.at[1 + i]))
    for look in looks:
        look.start()
    bulk = pltpu.make_async_copy(tiles_ref, held_ref, held_sem)
    bulk.start()
    for k in range(plane):
        slot_ref[k] = 0
    for i in range(spare):
        list_ref[i] = 0
    rows_ref[...] = jnp.zeros_like(rows_ref)
    for look in looks:
        look.wait()

    def step(t, carry):
        k = remainder(owners_ref[0, t], plane) ^ place
        slot = slot_ref[k]
        slot_ref[k] = slot + 1
        sent = (k > 0) & (remainder(slot, cols) == col)
        list_ref[jnp.where(sent, (k - 1) * slots + quotient(slot, cols), spare)] = t
        return carry

    lax.fori_loop(0, tiles, step, 0, unroll=4)
    owners = along_ref[0]
    rows_ref[0:1, :tiles] = remainder(owners, plane).astype(jnp.float32)
    rows_ref[1:2, :tiles] = along_ref[1].astype(jnp.float32)
    rows_ref[2:3, :tiles] = along_ref[2].astype(jnp.float32)
    rows_ref[3:4, :tiles] = quotient(owners, plane).astype(jnp.float32)
    codes = rows_ref[...].astype(codes_ref.dtype)
    codes_ref[...] = codes
    bulk.wait()
    for k, out_ref in enumerate(out_refs):
        for slot in range(slots):
            out_ref[slot * size : (slot + 1) * size] = held_ref[list_ref[k * slots + slot]]
        out_ref[slots * size :] = codes


def pack_tiles(owners, tile_row, source_block, tile_values, plane, cols, slots):
    tiles, size, wide = tile_values.shape
    shape = jax.ShapeDtypeStruct((slots * size + CODE_ROWS, wide), tile_values.dtype)
    codes = jax.ShapeDtypeStruct((CODE_ROWS, wide), tile_values.dtype)
    along = [x.reshape(1, tiles) for x in (owners, tile_row, source_block)]
    return pl.pallas_call(
        functools.partial(pack_kernel, plane, cols),
        out_shape=(shape,) * (plane - 1) + (codes,),
        in_specs=[HBM] * 4,
        out_specs=(VMEM,) * plane,
        scratch_shapes=[
            pltpu.SMEM(((plane - 1) * slots + 1,), jnp.int32),
            pltpu.SMEM((plane,), jnp.int32),
            pltpu.SMEM((1, tiles), jnp.int32),
            pltpu.VMEM((3, 1, tiles), jnp.int32),
            pltpu.VMEM((CODE_ROWS, wide), jnp.float32),
            pltpu.VMEM((tiles, size, wide), tile_values.dtype),
            pltpu.SemaphoreType.DMA((4,)),
            pltpu.SemaphoreType.DMA,
        ],
        compiler_params=pltpu.CompilerParams(vmem_limit_bytes=PACK_BYTES),
        name="pack_tiles",
    )(*along, tile_values)


DST_BIT, SRC_BIT, PLACE_BIT = 10, 16, 24


def own_kernel(tiles_ref, codes_ref, out_ref, own_ref, sems):
    rows = tiles_ref.shape[0]
    moves = ((tiles_ref, out_ref.at[pl.ds(0, rows)]), (codes_ref, own_ref))
    copies = [pltpu.make_async_copy(*move, sems.at[i]) for i, move in enumerate(moves)]
    for copy in copies:
        copy.start()
    out_ref[out_ref.shape[0] - out_ref.shape[1] :] = jnp.zeros(
        (out_ref.shape[1], out_ref.shape[1]), out_ref.dtype
    )
    for copy in copies:
        copy.wait()


def own_tiles(tiles, codes, spots):
    wide = tiles.shape[1]
    laid = jax.ShapeDtypeStruct((spots * wide, wide), tiles.dtype)
    return pl.pallas_call(
        own_kernel,
        out_shape=(laid, jax.ShapeDtypeStruct(codes.shape, codes.dtype)),
        in_specs=[ANY, ANY],
        out_specs=(VMEM, VMEM),
        scratch_shapes=[pltpu.SemaphoreType.DMA((2,))],
        compiler_params=params(laid),
        name="own_tiles",
    )(tiles, codes)


def collect_kernel(plane, cols, slots, blocks, tiles, own_ref, laid_ref, *refs):
    tile_refs, refs = refs[: (plane - 1) * cols], refs[(plane - 1) * cols :]
    out_ref, plan_ref, count_ref, *scratch = refs
    rows_ref, words_ref, codes_ref, row_sems, word_sem, tile_sems = scratch
    _, place, col, _ = position(plane)
    size = out_ref.shape[1]
    looks = []
    for k in range(plane):
        ref = own_ref
        if k > 0:
            ref = tile_refs[(k - 1) * cols].at[pl.ds(slots * size, CODE_ROWS)]
        copy = pltpu.make_async_copy(ref, rows_ref.at[k], row_sems.at[k])
        copy.start()
        looks.append(copy)
    copies, first, rows = [], tiles * size, slots * size
    for i, ref in enumerate(tile_refs):
        copy = pltpu.make_async_copy(
            ref.at[pl.ds(0, rows)], out_ref.at[pl.ds(first, rows)], tile_sems.at[i]
        )
        copy.start()
        copies.append(copy)
        first += rows
    words_ref[...] = jnp.zeros_like(words_ref)
    for k, copy in enumerate(looks):
        copy.wait()
        rows = rows_ref[k].astype(jnp.float32).astype(jnp.int32)
        source = rows[3:4] * blocks + rows[2:3]
        word = (rows[0:1] << PLACE_BIT) + (source << SRC_BIT)
        words_ref[k : k + 1] = word + ((rows[1:2] + k * blocks) << DST_BIT)
    copy = pltpu.make_async_copy(words_ref, codes_ref, word_sem)
    copy.start()
    copy.wait()
    found = jnp.int32(0)
    for k in range(plane):

        def step(t, carry, k=k):
            at, slot = carry
            code = codes_ref[k, t]
            if k == 0:
                spot = t
            else:
                column = remainder(slot + (cols - col), cols)
                spot = tiles + ((k - 1) * cols + column) * slots + quotient(slot, cols)
            plan_ref[at] = (code & ((1 << PLACE_BIT) - 1)) + spot
            one = ((code >> PLACE_BIT) == place).astype(jnp.int32)
            return at + one, slot + one

        found, _ = lax.fori_loop(0, tiles, step, (found, jnp.int32(0)), unroll=8)
    for i in range(UNROLL):
        plan_ref[found + i] = first // size
    count_ref[0] = quotient(found + UNROLL - 1, UNROLL)
    for copy in copies:
        copy.wait()


def collect_tiles(codes, laid, tile_parts, plane, cols, slots, blocks, tiles):
    wide = laid.shape[1]
    entries = plane * tiles + UNROLL
    high = -(-plane // 8) * 8
    return pl.pallas_call(
        functools.partial(collect_kernel, plane, cols, slots, blocks, tiles),
        out_shape=(
            jax.ShapeDtypeStruct(laid.shape, laid.dtype),
            jax.ShapeDtypeStruct((entries,), jnp.int32),
            jax.ShapeDtypeStruct((1,), jnp.int32),
        ),
        in_specs=[ANY] * (2 + len(tile_parts)),
        out_specs=(ANY, SMEM, SMEM),
        scratch_shapes=[
            pltpu.VMEM((plane, CODE_ROWS, wide), jnp.bfloat16),
            pltpu.VMEM((high, wide), jnp.int32),
            pltpu.SMEM((high, wide), jnp.int32),
            pltpu.SemaphoreType.DMA((plane,)),
            pltpu.SemaphoreType.DMA,
            pltpu.SemaphoreType.DMA((len(tile_parts),)),
        ],
        input_output_aliases={1: 0},
        compiler_params=params(),
        name="collect_tiles",
    )(codes, laid, *tile_parts)


def planned(plan_ref, t):
    entry = plan_ref[t]
    spot = entry & ((1 << DST_BIT) - 1)
    return spot, (entry >> DST_BIT) & ((1 << (SRC_BIT - DST_BIT)) - 1), entry >> SRC_BIT


def block_rows(index, size):
    return pl.ds(pl.multiple_of(index * size, size), size)


def forward_kernel(line, lanes, plane, plan_ref, count_ref, tiles_ref, *refs):
    part_refs, refs = refs[: 2 * line - 1], refs[2 * line - 1 :]
    out_refs, (nodes_ref, acc_ref, part_sems) = refs[:-3], refs[-3:]
    rows, width = part_refs[0].shape[0], nodes_ref.shape[1]
    size = tiles_ref.shape[1]
    mine, _, _, way = position(plane)

    def each_part(act):
        for i, ref in enumerate(part_refs):
            source = mine + way * (i - (line - 1))

            @pl.when((source >= 0) & (source < line))
            def _():
                here = ref.at[:, lanes] if ref.shape != (rows, width) else ref
                act(
                    pltpu.make_async_copy(
                        here, nodes_ref.at[block_rows(source, rows)], part_sems.at[i]
                    )
                )

    each_part(lambda copy: copy.start())
    acc_ref[...] = jnp.zeros_like(acc_ref)
    each_part(lambda copy: copy.wait())

    def step(i, carry):
        ready = None
        for spot, dst, src in [planned(plan_ref, i * UNROLL + j) for j in range(UNROLL)]:
            product = jnp.dot(
                tiles_ref[block_rows(spot, size)],
                nodes_ref[block_rows(src, size)],
                preferred_element_type=jnp.float32,
            )
            if ready is not None:
                acc_ref[ready[0]] += ready[1]
            ready = block_rows(dst, size), product
        acc_ref[ready[0]] += ready[1]
        return carry

    lax.fori_loop(0, count_ref[0], step, 0)
    for k, ref in enumerate(out_refs):
        ref[...] = acc_ref[k * rows : (k + 1) * rows].astype(ref.dtype)


def forward_tiles(plan, count, tiles, node_parts, plane, lanes):
    line = (len(node_parts) + 1) // 2
    rows, width = node_parts[0].shape[0], lanes.size
    kinds = [jnp.float32] + [jnp.bfloat16] * (plane - 1)
    outs = tuple(jax.ShapeDtypeStruct((rows, width), kind) for kind in kinds)
    scratch = [
        pltpu.VMEM((line * rows, width), jnp.bfloat16),
        pltpu.VMEM((plane * rows, width), jnp.float32),
    ]
    return pl.pallas_call(
        functools.partial(forward_kernel, line, lanes, plane),
        out_shape=outs,
        in_specs=[SMEM] * 2 + [VMEM] + [ANY] * len(node_parts),
        out_specs=(VMEM,) * plane,
        scratch_shapes=scratch + [pltpu.SemaphoreType.DMA((len(node_parts),))],
        compiler_params=params(tiles, *outs, *scratch),
        name="forward_tiles",
    )(plan, count, tiles, *node_parts)


def dense_kernel(chunk, halves, labels_ref, weight_ref, *refs):
    parts, (act_ref, out_grad_ref, agg_grad_ref) = refs[:-3], refs[-3:]
    rows, part_width = parts[0].shape
    width = part_width * halves
    features = weight_ref.shape[0]
    size = labels_ref.shape[1]

    def rows_step(i, carry):
        here = block_rows(i, chunk)
        agg = jnp.concatenate([part[here, :] for part in parts], axis=1)
        hidden = jnp.dot(agg, weight_ref[...], preferred_element_type=jnp.float32)
        sigmoid = jax.nn.sigmoid(hidden)
        activated = hidden * sigmoid
        act_ref[here, :] = activated[:, :width].astype(act_ref.dtype)
        slopes = sigmoid * (1.0 + hidden * (1.0 - sigmoid))
        named = []
        for b in range(chunk // size):
            across = labels_ref[pl.ds(i * (chunk // size) + b, 1), :]
            named.append(jnp.broadcast_to(across, (size, size)).T)
        named = jnp.concatenate(named, axis=0)
        ids = lax.broadcasted_iota(jnp.int32, (chunk, size), 1).astype(jnp.float32)
        target = jnp.concatenate(
            [(named == ids + f * size).astype(jnp.float32) for f in range(features // size)],
            axis=1,
        )
        out_grad = ((activated - target) * slopes).astype(jnp.bfloat16)
        out_grad_ref[here, :] = out_grad
        agg_grad_ref[here, :] = lax.dot_general(
            out_grad,
            weight_ref[:part_width, :],
            (((1,), (1,)), ((), ())),
            preferred_element_type=jnp.float32,
        ).astype(agg_grad_ref.dtype)
        return carry

    lax.fori_loop(0, rows // chunk, rows_step, 0)


def dense(labels, weight, parts, halves):
    rows, part_width = parts[0].shape
    chunk = math.gcd(rows, 256)
    outs = tuple(
        jax.ShapeDtypeStruct((rows, width), jnp.bfloat16)
        for width in (part_width * halves, weight.shape[0], part_width)
    )
    return pl.pallas_call(
        functools.partial(dense_kernel, chunk, halves),
        out_shape=outs,
        in_specs=[VMEM] * (2 + len(parts)),
        out_specs=(VMEM,) * 3,
        compiler_params=params(labels, weight, *parts, *outs),
        name="dense",
    )(labels, weight, *parts)


def grads_kernel(scale, halves, weight_ref, out_grad_ref, *refs):
    parts, (terms_ref, *agg_grad_refs) = refs[: -halves], refs[-halves:]
    part_width = parts[0].shape[1]
    for h, ref in enumerate(agg_grad_refs, 1):
        ref[...] = lax.dot_general(
            out_grad_ref[...],
            weight_ref[h * part_width : (h + 1) * part_width, :],
            (((1,), (1,)), ((), ())),
            preferred_element_type=jnp.float32,
        ).astype(ref.dtype)
    for i, part in enumerate(parts):
        terms = lax.dot_general(
            part[...],
            out_grad_ref[:, : part_width * halves],
            (((0,), (0,)), ((), ())),
            preferred_element_type=jnp.float32,
        )
        terms_ref[i * part_width : (i + 1) * part_width] = (terms * scale).astype(terms_ref.dtype)


def grads(weight, out_grad, parts, halves, node_total):
    rows, part_width = parts[0].shape
    outs = (jax.ShapeDtypeStruct((weight.shape[0], part_width * halves), jnp.bfloat16),) + (
        jax.ShapeDtypeStruct((rows, part_width), jnp.bfloat16),
    ) * (halves - 1)
    return pl.pallas_call(
        functools.partial(grads_kernel, 1.0 / math.sqrt(node_total), halves),
        out_shape=outs,
        in_specs=[VMEM] * (2 + len(parts)),
        out_specs=(VMEM,) * halves,
        compiler_params=params(weight, out_grad, *parts, *outs),
        name="grads",
    )(weight, out_grad, *parts)


def spread_kernel(line, plane, plan_ref, count_ref, tiles_ref, *refs):
    grad_refs, refs = refs[:plane], refs[plane:]
    out_refs, (grads_ref, acc_ref, grad_sems) = refs[:-3], refs[-3:]
    rows = grad_refs[0].shape[0]
    size = tiles_ref.shape[1]
    mine, _, _, way = position(plane)
    copies = []
    for k, ref in enumerate(grad_refs):
        copy = pltpu.make_async_copy(ref, grads_ref.at[pl.ds(k * rows, rows)], grad_sems.at[k])
        copy.start()
        copies.append(copy)
    acc_ref[...] = jnp.zeros_like(acc_ref)
    for copy in copies:
        copy.wait()

    def step(i, carry):
        ready = None
        for spot, dst, src in [planned(plan_ref, i * UNROLL + j) for j in range(UNROLL)]:
            product = lax.dot_general(
                tiles_ref[block_rows(spot, size)],
                grads_ref[block_rows(dst, size)],
                (((0,), (0,)), ((), ())),
                preferred_element_type=jnp.float32,
            )
            if ready is not None:
                acc_ref[ready[0]] += ready[1]
            ready = block_rows(src, size), product
        acc_ref[ready[0]] += ready[1]
        return carry

    lax.fori_loop(0, count_ref[0], step, 0)
    for i, ref in enumerate(out_refs):
        target = mine + way * (i - (line - 1))

        @pl.when((target >= 0) & (target < line))
        def _():
            ref[...] = acc_ref[block_rows(target, rows)].astype(ref.dtype)


def spread_tiles(plan, count, tiles, grad_parts, line):
    plane = len(grad_parts)
    rows, width = grad_parts[0].shape
    kinds = [jnp.float32 if i == line - 1 else jnp.bfloat16 for i in range(2 * line - 1)]
    outs = tuple(jax.ShapeDtypeStruct((rows, width), kind) for kind in kinds)
    scratch = [
        pltpu.VMEM((plane * rows, width), jnp.bfloat16),
        pltpu.VMEM((line * rows, width), jnp.float32),
    ]
    return pl.pallas_call(
        functools.partial(spread_kernel, line, plane),
        out_shape=outs,
        in_specs=[SMEM] * 2 + [VMEM] + [ANY] * plane,
        out_specs=(VMEM,) * (2 * line - 1),
        scratch_shapes=scratch + [pltpu.SemaphoreType.DMA((plane,))],
        compiler_params=params(tiles, *outs, *scratch),
        name="spread_tiles",
    )(plan, count, tiles, *grad_parts)


def along_line(x, line, plane, cols, step, reach):
    pairs = []
    for z in range(line):
        for q in range(plane):
            for c in range(cols):
                way = 1 - 2 * (c & 1)
                to, end = z + way * step, z + way * reach
                if 0 <= to < line and 0 <= end < line:
                    pairs.append(((z * plane + q) * cols + c, (to * plane + q) * cols + c))
    return lax.ppermute(x, ("rows", "cols"), pairs)


def line_gather(x, after, line, plane, cols, lanes):
    move = lambda part, step, reach: along_line(part, line, plane, cols, step, reach)
    later, _ = lax.optimization_barrier((x, after))
    up, down = [x], [later]
    for k in range(1, line - 1):
        up.append(move(up[-1], 1, 1 - k))
        down.append(move(down[-1], -1, k - 1))
    parts, high, low = [], up[-1], down[-1]
    for part in lanes:
        first = move(high[:, part], 1, 2 - line)
        last = move(low[:, part], -1, line - 2)
        parts.append([first] + up[:0:-1] + down + [last])
    return parts


def line_sum(terms, line, plane, cols, beside):
    moved, late = {1: None, -1: None}, None
    for k in range(line - 1, 0, -1):
        for step in moved:
            term = terms[line - 1 + step * k]
            if moved[step] is not None:
                total = term.astype(jnp.float32) + moved[step].astype(jnp.float32)
                term = total.astype(term.dtype)
            moved[step] = along_line(term, line, plane, cols, step, step * k)
        if k == line - 1 and beside is not None:
            moved, beside = lax.optimization_barrier((moved, beside))
        if k > 1:
            late = tuple(moved.values())
    return [terms[line - 1], moved[1], moved[-1]], beside, late


def finish_kernel(halves, cols, mine_ref, other_ref, *refs):
    (weight_ref, out_ref), refs = refs[-2:], refs[:-2]
    col = lax.axis_index("cols")
    wide = weight_ref.shape[1]
    for c in range(cols):
        here = pl.ds(c * wide, wide)
        total = mine_ref[here].astype(jnp.float32) + other_ref[here].astype(jnp.float32)
        row = remainder(col + c, cols) * wide
        weight_ref[pl.ds(pl.multiple_of(row, wide), wide)] = total
    each = len(refs) // halves
    width = refs[0].shape[1]
    for h in range(halves):
        total = refs[h * each][...]
        for ref in refs[h * each + 1 : (h + 1) * each]:
            total += ref[...].astype(jnp.float32)
        out_ref[:, h * width : (h + 1) * width] = total.astype(out_ref.dtype)


def finish(mine, other, pieces, cols):
    flat = [piece for half in pieces for piece in half]
    rows, width = flat[0].shape
    outs = (
        jax.ShapeDtypeStruct(mine.shape, jnp.float32),
        jax.ShapeDtypeStruct((rows, width * len(pieces)), jnp.bfloat16),
    )
    return pl.pallas_call(
        functools.partial(finish_kernel, len(pieces), cols),
        out_shape=outs,
        in_specs=[VMEM] * (2 + len(flat)),
        out_specs=(VMEM, VMEM),
        compiler_params=params(mine, other, *outs, *flat),
        name="finish",
    )(mine, other, *flat)


def sum_apart(terms, first, end, rows):
    while first < end:
        other = shuffle(terms, [(r, r ^ first) for r in range(rows)])
        total = terms.astype(jnp.float32) + other.astype(jnp.float32)
        terms = total.astype(terms.dtype)
        first *= 2
    return terms


def prepare_kernel(cols, labels_ref, weight_ref, own_labels_ref, own_first_ref, wide_ref):
    col = lax.axis_index("cols")
    features = weight_ref.shape[0]
    width = features // cols
    labels = labels_ref[...] - col * width
    own_labels_ref[...] = jnp.where(labels < 0, labels + features, labels).astype(jnp.float32)
    for c in range(cols):
        row = remainder(col + c, cols) * width
        rows = weight_ref[pl.ds(pl.multiple_of(row, width), width), :]
        wide_ref[c * width : (c + 1) * width] = rows.astype(jnp.float32)
    turned = pltpu.roll(wide_ref[...], remainder(cols - col, cols) * width, axis=1)
    own_first_ref[...] = turned.astype(own_first_ref.dtype)


def prepare(labels, weight, cols):
    outs = (jax.ShapeDtypeStruct(labels.shape, jnp.float32), weight)
    wide = pltpu.VMEM(weight.shape, jnp.float32)
    return pl.pallas_call(
        functools.partial(prepare_kernel, cols),
        out_shape=(outs[0], jax.ShapeDtypeStruct(weight.shape, weight.dtype)),
        in_specs=[VMEM, VMEM],
        out_specs=(VMEM, VMEM),
        scratch_shapes=[wide],
        compiler_params=params(weight, weight, wide, wide),
        name="prepare",
    )(labels, weight)


def per_device(node_features, weight, tile_values, tile_row, source_owner, source_block, labels):
    local_rows, width = node_features.shape
    n_tiles, block_size = tile_values.shape[:2]
    blocks = local_rows // block_size
    rows, cols = lax.axis_size("rows"), lax.axis_size("cols")
    plane = math.gcd(rows, LARGEST_PLANE)
    line = rows // plane
    halves = 2 if width % 256 == 0 else 1
    part_width = width // halves
    slots = -(-min(n_tiles, line * (2 * n_tiles // rows)) // cols)
    owners = source_owner[:, 0]

    def other_cols(x):
        return [
            lax.ppermute(x, "cols", [((c + k) % cols, c) for c in range(cols)])
            for k in range(1, cols)
        ]

    lanes = [slice(h * part_width, (h + 1) * part_width) for h in range(halves)]
    *packed, codes = pack_tiles(
        owners, tile_row, source_block, tile_values, plane, cols, slots
    )
    node_parts = line_gather(node_features, packed, line, plane, cols, lanes)
    spots = n_tiles + (plane - 1) * cols * slots + 1
    flat = tile_values.reshape(n_tiles * block_size, block_size)
    early = own_tiles(flat, codes, spots) + prepare(labels.reshape(blocks, block_size), weight, cols)
    tile_parts = []
    for k in range(1, plane):
        arrived = across_plane(packed[k - 1], k, line, plane)
        if k == 1:
            arrived, early = lax.optimization_barrier((arrived, early))
        tile_parts += [arrived] + other_cols(arrived)
    laid, codes, own_labels, own_first = early
    tiles, plan, count = collect_tiles(
        codes, laid, tile_parts, plane, cols, slots, blocks, n_tiles
    )

    aggregated = []
    for h in range(halves):
        here = pl.ds(h * part_width, part_width)
        sums = forward_tiles(plan, count, tiles, node_parts[h], plane, here)
        total = sums[0]
        for k in range(1, plane):
            total = total + across_plane(sums[k], k, line, plane).astype(jnp.float32)
        mine = total.astype(jnp.bfloat16)
        aggregated.append([mine] + other_cols(mine))
    parts = [aggregated[h][c] for c in range(cols) for h in range(halves)]

    activations, out_grad, agg_grad = dense(own_labels, own_first, parts, halves)
    weight_terms, *agg_grads = grads(own_first, out_grad, parts, halves, local_rows * rows)

    pieces = []
    for i, agg_grad in enumerate([agg_grad] + agg_grads):
        arrived = [agg_grad] + [across_plane(agg_grad, k, line, plane) for k in range(1, plane)]
        if i == 0:
            weight_terms = sum_apart(weight_terms, plane, 2 * plane, rows)
            arrived, weight_terms = lax.optimization_barrier((arrived, weight_terms))
            weight_terms = sum_apart(weight_terms, 2 * plane, rows, rows)
        terms = spread_tiles(plan, count, tiles, arrived, line)
        beside = weight_terms if i == 0 else None
        half, beside, late = line_sum(terms, line, plane, cols, beside)
        if i == 0:
            weight_terms, _ = lax.optimization_barrier((beside, late))
        pieces.append(half)
    weight_terms = sum_apart(weight_terms, 1, plane // 2, rows)
    weight_terms, _ = lax.optimization_barrier((weight_terms, late))
    other = across_plane(weight_terms, plane // 2, line, plane)
    return (activations,) + tuple(finish(weight_terms, other, pieces, cols))


def solution(mesh):
    return jax.shard_map(
        per_device,
        mesh=mesh,
        in_specs=(
            P("rows", "cols"),
            P(),
            P("rows", None, None),
            P("rows"),
            P("rows", None),
            P("rows"),
            P("rows"),
        ),
        out_specs=(P("rows", "cols"), P(None, "cols"), P("rows", "cols")),
        check_vma=False,
    )
```

```python
import functools
import math

import jax
import jax.numpy as jnp
from jax import lax
from jax.experimental import pallas as pl
from jax.experimental.pallas import tpu as pltpu
from jax.sharding import PartitionSpec as P

VMEM = pl.BlockSpec(memory_space=pltpu.VMEM)
SMEM = pl.BlockSpec(memory_space=pltpu.SMEM)
ANY = pl.BlockSpec(memory_space=pl.ANY)
HBM = pl.BlockSpec(memory_space=pltpu.HBM)
SPARE_BYTES = 2 * 1024 * 1024
PACK_BYTES = 56 * 1024 * 1024
UNROLL = 8
LARGEST_PLANE = 4


def params(*shapes):
    room = SPARE_BYTES
    for shape in shapes:
        *lead, high, wide = shape.shape
        room += math.prod(lead) * high * (-(-wide // 128) * 128) * jnp.dtype(shape.dtype).itemsize
    return pltpu.CompilerParams(vmem_limit_bytes=room)


def quotient(x, n):
    return x >> (n.bit_length() - 1) if n & (n - 1) == 0 else lax.div(x, n)


def remainder(x, n):
    return x & (n - 1) if n & (n - 1) == 0 else lax.rem(x, n)


def position(plane):
    index, col = lax.axis_index("rows"), lax.axis_index("cols")
    return quotient(index, plane), remainder(index, plane), col, 1 - 2 * (col & 1)


def shuffle(x, pairs):
    return lax.ppermute(x, "rows", pairs)


def across_plane(x, k, line, plane):
    return shuffle(x, [(r, r ^ k) for r in range(line * plane)])


CODE_ROWS = 16


def pack_kernel(plane, cols, owner_ref, row_ref, source_ref, tiles_ref, *refs):
    out_refs, (codes_ref, *scratch) = refs[: plane - 1], refs[plane - 1 :]
    list_ref, slot_ref, owners_ref, along_ref, rows_ref, held_ref, small_sems, held_sem = scratch
    _, place, col, _ = position(plane)
    tiles, size = tiles_ref.shape[:2]
    slots = (out_refs[0].shape[0] - CODE_ROWS) // size
    spare = (plane - 1) * slots
    looks = [pltpu.make_async_copy(owner_ref, owners_ref, small_sems.at[0])]
    for i, ref in enumerate((owner_ref, row_ref, source_ref)):
        looks.append(pltpu.make_async_copy(ref, along_ref.at[i], small_sems.at[1 + i]))
    for look in looks:
        look.start()
    bulk = pltpu.make_async_copy(tiles_ref, held_ref, held_sem)
    bulk.start()
    for k in range(plane):
        slot_ref[k] = 0
    for i in range(spare):
        list_ref[i] = 0
    rows_ref[...] = jnp.zeros_like(rows_ref)
    for look in looks:
        look.wait()

    def step(t, carry):
        k = remainder(owners_ref[0, t], plane) ^ place
        slot = slot_ref[k]
        slot_ref[k] = slot + 1
        sent = (k > 0) & (remainder(slot, cols) == col)
        list_ref[jnp.where(sent, (k - 1) * slots + quotient(slot, cols), spare)] = t
        return carry

    lax.fori_loop(0, tiles, step, 0, unroll=4)
    owners = along_ref[0]
    rows_ref[0:1, :tiles] = remainder(owners, plane).astype(jnp.float32)
    rows_ref[1:2, :tiles] = along_ref[1].astype(jnp.float32)
    rows_ref[2:3, :tiles] = along_ref[2].astype(jnp.float32)
    rows_ref[3:4, :tiles] = quotient(owners, plane).astype(jnp.float32)
    codes = rows_ref[...].astype(codes_ref.dtype)
    codes_ref[...] = codes
    bulk.wait()
    for k, out_ref in enumerate(out_refs):
        for slot in range(slots):
            out_ref[slot * size : (slot + 1) * size] = held_ref[list_ref[k * slots + slot]]
        out_ref[slots * size :] = codes


def pack_tiles(owners, tile_row, source_block, tile_values, plane, cols, slots):
    tiles, size, wide = tile_values.shape
    shape = jax.ShapeDtypeStruct((slots * size + CODE_ROWS, wide), tile_values.dtype)
    codes = jax.ShapeDtypeStruct((CODE_ROWS, wide), tile_values.dtype)
    along = [x.reshape(1, tiles) for x in (owners, tile_row, source_block)]
    return pl.pallas_call(
        functools.partial(pack_kernel, plane, cols),
        out_shape=(shape,) * (plane - 1) + (codes,),
        in_specs=[HBM] * 4,
        out_specs=(VMEM,) * plane,
        scratch_shapes=[
            pltpu.SMEM(((plane - 1) * slots + 1,), jnp.int32),
            pltpu.SMEM((plane,), jnp.int32),
            pltpu.SMEM((1, tiles), jnp.int32),
            pltpu.VMEM((3, 1, tiles), jnp.int32),
            pltpu.VMEM((CODE_ROWS, wide), jnp.float32),
            pltpu.VMEM((tiles, size, wide), tile_values.dtype),
            pltpu.SemaphoreType.DMA((4,)),
            pltpu.SemaphoreType.DMA,
        ],
        compiler_params=pltpu.CompilerParams(vmem_limit_bytes=PACK_BYTES),
        name="pack_tiles",
    )(*along, tile_values)


DST_BIT, SRC_BIT, PLACE_BIT = 10, 16, 24


def own_kernel(tiles_ref, codes_ref, out_ref, own_ref, sems):
    rows = tiles_ref.shape[0]
    moves = ((tiles_ref, out_ref.at[pl.ds(0, rows)]), (codes_ref, own_ref))
    copies = [pltpu.make_async_copy(*move, sems.at[i]) for i, move in enumerate(moves)]
    for copy in copies:
        copy.start()
    out_ref[out_ref.shape[0] - out_ref.shape[1] :] = jnp.zeros(
        (out_ref.shape[1], out_ref.shape[1]), out_ref.dtype
    )
    for copy in copies:
        copy.wait()


def own_tiles(tiles, codes, spots):
    wide = tiles.shape[1]
    laid = jax.ShapeDtypeStruct((spots * wide, wide), tiles.dtype)
    return pl.pallas_call(
        own_kernel,
        out_shape=(laid, jax.ShapeDtypeStruct(codes.shape, codes.dtype)),
        in_specs=[ANY, ANY],
        out_specs=(VMEM, VMEM),
        scratch_shapes=[pltpu.SemaphoreType.DMA((2,))],
        compiler_params=params(laid),
        name="own_tiles",
    )(tiles, codes)


def collect_kernel(plane, cols, slots, blocks, tiles, own_ref, laid_ref, *refs):
    tile_refs, refs = refs[: (plane - 1) * cols], refs[(plane - 1) * cols :]
    out_ref, plan_ref, count_ref, *scratch = refs
    rows_ref, words_ref, codes_ref, row_sems, word_sem, tile_sems = scratch
    _, place, col, _ = position(plane)
    size = out_ref.shape[1]
    looks = []
    for k in range(plane):
        ref = own_ref
        if k > 0:
            ref = tile_refs[(k - 1) * cols].at[pl.ds(slots * size, CODE_ROWS)]
        copy = pltpu.make_async_copy(ref, rows_ref.at[k], row_sems.at[k])
        copy.start()
        looks.append(copy)
    copies, first, rows = [], tiles * size, slots * size
    for i, ref in enumerate(tile_refs):
        copy = pltpu.make_async_copy(
            ref.at[pl.ds(0, rows)], out_ref.at[pl.ds(first, rows)], tile_sems.at[i]
        )
        copy.start()
        copies.append(copy)
        first += rows
    words_ref[...] = jnp.zeros_like(words_ref)
    for k, copy in enumerate(looks):
        copy.wait()
        rows = rows_ref[k].astype(jnp.float32).astype(jnp.int32)
        source = rows[3:4] * blocks + rows[2:3]
        word = (rows[0:1] << PLACE_BIT) + (source << SRC_BIT)
        words_ref[k : k + 1] = word + ((rows[1:2] + k * blocks) << DST_BIT)
    copy = pltpu.make_async_copy(words_ref, codes_ref, word_sem)
    copy.start()
    copy.wait()
    found = jnp.int32(0)
    for k in range(plane):

        def step(t, carry, k=k):
            at, slot = carry
            code = codes_ref[k, t]
            if k == 0:
                spot = t
            else:
                column = remainder(slot + (cols - col), cols)
                spot = tiles + ((k - 1) * cols + column) * slots + quotient(slot, cols)
            plan_ref[at] = (code & ((1 << PLACE_BIT) - 1)) + spot
            one = ((code >> PLACE_BIT) == place).astype(jnp.int32)
            return at + one, slot + one

        found, _ = lax.fori_loop(0, tiles, step, (found, jnp.int32(0)), unroll=8)
    for i in range(UNROLL):
        plan_ref[found + i] = first // size
    count_ref[0] = quotient(found + UNROLL - 1, UNROLL)
    for copy in copies:
        copy.wait()


def collect_tiles(codes, laid, tile_parts, plane, cols, slots, blocks, tiles):
    wide = laid.shape[1]
    entries = plane * tiles + UNROLL
    high = -(-plane // 8) * 8
    return pl.pallas_call(
        functools.partial(collect_kernel, plane, cols, slots, blocks, tiles),
        out_shape=(
            jax.ShapeDtypeStruct(laid.shape, laid.dtype),
            jax.ShapeDtypeStruct((entries,), jnp.int32),
            jax.ShapeDtypeStruct((1,), jnp.int32),
        ),
        in_specs=[ANY] * (2 + len(tile_parts)),
        out_specs=(ANY, SMEM, SMEM),
        scratch_shapes=[
            pltpu.VMEM((plane, CODE_ROWS, wide), jnp.bfloat16),
            pltpu.VMEM((high, wide), jnp.int32),
            pltpu.SMEM((high, wide), jnp.int32),
            pltpu.SemaphoreType.DMA((plane,)),
            pltpu.SemaphoreType.DMA,
            pltpu.SemaphoreType.DMA((len(tile_parts),)),
        ],
        input_output_aliases={1: 0},
        compiler_params=params(),
        name="collect_tiles",
    )(codes, laid, *tile_parts)


def planned(plan_ref, t):
    entry = plan_ref[t]
    spot = entry & ((1 << DST_BIT) - 1)
    return spot, (entry >> DST_BIT) & ((1 << (SRC_BIT - DST_BIT)) - 1), entry >> SRC_BIT


def block_rows(index, size):
    return pl.ds(pl.multiple_of(index * size, size), size)


def forward_kernel(line, lanes, plane, plan_ref, count_ref, tiles_ref, *refs):
    part_refs, refs = refs[: 2 * line - 1], refs[2 * line - 1 :]
    out_refs, (nodes_ref, acc_ref, part_sems) = refs[:-3], refs[-3:]
    rows, width = part_refs[0].shape[0], nodes_ref.shape[1]
    size = tiles_ref.shape[1]
    mine, _, _, way = position(plane)

    def each_part(act):
        for i, ref in enumerate(part_refs):
            source = mine + way * (i - (line - 1))

            @pl.when((source >= 0) & (source < line))
            def _():
                here = ref.at[:, lanes] if ref.shape != (rows, width) else ref
                act(
                    pltpu.make_async_copy(
                        here, nodes_ref.at[block_rows(source, rows)], part_sems.at[i]
                    )
                )

    each_part(lambda copy: copy.start())
    acc_ref[...] = jnp.zeros_like(acc_ref)
    each_part(lambda copy: copy.wait())

    def step(i, carry):
        ready = None
        for spot, dst, src in [planned(plan_ref, i * UNROLL + j) for j in range(UNROLL)]:
            product = jnp.dot(
                tiles_ref[block_rows(spot, size)],
                nodes_ref[block_rows(src, size)],
                preferred_element_type=jnp.float32,
            )
            if ready is not None:
                acc_ref[ready[0]] += ready[1]
            ready = block_rows(dst, size), product
        acc_ref[ready[0]] += ready[1]
        return carry

    lax.fori_loop(0, count_ref[0], step, 0)
    for k, ref in enumerate(out_refs):
        ref[...] = acc_ref[k * rows : (k + 1) * rows].astype(ref.dtype)


def forward_tiles(plan, count, tiles, node_parts, plane, lanes):
    line = (len(node_parts) + 1) // 2
    rows, width = node_parts[0].shape[0], lanes.size
    kinds = [jnp.float32] + [jnp.bfloat16] * (plane - 1)
    outs = tuple(jax.ShapeDtypeStruct((rows, width), kind) for kind in kinds)
    scratch = [
        pltpu.VMEM((line * rows, width), jnp.bfloat16),
        pltpu.VMEM((plane * rows, width), jnp.float32),
    ]
    return pl.pallas_call(
        functools.partial(forward_kernel, line, lanes, plane),
        out_shape=outs,
        in_specs=[SMEM] * 2 + [VMEM] + [ANY] * len(node_parts),
        out_specs=(VMEM,) * plane,
        scratch_shapes=scratch + [pltpu.SemaphoreType.DMA((len(node_parts),))],
        compiler_params=params(tiles, *outs, *scratch),
        name="forward_tiles",
    )(plan, count, tiles, *node_parts)


def dense_kernel(chunk, halves, labels_ref, weight_ref, *refs):
    parts, (act_ref, out_grad_ref, agg_grad_ref) = refs[:-3], refs[-3:]
    rows, part_width = parts[0].shape
    width = part_width * halves
    features = weight_ref.shape[0]
    size = labels_ref.shape[1]

    def rows_step(i, carry):
        here = block_rows(i, chunk)
        agg = jnp.concatenate([part[here, :] for part in parts], axis=1)
        hidden = jnp.dot(agg, weight_ref[...], preferred_element_type=jnp.float32)
        sigmoid = jax.nn.sigmoid(hidden)
        activated = hidden * sigmoid
        act_ref[here, :] = activated[:, :width].astype(act_ref.dtype)
        slopes = sigmoid * (1.0 + hidden * (1.0 - sigmoid))
        named = []
        for b in range(chunk // size):
            across = labels_ref[pl.ds(i * (chunk // size) + b, 1), :]
            named.append(jnp.broadcast_to(across, (size, size)).T)
        named = jnp.concatenate(named, axis=0)
        ids = lax.broadcasted_iota(jnp.int32, (chunk, size), 1).astype(jnp.float32)
        target = jnp.concatenate(
            [(named == ids + f * size).astype(jnp.float32) for f in range(features // size)],
            axis=1,
        )
        out_grad = ((activated - target) * slopes).astype(jnp.bfloat16)
        out_grad_ref[here, :] = out_grad
        agg_grad_ref[here, :] = lax.dot_general(
            out_grad,
            weight_ref[:part_width, :],
            (((1,), (1,)), ((), ())),
            preferred_element_type=jnp.float32,
        ).astype(agg_grad_ref.dtype)
        return carry

    lax.fori_loop(0, rows // chunk, rows_step, 0)


def dense(labels, weight, parts, halves):
    rows, part_width = parts[0].shape
    chunk = math.gcd(rows, 256)
    outs = tuple(
        jax.ShapeDtypeStruct((rows, width), jnp.bfloat16)
        for width in (part_width * halves, weight.shape[0], part_width)
    )
    return pl.pallas_call(
        functools.partial(dense_kernel, chunk, halves),
        out_shape=outs,
        in_specs=[VMEM] * (2 + len(parts)),
        out_specs=(VMEM,) * 3,
        compiler_params=params(labels, weight, *parts, *outs),
        name="dense",
    )(labels, weight, *parts)


def grads_kernel(scale, halves, weight_ref, out_grad_ref, *refs):
    parts, (terms_ref, *agg_grad_refs) = refs[: -halves], refs[-halves:]
    part_width = parts[0].shape[1]
    for h, ref in enumerate(agg_grad_refs, 1):
        ref[...] = lax.dot_general(
            out_grad_ref[...],
            weight_ref[h * part_width : (h + 1) * part_width, :],
            (((1,), (1,)), ((), ())),
            preferred_element_type=jnp.float32,
        ).astype(ref.dtype)
    for i, part in enumerate(parts):
        terms = lax.dot_general(
            part[...],
            out_grad_ref[:, : part_width * halves],
            (((0,), (0,)), ((), ())),
            preferred_element_type=jnp.float32,
        )
        terms_ref[i * part_width : (i + 1) * part_width] = (terms * scale).astype(terms_ref.dtype)


def grads(weight, out_grad, parts, halves, node_total):
    rows, part_width = parts[0].shape
    outs = (jax.ShapeDtypeStruct((weight.shape[0], part_width * halves), jnp.bfloat16),) + (
        jax.ShapeDtypeStruct((rows, part_width), jnp.bfloat16),
    ) * (halves - 1)
    return pl.pallas_call(
        functools.partial(grads_kernel, 1.0 / math.sqrt(node_total), halves),
        out_shape=outs,
        in_specs=[VMEM] * (2 + len(parts)),
        out_specs=(VMEM,) * halves,
        compiler_params=params(weight, out_grad, *parts, *outs),
        name="grads",
    )(weight, out_grad, *parts)


def spread_kernel(line, plane, plan_ref, count_ref, tiles_ref, *refs):
    grad_refs, refs = refs[:plane], refs[plane:]
    out_refs, (grads_ref, acc_ref, grad_sems) = refs[:-3], refs[-3:]
    rows = grad_refs[0].shape[0]
    size = tiles_ref.shape[1]
    mine, _, _, way = position(plane)
    copies = []
    for k, ref in enumerate(grad_refs):
        copy = pltpu.make_async_copy(ref, grads_ref.at[pl.ds(k * rows, rows)], grad_sems.at[k])
        copy.start()
        copies.append(copy)
    acc_ref[...] = jnp.zeros_like(acc_ref)
    for copy in copies:
        copy.wait()

    def step(i, carry):
        ready = None
        for spot, dst, src in [planned(plan_ref, i * UNROLL + j) for j in range(UNROLL)]:
            product = lax.dot_general(
                tiles_ref[block_rows(spot, size)],
                grads_ref[block_rows(dst, size)],
                (((0,), (0,)), ((), ())),
                preferred_element_type=jnp.float32,
            )
            if ready is not None:
                acc_ref[ready[0]] += ready[1]
            ready = block_rows(src, size), product
        acc_ref[ready[0]] += ready[1]
        return carry

    lax.fori_loop(0, count_ref[0], step, 0)
    for i, ref in enumerate(out_refs):
        target = mine + way * (i - (line - 1))

        @pl.when((target >= 0) & (target < line))
        def _():
            ref[...] = acc_ref[block_rows(target, rows)].astype(ref.dtype)


def spread_tiles(plan, count, tiles, grad_parts, line):
    plane = len(grad_parts)
    rows, width = grad_parts[0].shape
    kinds = [jnp.float32 if i == line - 1 else jnp.bfloat16 for i in range(2 * line - 1)]
    outs = tuple(jax.ShapeDtypeStruct((rows, width), kind) for kind in kinds)
    scratch = [
        pltpu.VMEM((plane * rows, width), jnp.bfloat16),
        pltpu.VMEM((line * rows, width), jnp.float32),
    ]
    return pl.pallas_call(
        functools.partial(spread_kernel, line, plane),
        out_shape=outs,
        in_specs=[SMEM] * 2 + [VMEM] + [ANY] * plane,
        out_specs=(VMEM,) * (2 * line - 1),
        scratch_shapes=scratch + [pltpu.SemaphoreType.DMA((plane,))],
        compiler_params=params(tiles, *outs, *scratch),
        name="spread_tiles",
    )(plan, count, tiles, *grad_parts)


def along_line(x, line, plane, cols, step, reach):
    pairs = []
    for z in range(line):
        for q in range(plane):
            for c in range(cols):
                way = 1 - 2 * (c & 1)
                to, end = z + way * step, z + way * reach
                if 0 <= to < line and 0 <= end < line:
                    pairs.append(((z * plane + q) * cols + c, (to * plane + q) * cols + c))
    return lax.ppermute(x, ("rows", "cols"), pairs)


def line_gather(x, after, line, plane, cols, lanes):
    move = lambda part, step, reach: along_line(part, line, plane, cols, step, reach)
    later, _ = lax.optimization_barrier((x, after))
    up, down = [x], [later]
    for k in range(1, line - 1):
        up.append(move(up[-1], 1, 1 - k))
        down.append(move(down[-1], -1, k - 1))
    parts, high, low = [], up[-1], down[-1]
    for part in lanes:
        first = move(high[:, part], 1, 2 - line)
        last = move(low[:, part], -1, line - 2)
        parts.append([first] + up[:0:-1] + down + [last])
    return parts


def line_sum(terms, line, plane, cols, beside):
    moved, late = {1: None, -1: None}, None
    for k in range(line - 1, 0, -1):
        for step in moved:
            term = terms[line - 1 + step * k]
            if moved[step] is not None:
                total = term.astype(jnp.float32) + moved[step].astype(jnp.float32)
                term = total.astype(term.dtype)
            moved[step] = along_line(term, line, plane, cols, step, step * k)
        if k == line - 1 and beside is not None:
            moved, beside = lax.optimization_barrier((moved, beside))
        if k > 1:
            late = tuple(moved.values())
    return [terms[line - 1], moved[1], moved[-1]], beside, late


def finish_kernel(halves, cols, mine_ref, other_ref, *refs):
    (weight_ref, out_ref), refs = refs[-2:], refs[:-2]
    col = lax.axis_index("cols")
    wide = weight_ref.shape[1]
    for c in range(cols):
        here = pl.ds(c * wide, wide)
        total = mine_ref[here].astype(jnp.float32) + other_ref[here].astype(jnp.float32)
        row = remainder(col + c, cols) * wide
        weight_ref[pl.ds(pl.multiple_of(row, wide), wide)] = total
    each = len(refs) // halves
    width = refs[0].shape[1]
    for h in range(halves):
        total = refs[h * each][...]
        for ref in refs[h * each + 1 : (h + 1) * each]:
            total += ref[...].astype(jnp.float32)
        out_ref[:, h * width : (h + 1) * width] = total.astype(out_ref.dtype)


def finish(mine, other, pieces, cols):
    flat = [piece for half in pieces for piece in half]
    rows, width = flat[0].shape
    outs = (
        jax.ShapeDtypeStruct(mine.shape, jnp.float32),
        jax.ShapeDtypeStruct((rows, width * len(pieces)), jnp.bfloat16),
    )
    return pl.pallas_call(
        functools.partial(finish_kernel, len(pieces), cols),
        out_shape=outs,
        in_specs=[VMEM] * (2 + len(flat)),
        out_specs=(VMEM, VMEM),
        compiler_params=params(mine, other, *outs, *flat),
        name="finish",
    )(mine, other, *flat)


def sum_apart(terms, first, end, rows):
    while first < end:
        other = shuffle(terms, [(r, r ^ first) for r in range(rows)])
        total = terms.astype(jnp.float32) + other.astype(jnp.float32)
        terms = total.astype(terms.dtype)
        first *= 2
    return terms


def prepare_kernel(cols, labels_ref, weight_ref, own_labels_ref, own_first_ref, wide_ref):
    col = lax.axis_index("cols")
    features = weight_ref.shape[0]
    width = features // cols
    labels = labels_ref[...] - col * width
    own_labels_ref[...] = jnp.where(labels < 0, labels + features, labels).astype(jnp.float32)
    for c in range(cols):
        row = remainder(col + c, cols) * width
        rows = weight_ref[pl.ds(pl.multiple_of(row, width), width), :]
        wide_ref[c * width : (c + 1) * width] = rows.astype(jnp.float32)
    turned = pltpu.roll(wide_ref[...], remainder(cols - col, cols) * width, axis=1)
    own_first_ref[...] = turned.astype(own_first_ref.dtype)


def prepare(labels, weight, cols):
    outs = (jax.ShapeDtypeStruct(labels.shape, jnp.float32), weight)
    wide = pltpu.VMEM(weight.shape, jnp.float32)
    return pl.pallas_call(
        functools.partial(prepare_kernel, cols),
        out_shape=(outs[0], jax.ShapeDtypeStruct(weight.shape, weight.dtype)),
        in_specs=[VMEM, VMEM],
        out_specs=(VMEM, VMEM),
        scratch_shapes=[wide],
        compiler_params=params(weight, weight, wide, wide),
        name="prepare",
    )(labels, weight)


def per_device(node_features, weight, tile_values, tile_row, source_owner, source_block, labels):
    local_rows, width = node_features.shape
    n_tiles, block_size = tile_values.shape[:2]
    blocks = local_rows // block_size
    rows, cols = lax.axis_size("rows"), lax.axis_size("cols")
    plane = math.gcd(rows, LARGEST_PLANE)
    line = rows // plane
    halves = 2 if width % 256 == 0 else 1
    part_width = width // halves
    slots = -(-min(n_tiles, line * (2 * n_tiles // rows)) // cols)
    owners = source_owner[:, 0]

    def other_cols(x):
        return [
            lax.ppermute(x, "cols", [((c + k) % cols, c) for c in range(cols)])
            for k in range(1, cols)
        ]

    lanes = [slice(h * part_width, (h + 1) * part_width) for h in range(halves)]
    *packed, codes = pack_tiles(
        owners, tile_row, source_block, tile_values, plane, cols, slots
    )
    node_parts = line_gather(node_features, packed, line, plane, cols, lanes)
    spots = n_tiles + (plane - 1) * cols * slots + 1
    flat = tile_values.reshape(n_tiles * block_size, block_size)
    early = own_tiles(flat, codes, spots) + prepare(labels.reshape(blocks, block_size), weight, cols)
    tile_parts = []
    for k in range(1, plane):
        arrived = across_plane(packed[k - 1], k, line, plane)
        if k == 1:
            arrived, early = lax.optimization_barrier((arrived, early))
        tile_parts += [arrived] + other_cols(arrived)
    laid, codes, own_labels, own_first = early
    tiles, plan, count = collect_tiles(
        codes, laid, tile_parts, plane, cols, slots, blocks, n_tiles
    )

    aggregated = []
    for h in range(halves):
        here = pl.ds(h * part_width, part_width)
        sums = forward_tiles(plan, count, tiles, node_parts[h], plane, here)
        total = sums[0]
        for k in range(1, plane):
            total = total + across_plane(sums[k], k, line, plane).astype(jnp.float32)
        mine = total.astype(jnp.bfloat16)
        aggregated.append([mine] + other_cols(mine))
    parts = [aggregated[h][c] for c in range(cols) for h in range(halves)]

    activations, out_grad, agg_grad = dense(own_labels, own_first, parts, halves)
    weight_terms, *agg_grads = grads(own_first, out_grad, parts, halves, local_rows * rows)

    pieces = []
    for i, agg_grad in enumerate([agg_grad] + agg_grads):
        arrived = [agg_grad] + [across_plane(agg_grad, k, line, plane) for k in range(1, plane)]
        if i == 0:
            weight_terms = sum_apart(weight_terms, plane, 2 * plane, rows)
            arrived[-1], weight_terms = lax.optimization_barrier((arrived[-1], weight_terms))
            weight_terms = sum_apart(weight_terms, 2 * plane, rows, rows)
        terms = spread_tiles(plan, count, tiles, arrived, line)
        beside = weight_terms if i == 0 else None
        half, beside, late = line_sum(terms, line, plane, cols, beside)
        if i == 0:
            weight_terms, _ = lax.optimization_barrier((beside, late))
        pieces.append(half)
    weight_terms = sum_apart(weight_terms, 1, plane // 2, rows)
    weight_terms, _ = lax.optimization_barrier((weight_terms, late))
    other = across_plane(weight_terms, plane // 2, line, plane)
    return (activations,) + tuple(finish(weight_terms, other, pieces, cols))


def solution(mesh):
    return jax.shard_map(
        per_device,
        mesh=mesh,
        in_specs=(
            P("rows", "cols"),
            P(),
            P("rows", None, None),
            P("rows"),
            P("rows", None),
            P("rows"),
            P("rows"),
        ),
        out_specs=(P("rows", "cols"), P(None, "cols"), P("rows", "cols")),
        check_vma=False,
    )
```
